32 devices in a mesh: seq: 8 (over y, x, core), head: 4 (over z).
Axes of the slice: x: 2, y: 2, z: 4, core: 2. Of those that a mesh axis runs over, the one named last changes fastest.
Arguments:
- inputs: bfloat16 [8192, 1024], P('seq', 'head'), may hold values from -6 to 6
- cotangent: bfloat16 [8192, 1024], P('seq', 'head'), may hold values from -6 to 6
- lengths: int32 [4], replicated, may hold values from 128 to 7424, as said below
- placement: int32 [64], replicated, may hold values from 0 to 63, as said below
- prenorm: float32 [1024], replicated, may hold values from 0.5 to 1.5
- gating: float32 [1024, 2048], P('seq', 'head'), may hold values from -0.1875 to 0.1875
- payload: float32 [1024, 2048], P('seq', 'head'), may hold values from -0.1875 to 0.1875
- address: float32 [1024, 256], P('seq'), may hold values from -0.1875 to 0.1875
- stepping: float32 [1024, 32], P('seq', 'head'), may hold values from -0.1875 to 0.1875
- kernels: float32 [4, 2048], P(None, 'head'), may hold values from -3 to 3
- offsets: float32 [2048], P('head'), may hold values from -3 to 3
- filters: float32 [4, 256], replicated, may hold values from -3 to 3
- shifts: float32 [256], replicated, may hold values from -3 to 3
- stepbias: float32 [32], P('head'), may hold values from -14 to -2.5
- decays: float32 [32], P('head'), may hold values from -0.7 to 0
- through: float32 [32], P('head'), may hold values from 0.1 to 1.9
- postnorm: float32 [2048], P('head'), may hold values from 0.5 to 1.5
- readout: float32 [2048, 1024], P('head', 'seq'), may hold values from -0.125 to 0.125
Outputs:
- outputs: bfloat16 [8192, 1024], P('seq', 'head')
- inputs_grad: bfloat16 [8192, 1024], P('seq', 'head')
- prenorm_grad: float32 [1024], P('head')
- gating_grad: float32 [1024, 2048], P('seq', 'head')
- payload_grad: float32 [1024, 2048], P('seq', 'head')
- address_grad: float32 [1024, 256], P('seq', 'head')
- stepping_grad: float32 [1024, 32], P('seq', 'head')
- kernels_grad: float32 [4, 2048], P(None, 'head')
- offsets_grad: float32 [2048], P('head')
- filters_grad: float32 [4, 256], P(None, 'head')
- shifts_grad: float32 [256], P('head')
- stepbias_grad: float32 [32], P('head')
- decays_grad: float32 [32], P('head')
- through_grad: float32 [32], P('head')
- postnorm_grad: float32 [2048], P('head')
- readout_grad: float32 [2048, 1024], P('head', 'seq')
The draws below stay inside these ranges and needn't reach their ends.
Inputs may be any that keep to these rules, and one draw needn't show every extreme that they name: `lengths`: each length is a multiple of 128; they sum to 8192; exactly one sequence has the largest length. `placement`: A permutation of the blocks: block k of a device's working rows is block k of some device's given rows, and the blocks of one device's given rows go to different devices.
All inputs are finite; a program needn't handle non-finite values.
Results may differ from the reference program's by a relative error of at most 0.02.
Values may be sent and summed in bfloat16 or wider, within the bound.
A program may use at most 256 MiB of HBM per device.

```python
import jax
import jax.numpy as jnp
from jax import lax

D = 1024
HEADS = 32
HDIM = 64
STATE = 128
KCONV = 4
GROUP = 256
BLOCK = 128
SEQS = 4
TOK_DEV = 1024
INNER = 2048
TOKENS = 8192


def draw_lengths(key, part):
    key = jax.random.fold_in(key, 11)
    first_key, second_key = jax.random.split(key)
    blocks_dev = TOK_DEV // BLOCK
    upper = max(1, (blocks_dev - 1) // (SEQS - 1))
    spare_count = (SEQS - 1) * (upper - 1)
    spare_bins = jax.random.randint(first_key, (spare_count,), 0, SEQS - 1).astype(jnp.int32)
    bin_ids = jnp.arange(SEQS - 1, dtype=jnp.int32)
    extra = jnp.sum((spare_bins[:, None] == bin_ids[None, :]).astype(jnp.int32), axis=0)
    others = (1 + extra).astype(jnp.int32)
    longest_slot = jax.random.randint(second_key, (), 0, SEQS).astype(jnp.int32)
    longest = jnp.int32(TOKENS // BLOCK - (SEQS - 1) * upper)
    slots = jnp.arange(SEQS, dtype=jnp.int32)
    before_list = jnp.concatenate([others, jnp.zeros((1,), jnp.int32)])
    after_list = jnp.concatenate([jnp.zeros((1,), jnp.int32), others])
    counts = jnp.where(slots < longest_slot, before_list, jnp.where(slots == longest_slot, longest, after_list))
    return (counts * BLOCK).astype(jnp.int32)


def draw_placement(key, part):
    key = jax.random.fold_in(key, 23)
    blocks_dev = TOK_DEV // BLOCK
    devices = TOKENS // TOK_DEV
    offsets_drawn = jax.random.permutation(key, devices)[:blocks_dev].astype(jnp.int32)
    device_index = jnp.arange(devices, dtype=jnp.int32)[:, None]
    slot_index = jnp.arange(blocks_dev, dtype=jnp.int32)[None, :]
    source = (device_index - offsets_drawn[None, :]) % devices
    return (source * blocks_dev + slot_index).reshape(-1).astype(jnp.int32)


def draw_stepbias(key, part):
    key = jax.random.fold_in(key, 37)
    first_key, second_key, third_key = jax.random.split(key, 3)
    share = 0.5
    slow = jax.random.bernoulli(first_key, share, (HEADS,))
    slow_step = 0.3 / TOKENS * jax.random.uniform(second_key, (HEADS,), jnp.float32, 0.5, 1.5)
    fast_step = jnp.exp(jax.random.uniform(third_key, (HEADS,), jnp.float32, jnp.log(0.005), jnp.log(0.05)))
    target = jnp.where(slow, slow_step, fast_step).astype(jnp.float32)
    return jnp.log(jnp.expm1(target)).astype(jnp.float32)


def levels(stream_key, extent, cuts, low, largest):
    def one(dim, blocks):
        heights = jax.random.uniform(jax.random.fold_in(jax.random.fold_in(stream_key, 6), dim), (blocks,), jnp.float32, low / len(cuts), largest / len(cuts))
        return jnp.repeat(jnp.exp(heights), extent[dim] // blocks).reshape((-1,) + (1,) * (len(extent) - dim - 1))

    level = one(*cuts[0])
    for cut in cuts[1:]:
        level = level * one(*cut)
    return level


def normal_values(rng, extent, scale, bound, cuts=(), held_as=jnp.bfloat16):
    level = levels(rng, extent, cuts, -0.22, 0.18) if cuts else 1.0
    values = jax.random.normal(rng, extent, jnp.float32) * scale * level
    return jnp.minimum(jnp.maximum(values, -bound), bound).astype(held_as)


def setup_inputs(seed: int = 0) -> dict:
    key_of = jax.random.split(jax.random.key(seed), 19)
    inputs = normal_values(key_of[0], (TOKENS, D), 1.0, 6.0, ((0, 8), (1, 4)))
    cotangent = normal_values(key_of[1], (TOKENS, D), 1.0, 6.0, ((0, 8), (1, 4)))
    lengths = draw_lengths(jax.random.fold_in(key_of[18], 71), 0)
    placement = draw_placement(jax.random.fold_in(key_of[18], 71), 0)
    prenorm = jnp.clip(1.0 + 0.1 * jax.random.normal(key_of[4], (D,), jnp.float32), 0.5, 1.5)
    gating = normal_values(key_of[5], (D, INNER), D ** -0.5, 0.1875, ((0, 8), (1, 4)), jnp.float32)
    payload = normal_values(key_of[6], (D, INNER), D ** -0.5, 0.1875, ((0, 8), (1, 4)), jnp.float32)
    address = normal_values(key_of[7], (D, 2 * STATE), D ** -0.5, 0.1875, ((0, 8),), jnp.float32)
    stepping = normal_values(key_of[8], (D, HEADS), D ** -0.5, 0.1875, ((0, 8), (1, 4)), jnp.float32)
    kernels = normal_values(key_of[9], (KCONV, INNER), KCONV ** -0.5, 3.0, ((1, 4),), jnp.float32)
    offsets = normal_values(key_of[10], (INNER,), 0.5, 3.0, ((0, 4),), jnp.float32)
    filters = normal_values(key_of[11], (KCONV, 2 * STATE), KCONV ** -0.5, 3.0, (), jnp.float32)
    shifts = normal_values(key_of[12], (2 * STATE,), 0.5, 3.0, (), jnp.float32)
    stepbias = draw_stepbias(jax.random.fold_in(key_of[18], 71), 0)
    decays = jnp.clip(-0.7 + 0.7 * jax.random.uniform(key_of[14], (HEADS,), jnp.float32) ** levels(key_of[14], (HEADS,), ((0, 4),), -0.2, 0.2), -0.7, 0.0)
    through = jnp.clip(1.0 + 0.18 * jax.random.normal(key_of[15], (HEADS,), jnp.float32), 0.1, 1.9)
    postnorm = jnp.clip(1.0 + 0.1 * jax.random.normal(key_of[16], (INNER,), jnp.float32), 0.5, 1.5)
    readout = normal_values(key_of[17], (INNER, D), INNER ** -0.5, 0.125, ((0, 4), (1, 8)), jnp.float32)
    return {"inputs": inputs, "cotangent": cotangent, "lengths": lengths, "placement": placement, "prenorm": prenorm, "gating": gating, "payload": payload, "address": address, "stepping": stepping, "kernels": kernels, "offsets": offsets, "filters": filters, "shifts": shifts, "stepbias": stepbias, "decays": decays, "through": through, "postnorm": postnorm, "readout": readout}


EPS = 1e-05
HIGH = lax.Precision.HIGHEST

@jax.custom_vjp
def low(v):
    return lax.optimization_barrier(v.astype(jnp.bfloat16)).astype(jnp.float32)

@jax.custom_vjp
def low_back(v):
    return v

def low_keep(v):
    return (low(v), None)

def low_pass(kept, grad):
    return (grad,)

def back_keep(v):
    return (v, None)

def back_low(kept, grad):
    return (low(grad),)
low.defvjp(low_keep, low_pass)
low_back.defvjp(back_keep, back_low)

def segment_of(position, seq_ends):
    counted = lax.optimization_barrier(jnp.sum((position[:, None] >= seq_ends[None, :]).astype(jnp.int32), axis=1))
    return jnp.where(position < 0, -1, counted).astype(jnp.int32)

def conv_apply(extended, weights, bias, conv_mask):
    tap_count = weights.shape[0]
    row_count = extended.shape[0] - tap_count + 1
    total_sum = jnp.broadcast_to(bias[None, :], (row_count, extended.shape[1]))
    for tap_index in range(tap_count):
        total_sum = total_sum + weights[tap_index][None, :] * extended[tap_index:tap_index + row_count] * conv_mask[:, tap_index:tap_index + 1]
    return jax.nn.silu(total_sum)

def decay_terms(step_sizes, scale_rate, segment, previous):
    block_len = step_sizes.shape[0]
    cumul_rate = jnp.cumsum(step_sizes * scale_rate[None, :], axis=0)
    index_row = jnp.arange(block_len)
    causal = (index_row[:, None] >= index_row[None, :]) & (segment[:, None] == segment[None, :])
    spread = cumul_rate.T[:, :, None] - cumul_rate.T[:, None, :]
    inside = jnp.where(causal[None], spread, 0.0)
    lower_mask = jnp.where(causal[None], jnp.exp(inside), 0.0) * step_sizes.T[:, None, :]
    entry_decay = jnp.exp(cumul_rate) * (segment == previous).astype(cumul_rate.dtype)[:, None]
    final_mask = (segment == segment[block_len - 1]).astype(cumul_rate.dtype)
    weight = step_sizes * jnp.exp(cumul_rate[block_len - 1][None, :] - cumul_rate) * final_mask[:, None]
    carry_decay = jnp.exp(cumul_rate[block_len - 1]) * (segment[block_len - 1] == previous).astype(cumul_rate.dtype)
    return (lower_mask, entry_decay, weight, carry_decay)

def reference(inputs, cotangent, lengths, placement, prenorm, gating, payload, address, stepping, kernels, offsets, filters, shifts, stepbias, decays, through, postnorm, readout):
    blocks = placement.shape[0]
    total_rows = inputs.shape[0]
    feature_width = inputs.shape[1]
    block_rows = total_rows // blocks
    working = inputs.reshape(blocks, block_rows, feature_width)[placement].reshape(total_rows, feature_width).astype(jnp.float32)
    upstream = cotangent.reshape(blocks, block_rows, feature_width)[placement].reshape(total_rows, feature_width).astype(jnp.float32)
    seq_ends = jnp.cumsum(lengths)
    tap_count = kernels.shape[0]
    position = jnp.arange(-(tap_count - 1), total_rows, dtype=jnp.int32)
    seg_ext = segment_of(position, seq_ends)
    segment = seg_ext[tap_count - 1:]
    conv_mask = jnp.stack([(seg_ext[tap_index:tap_index + total_rows] == segment).astype(jnp.float32) for tap_index in range(tap_count)], axis=1)
    block_len = min(GROUP, TOK_DEV)
    block_count = total_rows // block_len
    group_seg = segment.reshape(block_count, block_len)
    previous = seg_ext[tap_count - 2:tap_count - 2 + total_rows:block_len]
    params = (prenorm, gating, payload, address, stepping, kernels, offsets, filters, shifts, stepbias, decays, through, postnorm, readout)

    def forward(rows_in, weights):
        gain_outer, w_gate, w_pay, w_addr, w_step, conv_value, bias_value, conv_state, bias_state, step_bias, decay_log, skip_gain, gain_inner, w_read = weights
        inv_rms = lax.rsqrt(lax.optimization_barrier(jnp.mean(rows_in * rows_in, axis=1, keepdims=True)) + EPS)
        normed = low(rows_in * inv_rms * gain_outer[None, :])
        gate_pre = low_back(jnp.dot(normed, low(w_gate), precision=HIGH))
        value_pre = low(low_back(jnp.dot(normed, low(w_pay), precision=HIGH)))
        addr_pre = low(low_back(jnp.dot(normed, low(w_addr), precision=HIGH)))
        step_pre = low_back(jnp.dot(normed, low(w_step), precision=HIGH))
        value_ext = jnp.concatenate([jnp.zeros((tap_count - 1, value_pre.shape[1]), jnp.float32), value_pre], axis=0)
        addr_ext = jnp.concatenate([jnp.zeros((tap_count - 1, addr_pre.shape[1]), jnp.float32), addr_pre], axis=0)
        values = low(conv_apply(value_ext, conv_value, bias_value, conv_mask)).reshape(block_count, block_len, HEADS, HDIM)
        addr_conv = low(conv_apply(addr_ext, conv_state, bias_state, conv_mask))
        write_rows = addr_conv[:, :STATE].reshape(block_count, block_len, STATE)
        read_rows = addr_conv[:, STATE:].reshape(block_count, block_len, STATE)
        step_sizes = jax.nn.softplus(step_pre + step_bias[None, :]).reshape(block_count, block_len, HEADS)
        scale_rate = -jnp.exp(decay_log)

        def group_step(state, item):
            group_values, group_write, group_read, group_steps, group_segment, group_prev = item
            lower_mask, entry_decay, weight, carry_decay = decay_terms(group_steps, scale_rate, group_segment, group_prev)
            scores = low_back(jnp.einsum('tn,sn->ts', group_read, group_write, precision=HIGH))
            mixing = low(scores[None] * lower_mask)
            intra_out = jnp.einsum('hts,shp->thp', mixing, group_values, precision=HIGH)
            queried = low_back(jnp.einsum('tn,hpn->thp', group_read, low(state), precision=HIGH))
            mixed_out = intra_out + entry_decay[:, :, None] * queried + skip_gain[None, :, None] * group_values
            packed = low(group_values * weight[:, :, None])
            local_state = low_back(jnp.einsum('shp,sn->hpn', packed, group_write, precision=HIGH))
            return (carry_decay[:, None, None] * state + local_state, mixed_out)
        start_state = jnp.zeros((HEADS, HDIM, STATE), jnp.float32)
        _, mixed_all = lax.scan(jax.checkpoint(group_step), start_state, (values, write_rows, read_rows, step_sizes, group_seg, previous))
        ssd_out = low_back(mixed_all.reshape(total_rows, INNER))
        gated_rows = ssd_out * jax.nn.silu(gate_pre)
        inv_inner = lax.rsqrt(lax.optimization_barrier(jnp.mean(gated_rows * gated_rows, axis=1, keepdims=True)) + EPS)
        normed_inner = low(gated_rows * inv_inner * gain_inner[None, :])
        return rows_in + jnp.dot(normed_inner, low(w_read), precision=HIGH)
    result, pullback = jax.vjp(forward, working, params)
    grad_rows, grad_params = pullback(upstream)

    def to_given(rows_work):
        shaped = rows_work.reshape(blocks, block_rows, feature_width)
        return jnp.zeros_like(shaped).at[placement].set(shaped).reshape(total_rows, feature_width).astype(jnp.bfloat16)
    return (to_given(result), to_given(grad_rows), grad_params[0], grad_params[1], grad_params[2], grad_params[3], grad_params[4], grad_params[5], grad_params[6], grad_params[7], grad_params[8], grad_params[9], grad_params[10], grad_params[11], grad_params[12], grad_params[13])
```

```python
import functools

import jax
import jax.numpy as jnp
from jax import lax
from jax.experimental import pallas as pl
from jax.experimental.pallas import tpu as pltpu
from jax.sharding import PartitionSpec as P

D = 1024
GROUP = 256
BLOCK = 128
INNER = 2048
HALO = 16
LANES = 128
MESH = pl.DeviceIdType.MESH
VMEM = pltpu.MemorySpace.VMEM
SMEM = pltpu.MemorySpace.SMEM
DMA = pltpu.SemaphoreType.DMA
MIB = 1 << 20


def greet(seq_peers, head_peers):
    barrier = pltpu.get_barrier_semaphore()
    count = 0
    if seq_peers > 1:
        me = lax.axis_index("seq")

        @pl.loop(1, seq_peers)
        def _(i):
            pl.semaphore_signal(
                barrier, inc=1, device_id={"seq": lax.rem(me + i, seq_peers)}, device_id_type=MESH
            )

        count += seq_peers - 1
    if head_peers > 1:
        mine = lax.axis_index("head")

        @pl.loop(1, head_peers)
        def _(i):
            pl.semaphore_signal(
                barrier, inc=1, device_id={"head": lax.rem(mine + i, head_peers)}, device_id_type=MESH
            )

        count += head_peers - 1
    pl.semaphore_wait(barrier, count)


def remote(src, dst, send_sem, recv_sem, where):
    return pltpu.make_async_remote_copy(
        src_ref=src, dst_ref=dst, send_sem=send_sem, recv_sem=recv_sem, device_id=where, device_id_type=MESH
    )


class Line:
    def __init__(self, count, out, width, send, recv):
        self.count, self.out, self.width, self.send, self.recv = count, out, width, send, recv
        self.me = lax.axis_index("head")

    def view(self, shard):
        return self.out.at[:, pl.ds(pl.multiple_of(shard * self.width, LANES), self.width)]

    def copy(self, src, shard, way, step):
        return remote(
            src, self.view(shard), self.send.at[way, step], self.recv.at[shard], {"head": self.me + (1 - 2 * way)}
        )

    def first(self, own):
        self.pass_on(own, self.me, 0, 0)
        self.pass_on(own, self.me, 1, 0)

    def pass_on(self, src, shard, way, step):
        reach = (self.me < self.count - 1) if way == 0 else (self.me > 0)

        @pl.when(reach)
        def _():
            self.copy(src, shard, way, step).start()

    def hop(self, step):
        for way in (0, 1):
            shard = self.me - step if way == 0 else self.me + step
            there = (shard >= 0) if way == 0 else (shard < self.count)

            @pl.when(there)
            def _():
                self.copy(self.view(shard), shard, way, step).wait_recv()
                if step < self.count - 1:
                    self.pass_on(self.view(shard), shard, way, step)

    def finish(self, own):
        for way in (0, 1):
            reach = (self.me < self.count - 1) if way == 0 else (self.me > 0)
            for step in range(self.count - 1):
                shard = self.me - step if way == 0 else self.me + step
                there = (shard >= 0) if way == 0 else (shard < self.count)

                @pl.when(reach & there)
                def _():
                    src = own if step == 0 else self.view(shard)
                    self.copy(src, shard, way, step).wait_send()


def spread_kernel(
    seqs, heads, give, take, x, g, gating, payload, address, stepping, readout,
    x_out, g_out, w_out, r_out,
    send_x, send_g, recv_x, recv_g, work_x, work_g, w_own, r_own,
    sent, got, w_sent, w_got, r_sent, r_got, rim_sent, rim_got, own_sem,
    x_line_sent, x_line_got, g_line_sent, g_line_got,
):
    me, mine = lax.axis_index("seq"), lax.axis_index("head")
    blocks, _, width = x.shape
    rows = blocks * BLOCK
    depth = gating.shape[0]
    inner = gating.shape[1]
    greet(seqs, heads)

    @pl.loop(0, seqs)
    def _(i):
        to = lax.rem(me + i, seqs)
        send_x[to] = x[give[to]]
        send_g[to] = g[give[to]]

        @pl.when(i == 0)
        def _():
            recv_x[to] = x[give[to]]
            recv_g[to] = g[give[to]]

        @pl.when(i > 0)
        def _():
            remote(send_x.at[to], recv_x.at[me], sent.at[0, to], got.at[0, me], {"seq": to}).start()

    w_own[:, :inner] = gating[...].astype(jnp.bfloat16)
    w_own[:, inner : 2 * inner] = payload[...].astype(jnp.bfloat16)
    state2 = address.shape[1]
    w_own[:, 2 * inner : 2 * inner + state2] = address[...].astype(jnp.bfloat16)
    w_own[:, 2 * inner + state2 :] = jnp.zeros((depth, LANES), jnp.bfloat16)
    w_own[:, 2 * inner + state2 : 2 * inner + state2 + stepping.shape[1]] = stepping[...].astype(jnp.bfloat16)
    r_own[...] = readout[...].T.astype(jnp.bfloat16)

    def rows_of(device):
        return pl.ds(pl.multiple_of(device * depth, depth), depth)

    def shard_copy(own, out, send, recv, to):
        return remote(own, out.at[rows_of(me)], send.at[to], recv.at[me], {"seq": to})

    own_w = pltpu.make_async_copy(w_own, w_out.at[rows_of(me)], own_sem.at[0])
    own_r = pltpu.make_async_copy(r_own, r_out.at[rows_of(me)], own_sem.at[1])
    own_w.start()
    own_r.start()

    @pl.loop(1, seqs)
    def _(i):
        to = lax.rem(me + i, seqs)
        shard_copy(w_own, w_out, w_sent, w_got, to).start()
        remote(send_g.at[to], recv_g.at[me], sent.at[1, to], got.at[1, me], {"seq": to}).start()

    @pl.loop(1, seqs)
    def _(i):
        shard_copy(r_own, r_out, r_sent, r_got, lax.rem(me + i, seqs)).start()

    def arrange(which, received, work):
        @pl.loop(1, seqs)
        def _(i):
            source = lax.rem(me + i, seqs)
            remote(received.at[source], received.at[source], sent.at[which, source], got.at[which, source], {"seq": source}).wait_recv()

        for k in range(blocks):
            work[pl.ds(k * BLOCK, BLOCK), :] = received[take[k]]

    arrange(0, recv_x, work_x)
    after = lax.rem(me + 1, seqs)
    rim = remote(work_x.at[pl.ds(rows - HALO, HALO)], work_x.at[pl.ds(rows, HALO)], rim_sent, rim_got, {"seq": after})
    rim.start()
    rim.wait()
    x_line = Line(heads, x_out, width, x_line_sent, x_line_got)
    g_line = Line(heads, g_out, width, g_line_sent, g_line_got)
    own_x = pltpu.make_async_copy(work_x, x_line.view(mine), own_sem.at[2])
    own_x.start()
    x_line.first(work_x)
    arrange(1, recv_g, work_g)
    own_g = pltpu.make_async_copy(work_g, g_line.view(mine), own_sem.at[3])
    own_g.start()
    for step in range(1, heads):
        x_line.hop(step)
        if step == 1:
            g_line.first(work_g)
    for step in range(1, heads):
        g_line.hop(step)
    x_line.finish(work_x)
    g_line.finish(work_g)
    for copy in (own_w, own_r, own_x, own_g):
        copy.wait()

    @pl.loop(1, seqs)
    def _(i):
        other = lax.rem(me + i, seqs)
        for which, buffer in ((0, send_x), (1, send_g)):
            remote(buffer.at[other], buffer.at[other], sent.at[which, other], got.at[which, other], {"seq": other}).wait_send()
        for own, out, send, recv in ((w_own, w_out, w_sent, w_got), (r_own, r_out, r_sent, r_got)):
            copy = remote(own, out.at[rows_of(other)], send.at[other], recv.at[other], {"seq": other})
            copy.wait_send()
            copy.wait_recv()


def spread(give, take, x, g, gating, payload, address, stepping, readout):
    seqs, heads = lax.axis_size("seq"), lax.axis_size("head")
    rows, width = x.shape
    depth, inner = gating.shape
    total = depth * seqs
    columns = 2 * inner + address.shape[1] + LANES
    low = jnp.bfloat16
    block = (seqs, BLOCK, width)
    any_space = pl.BlockSpec(memory_space=pl.ANY)
    vmem = pl.BlockSpec(memory_space=VMEM)
    return pl.pallas_call(
        functools.partial(spread_kernel, seqs, heads),
        out_shape=(
            jax.ShapeDtypeStruct((rows + HALO, total), low),
            jax.ShapeDtypeStruct((rows, total), low),
            jax.ShapeDtypeStruct((total, columns), low),
            jax.ShapeDtypeStruct((total, inner), low),
        ),
        in_specs=[pl.BlockSpec(memory_space=SMEM)] * 2 + [vmem] * 7,
        out_specs=(any_space,) * 4,
        scratch_shapes=[
            pltpu.VMEM(block, low), pltpu.VMEM(block, low), pltpu.VMEM(block, low), pltpu.VMEM(block, low),
            pltpu.VMEM((rows + HALO, width), low), pltpu.VMEM((rows, width), low),
            pltpu.VMEM((depth, columns), low), pltpu.VMEM((depth, inner), low),
            DMA((2, seqs)), DMA((2, seqs)), DMA((seqs,)), DMA((seqs,)), DMA((seqs,)), DMA((seqs,)),
            DMA, DMA, DMA((4,)),
            DMA((2, heads)), DMA((heads,)), DMA((2, heads)), DMA((heads,)),
        ],
        compiler_params=pltpu.CompilerParams(
            collective_id=0, has_side_effects=True, vmem_limit_bytes=48 * MIB
        ),
        name="spread",
    )(give, take, x.reshape(-1, BLOCK, width), g.reshape(-1, BLOCK, width), gating, payload, address, stepping, readout)


EPS = 1e-05


def from_behind(value, axis, steps):
    count = lax.axis_size(axis)
    leading, last = (max(0, -steps), min(count, count - steps))
    return lax.ppermute(value, axis, [(source, source + steps) for source in range(leading, last)])


def carried_in(x, axis, combine, identity):
    length, mine = (lax.axis_size(axis), lax.axis_index(axis))
    everything = jax.tree.map(
        lambda part, kind: lax.all_gather(part.astype(kind), axis),
        x,
        jax.tree.map(lambda a: jnp.bfloat16 if a.dtype == jnp.float32 else a.dtype, x),
    )
    start = jax.tree.map(
        lambda part, zero: jnp.broadcast_to(jnp.asarray(zero, part.dtype), part.shape), x, identity
    )

    def hop(k, before):
        reached = k < mine
        new = combine(
            before, jax.tree.map(lambda part, own: part[k].astype(own.dtype), everything, x)
        )
        return jax.tree.map(lambda a, b: jnp.where(reached, a, b), new, before)

    return lax.fori_loop(0, length, hop, start)


def prefix(part, axis, combine, identity):
    count = lax.axis_size(axis)
    place = lax.axis_index(axis)
    ahead = count - 1 - place
    gathered = jax.tree.map(lambda a: lax.all_gather(a, axis), part)
    state = jax.tree.map(lambda a, e: jnp.zeros_like(a) + jnp.asarray(e, a.dtype), part, identity)

    def one(hop, state):
        source = count - 1 - hop
        return combine(
            state, jax.tree.map(lambda a: lax.dynamic_index_in_dim(a, source, 0, False), gathered)
        )

    return lax.fori_loop(0, ahead, one, state)


def segment_of(position, seq_ends):
    counted = jnp.sum((position[:, None] >= seq_ends[None, :]).astype(jnp.int32), axis=1)
    return jnp.where(position < 0, -1, counted)


def conv_apply(extended, weights, bias, conv_mask):
    tap_count = weights.shape[0]
    row_count = extended.shape[0] - tap_count + 1
    total_sum = jnp.broadcast_to(bias[None, :], (row_count, extended.shape[1]))
    for tap_index in range(tap_count):
        total_sum = (
            total_sum
            + weights[tap_index][None, :]
            * extended[tap_index : tap_index + row_count]
            * conv_mask[:, tap_index : tap_index + 1]
        )
    return jax.nn.silu(total_sum)


def decay_terms(step_sizes, scale_rate, segment, previous):
    block_len = step_sizes.shape[0]
    cumul_rate = jnp.cumsum(step_sizes * scale_rate[None, :], axis=0)
    index_row = jnp.arange(block_len)
    causal = (index_row[:, None] >= index_row[None, :]) & (segment[:, None] == segment[None, :])
    spread = cumul_rate.T[:, :, None] - cumul_rate.T[:, None, :]
    inside = jnp.where(causal[None], spread, 0.0)
    lower_mask = jnp.where(causal[None], jnp.exp(inside), 0.0) * step_sizes.T[:, None, :]
    entry_decay = jnp.exp(cumul_rate) * (segment == previous).astype(cumul_rate.dtype)[:, None]
    final_mask = (segment == segment[block_len - 1]).astype(cumul_rate.dtype)
    weight = (
        step_sizes * jnp.exp(cumul_rate[block_len - 1][None, :] - cumul_rate) * final_mask[:, None]
    )
    carry_decay = jnp.exp(cumul_rate[block_len - 1]) * (segment[block_len - 1] == previous).astype(
        cumul_rate.dtype
    )
    return (lower_mask, entry_decay, weight, carry_decay)


def combine(earlier, subsequent):
    return (earlier[0] * subsequent[0], subsequent[0][:, None, None] * earlier[1] + subsequent[1])


def fold_block(summary, item):
    return (combine(summary, item), None)


def walk_blocks(state, item):
    return (item[0][:, None, None] * state + item[1], state)


def route_blocks(block_data, owners, devices, block_size):
    shaped = block_data.reshape(owners.shape[0], block_size, block_data.shape[1])
    onehot_table = (devices[:, None] == owners[None, :]).astype(jnp.bfloat16)
    return jnp.einsum(
        "nk,kbf->nbf", onehot_table, shaped, preferred_element_type=jnp.float32
    ).astype(jnp.bfloat16)


def pick_blocks(arrived, owners, devices):
    onehot_table = (owners[:, None] == devices[None, :]).astype(jnp.bfloat16)
    taken_rows = jnp.einsum(
        "kn,nbf->kbf", onehot_table, arrived, preferred_element_type=jnp.float32
    ).astype(jnp.bfloat16)
    return taken_rows.reshape(-1, arrived.shape[2])


def on_device(
    inputs,
    cotangent,
    lengths,
    placement,
    prenorm,
    gating,
    payload,
    address,
    stepping,
    kernels,
    offsets,
    filters,
    shifts,
    stepbias,
    decays,
    through,
    postnorm,
    readout,
):
    seq_count = lax.axis_size("seq")
    seq_index = lax.axis_index("seq")
    head_index = lax.axis_index("head")
    row_count = inputs.shape[0]
    per_dev = row_count // BLOCK
    block_ids = seq_index * per_dev + jnp.arange(per_dev, dtype=jnp.int32)
    every_block = jnp.arange(placement.shape[0], dtype=jnp.int32)
    target = jnp.sum(
        jnp.where(placement[None, :] == block_ids[:, None], every_block[None, :], 0), axis=1
    )
    target_dev = target // per_dev
    source_dev = lax.dynamic_slice_in_dim(placement, seq_index * per_dev, per_dev, 0) // per_dev
    devices = jnp.arange(seq_count, dtype=jnp.int32)
    local_block = jnp.arange(per_dev, dtype=jnp.int32)
    give = jnp.sum(jnp.where(target_dev[None, :] == devices[:, None], local_block[None, :], 0), axis=1)
    x_rows, g_full, w_all, w_read_t = spread(
        give, source_dev, inputs, cotangent, gating, payload, address, stepping, readout
    )
    x_full = x_rows[:row_count]
    share = inputs.shape[1]
    x_local = lax.dynamic_slice_in_dim(x_full, head_index * share, share, 1)
    g_local = lax.dynamic_slice_in_dim(g_full, head_index * share, share, 1)
    w_read = w_read_t.T
    inner_width = gating.shape[1]
    w_gate, w_pay = w_all[:, :inner_width], w_all[:, inner_width : 2 * inner_width]
    addr_end = 2 * inner_width + address.shape[1]
    w_addr, w_step = w_all[:, 2 * inner_width : addr_end], w_all[:, addr_end : addr_end + stepping.shape[1]]
    u_full = x_full.astype(jnp.float32)
    inv_rms = lax.rsqrt(jnp.mean(u_full * u_full, axis=1, keepdims=True) + EPS)
    normed = (u_full * inv_rms * prenorm[None, :]).astype(jnp.bfloat16)
    gate_pre = jnp.dot(normed, w_gate, preferred_element_type=jnp.float32)
    value_pre = jnp.dot(normed, w_pay, preferred_element_type=jnp.float32).astype(jnp.bfloat16)
    addr_pre = jnp.dot(normed, w_addr, preferred_element_type=jnp.float32).astype(jnp.bfloat16)
    step_pre = jnp.dot(normed, w_step, preferred_element_type=jnp.float32)
    seq_ends = jnp.cumsum(lengths)
    tap_count = kernels.shape[0]
    position = seq_index * row_count + jnp.arange(-(tap_count - 1), row_count, dtype=jnp.int32)
    seg_ext = segment_of(position, seq_ends)
    segment = seg_ext[tap_count - 1 :]
    conv_mask = jnp.stack(
        [
            (seg_ext[tap_index : tap_index + row_count] == segment).astype(jnp.float32)
            for tap_index in range(tap_count)
        ],
        axis=1,
    )

    def conv_masked(extended, weights, bias):
        return conv_apply(extended, weights, bias, conv_mask)

    inner_local = value_pre.shape[1]
    rim_rows = jnp.concatenate(
        [value_pre[row_count - tap_count + 1 :], addr_pre[row_count - tap_count + 1 :]], axis=1
    )
    before = from_behind(rim_rows, "seq", 1)
    value_ext = jnp.concatenate([before[:, :inner_local], value_pre], axis=0).astype(jnp.float32)
    addr_ext = jnp.concatenate([before[:, inner_local:], addr_pre], axis=0).astype(jnp.float32)
    value_conv, value_back = jax.vjp(conv_masked, value_ext, kernels, offsets)
    values_all = value_conv.astype(jnp.bfloat16)
    addr_conv = conv_masked(addr_ext, filters, shifts).astype(jnp.bfloat16)
    block_len = min(GROUP, row_count)
    block_count = row_count // block_len
    heads_local = step_pre.shape[1]
    head_size = inner_local // heads_local
    state_size = addr_conv.shape[1] // 2
    values = values_all.reshape(block_count, block_len, heads_local, head_size)
    write_rows = addr_conv[:, :state_size].reshape(block_count, block_len, state_size)
    read_rows = addr_conv[:, state_size:].reshape(block_count, block_len, state_size)
    raw_steps = step_pre + stepbias[None, :]
    step_sizes = jax.nn.softplus(raw_steps).reshape(block_count, block_len, heads_local)
    scale_rate = -jnp.exp(decays)
    group_seg = segment.reshape(block_count, block_len)
    previous = seg_ext[tap_count - 2 : tap_count - 2 + row_count : block_len]

    def decay_all(step_arg, scale_arg):
        return jax.vmap(decay_terms, in_axes=(0, None, 0, 0))(
            step_arg, scale_arg, group_seg, previous
        )

    (lower_mask, entry_decay, weight, carry_decay), decay_back = jax.vjp(
        decay_all, step_sizes, scale_rate
    )
    scores = jnp.einsum("ctn,csn->cts", read_rows, write_rows, preferred_element_type=jnp.float32)
    mixing = (scores[:, None] * lower_mask).astype(jnp.bfloat16)
    intra_out = jnp.einsum("chts,cshp->cthp", mixing, values, preferred_element_type=jnp.float32)
    value_f = values.astype(jnp.float32)
    packed = (value_f * weight[..., None]).astype(jnp.bfloat16)
    local_state = jnp.einsum(
        "cshp,csn->chpn", packed, write_rows, preferred_element_type=jnp.float32
    )
    start_sum = (
        jnp.ones((heads_local,), jnp.float32),
        jnp.zeros((heads_local, head_size, state_size), jnp.float32),
    )
    summary, _ = lax.scan(fold_block, start_sum, (carry_decay, local_state))
    incoming = carried_in(summary, "seq", combine, start_sum)[1]
    _, starts = lax.scan(walk_blocks, incoming, (carry_decay, local_state))
    starts_low = starts.astype(jnp.bfloat16)
    queried = jnp.einsum(
        "ctn,chpn->cthp", read_rows, starts_low, preferred_element_type=jnp.float32
    )
    mixed_out = (
        intra_out + entry_decay[..., None] * queried + through[None, None, :, None] * value_f
    )
    ssd_out = mixed_out.reshape(row_count, inner_local)
    gate_act = jax.nn.silu(gate_pre)
    gated_rows = ssd_out * gate_act
    square_sum = lax.psum(jnp.sum(gated_rows * gated_rows, axis=1), "head")
    inv_inner = lax.rsqrt(square_sum / INNER + EPS)[:, None]
    normed_inner = (gated_rows * inv_inner * postnorm[None, :]).astype(jnp.bfloat16)
    out_part = jnp.dot(normed_inner, w_read, preferred_element_type=jnp.float32)
    trans_last = (((1,), (1,)), ((), ()))
    trans_first = (((0,), (0,)), ((), ()))
    grad_inner = lax.dot_general(g_full, w_read, trans_last, preferred_element_type=jnp.float32)
    grad_read = lax.dot_general(
        normed_inner, g_full, trans_first, preferred_element_type=jnp.float32
    )
    inner_dot = lax.psum(jnp.sum(gated_rows * postnorm[None, :] * grad_inner, axis=1), "head")
    cube_inner = inv_inner * inv_inner * inv_inner
    grad_gated = (
        inv_inner * postnorm[None, :] * grad_inner
        - gated_rows * cube_inner / INNER * inner_dot[:, None]
    )
    grad_post = jnp.sum(grad_inner * gated_rows * inv_inner, axis=0)
    grad_ssd = (grad_gated * gate_act).astype(jnp.bfloat16)
    gate_sigmoid = jax.nn.sigmoid(gate_pre)
    grad_gate_pre = (
        grad_gated * ssd_out * gate_sigmoid * (1.0 + gate_pre * (1.0 - gate_sigmoid))
    ).astype(jnp.bfloat16)
    grad_mixed = grad_ssd.reshape(block_count, block_len, heads_local, head_size)
    grad_mixed_f = grad_mixed.astype(jnp.float32)
    grad_query = (grad_mixed_f * entry_decay[..., None]).astype(jnp.bfloat16)
    grad_entry = jnp.sum(grad_mixed_f * queried, axis=3)
    grad_start_q = jnp.einsum(
        "cthp,ctn->chpn", grad_query, read_rows, preferred_element_type=jnp.float32
    )
    grad_read_rows = jnp.einsum(
        "cthp,chpn->ctn", grad_query, starts_low, preferred_element_type=jnp.float32
    )
    grad_mixing = jnp.einsum(
        "cthp,cshp->chts", grad_mixed, values, preferred_element_type=jnp.float32
    )
    grad_values = jnp.einsum(
        "chts,cthp->cshp", mixing, grad_mixed, preferred_element_type=jnp.float32
    )
    grad_scores = jnp.sum(grad_mixing * lower_mask, axis=1).astype(jnp.bfloat16)
    grad_lower = grad_mixing * scores[:, None]
    grad_read_rows = grad_read_rows + jnp.einsum(
        "cts,csn->ctn", grad_scores, write_rows, preferred_element_type=jnp.float32
    )
    grad_write_rows = jnp.einsum(
        "cts,ctn->csn", grad_scores, read_rows, preferred_element_type=jnp.float32
    )
    grad_through = jnp.sum(grad_mixed_f * value_f, axis=(0, 1, 3))
    grad_values = grad_values + through[None, None, :, None] * grad_mixed_f
    back_sum, _ = lax.scan(fold_block, start_sum, (carry_decay, grad_start_q), reverse=True)
    after = prefix(back_sum, "seq", combine, start_sum)[1]
    _, end_grads = lax.scan(walk_blocks, after, (carry_decay, grad_start_q), reverse=True)
    grad_carry = jnp.sum(end_grads * starts, axis=(2, 3))
    end_low = end_grads.astype(jnp.bfloat16)
    grad_packed = jnp.einsum(
        "csn,chpn->cshp", write_rows, end_low, preferred_element_type=jnp.float32
    )
    grad_write_rows = grad_write_rows + jnp.einsum(
        "cshp,chpn->csn", packed, end_low, preferred_element_type=jnp.float32
    )
    grad_values = grad_values + grad_packed * weight[..., None]
    grad_weight = jnp.sum(grad_packed * value_f, axis=3)
    grad_steps, grad_scale = decay_back((grad_lower, grad_entry, grad_weight, grad_carry))
    grad_decays = grad_scale * scale_rate
    grad_raw = grad_steps.reshape(row_count, heads_local) * jax.nn.sigmoid(raw_steps)
    grad_stepbias = jnp.sum(grad_raw, axis=0)
    grad_step_pre = grad_raw.astype(jnp.bfloat16)
    grad_addr_conv = jnp.concatenate(
        [
            grad_write_rows.reshape(row_count, state_size),
            grad_read_rows.reshape(row_count, state_size),
        ],
        axis=1,
    )
    grad_addr_share = lax.psum_scatter(
        grad_addr_conv.astype(jnp.bfloat16), "head", scatter_dimension=1, tiled=True
    ).astype(jnp.float32)
    col_count = grad_addr_share.shape[1]
    col_start = head_index * col_count
    addr_ext_share = lax.dynamic_slice_in_dim(addr_ext, col_start, col_count, 1)
    filter_share = lax.dynamic_slice_in_dim(filters, col_start, col_count, 1)
    shift_share = lax.dynamic_slice_in_dim(shifts, col_start, col_count, 0)
    _, addr_back = jax.vjp(conv_masked, addr_ext_share, filter_share, shift_share)
    grad_addr_ext, grad_filters, grad_shifts = addr_back(grad_addr_share)
    grad_value_ext, grad_kernels, grad_offsets = value_back(
        grad_values.reshape(row_count, inner_local)
    )
    head_rims = jnp.concatenate(
        [grad_value_ext[: tap_count - 1], grad_addr_ext[: tap_count - 1]], axis=1
    )
    after_rims = from_behind(head_rims, "seq", -1)
    tail_rows = jnp.concatenate(
        [jnp.zeros((row_count - tap_count + 1, after_rims.shape[1]), jnp.float32), after_rims],
        axis=0,
    )
    grad_value_pre = (grad_value_ext[tap_count - 1 :] + tail_rows[:, :inner_local]).astype(
        jnp.bfloat16
    )
    grad_addr_pre = (grad_addr_ext[tap_count - 1 :] + tail_rows[:, inner_local:]).astype(
        jnp.bfloat16
    )
    addr_share = lax.dynamic_slice_in_dim(w_addr, col_start, col_count, 1)
    grad_normed = lax.dot_general(
        grad_gate_pre, w_gate, trans_last, preferred_element_type=jnp.float32
    )
    grad_normed = grad_normed + lax.dot_general(
        grad_value_pre, w_pay, trans_last, preferred_element_type=jnp.float32
    )
    grad_normed = grad_normed + lax.dot_general(
        grad_addr_pre, addr_share, trans_last, preferred_element_type=jnp.float32
    )
    grad_normed = grad_normed + lax.dot_general(
        grad_step_pre, w_step, trans_last, preferred_element_type=jnp.float32
    )
    grad_gate_w = lax.dot_general(
        normed, grad_gate_pre, trans_first, preferred_element_type=jnp.float32
    )
    grad_pay_w = lax.dot_general(
        normed, grad_value_pre, trans_first, preferred_element_type=jnp.float32
    )
    grad_addr_w = lax.dot_general(
        normed, grad_addr_pre, trans_first, preferred_element_type=jnp.float32
    )
    grad_step_w = lax.dot_general(
        normed, grad_step_pre, trans_first, preferred_element_type=jnp.float32
    )
    cube_rms = inv_rms * inv_rms * inv_rms
    row_dot = jnp.sum(grad_normed * prenorm[None, :] * u_full, axis=1, keepdims=True)
    grad_part = inv_rms * prenorm[None, :] * grad_normed - u_full * cube_rms / D * row_dot
    extra_term = jnp.sum(grad_normed * u_full * inv_rms, axis=0)[None, :]
    out_sum, grad_sum, extra_sum = (
        lax.psum_scatter(
            out_part.astype(jnp.bfloat16), "head", scatter_dimension=1, tiled=True
        ).astype(jnp.float32),
        lax.psum_scatter(
            grad_part.astype(jnp.bfloat16), "head", scatter_dimension=1, tiled=True
        ).astype(jnp.float32),
        lax.psum_scatter(
            extra_term.astype(jnp.bfloat16), "head", scatter_dimension=1, tiled=True
        ).astype(jnp.float32),
    )
    u_local = x_local.astype(jnp.float32)
    input_grad = g_local.astype(jnp.float32) + grad_sum
    grad_prenorm = extra_sum[0]
    result = (u_local + out_sum).astype(jnp.bfloat16)
    grad_rows = input_grad.astype(jnp.bfloat16)
    moved_out = (
        lax.all_to_all(
            route_blocks(result, source_dev, devices, BLOCK),
            "seq",
            split_axis=0,
            concat_axis=0,
            tiled=True,
        ),
        lax.all_to_all(
            route_blocks(grad_rows, source_dev, devices, BLOCK),
            "seq",
            split_axis=0,
            concat_axis=0,
            tiled=True,
        ),
    )
    outputs = pick_blocks(moved_out[0], target_dev, devices)
    inputs_grad = pick_blocks(moved_out[1], target_dev, devices)
    gate_sum, pay_sum, addr_sum, step_sum, read_sum = (
        lax.psum_scatter(
            grad_gate_w.astype(jnp.bfloat16), "seq", scatter_dimension=0, tiled=True
        ).astype(jnp.float32),
        lax.psum_scatter(
            grad_pay_w.astype(jnp.bfloat16), "seq", scatter_dimension=0, tiled=True
        ).astype(jnp.float32),
        lax.psum_scatter(
            grad_addr_w.astype(jnp.bfloat16), "seq", scatter_dimension=0, tiled=True
        ).astype(jnp.float32),
        lax.psum_scatter(
            grad_step_w.astype(jnp.bfloat16), "seq", scatter_dimension=0, tiled=True
        ).astype(jnp.float32),
        lax.psum_scatter(
            grad_read.astype(jnp.bfloat16), "seq", scatter_dimension=1, tiled=True
        ).astype(jnp.float32),
    )
    smalls = lax.psum(
        (
            grad_prenorm,
            grad_kernels,
            grad_offsets,
            grad_filters,
            grad_shifts,
            grad_stepbias,
            grad_decays,
            grad_through,
            grad_post,
        ),
        "seq",
    )
    return (
        outputs,
        inputs_grad,
        smalls[0],
        gate_sum,
        pay_sum,
        addr_sum,
        step_sum,
        smalls[1],
        smalls[2],
        smalls[3],
        smalls[4],
        smalls[5],
        smalls[6],
        smalls[7],
        smalls[8],
        read_sum,
    )


def solution(mesh):
    in_specs = (
        P("seq", "head"),
        P("seq", "head"),
        P(),
        P(),
        P(),
        P("seq", "head"),
        P("seq", "head"),
        P("seq", None),
        P("seq", "head"),
        P(None, "head"),
        P("head"),
        P(),
        P(),
        P("head"),
        P("head"),
        P("head"),
        P("head"),
        P("head", "seq"),
    )
    out_specs = (
        P("seq", "head"),
        P("seq", "head"),
        P("head"),
        P("seq", "head"),
        P("seq", "head"),
        P("seq", "head"),
        P("seq", "head"),
        P(None, "head"),
        P("head"),
        P(None, "head"),
        P("head"),
        P("head"),
        P("head"),
        P("head"),
        P("head"),
        P("head", "seq"),
    )
    return jax.shard_map(
        on_device, mesh=mesh, in_specs=in_specs, out_specs=out_specs, check_vma=False
    )
```

```python
import functools

import jax
import jax.numpy as jnp
from jax import lax
from jax.experimental import pallas as pl
from jax.experimental.pallas import tpu as pltpu
from jax.sharding import PartitionSpec as P

D = 1024
GROUP = 256
BLOCK = 128
INNER = 2048
HDIM = 64
STATE = 128
TAPS = 4
HALO = 16
EDGE = 8
LANES = 128
EPS = 1e-05
MESH = pl.DeviceIdType.MESH
VMEM = pltpu.MemorySpace.VMEM
SMEM = pltpu.MemorySpace.SMEM
DMA = pltpu.SemaphoreType.DMA
MIB = 1 << 20
LOW = jnp.bfloat16
WIDE = jnp.float32


def shape(dims, kind):
    return jax.ShapeDtypeStruct(dims, kind)


def nn(a, b):
    return jnp.dot(a, b, preferred_element_type=WIDE)


def nt(a, b):
    return lax.dot_general(a, b, (((1,), (1,)), ((), ())), preferred_element_type=WIDE)


def tn(a, b):
    return lax.dot_general(a, b, (((0,), (0,)), ((), ())), preferred_element_type=WIDE)


def halves(x):
    high = x.astype(LOW)
    return high, (x - high.astype(WIDE)).astype(LOW)


def thirds(x):
    high = x.astype(LOW)
    rest = x - high.astype(WIDE)
    middle = rest.astype(LOW)
    return high, middle, (rest - middle.astype(WIDE)).astype(LOW)


def head_rows(inner):
    row = lax.broadcasted_iota(jnp.int32, (LANES, inner), 0)
    column = lax.broadcasted_iota(jnp.int32, (LANES, inner), 1)
    return jnp.where(column // HDIM == row, 1.0, 0.0).astype(LOW)


def head_columns(inner):
    row = lax.broadcasted_iota(jnp.int32, (inner, LANES), 0)
    column = lax.broadcasted_iota(jnp.int32, (inner, LANES), 1)
    return jnp.where(row // HDIM == column, 1.0, 0.0).astype(LOW)


def to_columns(x, spread):
    high, rest = halves(x)
    return nn(high, spread) + nn(rest, spread)


def to_heads(x, collect):
    high, rest = halves(x)
    return nn(high, collect) + nn(rest, collect)


def ones_before(count):
    row = lax.broadcasted_iota(jnp.int32, (count, count), 0)
    column = lax.broadcasted_iota(jnp.int32, (count, count), 1)
    return row >= column


def sum_before(x):
    matrix = jnp.where(ones_before(x.shape[0]), 1.0, 0.0).astype(LOW)
    high, middle, low = thirds(x)
    return nn(matrix, high) + (nn(matrix, middle) + nn(matrix, low))


def sum_after(x):
    count = x.shape[0]
    row = lax.broadcasted_iota(jnp.int32, (count, count), 0)
    column = lax.broadcasted_iota(jnp.int32, (count, count), 1)
    matrix = jnp.where(row <= column, 1.0, 0.0).astype(LOW)
    high, middle, low = thirds(x)
    return nn(matrix, high) + (nn(matrix, middle) + nn(matrix, low))


def sigmoid(x):
    return 0.5 * jnp.tanh(0.5 * x) + 0.5


def step_terms(raw, heads):
    z = jnp.exp(-jnp.abs(raw))
    series = 1.0 - z * (0.5 - z * (1.0 / 3.0 - z * (0.25 - z * 0.2)))
    small = z < 0.03
    log1p = jnp.where(small, z * series, jnp.log(1.0 + z))
    soft = jnp.maximum(raw, 0.0) + log1p
    one = 1.0 / (1.0 + z)
    sig = jnp.where(raw >= 0, one, z * one)
    ratio = jnp.where(small & (raw < 0), one / series, sig / jnp.maximum(soft, 1e-20))
    lane = lax.broadcasted_iota(jnp.int32, raw.shape, 1)
    return jnp.where(lane < heads, soft, 0.0), sig, ratio


def greet(seq_peers, head_peers):
    barrier = pltpu.get_barrier_semaphore()
    count = 0
    if seq_peers > 1:
        me = lax.axis_index("seq")

        @pl.loop(1, seq_peers)
        def _(i):
            pl.semaphore_signal(
                barrier, inc=1, device_id={"seq": lax.rem(me + i, seq_peers)}, device_id_type=MESH
            )

        count += seq_peers - 1
    if head_peers > 1:
        mine = lax.axis_index("head")

        @pl.loop(1, head_peers)
        def _(i):
            pl.semaphore_signal(
                barrier, inc=1, device_id={"head": lax.rem(mine + i, head_peers)}, device_id_type=MESH
            )

        count += head_peers - 1
    pl.semaphore_wait(barrier, count)


def remote(src, dst, send_sem, recv_sem, where):
    return pltpu.make_async_remote_copy(
        src_ref=src, dst_ref=dst, send_sem=send_sem, recv_sem=recv_sem, device_id=where, device_id_type=MESH
    )


class Line:
    def __init__(self, count, out, width, send, recv):
        self.count, self.out, self.width, self.send, self.recv = count, out, width, send, recv
        self.me = lax.axis_index("head")

    def view(self, shard):
        return self.out.at[:, pl.ds(pl.multiple_of(shard * self.width, LANES), self.width)]

    def copy(self, src, shard, way, step):
        return remote(
            src, self.view(shard), self.send.at[way, step], self.recv.at[shard], {"head": self.me + (1 - 2 * way)}
        )

    def first(self, own):
        self.pass_on(own, self.me, 0, 0)
        self.pass_on(own, self.me, 1, 0)

    def pass_on(self, src, shard, way, step):
        reach = (self.me < self.count - 1) if way == 0 else (self.me > 0)

        @pl.when(reach)
        def _():
            self.copy(src, shard, way, step).start()

    def hop(self, step):
        for way in (0, 1):
            shard = self.me - step if way == 0 else self.me + step
            there = (shard >= 0) if way == 0 else (shard < self.count)

            @pl.when(there)
            def _():
                self.copy(self.view(shard), shard, way, step).wait_recv()
                if step < self.count - 1:
                    self.pass_on(self.view(shard), shard, way, step)

    def finish(self, own):
        for way in (0, 1):
            reach = (self.me < self.count - 1) if way == 0 else (self.me > 0)
            for step in range(self.count - 1):
                shard = self.me - step if way == 0 else self.me + step
                there = (shard >= 0) if way == 0 else (shard < self.count)

                @pl.when(reach & there)
                def _():
                    src = own if step == 0 else self.view(shard)
                    self.copy(src, shard, way, step).wait_send()


class Plane:
    def __init__(self, seqs, view, sent, got, passed, way=0):
        self.chips, self.view, self.sent, self.got, self.passed, self.way = seqs // 2, view, sent, got, passed, way
        self.me = lax.axis_index("seq")
        self.core = lax.rem(self.me, 2)
        self.chip = self.me // 2
        self.mate = self.me + 1 - 2 * self.core

    def forward(self, chip):
        return (chip > self.chip) if self.way == 1 else (chip < self.chip) if self.way == -1 else (chip >= 0)

    def backward(self, chip):
        return (chip < self.chip) if self.way == 1 else (chip > self.chip) if self.way == -1 else (chip >= 0)

    def each_chip(self, body):
        @pl.loop(1, self.chips)
        def _(i):
            body(lax.rem(self.chip + i, self.chips))

    def copy(self, src, source, to, sem):
        return remote(src, self.view(source), sem, self.got.at[source], {"seq": to})

    def start(self, own):
        def send(chip):
            to = 2 * chip + self.core

            @pl.when(self.forward(chip))
            def _():
                self.copy(own, self.me, to, self.sent.at[to]).start()

        self.each_chip(send)
        self.copy(own, self.me, self.mate, self.sent.at[self.mate]).start()

    def relay(self):
        def take(chip):
            source = 2 * chip + self.core

            @pl.when(self.backward(chip))
            def _():
                landed = self.view(source)
                self.copy(landed, source, self.mate, self.passed.at[source]).wait_recv()
                self.copy(landed, source, self.mate, self.passed.at[source]).start()

        self.each_chip(take)

    def finish(self, own):
        def take(chip):
            source = 2 * chip + 1 - self.core

            @pl.when(self.backward(chip))
            def _():
                self.copy(self.view(source), source, self.mate, self.passed.at[source]).wait_recv()

        self.each_chip(take)
        self.copy(self.view(self.mate), self.mate, self.mate, self.sent.at[self.mate]).wait_recv()
        self.copy(own, self.me, self.mate, self.sent.at[self.mate]).wait_send()

        def drain(chip):
            same = 2 * chip + self.core

            @pl.when(self.forward(chip))
            def _():
                self.copy(own, self.me, same, self.sent.at[same]).wait_send()

            @pl.when(self.backward(chip))
            def _():
                self.copy(self.view(same), same, self.mate, self.passed.at[same]).wait_send()

        self.each_chip(drain)


def spread_kernel(
    seqs, heads, give, take, x, g, gating, payload, address, stepping, readout,
    x_out, g_out, w_out, r_out, work_x, work_g,
    send_x, send_g, recv_x, recv_g, w_own, r_own,
    sent, got, w_sent, w_got, w_passed, r_sent, r_got, r_passed, rim_sent, rim_got, own_sem,
    x_line_sent, x_line_got, g_line_sent, g_line_got,
):
    me, mine = lax.axis_index("seq"), lax.axis_index("head")
    blocks, _, width = x.shape
    rows = blocks * BLOCK
    depth, inner = gating.shape
    greet(seqs, heads)

    def post(which, source, outgoing, incoming):
        @pl.loop(1, seqs)
        def _(i):
            to = lax.rem(me + i, seqs)
            outgoing[to] = source[give[to]]
            remote(outgoing.at[to], incoming.at[me], sent.at[which, to], got.at[which, me], {"seq": to}).start()

        incoming[me] = source[give[me]]

    post(0, x, send_x, recv_x)
    post(1, g, send_g, recv_g)

    w_own[:, :inner] = gating[...].astype(LOW)
    w_own[:, inner : 2 * inner] = payload[...].astype(LOW)
    state2 = address.shape[1]
    w_own[:, 2 * inner : 2 * inner + state2] = address[...].astype(LOW)
    w_own[:, 2 * inner + state2 :] = jnp.zeros((depth, LANES), LOW)
    w_own[:, 2 * inner + state2 : 2 * inner + state2 + stepping.shape[1]] = stepping[...].astype(LOW)
    r_own[...] = readout[...].T.astype(LOW)

    def rows_of(device):
        return pl.ds(pl.multiple_of(device * depth, depth), depth)

    own_w = pltpu.make_async_copy(w_own, w_out.at[rows_of(me)], own_sem.at[0])
    own_r = pltpu.make_async_copy(r_own, r_out.at[rows_of(me)], own_sem.at[1])
    own_w.start()
    own_r.start()
    w_plane = Plane(seqs, lambda s: w_out.at[rows_of(s)], w_sent, w_got, w_passed)
    r_plane = Plane(seqs, lambda s: r_out.at[rows_of(s)], r_sent, r_got, r_passed)
    w_plane.start(w_own)
    r_plane.start(r_own)

    def arrange(which, received, work):
        @pl.loop(1, seqs)
        def _(i):
            source = lax.rem(me + i, seqs)
            remote(
                received.at[source], received.at[source], sent.at[which, source], got.at[which, source], {"seq": source}
            ).wait_recv()

        for k in range(blocks):
            work[pl.ds(k * BLOCK, BLOCK), :] = received[take[k]]

    arrange(0, recv_x, work_x)
    after = lax.rem(me + 1, seqs)
    rim = remote(
        work_x.at[pl.ds(rows - HALO, HALO)], work_x.at[pl.ds(rows, HALO)], rim_sent, rim_got, {"seq": after}
    )
    rim.start()
    rim.wait()
    x_line = Line(heads, x_out, width, x_line_sent, x_line_got)
    g_line = Line(heads, g_out, width, g_line_sent, g_line_got)
    own_x = pltpu.make_async_copy(work_x, x_line.view(mine), own_sem.at[2])
    own_x.start()
    x_line.first(work_x)
    arrange(1, recv_g, work_g)
    own_g = pltpu.make_async_copy(work_g, g_line.view(mine), own_sem.at[3])
    own_g.start()
    for step in range(1, heads):
        x_line.hop(step)
        if step == 1:
            g_line.first(work_g)
            w_plane.relay()
    r_plane.relay()
    for step in range(1, heads):
        g_line.hop(step)
    x_line.finish(work_x)
    g_line.finish(work_g)
    w_plane.finish(w_own)
    r_plane.finish(r_own)
    for copy in (own_w, own_r, own_x, own_g):
        copy.wait()

    @pl.loop(1, seqs)
    def _(i):
        other = lax.rem(me + i, seqs)
        for which, buffer in ((0, send_x), (1, send_g)):
            remote(
                buffer.at[other], buffer.at[other], sent.at[which, other], got.at[which, other], {"seq": other}
            ).wait_send()


ANY_SPEC = pl.BlockSpec(memory_space=pl.ANY)
VMEM_SPEC = pl.BlockSpec(memory_space=VMEM)
SMEM_SPEC = pl.BlockSpec(memory_space=SMEM)


def spread(give, take, x, g, gating, payload, address, stepping, readout):
    seqs, heads = lax.axis_size("seq"), lax.axis_size("head")
    rows, width = x.shape
    depth, inner = gating.shape
    total = depth * seqs
    columns = 2 * inner + address.shape[1] + LANES
    block = (seqs, BLOCK, width)
    return pl.pallas_call(
        functools.partial(spread_kernel, seqs, heads),
        out_shape=(
            shape((rows + HALO, total), LOW),
            shape((rows, total), LOW),
            shape((total, columns), LOW),
            shape((total, inner), LOW),
            shape((rows + HALO, width), LOW),
            shape((rows, width), LOW),
        ),
        in_specs=[SMEM_SPEC] * 2 + [VMEM_SPEC] * 7,
        out_specs=(ANY_SPEC,) * 4 + (VMEM_SPEC,) * 2,
        scratch_shapes=[
            pltpu.VMEM(block, LOW), pltpu.VMEM(block, LOW), pltpu.VMEM(block, LOW), pltpu.VMEM(block, LOW),
            pltpu.VMEM((depth, columns), LOW), pltpu.VMEM((depth, inner), LOW),
            DMA((2, seqs)), DMA((2, seqs)),
            DMA((seqs,)), DMA((seqs,)), DMA((seqs,)), DMA((seqs,)), DMA((seqs,)), DMA((seqs,)),
            DMA, DMA, DMA((4,)),
            DMA((2, heads)), DMA((heads,)), DMA((2, heads)), DMA((heads,)),
        ],
        compiler_params=pltpu.CompilerParams(
            collective_id=0, has_side_effects=True, vmem_limit_bytes=48 * MIB
        ),
        name="spread",
    )(give, take, x.reshape(-1, BLOCK, width), g.reshape(-1, BLOCK, width), gating, payload, address, stepping, readout)


def blockwise(dims, index):
    return pl.BlockSpec(dims, index)


def fixed(dims):
    return pl.BlockSpec(dims, lambda i: (0,) * len(dims))


def carry_columns(carry_row_t, collect):
    high, middle, low = thirds(jnp.broadcast_to(carry_row_t, (LANES, LANES)))
    return nn(collect, high) + (nn(collect, middle) + nn(collect, low))


def pair_lanes(slab):
    lane = lax.broadcasted_iota(jnp.int32, slab.shape, 1)
    zero = jnp.zeros_like(slab)
    return jnp.where(lane < HDIM, slab, zero), jnp.where(lane >= HDIM, slab, zero)


def front_kernel(
    heads, flags, u, rim, w, vec, prenorm, kernels, filters, offsets, shifts,
    normed_o, gate_o, pre_o, conv_o, act_o, raw_o, cum_o, part_o, local_o, msg_o, rim_o,
    ext, prev, state, prod,
):
    i = pl.program_id(0)
    inner = gate_o.shape[1]
    wide = pre_o.shape[1]
    taps = jnp.concatenate([kernels[...], filters[...]], axis=1)
    bias = jnp.concatenate([offsets[...], shifts[...]], axis=1)
    spread_m, collect = head_rows(inner), head_columns(inner)

    def normalize(block):
        rows = block.astype(WIDE)
        scale = lax.rsqrt(jnp.mean(rows * rows, axis=1, keepdims=True) + EPS)
        return (rows * scale * prenorm[...]).astype(LOW)

    @pl.when(i == 0)
    def _():
        before = nn(normalize(rim[...]), w[:, inner : inner + wide]).astype(LOW).astype(WIDE)
        prev[...] = before[HALO - EDGE :]
        rim_o[...] = before[HALO - EDGE :]
        state[...] = jnp.zeros_like(state)
        prod[...] = jnp.ones_like(prod)

    normed = normalize(u[...])
    normed_o[...] = normed
    gate_o[...] = nn(normed, w[:, :inner])
    pre = nn(normed, w[:, inner : inner + wide]).astype(LOW)
    pre_o[...] = pre
    lane = lax.broadcasted_iota(jnp.int32, (GROUP, LANES), 1)
    raw = jnp.where(lane < heads, nn(normed, w[:, inner + wide :]) + vec[0:1, :], 0.0)
    raw_o[...] = raw
    first, second = flags[2 * i], flags[2 * i + 1]
    same = (first, second)
    for half in range(2):
        rows = pl.ds(half * BLOCK, BLOCK)
        ext[0:EDGE, :] = prev[...] * same[half]
        ext[EDGE:, :] = pre[half * BLOCK : (half + 1) * BLOCK].astype(WIDE)
        prev[...] = ext[BLOCK:, :]
        total = bias + taps[TAPS - 1 : TAPS] * ext[EDGE:, :]
        for tap in range(TAPS - 1):
            total = total + taps[tap : tap + 1] * ext[pl.ds(EDGE - (TAPS - 1) + tap, BLOCK), :]
        conv_o[rows, :] = total
        act_o[rows, :] = (total * sigmoid(total)).astype(LOW)

    steps, _, _ = step_terms(raw, heads)
    scale = -jnp.exp(vec[1:2, :])
    cum = sum_before(steps * scale)
    cum_o[...] = cum
    cum_t, steps_t = cum.T, steps.T
    write = act_o[:, inner : inner + STATE]
    read = act_o[:, inner + STATE :]
    lower = ones_before(BLOCK)
    top, low = slice(0, BLOCK), slice(BLOCK, GROUP)
    s00 = jnp.where(lower, nt(read[top], write[top]), 0.0)
    s10 = nt(read[low], write[top]) * second
    s11 = jnp.where(lower, nt(read[low], write[low]), 0.0)

    def mix(scores, head, t, s):
        decay = jnp.exp(jnp.minimum(cum[t, head : head + 1] - cum_t[head : head + 1, s], 0.0))
        return (scores * (decay * steps_t[head : head + 1, s])).astype(LOW)

    last = cum[GROUP - 1 : GROUP, :]
    row = lax.broadcasted_iota(jnp.int32, (GROUP, LANES), 0)
    weight = steps * jnp.exp(last - cum) * jnp.where(row < BLOCK, second, 1.0)
    weight_w = to_columns(weight, spread_m)
    packed = []
    for pair in range(inner // LANES):
        columns = slice(pair * LANES, (pair + 1) * LANES)
        slab = act_o[:, columns]
        slab_f = slab.astype(WIDE)
        ones = pair_lanes(slab)
        h0, h1 = 2 * pair, 2 * pair + 1
        y0 = nn(
            jnp.concatenate([mix(s00, h0, top, top), mix(s00, h1, top, top)], axis=1),
            jnp.concatenate([ones[0][top], ones[1][top]], axis=0),
        )
        y1 = nn(
            jnp.concatenate(
                [mix(s10, h0, low, top), mix(s11, h0, low, low), mix(s10, h1, low, top), mix(s11, h1, low, low)], axis=1
            ),
            jnp.concatenate([ones[0], ones[1]], axis=0),
        )
        skip = to_columns(jnp.broadcast_to(vec[2:3, :], (EDGE, LANES)), spread_m[:, columns])[0:1]
        part_o[top, columns] = y0 + skip * slab_f[top]
        part_o[low, columns] = y1 + skip * slab_f[low]
        packed.append((slab_f * weight_w[:, columns]).astype(LOW))
    local = tn(jnp.concatenate(packed, axis=1), write)
    local_o[0] = local
    carry = jnp.exp(cum_t[:, GROUP - 1 : GROUP]) * (first * second)
    state[...] = carry_columns(carry, collect) * state[...] + local
    prod[...] = jnp.broadcast_to(carry[:HALO], (HALO, STATE)) * prod[...]
    msg_o[:inner, :] = state[...].astype(LOW)
    msg_o[inner:, :] = prod[...].astype(LOW)


def front(flags, x_full, w_all, vec, prenorm, kernels, filters, offsets, shifts, heads):
    rows = x_full.shape[0] - HALO
    inner = kernels.shape[1]
    wide = inner + filters.shape[1]
    blocks = rows // GROUP
    total = x_full.shape[1]

    def by_rows(width):
        return blockwise((GROUP, width), lambda i: (i, 0))

    return pl.pallas_call(
        functools.partial(front_kernel, heads),
        grid=(blocks,),
        out_shape=(
            shape((rows, total), LOW), shape((rows, inner), WIDE), shape((rows, wide), LOW), shape((rows, wide), WIDE),
            shape((rows, wide), LOW), shape((rows, LANES), WIDE), shape((rows, LANES), WIDE), shape((rows, inner), WIDE),
            shape((blocks, inner, STATE), WIDE), shape((inner + HALO, STATE), LOW),
            shape((EDGE, wide), WIDE),
        ),
        in_specs=[
            SMEM_SPEC, by_rows(total), blockwise((HALO, total), lambda i: (rows // HALO, 0)), fixed(w_all.shape),
            fixed(vec.shape), fixed(prenorm.shape), fixed(kernels.shape), fixed(filters.shape), fixed(offsets.shape),
            fixed(shifts.shape),
        ],
        out_specs=(
            by_rows(total), by_rows(inner), by_rows(wide), by_rows(wide), by_rows(wide), by_rows(LANES), by_rows(LANES),
            by_rows(inner), blockwise((1, inner, STATE), lambda i: (i, 0, 0)), fixed((inner + HALO, STATE)),
            fixed((EDGE, wide)),
        ),
        scratch_shapes=[
            pltpu.VMEM((EDGE + BLOCK, wide), WIDE), pltpu.VMEM((EDGE, wide), WIDE),
            pltpu.VMEM((inner, STATE), WIDE), pltpu.VMEM((HALO, STATE), WIDE),
        ],
        compiler_params=pltpu.CompilerParams(vmem_limit_bytes=56 * MIB, dimension_semantics=("arbitrary",)),
        name="front",
    )(flags, x_full, x_full, w_all, vec, prenorm, kernels, filters, offsets, shifts)


def fold_states(slots, collect, inner, first, last, step, start):
    def hop(n, state):
        message = slots[first + n * step]
        carry = nn(collect[:, :HALO], message[inner:])
        return carry * state + message[:inner].astype(WIDE)

    return lax.fori_loop(0, (last - first) * step, hop, start)


def middle_kernel(
    seqs, line, blocks, flags, msg, gate, part, read, cum, local, g, normed, r_t, postnorm,
    ssd_o, starts_o, dssd_o, dgate_o, out_o, back_o, q_o, sums_o, gread_o, ggate_o, gpost_o,
    ssd_s, din_s, state, slots, sums, gread, ggate, prod,
    sent, got, passed, sum_sent, sum_got,
):
    i = pl.program_id(0)
    me, mine = lax.axis_index("seq"), lax.axis_index("head")
    inner = gate.shape[1]
    width = out_o.shape[2]
    spread_m, collect = head_rows(inner), head_columns(inner)
    first_phase = i < blocks
    block = lax.rem(i, blocks)
    here = pl.ds(pl.multiple_of(block * GROUP, GROUP), GROUP)
    first, second = flags[2 * block], flags[2 * block + 1]
    plane = Plane(seqs, lambda s: slots.at[s], sent, got, passed, way=1)

    @pl.when(i == 0)
    def _():
        greet(seqs, line)
        plane.start(msg)
        plane.relay()
        plane.finish(msg)
        state[...] = fold_states(slots, collect, inner, 0, me, 1, jnp.zeros((inner, STATE), WIDE))

    row = lax.broadcasted_iota(jnp.int32, (GROUP, LANES), 0)
    lane = lax.broadcasted_iota(jnp.int32, (GROUP, LANES), 1)
    entry = to_columns(jnp.exp(cum[...]) * (first * jnp.where(row < BLOCK, 1.0, second)), spread_m)
    gate_v = gate[...]
    sig = sigmoid(gate_v)
    act = gate_v * sig
    cum_t = cum[...].T
    carry = jnp.exp(cum_t[:, GROUP - 1 : GROUP]) * (first * second)

    @pl.when(first_phase)
    def _():
        start = state[...]
        starts_o[0] = start
        queried = nt(read[...], start.astype(LOW))
        ssd = part[...] + entry * queried
        ssd_s[here, :] = ssd
        ssd_o[...] = ssd
        state[...] = carry_columns(carry, collect) * start + local[0]
        gated = ssd * act
        scaled = gated * postnorm[...]
        d_inner = nn(g[...], r_t[...])
        din_s[here, :] = d_inner
        out = nt(scaled.astype(LOW), r_t[...])
        for z in range(line):
            out_o[z] = out[:, z * width : (z + 1) * width].astype(LOW)
        squares = jnp.sum(gated * gated, axis=1, keepdims=True)
        dots = jnp.sum(scaled * d_inner, axis=1, keepdims=True)
        both = jnp.where(lane == 0, squares, jnp.where(lane == 1, dots, 0.0)).T
        sums[mine, block] = both[:EDGE]

    def sum_copy(to, slot):
        return remote(sums.at[mine], sums.at[slot], sum_sent.at[to], sum_got.at[slot], {"head": to})

    @pl.when(i == blocks - 1)
    def _():
        if line > 1:

            @pl.loop(1, line)
            def _(n):
                sum_copy(lax.rem(mine + n, line), mine).start()

            @pl.loop(1, line)
            def _(n):
                other = lax.rem(mine + n, line)
                sum_copy(other, other).wait()

        sums_o[...] = jnp.sum(sums[...], axis=0)
        gread[...] = jnp.zeros_like(gread)
        ggate[...] = jnp.zeros_like(ggate)
        gpost_o[...] = jnp.zeros_like(gpost_o)
        state[...] = jnp.zeros_like(state)
        prod[...] = jnp.ones_like(prod)

    @pl.when(jnp.logical_not(first_phase))
    def _():
        total = sums_o[block]
        stats = jnp.concatenate([total, jnp.zeros((LANES - EDGE, GROUP), WIDE)], axis=0).T
        inv = lax.rsqrt(stats[:, 0:1] / INNER + EPS)
        dot = stats[:, 1:2]
        ssd = ssd_s[here, :]
        d_inner = din_s[here, :]
        gated = ssd * act
        gated_inv = gated * inv
        inner_normed = (gated_inv * postnorm[...]).astype(LOW)
        d_gated = (inv * postnorm[...]) * d_inner - gated * (inv * inv * inv / INNER * dot)
        gpost_o[...] += jnp.sum(d_inner * gated_inv, axis=0, keepdims=True)
        d_ssd = (d_gated * act).astype(LOW)
        d_gate = (d_gated * ssd * sig * (1.0 + gate_v * (1.0 - sig))).astype(LOW)
        dssd_o[...] = d_ssd
        dgate_o[...] = d_gate
        gread[...] += tn(g[...], inner_normed)
        ggate[...] += tn(normed[...], d_gate)
        query_grad = (d_ssd.astype(WIDE) * entry).astype(LOW)
        q = tn(query_grad, read[...])
        q_o[0] = q
        state[...] += carry_columns(prod[...], collect) * q
        prod[...] = prod[...] * carry

    @pl.when(i == 2 * blocks - 1)
    def _():
        gread_o[...] = gread[...].astype(LOW)
        ggate_o[...] = ggate[...].astype(LOW)
        back_o[:inner, :] = state[...].astype(LOW)
        back_o[inner:, :] = jnp.broadcast_to(prod[:HALO], (HALO, STATE)).astype(LOW)


def middle(flags, msg, gate, part, act, cum, local, g_full, normed, r_t, postnorm):
    seqs, line = lax.axis_size("seq"), lax.axis_size("head")
    rows, inner = gate.shape
    total = g_full.shape[1]
    width = total // line
    blocks = rows // GROUP

    def in_both(columns, at=0):
        return blockwise((GROUP, columns), lambda i: (lax.rem(i, blocks), at))

    def in_first(columns):
        return blockwise((GROUP, columns), lambda i: (jnp.minimum(i, blocks - 1), 0))

    def in_second(columns):
        return blockwise((GROUP, columns), lambda i: (jnp.maximum(i - blocks, 0), 0))

    state = (1, inner, STATE)
    return pl.pallas_call(
        functools.partial(middle_kernel, seqs, line, blocks),
        grid=(2 * blocks,),
        out_shape=(
            shape((rows, inner), WIDE), shape((blocks, inner, STATE), WIDE), shape((rows, inner), LOW),
            shape((rows, inner), LOW), shape((line, rows, width), LOW), shape((inner + HALO, STATE), LOW),
            shape((blocks, inner, STATE), WIDE), shape((blocks, EDGE, GROUP), WIDE), shape((total, inner), LOW),
            shape((total, inner), LOW), shape((1, inner), WIDE),
        ),
        in_specs=[
            SMEM_SPEC, VMEM_SPEC, in_both(inner), in_first(inner), in_both(STATE, (inner + STATE) // STATE),
            in_both(LANES), blockwise(state, lambda i: (jnp.minimum(i, blocks - 1), 0, 0)), in_both(total),
            in_second(total), fixed(r_t.shape), fixed(postnorm.shape),
        ],
        out_specs=(
            in_first(inner), blockwise(state, lambda i: (jnp.minimum(i, blocks - 1), 0, 0)), in_second(inner),
            in_second(inner), blockwise((line, GROUP, width), lambda i: (0, jnp.minimum(i, blocks - 1), 0)),
            fixed((inner + HALO, STATE)), blockwise(state, lambda i: (jnp.maximum(i - blocks, 0), 0, 0)),
            fixed((blocks, EDGE, GROUP)), fixed((total, inner)), fixed((total, inner)), fixed((1, inner)),
        ),
        scratch_shapes=[
            pltpu.VMEM((rows, inner), WIDE), pltpu.VMEM((rows, inner), WIDE), pltpu.VMEM((inner, STATE), WIDE),
            pltpu.VMEM((seqs, inner + HALO, STATE), LOW), pltpu.VMEM((line, blocks, EDGE, GROUP), WIDE),
            pltpu.VMEM((total, inner), WIDE), pltpu.VMEM((total, inner), WIDE), pltpu.VMEM((LANES, 1), WIDE),
            DMA((seqs,)), DMA((seqs,)), DMA((seqs,)), DMA((line,)), DMA((line,)),
        ],
        compiler_params=pltpu.CompilerParams(
            collective_id=1, has_side_effects=True, vmem_limit_bytes=60 * MIB, dimension_semantics=("arbitrary",)
        ),
        name="middle",
    )(flags, msg, gate, part, act, cum, local, g_full, normed, r_t, postnorm)


def chunk_lanes(x, count):
    size = x.shape[1] // count
    fold = LANES // size
    tall = GROUP // fold
    lane = lax.broadcasted_iota(jnp.int32, (tall, LANES), 1)
    out = []
    for chunk in range(count):
        slab, offset = chunk * size // LANES, chunk * size % LANES
        total = jnp.zeros((tall, LANES), WIDE)
        for group in range(fold):
            piece = x[group * tall : (group + 1) * tall, slab * LANES : (slab + 1) * LANES]
            shift = (group * size - offset) % LANES
            if shift:
                piece = pltpu.roll(piece, shift, 1)
            inside = (lane >= group * size) & (lane < (group + 1) * size)
            total = jnp.where(inside, piece, total)
        out.append(total)
    return out


def back_kernel(
    seqs, line, heads, blocks, flags, msg, d_ssd, ssd, act, cum, raw, starts, q, vec, out_part, gread, ggate,
    dval_o, daddr_o, dstep_o, tiny_o, out_got, gread_got, ggate_got,
    state, slots,
    sent, got, passed, out_sent, out_sem, w_sent, w_sem, own_sem,
):
    i = pl.program_id(0)
    me, mine = lax.axis_index("seq"), lax.axis_index("head")
    block = blocks - 1 - i
    inner = d_ssd.shape[1]
    depth = gread_got.shape[1]
    spread_m, collect = head_rows(inner), head_columns(inner)
    plane = Plane(seqs, lambda s: slots.at[s], sent, got, passed, way=-1)

    def out_copy(to, slot):
        return remote(out_part.at[to], out_got.at[slot], out_sent.at[to], out_sem.at[slot], {"head": to})

    def rows_of(device):
        return pl.ds(pl.multiple_of(device * depth, depth), depth)

    weights = ((gread, gread_got), (ggate, ggate_got))

    def w_copy(which, to, slot):
        src, dst = weights[which]
        return remote(
            src.at[rows_of(to)], dst.at[slot], w_sent.at[which, to], w_sem.at[which, slot], {"seq": to}
        )

    own_copies = [
        pltpu.make_async_copy(out_part.at[mine], out_got.at[mine], own_sem.at[0]),
        pltpu.make_async_copy(gread.at[rows_of(me)], gread_got.at[me], own_sem.at[1]),
        pltpu.make_async_copy(ggate.at[rows_of(me)], ggate_got.at[me], own_sem.at[2]),
    ]

    @pl.when(i == 0)
    def _():
        greet(seqs, line)
        plane.start(msg)
        plane.relay()
        plane.finish(msg)
        state[...] = fold_states(slots, collect, inner, seqs - 1, me, -1, jnp.zeros((inner, STATE), WIDE))
        tiny_o[...] = jnp.zeros_like(tiny_o)
        if line > 1:

            @pl.loop(1, line)
            def _(n):
                out_copy(lax.rem(mine + n, line), mine).start()

        for which in range(2):

            @pl.loop(1, seqs)
            def _(n):
                w_copy(which, lax.rem(me + n, seqs), me).start()

        for copy in own_copies:
            copy.start()

    first, second = flags[2 * block], flags[2 * block + 1]
    row = lax.broadcasted_iota(jnp.int32, (GROUP, LANES), 0)
    lower_mask = ones_before(BLOCK)
    top, low = slice(0, BLOCK), slice(BLOCK, GROUP)
    cum_v = cum[...]
    cum_t = cum_v.T
    steps, sig, ratio = step_terms(raw[...], heads)
    steps_t = steps.T
    scale = -jnp.exp(vec[1:2, :])
    last = cum_v[GROUP - 1 : GROUP, :]
    write = act[:, inner : inner + STATE]
    read = act[:, inner + STATE :]
    s00 = jnp.where(lower_mask, nt(read[top], write[top]), 0.0)
    s10 = nt(read[low], write[top]) * second
    s11 = jnp.where(lower_mask, nt(read[low], write[low]), 0.0)

    end = state[...]
    end_low = end.astype(LOW)
    start = starts[0]
    carry = jnp.exp(cum_t[:, GROUP - 1 : GROUP]) * (first * second)
    state[...] = carry_columns(carry, collect) * end + q[0]
    weight = steps * jnp.exp(last - cum_v) * jnp.where(row < BLOCK, second, 1.0)
    weight_w = to_columns(weight, spread_m)
    entry_w = to_columns(jnp.exp(cum_v) * (first * jnp.where(row < BLOCK, 1.0, second)), spread_m)
    d_query = (d_ssd[...].astype(WIDE) * entry_w).astype(LOW)
    through_w = to_columns(jnp.broadcast_to(vec[2:3, :], (EDGE, LANES)), spread_m)[0:1]

    def decay_of(head, t, s):
        decay = jnp.exp(jnp.minimum(cum_v[t, head : head + 1] - cum_t[head : head + 1, s], 0.0))
        return decay * steps_t[head : head + 1, s]

    ds00 = jnp.zeros((BLOCK, BLOCK), WIDE)
    ds10 = jnp.zeros((BLOCK, BLOCK), WIDE)
    ds11 = jnp.zeros((BLOCK, BLOCK), WIDE)
    packed, value_parts, tails = [], [], []
    d_packed = nt(write, end_low)
    for pair in range(inner // LANES):
        columns = slice(pair * LANES, (pair + 1) * LANES)
        values = act[:, columns]
        values_f = values.astype(WIDE)
        dy = d_ssd[:, columns]
        dys = pair_lanes(dy)
        m00, m10, m11 = [], [], []
        for k in range(2):
            head = 2 * pair + k
            l00, l10, l11 = decay_of(head, top, top), decay_of(head, low, top), decay_of(head, low, low)
            m00.append((s00 * l00).astype(LOW))
            m10.append((s10 * l10).astype(LOW))
            m11.append((s11 * l11).astype(LOW))
            ds00 = ds00 + nt(dys[k][top], values[top]) * l00
            ds10 = ds10 + nt(dys[k][low], values[top]) * l10
            ds11 = ds11 + nt(dys[k][low], values[low]) * l11
        v0 = tn(
            jnp.concatenate([m00[0], m10[0], m00[1], m10[1]], axis=0), jnp.concatenate([dys[0], dys[1]], axis=0)
        )
        v1 = tn(
            jnp.concatenate([m11[0], m11[1]], axis=0), jnp.concatenate([dys[0][low], dys[1][low]], axis=0)
        )
        tail = d_packed[:, columns] * weight_w[:, columns]
        part = jnp.concatenate([v0, v1], axis=0) + tail
        dval_o[:, columns] = part + through_w[:, columns] * dy.astype(WIDE)
        value_parts.append(values_f * part)
        tails.append(jnp.sum(tail * values_f, axis=0, keepdims=True))
        packed.append((values_f * weight_w[:, columns]).astype(LOW))

    ds = jnp.concatenate(
        [
            jnp.concatenate([jnp.where(lower_mask, ds00, 0.0), jnp.zeros((BLOCK, BLOCK), WIDE)], axis=1),
            jnp.concatenate([ds10 * second, jnp.where(lower_mask, ds11, 0.0)], axis=1),
        ],
        axis=0,
    ).astype(LOW)
    d_read = nn(ds, write) + nn(d_query, start.astype(LOW))
    d_write = tn(ds, read) + nn(jnp.concatenate(packed, axis=1), end_low)
    for z, chunk in enumerate(chunk_lanes(jnp.concatenate([d_write, d_read], axis=1), line)):
        daddr_o[z] = chunk.astype(LOW)

    dy_f = d_ssd[...].astype(WIDE)
    own = to_heads(dy_f * act[:, :inner].astype(WIDE), collect)
    r1 = to_heads(dy_f * ssd[...], collect) - vec[2:3, :] * own
    w = to_heads(jnp.concatenate(value_parts, axis=1), collect)
    tail_row = to_heads(jnp.broadcast_to(jnp.concatenate(tails, axis=1), (EDGE, inner)), collect)[0:1]
    high, rest = halves(end * start)
    ones = jnp.ones((EDGE, STATE), LOW)
    carry_grad = to_heads(nt(ones, high) + nt(ones, rest), collect)[0:1]
    d_last = tail_row + carry_grad * (jnp.exp(last) * (first * second))
    d_cum = r1 - w + jnp.where(row == GROUP - 1, d_last, 0.0)
    d_rate = sum_after(d_cum)
    d_raw = d_rate * scale * sig + w * ratio
    dstep_o[...] = d_raw.astype(LOW)
    tiny_o[0:1, :] += jnp.sum(d_raw, axis=0, keepdims=True)
    tiny_o[1:2, :] += jnp.sum(d_rate * steps, axis=0, keepdims=True) * scale
    tiny_o[2:3, :] += jnp.sum(own, axis=0, keepdims=True)

    @pl.when(i == blocks - 1)
    def _():
        if line > 1:

            @pl.loop(1, line)
            def _(n):
                other = lax.rem(mine + n, line)
                out_copy(other, other).wait()

        for which in range(2):

            @pl.loop(1, seqs)
            def _(n):
                other = lax.rem(me + n, seqs)
                w_copy(which, other, other).wait()

        for copy in own_copies:
            copy.wait()


def back(flags, msg, d_ssd, ssd, act, cum, raw, starts, q, vec, out_part, gread, ggate, heads):
    seqs, line = lax.axis_size("seq"), lax.axis_size("head")
    rows, inner = d_ssd.shape
    wide = act.shape[1]
    total = gread.shape[0]
    depth = total // seqs
    blocks = rows // GROUP
    fold = LANES * line // (2 * STATE)

    def by_rows(width):
        return blockwise((GROUP, width), lambda i: (blocks - 1 - i, 0))

    state = blockwise((1, inner, STATE), lambda i: (blocks - 1 - i, 0, 0))
    return pl.pallas_call(
        functools.partial(back_kernel, seqs, line, heads, blocks),
        grid=(blocks,),
        out_shape=(
            shape((rows, inner), WIDE), shape((line, rows // fold, LANES), LOW), shape((rows, LANES), LOW),
            shape((EDGE, LANES), WIDE), shape(out_part.shape, LOW), shape((seqs, depth, inner), LOW),
            shape((seqs, depth, inner), LOW),
        ),
        in_specs=[
            SMEM_SPEC, VMEM_SPEC, by_rows(inner), by_rows(inner), by_rows(wide), by_rows(LANES), by_rows(LANES),
            state, state, fixed(vec.shape), ANY_SPEC, ANY_SPEC, ANY_SPEC,
        ],
        out_specs=(
            by_rows(inner), blockwise((line, GROUP // fold, LANES), lambda i: (0, blocks - 1 - i, 0)), by_rows(LANES),
            fixed((EDGE, LANES)), ANY_SPEC, ANY_SPEC, ANY_SPEC,
        ),
        scratch_shapes=[
            pltpu.VMEM((inner, STATE), WIDE), pltpu.VMEM((seqs, inner + HALO, STATE), LOW),
            DMA((seqs,)), DMA((seqs,)), DMA((seqs,)), DMA((line,)), DMA((line,)), DMA((2, seqs)), DMA((2, seqs)),
            DMA((3,)),
        ],
        compiler_params=pltpu.CompilerParams(
            collective_id=2, has_side_effects=True, vmem_limit_bytes=56 * MIB, dimension_semantics=("arbitrary",)
        ),
        name="back",
    )(flags, msg, d_ssd, ssd, act, cum, raw, starts, q, vec, out_part, gread, ggate)


def conv_grad(d_act, conv):
    sig = sigmoid(conv)
    return d_act * (sig * (1.0 + conv * (1.0 - sig)))


def last_kernel(
    seqs, line, heads, blocks, flags, give, take,
    daddr, dval, dval_next, conv, conv_next, pre, normed, u, dgate, dstep, w, prenorm, kernels, filters, rim,
    out_got, work_x, work_g, sums, gread_got, ggate_got, tiny, gpost,
    out_o, dx_o, prenorm_o, gate_o, pay_o, addr_o, step_o, kernels_o, offsets_o, filters_o, shifts_o,
    tiny_o, post_o, read_o,
    d_addr, addr_got, edge_own, edge_got, ext, after, prev, taps_g, bias_g, dx_send, dx_got, dw, dw_low, dw_got,
    pn, pn_send, pn_got, small, small_got, result, fin_send, out_recv, grad_recv,
    addr_sent, addr_sem, edge_sent, edge_sem, dx_sent, dx_sem, dw_sent, dw_sem, pn_sent, pn_sem,
    small_sent, small_sem, fin_sent, fin_sem, own_sem,
):
    i = pl.program_id(0)
    me, mine = lax.axis_index("seq"), lax.axis_index("head")
    inner = dgate.shape[1]
    tiles = work_g.shape[0] // BLOCK
    rows = work_g.shape[0]
    width = work_g.shape[1]
    depth = dw_got.shape[1]
    size = 2 * STATE // line
    fold = LANES // size
    tall = GROUP // fold
    slab = mine * size // LANES
    offset = lax.rem(mine * size, LANES)
    here = pl.ds(pl.multiple_of(i * GROUP, GROUP), GROUP)
    wide = inner + LANES

    def slab_of(ref, at):
        return ref[:, pl.ds(pl.multiple_of(at + slab * LANES, LANES), LANES)]

    def addr_copy(to, slot):
        return remote(daddr.at[to], addr_got.at[slot], addr_sent.at[to], addr_sem.at[slot], {"head": to})

    def edge_copy(to):
        return remote(edge_own, edge_got, edge_sent, edge_sem, {"seq": to})

    def dx_copy(to, slot, block):
        part = pl.ds(pl.multiple_of(block * GROUP, GROUP), GROUP)
        return remote(
            dx_send.at[to, part], dx_got.at[slot, part], dx_sent.at[to, block], dx_sem.at[slot, block], {"head": to}
        )

    def rows_of(device):
        return pl.ds(pl.multiple_of(device * depth, depth), depth)

    def dw_copy(to, slot):
        return remote(dw_low.at[rows_of(to)], dw_got.at[slot], dw_sent.at[to], dw_sem.at[slot], {"seq": to})

    def pn_copy(to, slot):
        return remote(pn_send.at[to], pn_got.at[slot], pn_sent.at[to], pn_sem.at[slot], {"head": to})

    def small_copy(to, slot):
        return remote(small, small_got.at[slot], small_sent.at[to], small_sem.at[slot], {"seq": to})

    arrivals = (out_recv, grad_recv)

    def fin_copy(which, to, slot):
        return remote(
            fin_send.at[which, to], arrivals[which].at[slot], fin_sent.at[which, to], fin_sem.at[which, slot],
            {"seq": to},
        )

    def all_seq(body):
        @pl.loop(1, seqs)
        def _(n):
            body(lax.rem(me + n, seqs))

    def all_line(body):
        if line > 1:

            @pl.loop(1, line)
            def _(n):
                body(lax.rem(mine + n, line))

    def route(which):
        def send(to):
            fin_send[which, to] = result[which, give[to]]
            fin_copy(which, to, me).start()

        all_seq(send)
        arrivals[which][me] = result[which, give[me]]

    def land(which, out):
        all_seq(lambda other: fin_copy(which, other, other).wait())
        for k in range(tiles):
            out[k] = arrivals[which][take[k]]

    @pl.when(i == 0)
    def _():
        greet(seqs, line)
        all_line(lambda to: addr_copy(to, mine).start())
        own = pltpu.make_async_copy(daddr.at[mine], addr_got.at[mine], own_sem)
        own.start()

        @pl.loop(0, blocks)
        def _(b):
            part = pl.ds(pl.multiple_of(b * GROUP, GROUP), GROUP)
            stats = jnp.concatenate([sums[b], jnp.zeros((LANES - EDGE, GROUP), WIDE)], axis=0).T
            inv = lax.rsqrt(stats[:, 0:1] / INNER + EPS)
            total = out_got[0, part].astype(WIDE)
            for z in range(1, line):
                total = total + out_got[z, part].astype(WIDE)
            done = (work_x[part].astype(WIDE) + total * inv).astype(LOW)
            result[0, 2 * b] = done[:BLOCK]
            result[0, 2 * b + 1] = done[BLOCK:]

        route(0)
        all_line(lambda other: addr_copy(other, other).wait())
        own.wait()
        lane = lax.broadcasted_iota(jnp.int32, (tall, LANES), 1)
        inside = (lane >= offset) & (lane < offset + size)

        @pl.loop(0, blocks)
        def _(b):
            part = pl.ds(pl.multiple_of(b * tall, tall), tall)
            total = addr_got[0, part].astype(WIDE)
            for z in range(1, line):
                total = total + addr_got[z, part].astype(WIDE)
            for group in range(fold):
                turned = pltpu.roll(total, lax.rem(offset + (LANES - group * size), LANES), 1)
                at = pl.ds(pl.multiple_of(b * GROUP + group * tall, tall), tall)
                d_addr[at, :] = jnp.where(inside, turned, 0.0)

        edge_own[:, :inner] = conv_grad(dval[0:EDGE, :], conv[0:EDGE, :inner])
        edge_own[:, inner:] = conv_grad(d_addr[0:EDGE, :], slab_of(conv, inner)[0:EDGE])
        edge_copy(lax.rem(me + seqs - 1, seqs)).start()
        prev[:, :inner] = rim[:, :inner]
        prev[:, inner:] = slab_of(rim, inner)
        taps_g[...] = jnp.zeros_like(taps_g)
        bias_g[...] = jnp.zeros_like(bias_g)
        dw[...] = jnp.zeros_like(dw)
        pn[...] = jnp.zeros_like(pn)

    @pl.when(i < blocks - 1)
    def _():
        after[:, :inner] = conv_grad(dval_next[...], conv_next[:, :inner])
        following = pl.ds(pl.multiple_of((i + 1) * GROUP, GROUP), EDGE)
        after[:, inner:] = conv_grad(d_addr[following, :], slab_of(conv_next, inner))

    @pl.when(i == blocks - 1)
    def _():
        edge_copy(lax.rem(me + 1, seqs)).wait()
        after[...] = edge_got[...]

    taps = jnp.concatenate([kernels[...], slab_of(filters, 0)], axis=1)
    conv_v = jnp.concatenate([conv[:, :inner], slab_of(conv, inner)], axis=1)
    pre_v = jnp.concatenate([pre[:, :inner], slab_of(pre, inner)], axis=1).astype(WIDE)
    d_conv = conv_grad(jnp.concatenate([dval[...], d_addr[here, :]], axis=1), conv_v)
    bias_g[...] += jnp.sum(d_conv, axis=0, keepdims=True)
    d_pre = []
    for half in range(2):
        at = slice(half * BLOCK, (half + 1) * BLOCK)
        tile = d_conv[at]
        ext[0:EDGE, :] = prev[...] * flags[2 * i + half]
        ext[EDGE:, :] = pre_v[at]
        prev[...] = ext[BLOCK:, :]
        for tap in range(TAPS):
            taps_g[tap : tap + 1, :] += jnp.sum(
                tile * ext[pl.ds(EDGE - (TAPS - 1) + tap, BLOCK), :], axis=0, keepdims=True
            )
        ext[:BLOCK, :] = tile
        following = d_conv[BLOCK : BLOCK + EDGE] if half == 0 else after[...]
        ext[BLOCK:, :] = following * flags[2 * i + half + 1]
        total = taps[TAPS - 1 : TAPS] * ext[:BLOCK, :]
        for tap in range(TAPS - 1):
            total = total + taps[tap : tap + 1] * ext[pl.ds(TAPS - 1 - tap, BLOCK), :]
        d_pre.append(total.astype(LOW))
    d_pre = jnp.concatenate(d_pre, axis=0)
    d_value, d_slab = d_pre[:, :inner], d_pre[:, inner:]
    d_step = dstep[...]
    normed_v = normed[...]
    dw[:, :wide] += tn(normed_v, d_pre)
    dw[:, wide:] += tn(normed_v, d_step)
    d_normed = (
        nt(dgate[...], w[:, :inner])
        + nt(d_value, w[:, inner : 2 * inner])
        + nt(d_slab, slab_of(w, 2 * inner))
        + nt(d_step, w[:, 2 * inner + 2 * STATE :])
    )
    u_f = u[...].astype(WIDE)
    inv = lax.rsqrt(jnp.mean(u_f * u_f, axis=1, keepdims=True) + EPS)
    gained = d_normed * prenorm[...]
    dot = jnp.sum(gained * u_f, axis=1, keepdims=True)
    grad = gained * inv - u_f * (inv * inv * inv / D * dot)
    pn[...] += jnp.sum(d_normed * (u_f * inv), axis=0, keepdims=True)
    for z in range(line):
        dx_send[z, here] = grad[:, z * width : (z + 1) * width].astype(LOW)
    dx_got[mine, here] = dx_send[mine, here]
    all_line(lambda to: dx_copy(to, mine, i).start())

    @pl.when(i == blocks - 1)
    def _():
        dw_low[...] = dw[...].astype(LOW)
        all_seq(lambda to: dw_copy(to, me).start())
        for z in range(line):
            pn_send[z] = jnp.broadcast_to(pn[:, z * width : (z + 1) * width], (EDGE, width))
        pn_got[mine] = pn_send[mine]
        all_line(lambda to: pn_copy(to, mine).start())
        dw_got[me] = dw_low[rows_of(me), :]

        def summed(ref):
            total = ref[0].astype(WIDE)
            for n in range(1, seqs):
                total = total + ref[n].astype(WIDE)
            return total

        read_o[...] = summed(gread_got).T
        gate_o[...] = summed(ggate_got)
        all_line(lambda other: pn_copy(other, other).wait())
        small[...] = jnp.zeros_like(small)
        small[0:TAPS, :] = taps_g[0:TAPS, :]
        small[4:5, :] = bias_g[...]
        small[5:6, :inner] = gpost[...]
        small[6:7, :width] = jnp.sum(pn_got[...], axis=0)[0:1]
        for n in range(3):
            small[7:8, n * LANES : (n + 1) * LANES] = tiny[n : n + 1, :]
        small_got[me] = small[...]
        all_seq(lambda to: small_copy(to, me).start())

        @pl.loop(0, blocks)
        def _(b):
            all_line(lambda other: dx_copy(other, other, b).wait())
            part = pl.ds(pl.multiple_of(b * GROUP, GROUP), GROUP)
            total = dx_got[0, part].astype(WIDE)
            for z in range(1, line):
                total = total + dx_got[z, part].astype(WIDE)
            done = (work_g[part].astype(WIDE) + total).astype(LOW)
            result[1, 2 * b] = done[:BLOCK]
            result[1, 2 * b + 1] = done[BLOCK:]

        route(1)
        all_seq(lambda other: dw_copy(other, other).wait())
        grads = summed(dw_got)
        pay_o[...] = grads[:, :inner]
        back_turn = lax.rem(LANES - offset, LANES)
        addr_o[...] = pltpu.roll(grads[:, inner:wide], back_turn, 1)[:, :size]
        step_o[...] = grads[:, wide : wide + heads]
        all_seq(lambda other: small_copy(other, other).wait())
        totals = jnp.sum(small_got[...], axis=0)
        kernels_o[...] = totals[0:TAPS, :inner]
        offsets_o[...] = totals[4:5, :inner]
        turned = pltpu.roll(totals[:, inner:], back_turn, 1)
        filters_o[...] = turned[0:TAPS, :size]
        shifts_o[...] = turned[4:5, :size]
        post_o[...] = totals[5:6, :inner]
        prenorm_o[...] = totals[6:7, :width]
        for n in range(3):
            tiny_o[n : n + 1, :] = totals[7:8, n * LANES : n * LANES + heads]
        land(0, out_o)
        land(1, dx_o)


def last(
    flags, give, take, daddr, dval, conv, pre, normed, x_full, dgate, dstep, w_all, prenorm, kernels, filters, rim,
    out_got, work_x, work_g, sums, gread_got, ggate_got, tiny, gpost, heads,
):
    seqs, line = lax.axis_size("seq"), lax.axis_size("head")
    rows, width = work_g.shape
    inner = dgate.shape[1]
    wide = conv.shape[1]
    total = x_full.shape[1]
    depth = total // seqs
    blocks, tiles = rows // GROUP, rows // BLOCK
    size = 2 * STATE // line
    part = inner + LANES
    step = GROUP // EDGE

    def by_rows(columns):
        return blockwise((GROUP, columns), lambda i: (i, 0))

    def next_rows(columns):
        return blockwise((EDGE, columns), lambda i: (jnp.minimum((i + 1) * step, rows // EDGE - 1), 0))

    grid_whole = (VMEM_SPEC,)
    return pl.pallas_call(
        functools.partial(last_kernel, seqs, line, heads, blocks),
        grid=(blocks,),
        out_shape=(
            shape((tiles, BLOCK, width), LOW), shape((tiles, BLOCK, width), LOW), shape((1, width), WIDE),
            shape((depth, inner), WIDE), shape((depth, inner), WIDE), shape((depth, size), WIDE),
            shape((depth, heads), WIDE), shape((TAPS, inner), WIDE), shape((1, inner), WIDE),
            shape((TAPS, size), WIDE), shape((1, size), WIDE), shape((3, heads), WIDE), shape((1, inner), WIDE),
            shape((inner, depth), WIDE),
        ),
        in_specs=[SMEM_SPEC] * 3 + [
            ANY_SPEC, by_rows(inner), next_rows(inner), by_rows(wide), next_rows(wide), by_rows(wide), by_rows(total),
            by_rows(total), by_rows(inner), by_rows(LANES), VMEM_SPEC, VMEM_SPEC, VMEM_SPEC, VMEM_SPEC, VMEM_SPEC,
        ] + [VMEM_SPEC] * 8,
        out_specs=grid_whole * 14,
        scratch_shapes=[
            pltpu.VMEM((rows, LANES), WIDE), pltpu.VMEM(daddr.shape, LOW),
            pltpu.VMEM((EDGE, part), WIDE), pltpu.VMEM((EDGE, part), WIDE),
            pltpu.VMEM((BLOCK + EDGE, part), WIDE), pltpu.VMEM((EDGE, part), WIDE), pltpu.VMEM((EDGE, part), WIDE),
            pltpu.VMEM((EDGE, part), WIDE), pltpu.VMEM((1, part), WIDE),
            pltpu.VMEM((line, rows, width), LOW), pltpu.VMEM((line, rows, width), LOW),
            pltpu.VMEM((total, part + LANES), WIDE), pltpu.VMEM((total, part + LANES), LOW),
            pltpu.VMEM((seqs, depth, part + LANES), LOW),
            pltpu.VMEM((1, total), WIDE), pltpu.VMEM((line, EDGE, width), WIDE), pltpu.VMEM((line, EDGE, width), WIDE),
            pltpu.VMEM((EDGE, part), WIDE), pltpu.VMEM((seqs, EDGE, part), WIDE),
            pltpu.VMEM((2, tiles, BLOCK, width), LOW), pltpu.VMEM((2, seqs, BLOCK, width), LOW),
            pltpu.VMEM((seqs, BLOCK, width), LOW), pltpu.VMEM((seqs, BLOCK, width), LOW),
            DMA((line,)), DMA((line,)), DMA, DMA, DMA((line, blocks)), DMA((line, blocks)), DMA((seqs,)), DMA((seqs,)),
            DMA((line,)), DMA((line,)), DMA((seqs,)), DMA((seqs,)), DMA((2, seqs)), DMA((2, seqs)), DMA,
        ],
        compiler_params=pltpu.CompilerParams(
            collective_id=3, has_side_effects=True, vmem_limit_bytes=62 * MIB, dimension_semantics=("arbitrary",)
        ),
        name="last",
    )(
        flags, give, take, daddr, dval, dval, conv, conv, pre, normed, x_full, dgate, dstep, w_all, prenorm, kernels,
        filters, rim, out_got, work_x, work_g, sums, gread_got, ggate_got, tiny, gpost,
    )


def on_device(
    inputs,
    cotangent,
    lengths,
    placement,
    prenorm,
    gating,
    payload,
    address,
    stepping,
    kernels,
    offsets,
    filters,
    shifts,
    stepbias,
    decays,
    through,
    postnorm,
    readout,
):
    seq_count = lax.axis_size("seq")
    seq_index = lax.axis_index("seq")
    row_count, width = inputs.shape
    heads = stepbias.shape[0]
    per_dev = row_count // BLOCK
    devices = jnp.arange(seq_count, dtype=jnp.int32)
    slots = jnp.arange(per_dev, dtype=jnp.int32)
    block_ids = seq_index * per_dev + slots
    every_block = jnp.arange(placement.shape[0], dtype=jnp.int32)
    target = jnp.sum(
        jnp.where(placement[None, :] == block_ids[:, None], every_block[None, :], 0), axis=1
    )
    target_dev = target // per_dev
    source_dev = lax.dynamic_slice_in_dim(placement, seq_index * per_dev, per_dev, 0) // per_dev

    def block_for(owners):
        return jnp.sum(jnp.where(owners[None, :] == devices[:, None], slots[None, :], 0), axis=1)

    give_in, give_out = block_for(target_dev), block_for(source_dev)
    bounds = jnp.arange(per_dev + 1, dtype=jnp.int32) + seq_index * per_dev
    starts = bounds[:, None] * BLOCK == jnp.cumsum(lengths)[None, :]
    flags = jnp.where((bounds == 0) | jnp.any(starts, axis=1), 0.0, 1.0).astype(WIDE)

    x_full, g_full, w_all, r_t, work_x, work_g = spread(
        give_in, source_dev, inputs, cotangent, gating, payload, address, stepping, readout
    )
    vec = jnp.pad(jnp.stack([stepbias, decays, through]), ((0, EDGE - 3), (0, LANES - heads)))
    gain, post = prenorm[None, :], postnorm[None, :]
    normed, gate, pre, conv, act, raw, cum, part, local, msg, rim = front(
        flags, x_full, w_all, vec, gain, kernels, filters, offsets[None, :], shifts[None, :], heads
    )
    ssd, states, d_ssd, d_gate, out_part, back_msg, q, sums, gread, ggate, gpost = middle(
        flags, msg, gate, part, act, cum, local, g_full, normed, r_t, post
    )
    dval, daddr, dstep, tiny, out_got, gread_got, ggate_got = back(
        flags, back_msg, d_ssd, ssd, act, cum, raw, states, q, vec, out_part, gread, ggate, heads
    )
    (
        out, dx, prenorm_g, gate_g, pay_g, addr_g, step_g, kernels_g, offsets_g, filters_g, shifts_g, tiny_g,
        post_g, read_g,
    ) = last(
        flags, give_out, target_dev, daddr, dval, conv, pre, normed, x_full, d_gate, dstep, w_all, gain, kernels,
        filters, rim, out_got, work_x, work_g, sums, gread_got, ggate_got, tiny, gpost, heads
    )
    return (
        out.reshape(row_count, width),
        dx.reshape(row_count, width),
        prenorm_g[0],
        gate_g,
        pay_g,
        addr_g,
        step_g,
        kernels_g,
        offsets_g[0],
        filters_g,
        shifts_g[0],
        tiny_g[0],
        tiny_g[1],
        tiny_g[2],
        post_g[0],
        read_g,
    )


def solution(mesh):
    in_specs = (
        P("seq", "head"),
        P("seq", "head"),
        P(),
        P(),
        P(),
        P("seq", "head"),
        P("seq", "head"),
        P("seq", None),
        P("seq", "head"),
        P(None, "head"),
        P("head"),
        P(),
        P(),
        P("head"),
        P("head"),
        P("head"),
        P("head"),
        P("head", "seq"),
    )
    out_specs = (
        P("seq", "head"),
        P("seq", "head"),
        P("head"),
        P("seq", "head"),
        P("seq", "head"),
        P("seq", "head"),
        P("seq", "head"),
        P(None, "head"),
        P("head"),
        P(None, "head"),
        P("head"),
        P("head"),
        P("head"),
        P("head"),
        P("head"),
        P("head", "seq"),
    )
    return jax.shard_map(
        on_device, mesh=mesh, in_specs=in_specs, out_specs=out_specs, check_vma=False
    )
```

```python
import functools

import jax
import jax.numpy as jnp
from jax import lax
from jax.experimental import pallas as pl
from jax.experimental.pallas import tpu as pltpu
from jax.sharding import PartitionSpec as P

D = 1024
GROUP = 256
BLOCK = 128
INNER = 2048
HDIM = 64
STATE = 128
TAPS = 4
HALO = 16
EDGE = 8
LANES = 128
EPS = 1e-05
MESH = pl.DeviceIdType.MESH
VMEM = pltpu.MemorySpace.VMEM
SMEM = pltpu.MemorySpace.SMEM
DMA = pltpu.SemaphoreType.DMA
VMEM_LIMIT = 63 << 20
LOW = jnp.bfloat16
WIDE = jnp.float32


def shape(dims, kind):
    return jax.ShapeDtypeStruct(dims, kind)


def nn(a, b):
    return jnp.dot(a, b, preferred_element_type=WIDE)


def nt(a, b):
    return lax.dot_general(a, b, (((1,), (1,)), ((), ())), preferred_element_type=WIDE)


def tn(a, b):
    return lax.dot_general(a, b, (((0,), (0,)), ((), ())), preferred_element_type=WIDE)


def halves(x):
    high = x.astype(LOW)
    return high, (x - high.astype(WIDE)).astype(LOW)


def thirds(x):
    high = x.astype(LOW)
    rest = x - high.astype(WIDE)
    middle = rest.astype(LOW)
    return high, middle, (rest - middle.astype(WIDE)).astype(LOW)


def head_rows(inner):
    row = lax.broadcasted_iota(jnp.int32, (LANES, inner), 0)
    column = lax.broadcasted_iota(jnp.int32, (LANES, inner), 1)
    return jnp.where(column // HDIM == row, 1.0, 0.0).astype(LOW)


def head_columns(inner):
    row = lax.broadcasted_iota(jnp.int32, (inner, LANES), 0)
    column = lax.broadcasted_iota(jnp.int32, (inner, LANES), 1)
    return jnp.where(row // HDIM == column, 1.0, 0.0).astype(LOW)


def to_columns(x, spread):
    high, rest = halves(x)
    return nn(high, spread) + nn(rest, spread)


def to_heads(x, collect):
    high, rest = halves(x)
    return nn(high, collect) + nn(rest, collect)


def ones_before(count):
    row = lax.broadcasted_iota(jnp.int32, (count, count), 0)
    column = lax.broadcasted_iota(jnp.int32, (count, count), 1)
    return row >= column


def sum_before(x):
    matrix = jnp.where(ones_before(x.shape[0]), 1.0, 0.0).astype(LOW)
    high, middle, low = thirds(x)
    return nn(matrix, high) + (nn(matrix, middle) + nn(matrix, low))


def sum_after(x):
    count = x.shape[0]
    row = lax.broadcasted_iota(jnp.int32, (count, count), 0)
    column = lax.broadcasted_iota(jnp.int32, (count, count), 1)
    matrix = jnp.where(row <= column, 1.0, 0.0).astype(LOW)
    high, middle, low = thirds(x)
    return nn(matrix, high) + (nn(matrix, middle) + nn(matrix, low))


def sigmoid(x):
    return 0.5 * jnp.tanh(0.5 * x) + 0.5


def step_terms(raw, heads):
    z = jnp.exp(-jnp.abs(raw))
    series = 1.0 - z * (0.5 - z * (1.0 / 3.0 - z * (0.25 - z * 0.2)))
    small = z < 0.03
    log1p = jnp.where(small, z * series, jnp.log(1.0 + z))
    soft = jnp.maximum(raw, 0.0) + log1p
    one = 1.0 / (1.0 + z)
    sig = jnp.where(raw >= 0, one, z * one)
    ratio = jnp.where(small & (raw < 0), one / series, sig / jnp.maximum(soft, 1e-20))
    lane = lax.broadcasted_iota(jnp.int32, raw.shape, 1)
    return jnp.where(lane < heads, soft, 0.0), sig, ratio


def greet(seq_peers, head_peers):
    barrier = pltpu.get_barrier_semaphore()
    count = 0
    if seq_peers > 1:
        me = lax.axis_index("seq")

        @pl.loop(1, seq_peers)
        def _(i):
            pl.semaphore_signal(
                barrier, inc=1, device_id={"seq": lax.rem(me + i, seq_peers)}, device_id_type=MESH
            )

        count += seq_peers - 1
    if head_peers > 1:
        mine = lax.axis_index("head")

        @pl.loop(1, head_peers)
        def _(i):
            pl.semaphore_signal(
                barrier, inc=1, device_id={"head": lax.rem(mine + i, head_peers)}, device_id_type=MESH
            )

        count += head_peers - 1
    pl.semaphore_wait(barrier, count)


def remote(src, dst, send_sem, recv_sem, where):
    return pltpu.make_async_remote_copy(
        src_ref=src, dst_ref=dst, send_sem=send_sem, recv_sem=recv_sem, device_id=where, device_id_type=MESH
    )


class Line:
    def __init__(self, count, out, width, send, recv):
        self.count, self.out, self.width, self.send, self.recv = count, out, width, send, recv
        self.me = lax.axis_index("head")

    def view(self, shard):
        return self.out.at[:, pl.ds(pl.multiple_of(shard * self.width, LANES), self.width)]

    def copy(self, src, shard, way, step):
        return remote(
            src, self.view(shard), self.send.at[way, step], self.recv.at[shard], {"head": self.me + (1 - 2 * way)}
        )

    def first(self, own):
        self.pass_on(own, self.me, 0, 0)
        self.pass_on(own, self.me, 1, 0)

    def pass_on(self, src, shard, way, step):
        reach = (self.me < self.count - 1) if way == 0 else (self.me > 0)

        @pl.when(reach)
        def _():
            self.copy(src, shard, way, step).start()

    def hop(self, step, take=True, give=True, source=None):
        for way in (0, 1):
            shard = self.me - step if way == 0 else self.me + step
            there = (shard >= 0) if way == 0 else (shard < self.count)

            @pl.when(there)
            def _():
                if take:
                    self.copy(self.view(shard), shard, way, step).wait_recv()
                if give and step < self.count - 1:
                    self.pass_on(self.view(shard) if source is None else source(shard), shard, way, step)

    def finish(self, own, steps=None):
        for way in (0, 1):
            reach = (self.me < self.count - 1) if way == 0 else (self.me > 0)
            for step in range(self.count - 1) if steps is None else steps:
                shard = self.me - step if way == 0 else self.me + step
                there = (shard >= 0) if way == 0 else (shard < self.count)

                @pl.when(reach & there)
                def _():
                    src = own if step == 0 else self.view(shard)
                    self.copy(src, shard, way, step).wait_send()


class Plane:
    def __init__(self, seqs, view, sent, got, passed, way=0):
        self.chips, self.view, self.sent, self.got, self.passed, self.way = seqs // 2, view, sent, got, passed, way
        self.me = lax.axis_index("seq")
        self.core = lax.rem(self.me, 2)
        self.chip = self.me // 2
        self.mate = self.me + 1 - 2 * self.core

    def forward(self, chip):
        return (chip > self.chip) if self.way == 1 else (chip < self.chip) if self.way == -1 else (chip >= 0)

    def backward(self, chip):
        return (chip < self.chip) if self.way == 1 else (chip > self.chip) if self.way == -1 else (chip >= 0)

    def each_chip(self, body):
        @pl.loop(1, self.chips)
        def _(i):
            body(lax.rem(self.chip + i, self.chips))

    def copy(self, src, source, to, sem):
        return remote(src, self.view(source), sem, self.got.at[source], {"seq": to})

    def start(self, own):
        def send(chip):
            to = 2 * chip + self.core

            @pl.when(self.forward(chip))
            def _():
                self.copy(own, self.me, to, self.sent.at[to]).start()

        self.each_chip(send)
        self.copy(own, self.me, self.mate, self.sent.at[self.mate]).start()

    def relay(self):
        def take(chip):
            source = 2 * chip + self.core

            @pl.when(self.backward(chip))
            def _():
                landed = self.view(source)
                self.copy(landed, source, self.mate, self.passed.at[source]).wait_recv()
                self.copy(landed, source, self.mate, self.passed.at[source]).start()

        self.each_chip(take)

    def finish(self, own):
        def take(chip):
            source = 2 * chip + 1 - self.core

            @pl.when(self.backward(chip))
            def _():
                self.copy(self.view(source), source, self.mate, self.passed.at[source]).wait_recv()

        self.each_chip(take)
        self.copy(self.view(self.mate), self.mate, self.mate, self.sent.at[self.mate]).wait_recv()
        self.copy(own, self.me, self.mate, self.sent.at[self.mate]).wait_send()

        def drain(chip):
            same = 2 * chip + self.core

            @pl.when(self.forward(chip))
            def _():
                self.copy(own, self.me, same, self.sent.at[same]).wait_send()

            @pl.when(self.backward(chip))
            def _():
                self.copy(self.view(same), same, self.mate, self.passed.at[same]).wait_send()

        self.each_chip(drain)


ANY_SPEC = pl.BlockSpec(memory_space=pl.ANY)
VMEM_SPEC = pl.BlockSpec(memory_space=VMEM)
SMEM_SPEC = pl.BlockSpec(memory_space=SMEM)


def index_kernel(
    seqs, tiles, place, lengths, stepbias, decays, through, give_in, take_in, give_out, take_out, flags, vec
):
    me = lax.axis_index("seq")

    @pl.loop(0, seqs * tiles)
    def _(j):
        block = place[j]

        @pl.when(lax.div(block, tiles) == me)
        def _():
            to = lax.div(j, tiles)
            give_in[to] = lax.rem(block, tiles)
            take_out[lax.rem(block, tiles)] = to

    @pl.loop(0, tiles)
    def _(k):
        source = lax.div(place[me * tiles + k], tiles)
        take_in[k] = source
        give_out[source] = k

    @pl.loop(0, tiles + 1)
    def _(k):
        position = (me * tiles + k) * BLOCK
        end = jnp.int32(0)
        border = position == 0
        for n in range(lengths.shape[0]):
            end = end + lengths[n]
            border = border | (position == end)
        flags[k] = jnp.where(border, 0.0, 1.0)

    heads = stepbias.shape[1]
    vec[...] = jnp.zeros_like(vec)
    vec[0:1, :heads] = stepbias[...]
    vec[1:2, :heads] = decays[...]
    vec[2:3, :heads] = through[...]


def index(place, lengths, stepbias, decays, through, tiles):
    seqs = lax.axis_size("seq")
    whole = jnp.int32
    return pl.pallas_call(
        functools.partial(index_kernel, seqs, tiles),
        out_shape=(
            shape((seqs,), whole), shape((tiles,), whole), shape((seqs,), whole), shape((tiles,), whole),
            shape((tiles + 1,), WIDE), shape((EDGE, LANES), WIDE),
        ),
        in_specs=[SMEM_SPEC] * 2 + [VMEM_SPEC] * 3,
        out_specs=(SMEM_SPEC,) * 5 + (VMEM_SPEC,),
        compiler_params=pltpu.CompilerParams(vmem_limit_bytes=VMEM_LIMIT),
        name="index",
    )(place, lengths, stepbias[None, :], decays[None, :], through[None, :])


def spread_kernel(
    seqs, heads, chunks, give, take, x_in, g_in, gating_in, payload_in, address_in, stepping_in, readout_in,
    x_out, w_out, r_out, work_x, work_g,
    x, g, gating, payload, address, stepping, readout, square,
    send_x, send_g, recv_x, recv_g, w_own, r_own,
    sent, got, w_sent, w_got, w_passed, r_sent, r_got, r_passed, rim_sent, rim_got, own_sem, load_sem,
    line_sent, line_got,
):
    me, mine = lax.axis_index("seq"), lax.axis_index("head")
    blocks, _, width = x.shape
    rows = blocks * BLOCK
    depth, inner = gating.shape
    pairs = (
        (x_in, x), (g_in, g), (gating_in, gating), (payload_in, payload), (address_in, address),
        (stepping_in, stepping), (readout_in, readout),
    )
    loads = [pltpu.make_async_copy(src, dst, load_sem.at[n]) for n, (src, dst) in enumerate(pairs)]
    for load in loads:
        load.start()
    greet(seqs, heads)

    def post(which, source, outgoing, incoming):
        @pl.loop(1, seqs)
        def _(i):
            to = lax.rem(me + i, seqs)
            outgoing[to] = source[give[to]]
            remote(outgoing.at[to], incoming.at[me], sent.at[which, to], got.at[which, me], {"seq": to}).start()

        incoming[me] = source[give[me]]

    loads[0].wait()
    post(0, x, send_x, recv_x)
    for load in loads[1:]:
        load.wait()

    w_own[:, :inner] = gating[...].astype(LOW)
    w_own[:, inner : 2 * inner] = payload[...].astype(LOW)
    state2 = address.shape[1]
    w_own[:, 2 * inner : 2 * inner + state2] = address[...].astype(LOW)
    square[...] = jnp.zeros_like(square)
    square[: stepping.shape[0], :depth] = stepping[...]
    w_own[:, 2 * inner + state2 :] = square[...].T[:depth].astype(LOW)
    r_own[...] = readout[...].T.astype(LOW)

    def rows_of(device):
        return pl.ds(pl.multiple_of(device * depth, depth), depth)

    own_w = pltpu.make_async_copy(w_own, w_out.at[rows_of(me)], own_sem.at[0])
    own_r = pltpu.make_async_copy(r_own, r_out.at[rows_of(me)], own_sem.at[1])
    own_w.start()
    own_r.start()
    w_plane = Plane(seqs, lambda s: w_out.at[rows_of(s)], w_sent, w_got, w_passed)
    r_plane = Plane(seqs, lambda s: r_out.at[rows_of(s)], r_sent, r_got, r_passed)

    def arrange(which, received, work):
        @pl.loop(1, seqs)
        def _(i):
            source = lax.rem(me + i, seqs)
            remote(
                received.at[source], received.at[source], sent.at[which, source], got.at[which, source], {"seq": source}
            ).wait_recv()

        for k in range(blocks):
            work[pl.ds(k * BLOCK, BLOCK), :] = received[take[k]]

    arrange(0, recv_x, work_x)
    part = rows // chunks
    pieces = [(n * part, part) for n in range(chunks)] + [(rows, HALO)]
    lines = [
        Line(heads, x_out.at[pl.ds(at, size)], width, line_sent.at[n], line_got.at[n])
        for n, (at, size) in enumerate(pieces)
    ]
    owns = [work_x.at[pl.ds(at, size)] for at, size in pieces]
    after = lax.rem(me + 1, seqs)
    rim = remote(
        work_x.at[pl.ds(rows - HALO, HALO)], work_x.at[pl.ds(rows, HALO)], rim_sent, rim_got, {"seq": after}
    )
    rim.start()
    for line, own in zip(lines[:-1], owns[:-1]):
        line.first(own)
    w_plane.start(w_own)
    own_columns = x_out.at[pl.ds(0, rows), pl.ds(pl.multiple_of(mine * width, LANES), width)]
    own_x = pltpu.make_async_copy(work_x.at[pl.ds(0, rows)], own_columns, own_sem.at[2])
    own_x.start()
    rim.wait()
    lines[-1].first(owns[-1])
    own_rim = pltpu.make_async_copy(owns[-1], lines[-1].view(mine), own_sem.at[3])
    own_rim.start()
    post(1, g, send_g, recv_g)
    r_plane.start(r_own)
    for step in range(1, heads):
        for line in lines:
            line.hop(step)
        if step == 1:
            w_plane.relay()
    arrange(1, recv_g, work_g)
    r_plane.relay()
    for line, own in zip(lines, owns):
        line.finish(own)
    w_plane.finish(w_own)
    r_plane.finish(r_own)
    for copy in (own_w, own_r, own_x, own_rim):
        copy.wait()

    @pl.loop(1, seqs)
    def _(i):
        other = lax.rem(me + i, seqs)
        for which, buffer in ((0, send_x), (1, send_g)):
            remote(
                buffer.at[other], buffer.at[other], sent.at[which, other], got.at[which, other], {"seq": other}
            ).wait_send()


def spread(give, take, x, g, gating, payload, address, stepping, readout):
    seqs, heads = lax.axis_size("seq"), lax.axis_size("head")
    rows, width = x.shape
    depth, inner = gating.shape
    total = depth * seqs
    columns = 2 * inner + address.shape[1] + LANES
    block = (seqs, BLOCK, width)
    given = (rows // BLOCK, BLOCK, width)
    chunks = 4
    operands = (x.reshape(given), g.reshape(given), gating, payload, address, stepping.T, readout)
    return pl.pallas_call(
        functools.partial(spread_kernel, seqs, heads, chunks),
        out_shape=(
            shape((rows + HALO, total), LOW),
            shape((total, columns), LOW),
            shape((total, inner), LOW),
            shape((rows + HALO, width), LOW),
            shape((rows, width), LOW),
        ),
        in_specs=[SMEM_SPEC] * 2 + [ANY_SPEC] * 7,
        out_specs=(ANY_SPEC,) * 3 + (VMEM_SPEC,) * 2,
        scratch_shapes=[pltpu.VMEM(a.shape, a.dtype) for a in operands] + [
            pltpu.VMEM((LANES, LANES), WIDE),
            pltpu.VMEM(block, LOW), pltpu.VMEM(block, LOW), pltpu.VMEM(block, LOW), pltpu.VMEM(block, LOW),
            pltpu.VMEM((depth, columns), LOW), pltpu.VMEM((depth, inner), LOW),
            DMA((2, seqs)), DMA((2, seqs)),
            DMA((seqs,)), DMA((seqs,)), DMA((seqs,)), DMA((seqs,)), DMA((seqs,)), DMA((seqs,)),
            DMA, DMA, DMA((4,)), DMA((7,)),
            DMA((chunks + 1, 2, heads)), DMA((chunks + 1, heads)),
        ],
        compiler_params=pltpu.CompilerParams(
            collective_id=0, has_side_effects=True, vmem_limit_bytes=VMEM_LIMIT
        ),
        name="spread",
    )(give, take, *operands)


def blockwise(dims, index):
    return pl.BlockSpec(dims, index)


def fixed(dims):
    return pl.BlockSpec(dims, lambda i: (0,) * len(dims), pipeline_mode=pl.Buffered(1))


def carry_columns(carry_row_t, collect):
    high, middle, low = thirds(jnp.broadcast_to(carry_row_t, (LANES, LANES)))
    return nn(collect, high) + (nn(collect, middle) + nn(collect, low))


def pair_lanes(slab):
    lane = lax.broadcasted_iota(jnp.int32, slab.shape, 1)
    zero = jnp.zeros_like(slab)
    return jnp.where(lane < HDIM, slab, zero), jnp.where(lane >= HDIM, slab, zero)


def front_kernel(
    heads, line, flags, u, rim, w, vec, prenorm, kernels, filters, offsets, shifts, g,
    normed_o, gate_o, pre_o, conv_o, act_o, raw_o, cum_o, part_o, local_o, msg_o, rim_o, g_o,
    ext, prev, state, prod, line_sent, line_got, own_sem,
):
    i = pl.program_id(0)
    g_line = Line(line, g_o, g.shape[1], line_sent, line_got)
    own_g = pltpu.make_async_copy(g, g_line.view(g_line.me), own_sem)
    inner = gate_o.shape[1]
    wide = pre_o.shape[1]
    taps = jnp.concatenate([kernels[...], filters[...]], axis=1)
    bias = jnp.concatenate([offsets[...], shifts[...]], axis=1)
    spread_m, collect = head_rows(inner), head_columns(inner)

    def normalize(block):
        rows = block.astype(WIDE)
        scale = lax.rsqrt(jnp.mean(rows * rows, axis=1, keepdims=True) + EPS)
        return (rows * scale * prenorm[...]).astype(LOW)

    @pl.when(i == 0)
    def _():
        greet(1, line)
        g_line.first(g)
        own_g.start()
        before = nn(normalize(rim[...]), w[:, inner : inner + wide]).astype(LOW).astype(WIDE)
        prev[...] = before[HALO - EDGE :]
        rim_o[...] = before[HALO - EDGE :]
        state[...] = jnp.zeros_like(state)
        prod[...] = jnp.ones_like(prod)

    normed = normalize(u[...])
    normed_o[...] = normed
    gate_o[...] = nn(normed, w[:, :inner])
    pre = nn(normed, w[:, inner : inner + wide]).astype(LOW)
    pre_o[...] = pre
    lane = lax.broadcasted_iota(jnp.int32, (GROUP, LANES), 1)
    raw = jnp.where(lane < heads, nn(normed, w[:, inner + wide :]) + vec[0:1, :], 0.0)
    raw_o[...] = raw
    first, second = flags[2 * i], flags[2 * i + 1]
    same = (first, second)
    for half in range(2):
        rows = pl.ds(half * BLOCK, BLOCK)
        ext[0:EDGE, :] = prev[...] * same[half]
        ext[EDGE:, :] = pre[half * BLOCK : (half + 1) * BLOCK].astype(WIDE)
        prev[...] = ext[BLOCK:, :]
        total = bias + taps[TAPS - 1 : TAPS] * ext[EDGE:, :]
        for tap in range(TAPS - 1):
            total = total + taps[tap : tap + 1] * ext[pl.ds(EDGE - (TAPS - 1) + tap, BLOCK), :]
        conv_o[rows, :] = total
        act_o[rows, :] = (total * sigmoid(total)).astype(LOW)

    steps, _, _ = step_terms(raw, heads)
    scale = -jnp.exp(vec[1:2, :])
    cum = sum_before(steps * scale)
    cum_o[...] = cum
    cum_t, steps_t = cum.T, steps.T
    write = act_o[:, inner : inner + STATE]
    read = act_o[:, inner + STATE :]
    lower = ones_before(BLOCK)
    top, low = slice(0, BLOCK), slice(BLOCK, GROUP)
    s00 = jnp.where(lower, nt(read[top], write[top]), 0.0)
    s10 = nt(read[low], write[top]) * second
    s11 = jnp.where(lower, nt(read[low], write[low]), 0.0)

    def mix(scores, head, t, s):
        decay = jnp.exp(jnp.minimum(cum[t, head : head + 1] - cum_t[head : head + 1, s], 0.0))
        return (scores * (decay * steps_t[head : head + 1, s])).astype(LOW)

    last = cum[GROUP - 1 : GROUP, :]
    row = lax.broadcasted_iota(jnp.int32, (GROUP, LANES), 0)
    weight = steps * jnp.exp(last - cum) * jnp.where(row < BLOCK, second, 1.0)
    weight_w = to_columns(weight, spread_m)
    packed = []
    for pair in range(inner // LANES):
        columns = slice(pair * LANES, (pair + 1) * LANES)
        slab = act_o[:, columns]
        slab_f = slab.astype(WIDE)
        ones = pair_lanes(slab)
        h0, h1 = 2 * pair, 2 * pair + 1
        y0 = nn(
            jnp.concatenate([mix(s00, h0, top, top), mix(s00, h1, top, top)], axis=1),
            jnp.concatenate([ones[0][top], ones[1][top]], axis=0),
        )
        y1 = nn(
            jnp.concatenate(
                [mix(s10, h0, low, top), mix(s11, h0, low, low), mix(s10, h1, low, top), mix(s11, h1, low, low)], axis=1
            ),
            jnp.concatenate([ones[0], ones[1]], axis=0),
        )
        skip = to_columns(jnp.broadcast_to(vec[2:3, :], (EDGE, LANES)), spread_m[:, columns])[0:1]
        part_o[top, columns] = y0 + skip * slab_f[top]
        part_o[low, columns] = y1 + skip * slab_f[low]
        packed.append((slab_f * weight_w[:, columns]).astype(LOW))
    local = tn(jnp.concatenate(packed, axis=1), write)
    local_o[0] = local
    carry = jnp.exp(cum_t[:, GROUP - 1 : GROUP]) * (first * second)
    state[...] = carry_columns(carry, collect) * state[...] + local
    prod[...] = jnp.broadcast_to(carry[:HALO], (HALO, STATE)) * prod[...]
    msg_o[:inner, :] = state[...].astype(LOW)
    msg_o[inner:, :] = prod[...].astype(LOW)

    @pl.when(i == pl.num_programs(0) - 1)
    def _():
        if line > 1:
            g_line.hop(1, give=False)
        g_line.finish(g, (0,))
        own_g.wait()


def front(flags, x_full, w_all, vec, prenorm, kernels, filters, offsets, shifts, g, heads):
    line = lax.axis_size("head")
    rows = x_full.shape[0] - HALO
    inner = kernels.shape[1]
    wide = inner + filters.shape[1]
    blocks = rows // GROUP
    total = x_full.shape[1]

    def by_rows(width):
        return blockwise((GROUP, width), lambda i: (i, 0))

    return pl.pallas_call(
        functools.partial(front_kernel, heads, line),
        grid=(blocks,),
        out_shape=(
            shape((rows, total), LOW), shape((rows, inner), WIDE), shape((rows, wide), LOW), shape((rows, wide), WIDE),
            shape((rows, wide), LOW), shape((rows, LANES), WIDE), shape((rows, LANES), WIDE), shape((rows, inner), WIDE),
            shape((blocks, inner, STATE), WIDE), shape((inner + HALO, STATE), LOW),
            shape((EDGE, wide), WIDE), shape((rows, total), LOW),
        ),
        in_specs=[
            SMEM_SPEC, by_rows(total), blockwise((HALO, total), lambda i: (rows // HALO, 0)), fixed(w_all.shape),
            fixed(vec.shape), fixed(prenorm.shape), fixed(kernels.shape), fixed(filters.shape), fixed(offsets.shape),
            fixed(shifts.shape), ANY_SPEC,
        ],
        out_specs=(
            by_rows(total), by_rows(inner), by_rows(wide), by_rows(wide), by_rows(wide), by_rows(LANES), by_rows(LANES),
            by_rows(inner), blockwise((1, inner, STATE), lambda i: (i, 0, 0)), fixed((inner + HALO, STATE)),
            fixed((EDGE, wide)), ANY_SPEC,
        ),
        scratch_shapes=[
            pltpu.VMEM((EDGE + BLOCK, wide), WIDE), pltpu.VMEM((EDGE, wide), WIDE),
            pltpu.VMEM((inner, STATE), WIDE), pltpu.VMEM((HALO, STATE), WIDE),
            DMA((2, line)), DMA((line,)), DMA,
        ],
        compiler_params=pltpu.CompilerParams(
            collective_id=1, has_side_effects=True, vmem_limit_bytes=VMEM_LIMIT, dimension_semantics=("arbitrary",)
        ),
        name="front",
    )(flags, x_full, x_full, w_all, vec, prenorm, kernels, filters, offsets, shifts, g)


def fold_states(slots, collect, inner, first, last, step, start):
    def hop(n, state):
        message = slots[first + n * step]
        carry = nn(collect[:, :HALO], message[inner:])
        return carry * state + message[:inner].astype(WIDE)

    return lax.fori_loop(0, (last - first) * step, hop, start)


def chunk_lanes(x, count):
    size = x.shape[1] // count
    fold = LANES // size
    tall = GROUP // fold
    lane = lax.broadcasted_iota(jnp.int32, (tall, LANES), 1)
    out = []
    for chunk in range(count):
        slab, offset = chunk * size // LANES, chunk * size % LANES
        total = jnp.zeros((tall, LANES), WIDE)
        for group in range(fold):
            piece = x[group * tall : (group + 1) * tall, slab * LANES : (slab + 1) * LANES]
            shift = (group * size - offset) % LANES
            if shift:
                piece = pltpu.roll(piece, shift, 1)
            inside = (lane >= group * size) & (lane < (group + 1) * size)
            total = jnp.where(inside, piece, total)
        out.append(total)
    return out


def core_kernel(
    seqs, line, heads, blocks, flags, msg, gate, part, read, act, cum, raw, local, g_part, normed, r_t, postnorm, vec,
    dgate_o, dval_o, daddr_o, dstep_o, tiny_o, gpost_o, sums_o, out_got, gread_got, ggate_got,
    ssd_s, gated_s, din_s, dssd_s, starts, q, state, prod, g_buf, out_part, slots, back_slots, back_msg, sums,
    gread, ggate, gread_low, ggate_low,
    sent, got, passed, back_sent, back_got, back_passed, sum_sent, sum_got, line_sent, line_got, load_sem,
    out_sent, out_sem, w_sent, w_sem, own_sem,
):
    i = pl.program_id(0)
    me, mine = lax.axis_index("seq"), lax.axis_index("head")
    inner = gate.shape[1]
    width = out_part.shape[2]
    depth = gread_got.shape[1]
    phase = i // blocks
    block = jnp.where(phase == 3, 4 * blocks - 1 - i, lax.rem(i, blocks))
    here = pl.ds(pl.multiple_of(block * GROUP, GROUP), GROUP)
    first, second = flags[2 * block], flags[2 * block + 1]
    plane = Plane(seqs, lambda s: slots.at[s], sent, got, passed, way=1)
    back_plane = Plane(seqs, lambda s: back_slots.at[s], back_sent, back_got, back_passed, way=-1)
    g_line = Line(line, g_buf, width, line_sent, line_got)

    def shard_of(ref, shard):
        return ref.at[:, pl.ds(pl.multiple_of(shard * width, LANES), width)]

    def load_copy(shard, n):
        return pltpu.make_async_copy(shard_of(g_part, shard), shard_of(g_buf, shard), load_sem.at[n])

    def each_load(body):
        body(load_copy(mine, 0))
        if line > 1:
            pl.when(mine > 0)(lambda: body(load_copy(mine - 1, 1)))
            pl.when(mine < line - 1)(lambda: body(load_copy(mine + 1, 2)))

    def sum_copy(to, slot):
        return remote(sums.at[mine], sums.at[slot], sum_sent.at[to], sum_got.at[slot], {"head": to})

    def out_copy(to, slot):
        return remote(out_part.at[to], out_got.at[slot], out_sent.at[to], out_sem.at[slot], {"head": to})

    def rows_of(device):
        return pl.ds(pl.multiple_of(device * depth, depth), depth)

    weights = ((gread_low, gread_got), (ggate_low, ggate_got))

    def w_copy(which, to, slot):
        src, dst = weights[which]
        return remote(
            src.at[rows_of(to)], dst.at[slot], w_sent.at[which, to], w_sem.at[which, slot], {"seq": to}
        )

    own_copies = [
        pltpu.make_async_copy(out_part.at[mine], out_got.at[mine], own_sem.at[0]),
        pltpu.make_async_copy(gread_low.at[rows_of(me)], gread_got.at[me], own_sem.at[1]),
        pltpu.make_async_copy(ggate_low.at[rows_of(me)], ggate_got.at[me], own_sem.at[2]),
    ]

    def all_line(body):
        if line > 1:

            @pl.loop(1, line)
            def _(n):
                body(lax.rem(mine + n, line))

    def all_seq(body):
        @pl.loop(1, seqs)
        def _(n):
            body(lax.rem(me + n, seqs))

    row = lax.broadcasted_iota(jnp.int32, (GROUP, LANES), 0)
    lane = lax.broadcasted_iota(jnp.int32, (GROUP, LANES), 1)

    def entry_of(cum_v, spread_m):
        return to_columns(jnp.exp(cum_v) * (first * jnp.where(row < BLOCK, 1.0, second)), spread_m)

    @pl.when(i == 0)
    def _():
        greet(seqs, line)
        g_line.hop(1, take=False, source=lambda shard: shard_of(g_part, shard))
        plane.start(msg)
        each_load(lambda copy: copy.start())
        plane.relay()
        plane.finish(msg)
        state[...] = fold_states(
            slots, head_columns(inner), inner, 0, me, 1, jnp.zeros((inner, STATE), WIDE)
        )

    @pl.when(phase == 0)
    def _():
        spread_m, collect = head_rows(inner), head_columns(inner)
        cum_v = cum[...]
        carry = jnp.exp(cum_v.T[:, GROUP - 1 : GROUP]) * (first * second)
        start = state[...]
        starts[block] = start
        ssd = part[...] + entry_of(cum_v, spread_m) * nt(read[...], start.astype(LOW))
        ssd_s[here, :] = ssd
        state[...] = carry_columns(carry, collect) * start + local[0]
        gate_v = gate[...]
        gated = ssd * (gate_v * sigmoid(gate_v))
        gated_s[here, :] = gated
        out = nt((gated * postnorm[...]).astype(LOW), r_t[...])
        for z in range(line):
            out_part[z, here] = out[:, z * width : (z + 1) * width].astype(LOW)

    @pl.when(i == blocks - 1)
    def _():
        for step in range(2, line):
            g_line.hop(step)
        each_load(lambda copy: copy.wait())
        g_line.finish(None, range(1, line - 1))

    @pl.when(phase == 1)
    def _():
        gated = gated_s[here, :]
        d_inner = nn(g_buf[here, :], r_t[...])
        din_s[here, :] = d_inner
        squares = jnp.sum(gated * gated, axis=1, keepdims=True)
        dots = jnp.sum(gated * postnorm[...] * d_inner, axis=1, keepdims=True)
        both = jnp.where(lane == 0, squares, jnp.where(lane == 1, dots, 0.0)).T
        sums[mine, block] = both[:EDGE]

    @pl.when(i == 2 * blocks - 1)
    def _():
        all_line(lambda to: sum_copy(to, mine).start())
        gread[...] = jnp.zeros_like(gread)
        ggate[...] = jnp.zeros_like(ggate)
        gpost_o[...] = jnp.zeros_like(gpost_o)
        state[...] = jnp.zeros_like(state)
        prod[...] = jnp.ones_like(prod)
        all_line(lambda other: sum_copy(other, other).wait())
        sums_o[...] = jnp.sum(sums[...], axis=0)
        all_line(lambda to: out_copy(to, mine).start())
        own_copies[0].start()

    @pl.when(phase == 2)
    def _():
        spread_m, collect = head_rows(inner), head_columns(inner)
        cum_v = cum[...]
        carry = jnp.exp(cum_v.T[:, GROUP - 1 : GROUP]) * (first * second)
        stats = jnp.concatenate([sums_o[block], jnp.zeros((LANES - EDGE, GROUP), WIDE)], axis=0).T
        inv = lax.rsqrt(stats[:, 0:1] / INNER + EPS)
        dot = stats[:, 1:2]
        gate_v = gate[...]
        sig = sigmoid(gate_v)
        ssd = ssd_s[here, :]
        d_inner = din_s[here, :]
        gated = gated_s[here, :]
        gated_inv = gated * inv
        inner_normed = (gated_inv * postnorm[...]).astype(LOW)
        d_gated = (inv * postnorm[...]) * d_inner - gated * (inv * inv * inv / INNER * dot)
        gpost_o[...] += jnp.sum(d_inner * gated_inv, axis=0, keepdims=True)
        d_ssd = (d_gated * (gate_v * sig)).astype(LOW)
        d_gate = (d_gated * ssd * sig * (1.0 + gate_v * (1.0 - sig))).astype(LOW)
        dssd_s[here, :] = d_ssd
        dgate_o[...] = d_gate
        gread[...] += tn(g_buf[here, :], inner_normed)
        ggate[...] += tn(normed[...], d_gate)
        query_grad = (d_ssd.astype(WIDE) * entry_of(cum_v, spread_m)).astype(LOW)
        found = tn(query_grad, read[...])
        q[block] = found
        state[...] += carry_columns(prod[...], collect) * found
        prod[...] = prod[...] * carry

    @pl.when(i == 3 * blocks - 1)
    def _():
        back_msg[:inner, :] = state[...].astype(LOW)
        back_msg[inner:, :] = jnp.broadcast_to(prod[:HALO], (HALO, STATE)).astype(LOW)
        back_plane.start(back_msg)
        gread_low[...] = gread[...].astype(LOW)
        ggate_low[...] = ggate[...].astype(LOW)
        tiny_o[...] = jnp.zeros_like(tiny_o)
        back_plane.relay()
        back_plane.finish(back_msg)
        for which in range(2):
            all_seq(lambda to: w_copy(which, to, me).start())
        own_copies[1].start()
        own_copies[2].start()
        state[...] = fold_states(
            back_slots, head_columns(inner), inner, seqs - 1, me, -1, jnp.zeros((inner, STATE), WIDE)
        )

    @pl.when(phase == 3)
    def _():
        spread_m, collect = head_rows(inner), head_columns(inner)
        lower_mask = ones_before(BLOCK)
        top, low = slice(0, BLOCK), slice(BLOCK, GROUP)
        cum_v = cum[...]
        cum_t = cum_v.T
        steps, sig, ratio = step_terms(raw[...], heads)
        steps_t = steps.T
        scale = -jnp.exp(vec[1:2, :])
        last = cum_v[GROUP - 1 : GROUP, :]
        write = act[:, inner : inner + STATE]
        read_v = act[:, inner + STATE :]
        s00 = jnp.where(lower_mask, nt(read_v[top], write[top]), 0.0)
        s10 = nt(read_v[low], write[top]) * second
        s11 = jnp.where(lower_mask, nt(read_v[low], write[low]), 0.0)

        end = state[...]
        end_low = end.astype(LOW)
        start = starts[block]
        carry = jnp.exp(cum_t[:, GROUP - 1 : GROUP]) * (first * second)
        state[...] = carry_columns(carry, collect) * end + q[block]
        weight = steps * jnp.exp(last - cum_v) * jnp.where(row < BLOCK, second, 1.0)
        weight_w = to_columns(weight, spread_m)
        d_ssd = dssd_s[here, :]
        d_query = (d_ssd.astype(WIDE) * entry_of(cum_v, spread_m)).astype(LOW)
        through_w = to_columns(jnp.broadcast_to(vec[2:3, :], (EDGE, LANES)), spread_m)[0:1]

        def decay_of(head, t, s):
            decay = jnp.exp(jnp.minimum(cum_v[t, head : head + 1] - cum_t[head : head + 1, s], 0.0))
            return decay * steps_t[head : head + 1, s]

        ds00 = jnp.zeros((BLOCK, BLOCK), WIDE)
        ds10 = jnp.zeros((BLOCK, BLOCK), WIDE)
        ds11 = jnp.zeros((BLOCK, BLOCK), WIDE)
        packed, value_parts, tails = [], [], []
        d_packed = nt(write, end_low)
        for pair in range(inner // LANES):
            columns = slice(pair * LANES, (pair + 1) * LANES)
            values = act[:, columns]
            values_f = values.astype(WIDE)
            dy = d_ssd[:, columns]
            dys = pair_lanes(dy)
            m00, m10, m11 = [], [], []
            for k in range(2):
                head = 2 * pair + k
                l00, l10, l11 = decay_of(head, top, top), decay_of(head, low, top), decay_of(head, low, low)
                m00.append((s00 * l00).astype(LOW))
                m10.append((s10 * l10).astype(LOW))
                m11.append((s11 * l11).astype(LOW))
                ds00 = ds00 + nt(dys[k][top], values[top]) * l00
                ds10 = ds10 + nt(dys[k][low], values[top]) * l10
                ds11 = ds11 + nt(dys[k][low], values[low]) * l11
            v0 = tn(
                jnp.concatenate([m00[0], m10[0], m00[1], m10[1]], axis=0), jnp.concatenate([dys[0], dys[1]], axis=0)
            )
            v1 = tn(
                jnp.concatenate([m11[0], m11[1]], axis=0), jnp.concatenate([dys[0][low], dys[1][low]], axis=0)
            )
            tail = d_packed[:, columns] * weight_w[:, columns]
            whole = jnp.concatenate([v0, v1], axis=0) + tail
            dval_o[:, columns] = whole + through_w[:, columns] * dy.astype(WIDE)
            value_parts.append(values_f * whole)
            tails.append(jnp.sum(tail * values_f, axis=0, keepdims=True))
            packed.append((values_f * weight_w[:, columns]).astype(LOW))

        ds = jnp.concatenate(
            [
                jnp.concatenate([jnp.where(lower_mask, ds00, 0.0), jnp.zeros((BLOCK, BLOCK), WIDE)], axis=1),
                jnp.concatenate([ds10 * second, jnp.where(lower_mask, ds11, 0.0)], axis=1),
            ],
            axis=0,
        ).astype(LOW)
        d_read = nn(ds, write) + nn(d_query, start.astype(LOW))
        d_write = tn(ds, read_v) + nn(jnp.concatenate(packed, axis=1), end_low)
        for z, chunk in enumerate(chunk_lanes(jnp.concatenate([d_write, d_read], axis=1), line)):
            daddr_o[z] = chunk.astype(LOW)

        dy_f = d_ssd.astype(WIDE)
        own = to_heads(dy_f * act[:, :inner].astype(WIDE), collect)
        r1 = to_heads(dy_f * ssd_s[here, :], collect) - vec[2:3, :] * own
        w = to_heads(jnp.concatenate(value_parts, axis=1), collect)
        tail_row = to_heads(jnp.broadcast_to(jnp.concatenate(tails, axis=1), (EDGE, inner)), collect)[0:1]
        high, rest = halves(end * start)
        ones = jnp.ones((EDGE, STATE), LOW)
        carry_grad = to_heads(nt(ones, high) + nt(ones, rest), collect)[0:1]
        d_last = tail_row + carry_grad * (jnp.exp(last) * (first * second))
        d_cum = r1 - w + jnp.where(row == GROUP - 1, d_last, 0.0)
        d_rate = sum_after(d_cum)
        d_raw = d_rate * scale * sig + w * ratio
        dstep_o[...] = d_raw.astype(LOW)
        tiny_o[0:1, :] += jnp.sum(d_raw, axis=0, keepdims=True)
        tiny_o[1:2, :] += jnp.sum(d_rate * steps, axis=0, keepdims=True) * scale
        tiny_o[2:3, :] += jnp.sum(own, axis=0, keepdims=True)

    @pl.when(i == 4 * blocks - 1)
    def _():
        all_line(lambda other: out_copy(other, other).wait())
        for which in range(2):
            all_seq(lambda other: w_copy(which, other, other).wait())
        for copy in own_copies:
            copy.wait()


def core(flags, msg, gate, part, act, cum, raw, local, g_part, normed, r_t, postnorm, vec, heads):
    seqs, line = lax.axis_size("seq"), lax.axis_size("head")
    rows, inner = gate.shape
    wide = act.shape[1]
    total = g_part.shape[1]
    width = total // line
    depth = total // seqs
    blocks = rows // GROUP
    fold = LANES * line // (2 * STATE)

    def place(phases):
        def at(i):
            phase = i // blocks
            index = jnp.int32(0)
            held = jnp.int32(0)
            for n in range(4):
                if n in phases:
                    now = (4 * blocks - 1 - i) if n == 3 else i - n * blocks
                    held = jnp.int32(0 if n == 3 else blocks - 1)
                else:
                    later = [m for m in phases if m > n]
                    now = held if not later else jnp.int32(blocks - 1 if later[0] == 3 else 0)
                index = jnp.where(phase == n, now, index)
            return index

        return at

    def by_rows(columns, phases, column=0):
        at = place(phases)
        return blockwise((GROUP, columns), lambda i: (at(i), column))

    at_first, at_last = place((0,)), place((3,))
    message = (inner + HALO, STATE)
    return pl.pallas_call(
        functools.partial(core_kernel, seqs, line, heads, blocks),
        grid=(4 * blocks,),
        out_shape=(
            shape((rows, inner), LOW), shape((rows, inner), WIDE), shape((line, rows // fold, LANES), LOW),
            shape((rows, LANES), LOW), shape((EDGE, LANES), WIDE), shape((1, inner), WIDE),
            shape((blocks, EDGE, GROUP), WIDE), shape((line, rows, width), LOW), shape((seqs, depth, inner), LOW),
            shape((seqs, depth, inner), LOW),
        ),
        in_specs=[
            SMEM_SPEC, ANY_SPEC, by_rows(inner, (0, 2)), by_rows(inner, (0,)),
            by_rows(STATE, (0, 2), (inner + STATE) // STATE), by_rows(wide, (3,)), by_rows(LANES, (0, 2, 3)),
            by_rows(LANES, (3,)), blockwise((1, inner, STATE), lambda i: (at_first(i), 0, 0)), ANY_SPEC,
            by_rows(total, (2,)), fixed(r_t.shape), fixed(postnorm.shape), fixed(vec.shape),
        ],
        out_specs=(
            by_rows(inner, (2,)), by_rows(inner, (3,)),
            blockwise((line, GROUP // fold, LANES), lambda i: (0, at_last(i), 0)), by_rows(LANES, (3,)),
            fixed((EDGE, LANES)), fixed((1, inner)), fixed((blocks, EDGE, GROUP)), ANY_SPEC, ANY_SPEC, ANY_SPEC,
        ),
        scratch_shapes=[
            pltpu.VMEM((rows, inner), WIDE), pltpu.VMEM((rows, inner), WIDE), pltpu.VMEM((rows, inner), WIDE),
            pltpu.VMEM((rows, inner), LOW), pltpu.VMEM((blocks, inner, STATE), WIDE),
            pltpu.VMEM((blocks, inner, STATE), WIDE), pltpu.VMEM((inner, STATE), WIDE), pltpu.VMEM((LANES, 1), WIDE),
            pltpu.VMEM((rows, total), LOW), pltpu.VMEM((line, rows, width), LOW), pltpu.VMEM((seqs,) + message, LOW),
            pltpu.VMEM((seqs,) + message, LOW), pltpu.VMEM(message, LOW), pltpu.VMEM((line, blocks, EDGE, GROUP), WIDE),
            pltpu.VMEM((total, inner), WIDE), pltpu.VMEM((total, inner), WIDE), pltpu.VMEM((total, inner), LOW),
            pltpu.VMEM((total, inner), LOW),
            DMA((seqs,)), DMA((seqs,)), DMA((seqs,)), DMA((seqs,)), DMA((seqs,)), DMA((seqs,)), DMA((line,)),
            DMA((line,)), DMA((2, line)), DMA((line,)), DMA((3,)), DMA((line,)), DMA((line,)), DMA((2, seqs)),
            DMA((2, seqs)), DMA((3,)),
        ],
        compiler_params=pltpu.CompilerParams(
            collective_id=2, has_side_effects=True, vmem_limit_bytes=VMEM_LIMIT, dimension_semantics=("arbitrary",)
        ),
        name="core",
    )(flags, msg, gate, part, act, act, cum, raw, local, g_part, normed, r_t, postnorm, vec)


def conv_grad(d_act, conv):
    sig = sigmoid(conv)
    return d_act * (sig * (1.0 + conv * (1.0 - sig)))


def last_kernel(
    seqs, line, blocks, flags, give,
    daddr, dval, dval_next, conv, conv_next, pre, normed, u, dgate, dstep, w, prenorm, kernels, filters, rim,
    out_got, work_x, work_g, sums, tiny, gpost,
    out_recv, grad_recv, dw_got, small_got,
    d_addr, addr_got, edge_own, edge_got, ext, after, prev, taps_g, bias_g, dx_send, dx_got, dw, dw_low,
    pn, pn_send, pn_got, small, result, fin_send,
    addr_sent, addr_sem, edge_sent, edge_sem, dx_sent, dx_sem, dw_sent, dw_sem, pn_sent, pn_sem,
    small_sent, small_sem, fin_sent, fin_sem, own_sem,
):
    i = pl.program_id(0)
    me, mine = lax.axis_index("seq"), lax.axis_index("head")
    inner = dgate.shape[1]
    tiles = work_g.shape[0] // BLOCK
    rows = work_g.shape[0]
    width = work_g.shape[1]
    depth = dw_got.shape[1]
    size = 2 * STATE // line
    fold = LANES // size
    tall = GROUP // fold
    slab = mine * size // LANES
    offset = lax.rem(mine * size, LANES)
    here = pl.ds(pl.multiple_of(i * GROUP, GROUP), GROUP)
    wide = inner + LANES

    def slab_of(ref, at):
        return ref[:, pl.ds(pl.multiple_of(at + slab * LANES, LANES), LANES)]

    def addr_copy(to, slot):
        return remote(daddr.at[to], addr_got.at[slot], addr_sent.at[to], addr_sem.at[slot], {"head": to})

    def edge_copy(to):
        return remote(edge_own, edge_got, edge_sent, edge_sem, {"seq": to})

    def dx_copy(to, slot, block):
        part = pl.ds(pl.multiple_of(block * GROUP, GROUP), GROUP)
        return remote(
            dx_send.at[to, part], dx_got.at[slot, part], dx_sent.at[to, block], dx_sem.at[slot, block], {"head": to}
        )

    def rows_of(device):
        return pl.ds(pl.multiple_of(device * depth, depth), depth)

    def dw_copy(to, slot):
        return remote(dw_low.at[rows_of(to)], dw_got.at[slot], dw_sent.at[to], dw_sem.at[slot], {"seq": to})

    def pn_copy(to, slot):
        return remote(pn_send.at[to], pn_got.at[slot], pn_sent.at[to], pn_sem.at[slot], {"head": to})

    def small_copy(to, slot):
        return remote(small, small_got.at[slot], small_sent.at[to], small_sem.at[slot], {"seq": to})

    arrivals = (out_recv, grad_recv)

    def fin_copy(which, to, slot):
        return remote(
            fin_send.at[which, to], arrivals[which].at[slot], fin_sent.at[which, to], fin_sem.at[which, slot],
            {"seq": to},
        )

    def all_seq(body):
        @pl.loop(1, seqs)
        def _(n):
            body(lax.rem(me + n, seqs))

    def all_line(body):
        if line > 1:

            @pl.loop(1, line)
            def _(n):
                body(lax.rem(mine + n, line))

    def kept(which):
        return pltpu.make_async_copy(fin_send.at[which, me], arrivals[which].at[me], own_sem.at[which])

    def route(which):
        def send(to):
            fin_send[which, to] = result[which, give[to]]
            fin_copy(which, to, me).start()

        all_seq(send)
        fin_send[which, me] = result[which, give[me]]
        kept(which).start()

    def land(which):
        all_seq(lambda other: fin_copy(which, other, other).wait())
        kept(which).wait()

    own_dw = pltpu.make_async_copy(dw_low.at[rows_of(me)], dw_got.at[me], own_sem.at[3])
    own_small = pltpu.make_async_copy(small, small_got.at[me], own_sem.at[4])

    @pl.when(i == 0)
    def _():
        greet(seqs, line)
        all_line(lambda to: addr_copy(to, mine).start())
        own = pltpu.make_async_copy(daddr.at[mine], addr_got.at[mine], own_sem.at[2])
        own.start()

        @pl.loop(0, blocks)
        def _(b):
            part = pl.ds(pl.multiple_of(b * GROUP, GROUP), GROUP)
            stats = jnp.concatenate([sums[b], jnp.zeros((LANES - EDGE, GROUP), WIDE)], axis=0).T
            inv = lax.rsqrt(stats[:, 0:1] / INNER + EPS)
            total = out_got[0, part].astype(WIDE)
            for z in range(1, line):
                total = total + out_got[z, part].astype(WIDE)
            done = (work_x[part].astype(WIDE) + total * inv).astype(LOW)
            result[0, 2 * b] = done[:BLOCK]
            result[0, 2 * b + 1] = done[BLOCK:]

        route(0)
        all_line(lambda other: addr_copy(other, other).wait())
        own.wait()
        lane = lax.broadcasted_iota(jnp.int32, (tall, LANES), 1)
        inside = (lane >= offset) & (lane < offset + size)

        @pl.loop(0, blocks)
        def _(b):
            part = pl.ds(pl.multiple_of(b * tall, tall), tall)
            total = addr_got[0, part].astype(WIDE)
            for z in range(1, line):
                total = total + addr_got[z, part].astype(WIDE)
            for group in range(fold):
                turned = pltpu.roll(total, lax.rem(offset + (LANES - group * size), LANES), 1)
                at = pl.ds(pl.multiple_of(b * GROUP + group * tall, tall), tall)
                d_addr[at, :] = jnp.where(inside, turned, 0.0)

        edge_own[:, :inner] = conv_grad(dval[0:EDGE, :], conv[0:EDGE, :inner])
        edge_own[:, inner:] = conv_grad(d_addr[0:EDGE, :], slab_of(conv, inner)[0:EDGE])
        edge_copy(lax.rem(me + seqs - 1, seqs)).start()
        prev[:, :inner] = rim[:, :inner]
        prev[:, inner:] = slab_of(rim, inner)
        taps_g[...] = jnp.zeros_like(taps_g)
        bias_g[...] = jnp.zeros_like(bias_g)
        dw[...] = jnp.zeros_like(dw)
        pn[...] = jnp.zeros_like(pn)

    @pl.when(i < blocks - 1)
    def _():
        after[:, :inner] = conv_grad(dval_next[...], conv_next[:, :inner])
        following = pl.ds(pl.multiple_of((i + 1) * GROUP, GROUP), EDGE)
        after[:, inner:] = conv_grad(d_addr[following, :], slab_of(conv_next, inner))

    @pl.when(i == blocks - 1)
    def _():
        edge_copy(lax.rem(me + 1, seqs)).wait()
        after[...] = edge_got[...]

    taps = jnp.concatenate([kernels[...], slab_of(filters, 0)], axis=1)
    conv_v = jnp.concatenate([conv[:, :inner], slab_of(conv, inner)], axis=1)
    pre_v = jnp.concatenate([pre[:, :inner], slab_of(pre, inner)], axis=1).astype(WIDE)
    d_conv = conv_grad(jnp.concatenate([dval[...], d_addr[here, :]], axis=1), conv_v)
    bias_g[...] += jnp.sum(d_conv, axis=0, keepdims=True)
    d_pre = []
    for half in range(2):
        at = slice(half * BLOCK, (half + 1) * BLOCK)
        tile = d_conv[at]
        ext[0:EDGE, :] = prev[...] * flags[2 * i + half]
        ext[EDGE:, :] = pre_v[at]
        prev[...] = ext[BLOCK:, :]
        for tap in range(TAPS):
            taps_g[tap : tap + 1, :] += jnp.sum(
                tile * ext[pl.ds(EDGE - (TAPS - 1) + tap, BLOCK), :], axis=0, keepdims=True
            )
        ext[:BLOCK, :] = tile
        following = d_conv[BLOCK : BLOCK + EDGE] if half == 0 else after[...]
        ext[BLOCK:, :] = following * flags[2 * i + half + 1]
        total = taps[TAPS - 1 : TAPS] * ext[:BLOCK, :]
        for tap in range(TAPS - 1):
            total = total + taps[tap : tap + 1] * ext[pl.ds(TAPS - 1 - tap, BLOCK), :]
        d_pre.append(total.astype(LOW))
    d_pre = jnp.concatenate(d_pre, axis=0)
    d_value, d_slab = d_pre[:, :inner], d_pre[:, inner:]
    d_step = dstep[...]
    normed_v = normed[...]
    dw[:, :wide] += tn(normed_v, d_pre)
    dw[:, wide:] += tn(normed_v, d_step)
    d_normed = (
        nt(dgate[...], w[:, :inner])
        + nt(d_value, w[:, inner : 2 * inner])
        + nt(d_slab, slab_of(w, 2 * inner))
        + nt(d_step, w[:, 2 * inner + 2 * STATE :])
    )
    u_f = u[...].astype(WIDE)
    inv = lax.rsqrt(jnp.mean(u_f * u_f, axis=1, keepdims=True) + EPS)
    gained = d_normed * prenorm[...]
    dot = jnp.sum(gained * u_f, axis=1, keepdims=True)
    grad = gained * inv - u_f * (inv * inv * inv / D * dot)
    pn[...] += jnp.sum(d_normed * (u_f * inv), axis=0, keepdims=True)
    for z in range(line):
        dx_send[z, here] = grad[:, z * width : (z + 1) * width].astype(LOW)
    dx_got[mine, here] = dx_send[mine, here]
    all_line(lambda to: dx_copy(to, mine, i).start())

    @pl.when(i == blocks - 1)
    def _():
        dw_low[...] = dw[...].astype(LOW)
        all_seq(lambda to: dw_copy(to, me).start())
        for z in range(line):
            pn_send[z] = jnp.broadcast_to(pn[:, z * width : (z + 1) * width], (EDGE, width))
        pn_got[mine] = pn_send[mine]
        all_line(lambda to: pn_copy(to, mine).start())
        own_dw.start()
        all_line(lambda other: pn_copy(other, other).wait())
        small[...] = jnp.zeros_like(small)
        small[0:TAPS, :] = taps_g[0:TAPS, :]
        small[4:5, :] = bias_g[...]
        small[5:6, :inner] = gpost[...]
        small[6:7, :width] = jnp.sum(pn_got[...], axis=0)[0:1]
        for n in range(3):
            small[7:8, n * LANES : (n + 1) * LANES] = tiny[n : n + 1, :]
        own_small.start()
        all_seq(lambda to: small_copy(to, me).start())

        @pl.loop(0, blocks)
        def _(b):
            all_line(lambda other: dx_copy(other, other, b).wait())
            part = pl.ds(pl.multiple_of(b * GROUP, GROUP), GROUP)
            total = dx_got[0, part].astype(WIDE)
            for z in range(1, line):
                total = total + dx_got[z, part].astype(WIDE)
            done = (work_g[part].astype(WIDE) + total).astype(LOW)
            result[1, 2 * b] = done[:BLOCK]
            result[1, 2 * b + 1] = done[BLOCK:]

        route(1)
        all_seq(lambda other: dw_copy(other, other).wait())
        all_seq(lambda other: small_copy(other, other).wait())
        land(0)
        land(1)
        own_dw.wait()
        own_small.wait()


def finish_kernel(
    take, out_recv, grad_recv, gread_got, ggate_got, dw_got, small_got,
    out_o, dx_o, prenorm_o, gate_o, pay_o, addr_o, step_o, kernels_o, offsets_o, filters_o, shifts_o,
    stepbias_o, decays_o, through_o, post_o, read_o,
):
    inner, size, heads, width = gate_o.shape[1], addr_o.shape[1], step_o.shape[0], prenorm_o.shape[1]
    wide = inner + LANES
    offset = lax.rem(lax.axis_index("head") * size, LANES)
    back_turn = lax.rem(LANES - offset, LANES)
    for k in range(out_o.shape[0]):
        out_o[k] = out_recv[take[k]]
        dx_o[k] = grad_recv[take[k]]

    def summed(ref):
        total = ref[0].astype(WIDE)
        for n in range(1, ref.shape[0]):
            total = total + ref[n].astype(WIDE)
        return total

    read_o[...] = summed(gread_got).T
    gate_o[...] = summed(ggate_got)
    grads = summed(dw_got)
    pay_o[...] = grads[:, :inner]
    addr_o[...] = pltpu.roll(grads[:, inner:wide], back_turn, 1)[:, :size]
    step_o[...] = grads[:, wide:].T[:heads]
    totals = jnp.sum(small_got[...], axis=0)
    kernels_o[...] = totals[0:TAPS, :inner]
    offsets_o[...] = totals[4:5, :inner]
    turned = pltpu.roll(totals[:, inner:], back_turn, 1)
    filters_o[...] = turned[0:TAPS, :size]
    shifts_o[...] = turned[4:5, :size]
    post_o[...] = totals[5:6, :inner]
    prenorm_o[...] = totals[6:7, :width]
    for n, ref in enumerate((stepbias_o, decays_o, through_o)):
        ref[...] = totals[7:8, n * LANES : n * LANES + heads]


def finish(take, out_recv, grad_recv, gread_got, ggate_got, dw_got, small_got, heads, line):
    seqs, _, width = out_recv.shape
    tiles = take.shape[0]
    _, depth, inner = gread_got.shape
    size = 2 * STATE // line
    operands = (out_recv, grad_recv, gread_got, ggate_got, dw_got, small_got)
    outs = (
        shape((tiles, BLOCK, width), LOW), shape((tiles, BLOCK, width), LOW), shape((1, width), WIDE),
        shape((depth, inner), WIDE), shape((depth, inner), WIDE), shape((depth, size), WIDE),
        shape((heads, depth), WIDE), shape((TAPS, inner), WIDE), shape((1, inner), WIDE),
        shape((TAPS, size), WIDE), shape((1, size), WIDE), shape((1, heads), WIDE), shape((1, heads), WIDE),
        shape((1, heads), WIDE), shape((1, inner), WIDE), shape((inner, depth), WIDE),
    )
    return pl.pallas_call(
        finish_kernel,
        grid=(1,),
        out_shape=outs,
        in_specs=[SMEM_SPEC] + [fixed(a.shape) for a in operands],
        out_specs=tuple(fixed(a.shape) for a in outs),
        compiler_params=pltpu.CompilerParams(vmem_limit_bytes=VMEM_LIMIT, dimension_semantics=("arbitrary",)),
        name="finish",
    )(take, *operands)


def last(
    flags, give, daddr, dval, conv, pre, normed, x_full, dgate, dstep, w_all, prenorm, kernels, filters, rim,
    out_got, work_x, work_g, sums, tiny, gpost,
):
    seqs, line = lax.axis_size("seq"), lax.axis_size("head")
    rows, width = work_g.shape
    inner = dgate.shape[1]
    wide = conv.shape[1]
    total = x_full.shape[1]
    depth = total // seqs
    blocks, tiles = rows // GROUP, rows // BLOCK
    part = inner + LANES
    step = GROUP // EDGE

    def by_rows(columns):
        return blockwise((GROUP, columns), lambda i: (i, 0))

    def next_rows(columns):
        return blockwise((EDGE, columns), lambda i: (jnp.minimum((i + 1) * step, rows // EDGE - 1), 0))

    whole = (w_all, prenorm, kernels, filters, rim, out_got, work_x, work_g, sums, tiny, gpost)
    return pl.pallas_call(
        functools.partial(last_kernel, seqs, line, blocks),
        grid=(blocks,),
        out_shape=(
            shape((seqs, BLOCK, width), LOW), shape((seqs, BLOCK, width), LOW),
            shape((seqs, depth, part + LANES), LOW), shape((seqs, EDGE, part), WIDE),
        ),
        in_specs=[SMEM_SPEC] * 2 + [
            ANY_SPEC, by_rows(inner), next_rows(inner), by_rows(wide), next_rows(wide), by_rows(wide), by_rows(total),
            by_rows(total), by_rows(inner), by_rows(LANES),
        ] + [fixed(a.shape) for a in whole],
        out_specs=(ANY_SPEC,) * 4,
        scratch_shapes=[
            pltpu.VMEM((rows, LANES), WIDE), pltpu.VMEM(daddr.shape, LOW),
            pltpu.VMEM((EDGE, part), WIDE), pltpu.VMEM((EDGE, part), WIDE),
            pltpu.VMEM((BLOCK + EDGE, part), WIDE), pltpu.VMEM((EDGE, part), WIDE), pltpu.VMEM((EDGE, part), WIDE),
            pltpu.VMEM((EDGE, part), WIDE), pltpu.VMEM((1, part), WIDE),
            pltpu.VMEM((line, rows, width), LOW), pltpu.VMEM((line, rows, width), LOW),
            pltpu.VMEM((total, part + LANES), WIDE), pltpu.VMEM((total, part + LANES), LOW),
            pltpu.VMEM((1, total), WIDE), pltpu.VMEM((line, EDGE, width), WIDE), pltpu.VMEM((line, EDGE, width), WIDE),
            pltpu.VMEM((EDGE, part), WIDE),
            pltpu.VMEM((2, tiles, BLOCK, width), LOW), pltpu.VMEM((2, seqs, BLOCK, width), LOW),
            DMA((line,)), DMA((line,)), DMA, DMA, DMA((line, blocks)), DMA((line, blocks)), DMA((seqs,)), DMA((seqs,)),
            DMA((line,)), DMA((line,)), DMA((seqs,)), DMA((seqs,)), DMA((2, seqs)), DMA((2, seqs)), DMA((5,)),
        ],
        compiler_params=pltpu.CompilerParams(
            collective_id=3, has_side_effects=True, vmem_limit_bytes=VMEM_LIMIT, dimension_semantics=("arbitrary",)
        ),
        name="last",
    )(
        flags, give, daddr, dval, dval, conv, conv, pre, normed, x_full, dgate, dstep, *whole
    )


def on_device(
    inputs,
    cotangent,
    lengths,
    placement,
    prenorm,
    gating,
    payload,
    address,
    stepping,
    kernels,
    offsets,
    filters,
    shifts,
    stepbias,
    decays,
    through,
    postnorm,
    readout,
):
    rows, width = inputs.shape
    heads = stepbias.shape[0]
    tiles = rows // BLOCK
    give_in, take_in, give_out, take_out, flags, vec = index(placement, lengths, stepbias, decays, through, tiles)
    x_full, w_all, r_t, work_x, work_g = spread(
        give_in, take_in, inputs, cotangent, gating, payload, address, stepping, readout
    )
    gain, post = prenorm[None, :], postnorm[None, :]
    normed, gate, pre, conv, act, raw, cum, part, local, msg, rim, g_part = front(
        flags, x_full, w_all, vec, gain, kernels, filters, offsets[None, :], shifts[None, :], work_g, heads
    )
    d_gate, dval, daddr, dstep, tiny, gpost, sums, out_got, gread_got, ggate_got = core(
        flags, msg, gate, part, act, cum, raw, local, g_part, normed, r_t, post, vec, heads
    )
    out_recv, grad_recv, dw_got, small_got = last(
        flags, give_out, daddr, dval, conv, pre, normed, x_full, d_gate, dstep, w_all, gain, kernels, filters, rim,
        out_got, work_x, work_g, sums, tiny, gpost
    )
    (
        out, dx, prenorm_g, gate_g, pay_g, addr_g, step_g, kernels_g, offsets_g, filters_g, shifts_g, stepbias_g,
        decays_g, through_g, post_g, read_g,
    ) = finish(take_out, out_recv, grad_recv, gread_got, ggate_got, dw_got, small_got, heads, lax.axis_size("head"))
    return (
        out.reshape(rows, width),
        dx.reshape(rows, width),
        prenorm_g.reshape(-1),
        gate_g,
        pay_g,
        addr_g,
        step_g.T,
        kernels_g,
        offsets_g.reshape(-1),
        filters_g,
        shifts_g.reshape(-1),
        stepbias_g.reshape(-1),
        decays_g.reshape(-1),
        through_g.reshape(-1),
        post_g.reshape(-1),
        read_g,
    )


def solution(mesh):
    in_specs = (
        P("seq", "head"),
        P("seq", "head"),
        P(),
        P(),
        P(),
        P("seq", "head"),
        P("seq", "head"),
        P("seq", None),
        P("seq", "head"),
        P(None, "head"),
        P("head"),
        P(),
        P(),
        P("head"),
        P("head"),
        P("head"),
        P("head"),
        P("head", "seq"),
    )
    out_specs = (
        P("seq", "head"),
        P("seq", "head"),
        P("head"),
        P("seq", "head"),
        P("seq", "head"),
        P("seq", "head"),
        P("seq", "head"),
        P(None, "head"),
        P("head"),
        P(None, "head"),
        P("head"),
        P("head"),
        P("head"),
        P("head"),
        P("head"),
        P("head", "seq"),
    )
    return jax.shard_map(
        on_device, mesh=mesh, in_specs=in_specs, out_specs=out_specs, check_vma=False
    )
```

```python
import functools

import jax
import jax.numpy as jnp
from jax import lax
from jax.experimental import pallas as pl
from jax.experimental.pallas import tpu as pltpu
from jax.sharding import PartitionSpec as P

D = 1024
GROUP = 256
BLOCK = 128
INNER = 2048
HDIM = 64
STATE = 128
TAPS = 4
HALO = 16
EDGE = 8
LANES = 128
EPS = 1e-05
MESH = pl.DeviceIdType.MESH
VMEM = pltpu.MemorySpace.VMEM
SMEM = pltpu.MemorySpace.SMEM
DMA = pltpu.SemaphoreType.DMA
VMEM_LIMIT = 63 << 20
LOW = jnp.bfloat16
WIDE = jnp.float32


def shape(dims, kind):
    return jax.ShapeDtypeStruct(dims, kind)


def nn(a, b):
    return jnp.dot(a, b, preferred_element_type=WIDE)


def nt(a, b):
    return lax.dot_general(a, b, (((1,), (1,)), ((), ())), preferred_element_type=WIDE)


def tn(a, b):
    return lax.dot_general(a, b, (((0,), (0,)), ((), ())), preferred_element_type=WIDE)


def halves(x):
    high = x.astype(LOW)
    return high, (x - high.astype(WIDE)).astype(LOW)


def thirds(x):
    high = x.astype(LOW)
    rest = x - high.astype(WIDE)
    middle = rest.astype(LOW)
    return high, middle, (rest - middle.astype(WIDE)).astype(LOW)


def head_rows(inner):
    row = lax.broadcasted_iota(jnp.int32, (LANES, inner), 0)
    column = lax.broadcasted_iota(jnp.int32, (LANES, inner), 1)
    return jnp.where(column // HDIM == row, 1.0, 0.0).astype(LOW)


def head_columns(inner):
    row = lax.broadcasted_iota(jnp.int32, (inner, LANES), 0)
    column = lax.broadcasted_iota(jnp.int32, (inner, LANES), 1)
    return jnp.where(row // HDIM == column, 1.0, 0.0).astype(LOW)


def to_columns(x, spread):
    high, rest = halves(x)
    return nn(high, spread) + nn(rest, spread)


def to_heads(x, collect):
    high, rest = halves(x)
    return nn(high, collect) + nn(rest, collect)


def ones_before(count):
    row = lax.broadcasted_iota(jnp.int32, (count, count), 0)
    column = lax.broadcasted_iota(jnp.int32, (count, count), 1)
    return row >= column


def sum_before(x):
    matrix = jnp.where(ones_before(x.shape[0]), 1.0, 0.0).astype(LOW)
    high, middle, low = thirds(x)
    return nn(matrix, high) + (nn(matrix, middle) + nn(matrix, low))


def sum_after(x):
    count = x.shape[0]
    row = lax.broadcasted_iota(jnp.int32, (count, count), 0)
    column = lax.broadcasted_iota(jnp.int32, (count, count), 1)
    matrix = jnp.where(row <= column, 1.0, 0.0).astype(LOW)
    high, middle, low = thirds(x)
    return nn(matrix, high) + (nn(matrix, middle) + nn(matrix, low))


def sigmoid(x):
    return 0.5 * jnp.tanh(0.5 * x) + 0.5


def step_terms(raw, heads):
    z = jnp.exp(-jnp.abs(raw))
    series = 1.0 - z * (0.5 - z * (1.0 / 3.0 - z * (0.25 - z * 0.2)))
    small = z < 0.03
    log1p = jnp.where(small, z * series, jnp.log(1.0 + z))
    soft = jnp.maximum(raw, 0.0) + log1p
    one = 1.0 / (1.0 + z)
    sig = jnp.where(raw >= 0, one, z * one)
    ratio = jnp.where(small & (raw < 0), one / series, sig / jnp.maximum(soft, 1e-20))
    lane = lax.broadcasted_iota(jnp.int32, raw.shape, 1)
    return jnp.where(lane < heads, soft, 0.0), sig, ratio


def greet(seq_peers, head_peers):
    barrier = pltpu.get_barrier_semaphore()
    count = 0
    if seq_peers > 1:
        me = lax.axis_index("seq")

        @pl.loop(1, seq_peers)
        def _(i):
            pl.semaphore_signal(
                barrier, inc=1, device_id={"seq": lax.rem(me + i, seq_peers)}, device_id_type=MESH
            )

        count += seq_peers - 1
    if head_peers > 1:
        mine = lax.axis_index("head")

        @pl.loop(1, head_peers)
        def _(i):
            pl.semaphore_signal(
                barrier, inc=1, device_id={"head": lax.rem(mine + i, head_peers)}, device_id_type=MESH
            )

        count += head_peers - 1
    pl.semaphore_wait(barrier, count)


def remote(src, dst, send_sem, recv_sem, where):
    return pltpu.make_async_remote_copy(
        src_ref=src, dst_ref=dst, send_sem=send_sem, recv_sem=recv_sem, device_id=where, device_id_type=MESH
    )


class Line:
    def __init__(self, count, out, width, send, recv):
        self.count, self.out, self.width, self.send, self.recv = count, out, width, send, recv
        self.me = lax.axis_index("head")

    def view(self, shard):
        return self.out.at[:, pl.ds(pl.multiple_of(shard * self.width, LANES), self.width)]

    def copy(self, src, shard, way, step):
        return remote(
            src, self.view(shard), self.send.at[way, step], self.recv.at[shard], {"head": self.me + (1 - 2 * way)}
        )

    def first(self, own):
        self.pass_on(own, self.me, 0, 0)
        self.pass_on(own, self.me, 1, 0)

    def pass_on(self, src, shard, way, step):
        reach = (self.me < self.count - 1) if way == 0 else (self.me > 0)

        @pl.when(reach)
        def _():
            self.copy(src, shard, way, step).start()

    def hop(self, step, take=True, give=True, source=None):
        for way in (0, 1):
            shard = self.me - step if way == 0 else self.me + step
            there = (shard >= 0) if way == 0 else (shard < self.count)

            @pl.when(there)
            def _():
                if take:
                    self.copy(self.view(shard), shard, way, step).wait_recv()
                if give and step < self.count - 1:
                    self.pass_on(self.view(shard) if source is None else source(shard), shard, way, step)

    def finish(self, own, steps=None):
        for way in (0, 1):
            reach = (self.me < self.count - 1) if way == 0 else (self.me > 0)
            for step in range(self.count - 1) if steps is None else steps:
                shard = self.me - step if way == 0 else self.me + step
                there = (shard >= 0) if way == 0 else (shard < self.count)

                @pl.when(reach & there)
                def _():
                    src = own if step == 0 else self.view(shard)
                    self.copy(src, shard, way, step).wait_send()


class Plane:
    def __init__(self, seqs, view, sent, got, passed, way=0):
        self.chips, self.view, self.sent, self.got, self.passed, self.way = seqs // 2, view, sent, got, passed, way
        self.me = lax.axis_index("seq")
        self.core = lax.rem(self.me, 2)
        self.chip = self.me // 2
        self.mate = self.me + 1 - 2 * self.core

    def forward(self, chip):
        return (chip > self.chip) if self.way == 1 else (chip < self.chip) if self.way == -1 else (chip >= 0)

    def backward(self, chip):
        return (chip < self.chip) if self.way == 1 else (chip > self.chip) if self.way == -1 else (chip >= 0)

    def each_chip(self, body):
        @pl.loop(1, self.chips)
        def _(i):
            body(lax.rem(self.chip + i, self.chips))

    def copy(self, src, source, to, sem):
        return remote(src, self.view(source), sem, self.got.at[source], {"seq": to})

    def start(self, own):
        def send(chip):
            to = 2 * chip + self.core

            @pl.when(self.forward(chip))
            def _():
                self.copy(own, self.me, to, self.sent.at[to]).start()

        self.each_chip(send)
        self.copy(own, self.me, self.mate, self.sent.at[self.mate]).start()

    def relay(self):
        def take(chip):
            source = 2 * chip + self.core

            @pl.when(self.backward(chip))
            def _():
                landed = self.view(source)
                self.copy(landed, source, self.mate, self.passed.at[source]).wait_recv()
                self.copy(landed, source, self.mate, self.passed.at[source]).start()

        self.each_chip(take)

    def finish(self, own):
        def take(chip):
            source = 2 * chip + 1 - self.core

            @pl.when(self.backward(chip))
            def _():
                self.copy(self.view(source), source, self.mate, self.passed.at[source]).wait_recv()

        self.each_chip(take)
        self.copy(self.view(self.mate), self.mate, self.mate, self.sent.at[self.mate]).wait_recv()
        self.copy(own, self.me, self.mate, self.sent.at[self.mate]).wait_send()

        def drain(chip):
            same = 2 * chip + self.core

            @pl.when(self.forward(chip))
            def _():
                self.copy(own, self.me, same, self.sent.at[same]).wait_send()

            @pl.when(self.backward(chip))
            def _():
                self.copy(self.view(same), same, self.mate, self.passed.at[same]).wait_send()

        self.each_chip(drain)


ANY_SPEC = pl.BlockSpec(memory_space=pl.ANY)
VMEM_SPEC = pl.BlockSpec(memory_space=VMEM)
SMEM_SPEC = pl.BlockSpec(memory_space=SMEM)


def index_kernel(
    seqs, tiles, place, lengths, stepbias, decays, through, give_in, take_in, give_out, take_out, flags, vec
):
    me = lax.axis_index("seq")

    @pl.loop(0, seqs * tiles)
    def _(j):
        block = place[j]

        @pl.when(lax.div(block, tiles) == me)
        def _():
            to = lax.div(j, tiles)
            give_in[to] = lax.rem(block, tiles)
            take_out[lax.rem(block, tiles)] = to

    @pl.loop(0, tiles)
    def _(k):
        source = lax.div(place[me * tiles + k], tiles)
        take_in[k] = source
        give_out[source] = k

    @pl.loop(0, tiles + 1)
    def _(k):
        position = (me * tiles + k) * BLOCK
        end = jnp.int32(0)
        border = position == 0
        for n in range(lengths.shape[0]):
            end = end + lengths[n]
            border = border | (position == end)
        flags[k] = jnp.where(border, 0.0, 1.0)

    heads = stepbias.shape[1]
    vec[...] = jnp.zeros_like(vec)
    vec[0:1, :heads] = stepbias[...]
    vec[1:2, :heads] = decays[...]
    vec[2:3, :heads] = through[...]


def index(place, lengths, stepbias, decays, through, tiles):
    seqs = lax.axis_size("seq")
    whole = jnp.int32
    return pl.pallas_call(
        functools.partial(index_kernel, seqs, tiles),
        out_shape=(
            shape((seqs,), whole), shape((tiles,), whole), shape((seqs,), whole), shape((tiles,), whole),
            shape((tiles + 1,), WIDE), shape((EDGE, LANES), WIDE),
        ),
        in_specs=[SMEM_SPEC] * 2 + [VMEM_SPEC] * 3,
        out_specs=(SMEM_SPEC,) * 5 + (VMEM_SPEC,),
        compiler_params=pltpu.CompilerParams(vmem_limit_bytes=VMEM_LIMIT),
        name="index",
    )(place, lengths, stepbias[None, :], decays[None, :], through[None, :])


def blockwise(dims, index):
    return pl.BlockSpec(dims, index)


def fixed(dims):
    return pl.BlockSpec(dims, lambda i: (0,) * len(dims), pipeline_mode=pl.Buffered(1))


def carry_columns(carry_row_t, collect):
    high, middle, low = thirds(jnp.broadcast_to(carry_row_t, (LANES, LANES)))
    return nn(collect, high) + (nn(collect, middle) + nn(collect, low))


def pair_lanes(slab):
    lane = lax.broadcasted_iota(jnp.int32, slab.shape, 1)
    zero = jnp.zeros_like(slab)
    return jnp.where(lane < HDIM, slab, zero), jnp.where(lane >= HDIM, slab, zero)


def fold_states(slots, collect, inner, first, last, step, start):
    def hop(n, state):
        message = slots[first + n * step]
        carry = nn(collect[:, :HALO], message[inner:])
        return carry * state + message[:inner].astype(WIDE)

    return lax.fori_loop(0, (last - first) * step, hop, start)


def front_kernel(
    seqs, line, heads, blocks, chunks, give, take, flags,
    x_in, g_in, gating_in, payload_in, address_in, stepping_in, readout_in,
    vec, prenorm, kernels, filters, offsets, shifts,
    u_o, normed_o, gate_o, pre_o, conv_o, act_o, raw_o, cum_o, part_o, local_o, state_o, rim_o, g_o, w_o, r_o,
    x, g, gating, payload, address, stepping, readout, square,
    send_x, send_g, recv_x, recv_g, work_x, work_g, w_own, r_own, u, w, msg, slots,
    ext, prev, state, prod,
    sent, got, w_sent, w_got, w_passed, r_sent, r_got, r_passed, s_sent, s_got, s_passed, rim_sent, rim_got, own_sem,
    load_sem, line_sent, line_got, g_sent, g_got,
):
    i = pl.program_id(0)
    me, mine = lax.axis_index("seq"), lax.axis_index("head")
    tiles, _, width = x.shape
    rows = tiles * BLOCK
    depth, inner = gating.shape
    wide = pre_o.shape[1]
    part = rows // chunks
    per = blocks // chunks

    def rows_of(device):
        return pl.ds(pl.multiple_of(device * depth, depth), depth)

    def piece(n):
        if isinstance(n, int):
            return pl.ds(rows, HALO) if n == chunks else pl.ds(n * part, part)
        return pl.ds(pl.multiple_of(n * part, part), part)

    def u_line(n):
        return Line(line, u.at[piece(n)], width, line_sent.at[n], line_got.at[n])

    def own_columns(ref):
        return ref.at[:, pl.ds(pl.multiple_of(mine * width, LANES), width)]

    w_plane = Plane(seqs, lambda s: w.at[rows_of(s)], w_sent, w_got, w_passed)
    r_plane = Plane(seqs, lambda s: r_o.at[rows_of(s)], r_sent, r_got, r_passed)
    s_plane = Plane(seqs, lambda s: slots.at[s], s_sent, s_got, s_passed, way=1)
    g_line = Line(line, g_o, width, g_sent, g_got)
    own_r = pltpu.make_async_copy(r_own, r_o.at[rows_of(me)], own_sem.at[0])
    own_g = pltpu.make_async_copy(work_g, g_line.view(mine), own_sem.at[1])
    save_w = pltpu.make_async_copy(w, w_o, own_sem.at[2])

    def arrange(which, received, work):
        @pl.loop(1, seqs)
        def _(n):
            source = lax.rem(me + n, seqs)
            remote(
                received.at[source], received.at[source], sent.at[which, source], got.at[which, source], {"seq": source}
            ).wait_recv()

        for k in range(tiles):
            work[pl.ds(k * BLOCK, BLOCK), :] = received[take[k]]

    @pl.when(i == 0)
    def _():
        pairs = (
            (x_in, x), (g_in, g), (gating_in, gating), (payload_in, payload), (address_in, address),
            (stepping_in, stepping), (readout_in, readout),
        )
        loads = [pltpu.make_async_copy(src, dst, load_sem.at[n]) for n, (src, dst) in enumerate(pairs)]
        for load in loads:
            load.start()
        greet(seqs, line)

        def post(which, source, outgoing, incoming):
            @pl.loop(1, seqs)
            def _(n):
                to = lax.rem(me + n, seqs)
                outgoing[to] = source[give[to]]
                remote(outgoing.at[to], incoming.at[me], sent.at[which, to], got.at[which, me], {"seq": to}).start()

            incoming[me] = source[give[me]]

        loads[0].wait()
        post(0, x, send_x, recv_x)
        for load in loads[1:]:
            load.wait()

        w_own[:, :inner] = gating[...].astype(LOW)
        w_own[:, inner : 2 * inner] = payload[...].astype(LOW)
        state2 = address.shape[1]
        w_own[:, 2 * inner : 2 * inner + state2] = address[...].astype(LOW)
        square[...] = jnp.zeros_like(square)
        square[: stepping.shape[0], :depth] = stepping[...]
        w_own[:, 2 * inner + state2 :] = square[...].T[:depth].astype(LOW)
        r_own[...] = readout[...].T.astype(LOW)
        w[rows_of(me), :] = w_own[...]
        own_r.start()

        arrange(0, recv_x, work_x)
        after = lax.rem(me + 1, seqs)
        rim = remote(
            work_x.at[pl.ds(rows - HALO, HALO)], work_x.at[pl.ds(rows, HALO)], rim_sent, rim_got, {"seq": after}
        )
        rim.start()
        for n in range(chunks):
            u_line(n).first(work_x.at[piece(n)])
        w_plane.start(w_own)
        rim.wait()
        u_line(chunks).first(work_x.at[piece(chunks)])
        own = pltpu.make_async_copy(work_x, own_columns(u), own_sem.at[3])
        own.start()
        post(1, g, send_g, recv_g)
        r_plane.start(r_own)
        for step in range(1, line - 1):
            for n in range(chunks + 1):
                u_line(n).hop(step)
            if step == 1:
                w_plane.relay()
        if line > 1:
            u_line(chunks).hop(line - 1)
        own.wait()
        w_plane.finish(w_own)
        save_w.start()

    if line > 1:

        @pl.when(lax.rem(i, per) == 0)
        def _():
            u_line(lax.div(i, per)).hop(line - 1)

    @pl.when(i == blocks - 1)
    def _():
        arrange(1, recv_g, work_g)
        g_line.first(work_g)
        own_g.start()

    taps = jnp.concatenate([kernels[...], filters[...]], axis=1)
    bias = jnp.concatenate([offsets[...], shifts[...]], axis=1)
    spread_m, collect = head_rows(inner), head_columns(inner)

    def normalize(block):
        wide_rows = block.astype(WIDE)
        scale = lax.rsqrt(jnp.mean(wide_rows * wide_rows, axis=1, keepdims=True) + EPS)
        return (wide_rows * scale * prenorm[...]).astype(LOW)

    @pl.when(i == 0)
    def _():
        before = nn(normalize(u[pl.ds(rows, HALO), :]), w[:, inner : inner + wide]).astype(LOW).astype(WIDE)
        prev[...] = before[HALO - EDGE :]
        rim_o[...] = before[HALO - EDGE :]
        state[...] = jnp.zeros_like(state)
        prod[...] = jnp.ones_like(prod)

    u_v = u[pl.ds(pl.multiple_of(i * GROUP, GROUP), GROUP), :]
    u_o[...] = u_v
    normed = normalize(u_v)
    normed_o[...] = normed
    gate_o[...] = nn(normed, w[:, :inner])
    pre = nn(normed, w[:, inner : inner + wide]).astype(LOW)
    pre_o[...] = pre
    lane = lax.broadcasted_iota(jnp.int32, (GROUP, LANES), 1)
    raw = jnp.where(lane < heads, nn(normed, w[:, inner + wide :]) + vec[0:1, :], 0.0)
    raw_o[...] = raw
    first, second = flags[2 * i], flags[2 * i + 1]
    same = (first, second)
    for half in range(2):
        at = pl.ds(half * BLOCK, BLOCK)
        ext[0:EDGE, :] = prev[...] * same[half]
        ext[EDGE:, :] = pre[half * BLOCK : (half + 1) * BLOCK].astype(WIDE)
        prev[...] = ext[BLOCK:, :]
        total = bias + taps[TAPS - 1 : TAPS] * ext[EDGE:, :]
        for tap in range(TAPS - 1):
            total = total + taps[tap : tap + 1] * ext[pl.ds(EDGE - (TAPS - 1) + tap, BLOCK), :]
        conv_o[at, :] = total
        act_o[at, :] = (total * sigmoid(total)).astype(LOW)

    steps, _, _ = step_terms(raw, heads)
    scale = -jnp.exp(vec[1:2, :])
    cum = sum_before(steps * scale)
    cum_o[...] = cum
    cum_t, steps_t = cum.T, steps.T
    write = act_o[:, inner : inner + STATE]
    read = act_o[:, inner + STATE :]
    lower = ones_before(BLOCK)
    top, low = slice(0, BLOCK), slice(BLOCK, GROUP)
    s00 = jnp.where(lower, nt(read[top], write[top]), 0.0)
    s10 = nt(read[low], write[top]) * second
    s11 = jnp.where(lower, nt(read[low], write[low]), 0.0)

    def mix(scores, head, t, s):
        decay = jnp.exp(jnp.minimum(cum[t, head : head + 1] - cum_t[head : head + 1, s], 0.0))
        return (scores * (decay * steps_t[head : head + 1, s])).astype(LOW)

    last = cum[GROUP - 1 : GROUP, :]
    row = lax.broadcasted_iota(jnp.int32, (GROUP, LANES), 0)
    weight = steps * jnp.exp(last - cum) * jnp.where(row < BLOCK, second, 1.0)
    weight_w = to_columns(weight, spread_m)
    skip = to_columns(jnp.broadcast_to(vec[2:3, :], (EDGE, LANES)), spread_m)[0:1]
    packed = []
    for pair in range(inner // LANES):
        columns = slice(pair * LANES, (pair + 1) * LANES)
        slab = act_o[:, columns]
        slab_f = slab.astype(WIDE)
        ones = pair_lanes(slab)
        h0, h1 = 2 * pair, 2 * pair + 1
        y0 = nn(
            jnp.concatenate([mix(s00, h0, top, top), mix(s00, h1, top, top)], axis=1),
            jnp.concatenate([ones[0][top], ones[1][top]], axis=0),
        )
        y1 = nn(
            jnp.concatenate(
                [mix(s10, h0, low, top), mix(s11, h0, low, low), mix(s10, h1, low, top), mix(s11, h1, low, low)], axis=1
            ),
            jnp.concatenate([ones[0], ones[1]], axis=0),
        )
        part_o[top, columns] = y0 + skip[:, columns] * slab_f[top]
        part_o[low, columns] = y1 + skip[:, columns] * slab_f[low]
        packed.append((slab_f * weight_w[:, columns]).astype(LOW))
    local = tn(jnp.concatenate(packed, axis=1), write)
    local_o[0] = local
    carry = jnp.exp(cum_t[:, GROUP - 1 : GROUP]) * (first * second)
    state[...] = carry_columns(carry, collect) * state[...] + local
    prod[...] = jnp.broadcast_to(carry[:HALO], (HALO, STATE)) * prod[...]

    @pl.when(i == blocks - 1)
    def _():
        msg[:inner, :] = state[...].astype(LOW)
        msg[inner:, :] = prod[...].astype(LOW)
        s_plane.start(msg)
        s_plane.relay()
        s_plane.finish(msg)
        state_o[...] = fold_states(slots, collect, inner, 0, me, 1, jnp.zeros((inner, STATE), WIDE))
        r_plane.relay()
        r_plane.finish(r_own)
        if line > 1:
            g_line.hop(1, give=False)
        g_line.finish(work_g, (0,))
        for n in range(chunks + 1):
            u_line(n).finish(work_x.at[piece(n)])

        @pl.loop(1, seqs)
        def _(n):
            other = lax.rem(me + n, seqs)
            for which, buffer in ((0, send_x), (1, send_g)):
                remote(
                    buffer.at[other], buffer.at[other], sent.at[which, other], got.at[which, other], {"seq": other}
                ).wait_send()

        own_r.wait()
        own_g.wait()
        save_w.wait()


def front(give, take, flags, x, g, gating, payload, address, stepping, readout, vec, prenorm, kernels, filters, offsets, shifts):
    seqs, line = lax.axis_size("seq"), lax.axis_size("head")
    rows, width = x.shape
    depth, inner = gating.shape
    total = depth * seqs
    wide = inner + address.shape[1]
    columns = inner + wide + LANES
    blocks = rows // GROUP
    chunks = min(blocks, 4)
    heads = stepping.shape[1]
    routed = (seqs, BLOCK, width)
    given = (rows // BLOCK, BLOCK, width)
    message = (inner + HALO, STATE)
    operands = (x.reshape(given), g.reshape(given), gating, payload, address, stepping.T, readout)
    small = (vec, prenorm, kernels, filters, offsets, shifts)

    def by_rows(size):
        return blockwise((GROUP, size), lambda i: (i, 0))

    return pl.pallas_call(
        functools.partial(front_kernel, seqs, line, heads, blocks, chunks),
        grid=(blocks,),
        out_shape=(
            shape((rows, total), LOW), shape((rows, total), LOW), shape((rows, inner), WIDE), shape((rows, wide), LOW),
            shape((rows, wide), WIDE), shape((rows, wide), LOW), shape((rows, LANES), WIDE), shape((rows, LANES), WIDE),
            shape((rows, inner), WIDE), shape((blocks, inner, STATE), WIDE), shape((inner, STATE), WIDE),
            shape((EDGE, wide), WIDE), shape((rows, total), LOW), shape((total, columns), LOW),
            shape((total, inner), LOW),
        ),
        in_specs=[SMEM_SPEC] * 3 + [ANY_SPEC] * 7 + [fixed(a.shape) for a in small],
        out_specs=(
            by_rows(total), by_rows(total), by_rows(inner), by_rows(wide), by_rows(wide), by_rows(wide), by_rows(LANES),
            by_rows(LANES), by_rows(inner), blockwise((1, inner, STATE), lambda i: (i, 0, 0)), fixed((inner, STATE)),
            fixed((EDGE, wide)), ANY_SPEC, ANY_SPEC, ANY_SPEC,
        ),
        scratch_shapes=[pltpu.VMEM(a.shape, a.dtype) for a in operands] + [
            pltpu.VMEM((LANES, LANES), WIDE),
            pltpu.VMEM(routed, LOW), pltpu.VMEM(routed, LOW), pltpu.VMEM(routed, LOW), pltpu.VMEM(routed, LOW),
            pltpu.VMEM((rows + HALO, width), LOW), pltpu.VMEM((rows, width), LOW),
            pltpu.VMEM((depth, columns), LOW), pltpu.VMEM((depth, inner), LOW),
            pltpu.VMEM((rows + HALO, total), LOW), pltpu.VMEM((total, columns), LOW),
            pltpu.VMEM(message, LOW), pltpu.VMEM((seqs,) + message, LOW),
            pltpu.VMEM((EDGE + BLOCK, wide), WIDE), pltpu.VMEM((EDGE, wide), WIDE),
            pltpu.VMEM((inner, STATE), WIDE), pltpu.VMEM((HALO, STATE), WIDE),
            DMA((2, seqs)), DMA((2, seqs)),
            DMA((seqs,)), DMA((seqs,)), DMA((seqs,)), DMA((seqs,)), DMA((seqs,)), DMA((seqs,)),
            DMA((seqs,)), DMA((seqs,)), DMA((seqs,)), DMA, DMA, DMA((4,)), DMA((7,)),
            DMA((chunks + 1, 2, line)), DMA((chunks + 1, line)), DMA((2, line)), DMA((line,)),
        ],
        compiler_params=pltpu.CompilerParams(
            collective_id=0, has_side_effects=True, vmem_limit_bytes=VMEM_LIMIT, dimension_semantics=("arbitrary",)
        ),
        name="front",
    )(give, take, flags, *operands, *small)


def conv_grad(d_act, conv):
    sig = sigmoid(conv)
    return d_act * (sig * (1.0 + conv * (1.0 - sig)))


def core_kernel(
    seqs, line, heads, blocks, flags, give,
    gate, part, read, act, cum, raw, local, conv, pre, pre_before, normed, u, g_part,
    state_in, r_t, w, postnorm, vec, prenorm, kernels, filters, rim,
    out_recv, grad_recv, out_got, dx_got, gread_got, ggate_got, dw_got, addr_got, small_got,
    ssd_s, din_s, dssd_s, dgate_s, starts, q, state, prod, g_buf, g_own, out_part, back_slots, back_msg, sums,
    totals, gread, ggate, gread_low, ggate_low, gpost, tiny, d_conv, d_step, after, edge_own, edge_got, ext,
    taps_g, bias_g, dw, dw_low, da_low, da_got, da_send, pn, zs_send, zs_got, small, result, fin_send,
    back_sent, back_sem, back_passed, sum_sent, sum_sem, line_sent, line_sem, load_sem, out_sent, out_sem,
    w_sent, w_sem, dx_sent, dx_sem, edge_sent, edge_sem, zs_sent, zs_sem, da_sent, da_sem, small_sent, small_sem,
    fin_sent, fin_sem, own_sem,
):
    i = pl.program_id(0)
    me, mine = lax.axis_index("seq"), lax.axis_index("head")
    inner = gate.shape[1]
    wide = act.shape[1]
    width = out_part.shape[2]
    depth = gread_got.shape[1]
    size = 2 * STATE // line
    phase = jnp.minimum(lax.div(i, blocks), 3)
    turn = i - 3 * blocks
    block = jnp.where(phase == 3, jnp.maximum(blocks - 1 - turn, 0), lax.rem(i, blocks))
    first, second = flags[2 * block], flags[2 * block + 1]
    g_line = Line(line, g_buf, width, line_sent, line_sem)
    back_plane = Plane(seqs, lambda s: back_slots.at[s], back_sent, back_sem, back_passed, way=-1)

    def group_rows(b):
        return pl.ds(pl.multiple_of(b * GROUP, GROUP), GROUP)

    here = group_rows(block)

    def rows_of(device):
        return pl.ds(pl.multiple_of(device * depth, depth), depth)

    def shard_of(ref, shard):
        return ref.at[:, pl.ds(pl.multiple_of(shard * width, LANES), width)]

    def all_line(body):
        if line > 1:

            @pl.loop(1, line)
            def _(n):
                body(lax.rem(mine + n, line))

    def all_seq(body):
        @pl.loop(1, seqs)
        def _(n):
            body(lax.rem(me + n, seqs))

    def each_load(body):
        def load(shard, n):
            return pltpu.make_async_copy(shard_of(g_part, shard), shard_of(g_buf, shard), load_sem.at[n])

        body(load(mine, 0))
        body(pltpu.make_async_copy(shard_of(g_part, mine), g_own, load_sem.at[3]))
        if line > 1:
            pl.when(mine > 0)(lambda: body(load(mine - 1, 1)))
            pl.when(mine < line - 1)(lambda: body(load(mine + 1, 2)))

    def sum_copy(to, slot):
        return remote(sums.at[mine], sums.at[slot], sum_sent.at[to], sum_sem.at[slot], {"head": to})

    def out_copy(to, slot):
        return remote(out_part.at[to], out_got.at[slot], out_sent.at[to], out_sem.at[slot], {"head": to})

    weights = ((gread_low, gread_got), (ggate_low, ggate_got), (dw_low, dw_got), (da_low, da_got))

    def w_copy(which, to, slot):
        src, dst = weights[which]
        return remote(src.at[rows_of(to)], dst.at[slot], w_sent.at[which, to], w_sem.at[which, slot], {"seq": to})

    def w_start(which):
        all_seq(lambda to: w_copy(which, to, me).start())

    def w_wait(which):
        all_seq(lambda other: w_copy(which, other, other).wait())

    def dx_copy(to, slot, b):
        return remote(
            shard_of(g_buf.at[group_rows(b)], to), dx_got.at[slot, group_rows(b)], dx_sent.at[to, b],
            dx_sem.at[slot, b], {"head": to},
        )

    def edge_copy(to):
        return remote(edge_own, edge_got, edge_sent, edge_sem, {"seq": to})

    def zs_copy(to, slot):
        return remote(zs_send.at[to], zs_got.at[slot], zs_sent.at[to], zs_sem.at[slot], {"head": to})

    def da_copy(to, slot):
        return remote(da_send.at[to], addr_got.at[slot], da_sent.at[to], da_sem.at[slot], {"head": to})

    def small_copy(to, slot):
        return remote(small, small_got.at[slot], small_sent.at[to], small_sem.at[slot], {"seq": to})

    arrivals = (out_recv, grad_recv)

    def fin_copy(which, to, slot):
        return remote(
            fin_send.at[which, to], arrivals[which].at[slot], fin_sent.at[which, to], fin_sem.at[which, slot],
            {"seq": to},
        )

    own_copies = {
        "out": pltpu.make_async_copy(out_part.at[mine], out_got.at[mine], own_sem.at[0]),
        "gread": pltpu.make_async_copy(gread_low.at[rows_of(me)], gread_got.at[me], own_sem.at[1]),
        "ggate": pltpu.make_async_copy(ggate_low.at[rows_of(me)], ggate_got.at[me], own_sem.at[2]),
        "dw": pltpu.make_async_copy(dw_low.at[rows_of(me)], dw_got.at[me], own_sem.at[3]),
        "dx": pltpu.make_async_copy(shard_of(g_buf, mine), dx_got.at[mine], own_sem.at[4]),
        "addr": pltpu.make_async_copy(da_send.at[mine], addr_got.at[mine], own_sem.at[5]),
        "small": pltpu.make_async_copy(small, small_got.at[me], own_sem.at[6]),
        "fin0": pltpu.make_async_copy(fin_send.at[0, me], out_recv.at[me], own_sem.at[7]),
        "fin1": pltpu.make_async_copy(fin_send.at[1, me], grad_recv.at[me], own_sem.at[8]),
    }

    def route(which):
        def send(to):
            fin_send[which, to] = result[which, give[to]]
            fin_copy(which, to, me).start()

        all_seq(send)
        fin_send[which, me] = result[which, give[me]]
        own_copies["fin%d" % which].start()

    row = lax.broadcasted_iota(jnp.int32, (GROUP, LANES), 0)
    lane = lax.broadcasted_iota(jnp.int32, (GROUP, LANES), 1)

    def entry_of(cum_v, spread_m):
        return to_columns(jnp.exp(cum_v) * (first * jnp.where(row < BLOCK, 1.0, second)), spread_m)

    def row_stats(b):
        stats = jnp.concatenate([totals[b], jnp.zeros((LANES - EDGE, GROUP), WIDE)], axis=0).T
        return lax.rsqrt(stats[:, 0:1] / INNER + EPS), stats[:, 1:2]

    def gated_of(ssd):
        gate_v = gate[...]
        return ssd * (gate_v * sigmoid(gate_v))

    @pl.when(i == 0)
    def _():
        greet(seqs, line)
        g_line.hop(1, take=False, source=lambda shard: shard_of(g_part, shard))
        each_load(lambda copy: copy.start())
        state[...] = state_in[...]

    @pl.when(phase == 0)
    def _():
        spread_m, collect = head_rows(inner), head_columns(inner)
        cum_v = cum[...]
        carry = jnp.exp(cum_v.T[:, GROUP - 1 : GROUP]) * (first * second)
        start = state[...]
        starts[block] = start
        ssd = part[...] + entry_of(cum_v, spread_m) * nt(read[...], start.astype(LOW))
        ssd_s[here, :] = ssd
        state[...] = carry_columns(carry, collect) * start + local[0]
        out = nt((gated_of(ssd) * postnorm[...]).astype(LOW), r_t[...])
        for z in range(line):
            out_part[z, here] = out[:, z * width : (z + 1) * width].astype(LOW)

    @pl.when(i == blocks - 1)
    def _():
        for step in range(2, line):
            g_line.hop(step)
        each_load(lambda copy: copy.wait())
        g_line.finish(None, range(1, line - 1))

    @pl.when(phase == 1)
    def _():
        gated = gated_of(ssd_s[here, :])
        d_inner = nn(g_buf[here, :], r_t[...])
        din_s[here, :] = d_inner
        squares = jnp.sum(gated * gated, axis=1, keepdims=True)
        dots = jnp.sum(gated * postnorm[...] * d_inner, axis=1, keepdims=True)
        both = jnp.where(lane == 0, squares, jnp.where(lane == 1, dots, 0.0)).T
        sums[mine, block] = both[:EDGE]

    @pl.when(i == 2 * blocks - 1)
    def _():
        all_line(lambda to: sum_copy(to, mine).start())
        gread[...] = jnp.zeros_like(gread)
        ggate[...] = jnp.zeros_like(ggate)
        gpost[...] = jnp.zeros_like(gpost)
        state[...] = jnp.zeros_like(state)
        prod[...] = jnp.ones_like(prod)
        all_line(lambda other: sum_copy(other, other).wait())
        totals[...] = jnp.sum(sums[...], axis=0)
        all_line(lambda to: out_copy(to, mine).start())
        own_copies["out"].start()

    @pl.when(phase == 2)
    def _():
        spread_m, collect = head_rows(inner), head_columns(inner)
        cum_v = cum[...]
        carry = jnp.exp(cum_v.T[:, GROUP - 1 : GROUP]) * (first * second)
        inv, dot = row_stats(block)
        gate_v = gate[...]
        sig = sigmoid(gate_v)
        ssd = ssd_s[here, :]
        d_inner = din_s[here, :]
        gated = ssd * (gate_v * sig)
        gated_inv = gated * inv
        inner_normed = (gated_inv * postnorm[...]).astype(LOW)
        d_gated = (inv * postnorm[...]) * d_inner - gated * (inv * inv * inv / INNER * dot)
        gpost[...] += jnp.sum(d_inner * gated_inv, axis=0, keepdims=True)
        d_ssd = (d_gated * (gate_v * sig)).astype(LOW)
        d_gate = (d_gated * ssd * sig * (1.0 + gate_v * (1.0 - sig))).astype(LOW)
        dssd_s[here, :] = d_ssd
        dgate_s[here, :] = d_gate
        gread[...] += tn(g_buf[here, :], inner_normed)
        ggate[...] += tn(normed[...], d_gate)
        query_grad = (d_ssd.astype(WIDE) * entry_of(cum_v, spread_m)).astype(LOW)
        found = tn(query_grad, read[...])
        q[block] = found
        state[...] += carry_columns(prod[...], collect) * found
        prod[...] = prod[...] * carry

    @pl.when(i == 3 * blocks - 1)
    def _():
        back_msg[:inner, :] = state[...].astype(LOW)
        back_msg[inner:, :] = jnp.broadcast_to(prod[:HALO], (HALO, STATE)).astype(LOW)
        back_plane.start(back_msg)
        gread_low[...] = gread[...].astype(LOW)
        ggate_low[...] = ggate[...].astype(LOW)
        for ref in (tiny, taps_g, bias_g, dw, pn):
            ref[...] = jnp.zeros_like(ref)
        back_plane.relay()
        back_plane.finish(back_msg)
        w_start(0)
        w_start(1)
        own_copies["gread"].start()
        own_copies["ggate"].start()
        state[...] = fold_states(
            back_slots, head_columns(inner), inner, seqs - 1, me, -1, jnp.zeros((inner, STATE), WIDE)
        )

    @pl.when((phase == 3) & (turn < blocks))
    def _():
        slot = jnp.where(turn == 0, 1, 0)
        spread_m, collect = head_rows(inner), head_columns(inner)
        lower_mask = ones_before(BLOCK)
        top, low = slice(0, BLOCK), slice(BLOCK, GROUP)
        cum_v = cum[...]
        cum_t = cum_v.T
        steps, sig, ratio = step_terms(raw[...], heads)
        steps_t = steps.T
        scale = -jnp.exp(vec[1:2, :])
        last = cum_v[GROUP - 1 : GROUP, :]
        write = act[:, inner : inner + STATE]
        read_v = act[:, inner + STATE :]
        s00 = jnp.where(lower_mask, nt(read_v[top], write[top]), 0.0)
        s10 = nt(read_v[low], write[top]) * second
        s11 = jnp.where(lower_mask, nt(read_v[low], write[low]), 0.0)

        end = state[...]
        end_low = end.astype(LOW)
        start = starts[block]
        carry = jnp.exp(cum_t[:, GROUP - 1 : GROUP]) * (first * second)
        state[...] = carry_columns(carry, collect) * end + q[block]
        weight = steps * jnp.exp(last - cum_v) * jnp.where(row < BLOCK, second, 1.0)
        weight_w = to_columns(weight, spread_m)
        d_ssd = dssd_s[here, :]
        d_query = (d_ssd.astype(WIDE) * entry_of(cum_v, spread_m)).astype(LOW)
        through_w = to_columns(jnp.broadcast_to(vec[2:3, :], (EDGE, LANES)), spread_m)[0:1]

        def decay_of(head, t, s):
            decay = jnp.exp(jnp.minimum(cum_v[t, head : head + 1] - cum_t[head : head + 1, s], 0.0))
            return decay * steps_t[head : head + 1, s]

        ds00 = jnp.zeros((BLOCK, BLOCK), WIDE)
        ds10 = jnp.zeros((BLOCK, BLOCK), WIDE)
        ds11 = jnp.zeros((BLOCK, BLOCK), WIDE)
        packed, value_parts, tails = [], [], []
        d_packed = nt(write, end_low)
        for pair in range(inner // LANES):
            columns = slice(pair * LANES, (pair + 1) * LANES)
            values = act[:, columns]
            values_f = values.astype(WIDE)
            dy = d_ssd[:, columns]
            dys = pair_lanes(dy)
            m00, m10, m11 = [], [], []
            for k in range(2):
                head = 2 * pair + k
                l00, l10, l11 = decay_of(head, top, top), decay_of(head, low, top), decay_of(head, low, low)
                m00.append((s00 * l00).astype(LOW))
                m10.append((s10 * l10).astype(LOW))
                m11.append((s11 * l11).astype(LOW))
                ds00 = ds00 + nt(dys[k][top], values[top]) * l00
                ds10 = ds10 + nt(dys[k][low], values[top]) * l10
                ds11 = ds11 + nt(dys[k][low], values[low]) * l11
            v0 = tn(
                jnp.concatenate([m00[0], m10[0], m00[1], m10[1]], axis=0), jnp.concatenate([dys[0], dys[1]], axis=0)
            )
            v1 = tn(
                jnp.concatenate([m11[0], m11[1]], axis=0), jnp.concatenate([dys[0][low], dys[1][low]], axis=0)
            )
            tail = d_packed[:, columns] * weight_w[:, columns]
            whole = jnp.concatenate([v0, v1], axis=0) + tail
            d_conv[slot, :, columns] = conv_grad(
                whole + through_w[:, columns] * dy.astype(WIDE), conv[:, columns]
            )
            value_parts.append(values_f * whole)
            tails.append(jnp.sum(tail * values_f, axis=0, keepdims=True))
            packed.append((values_f * weight_w[:, columns]).astype(LOW))

        ds = jnp.concatenate(
            [
                jnp.concatenate([jnp.where(lower_mask, ds00, 0.0), jnp.zeros((BLOCK, BLOCK), WIDE)], axis=1),
                jnp.concatenate([ds10 * second, jnp.where(lower_mask, ds11, 0.0)], axis=1),
            ],
            axis=0,
        ).astype(LOW)
        d_read = nn(ds, write) + nn(d_query, start.astype(LOW))
        d_write = tn(ds, read_v) + nn(jnp.concatenate(packed, axis=1), end_low)
        d_conv[slot, :, inner : inner + STATE] = conv_grad(d_write, conv[:, inner : inner + STATE])
        d_conv[slot, :, inner + STATE :] = conv_grad(d_read, conv[:, inner + STATE :])

        dy_f = d_ssd.astype(WIDE)
        own = to_heads(dy_f * act[:, :inner].astype(WIDE), collect)
        r1 = to_heads(dy_f * ssd_s[here, :], collect) - vec[2:3, :] * own
        by_value = to_heads(jnp.concatenate(value_parts, axis=1), collect)
        tail_row = to_heads(jnp.broadcast_to(jnp.concatenate(tails, axis=1), (EDGE, inner)), collect)[0:1]
        high, rest = halves(end * start)
        ones = jnp.ones((EDGE, STATE), LOW)
        carry_grad = to_heads(nt(ones, high) + nt(ones, rest), collect)[0:1]
        d_last = tail_row + carry_grad * (jnp.exp(last) * (first * second))
        d_cum = r1 - by_value + jnp.where(row == GROUP - 1, d_last, 0.0)
        d_rate = sum_after(d_cum)
        d_raw = d_rate * scale * sig + by_value * ratio
        d_step[slot] = d_raw.astype(LOW)
        tiny[0:1, :] += jnp.sum(d_raw, axis=0, keepdims=True)
        tiny[1:2, :] += jnp.sum(d_rate * steps, axis=0, keepdims=True) * scale
        tiny[2:3, :] += jnp.sum(own, axis=0, keepdims=True)

    @pl.when(turn == blocks - 1)
    def _():
        edge_own[...] = d_conv[jnp.where(turn == 0, 1, 0), 0:EDGE, :]
        edge_copy(lax.rem(me + seqs - 1, seqs)).start()

    @pl.when(turn == blocks)
    def _():
        edge_copy(lax.rem(me + 1, seqs)).wait()
        after[...] = edge_got[...]

    @pl.when(turn >= 1)
    def _():
        final = turn == blocks
        slot = jnp.where(final, 1, 0)
        b = jnp.where(final, blocks - 1, blocks - 1 - turn)
        at_b = group_rows(b)
        taps = jnp.concatenate([kernels[...], filters[...]], axis=1)
        grad_c = d_conv[slot]
        pre_v = pre[...].astype(WIDE)
        before = jnp.where(b == 0, rim[...], pre_before[HALO - EDGE :, :].astype(WIDE))
        bias_g[...] += jnp.sum(grad_c, axis=0, keepdims=True)
        d_pre = []
        for half in range(2):
            part_rows = slice(half * BLOCK, (half + 1) * BLOCK)
            tile = grad_c[part_rows]
            ext[0:EDGE, :] = (before if half == 0 else pre_v[BLOCK - EDGE : BLOCK]) * flags[2 * b + half]
            ext[EDGE:, :] = pre_v[part_rows]
            for tap in range(TAPS):
                taps_g[tap : tap + 1, :] += jnp.sum(
                    tile * ext[pl.ds(EDGE - (TAPS - 1) + tap, BLOCK), :], axis=0, keepdims=True
                )
            ext[:BLOCK, :] = tile
            ext[BLOCK:, :] = (grad_c[BLOCK : BLOCK + EDGE] if half == 0 else after[...]) * flags[2 * b + half + 1]
            total = taps[TAPS - 1 : TAPS] * ext[:BLOCK, :]
            for tap in range(TAPS - 1):
                total = total + taps[tap : tap + 1] * ext[pl.ds(TAPS - 1 - tap, BLOCK), :]
            d_pre.append(total.astype(LOW))
        d_pre = jnp.concatenate(d_pre, axis=0)
        step_grad = d_step[slot]
        normed_v = normed[...]
        dw[:, :wide] += tn(normed_v, d_pre)
        dw[:, wide:] += tn(normed_v, step_grad)
        d_normed = (
            nt(dgate_s[at_b, :], w[:, :inner])
            + nt(d_pre, w[:, inner : inner + wide])
            + nt(step_grad, w[:, inner + wide :])
        )
        u_f = u[...].astype(WIDE)
        inv = lax.rsqrt(jnp.mean(u_f * u_f, axis=1, keepdims=True) + EPS)
        gained = d_normed * prenorm[...]
        dot = jnp.sum(gained * u_f, axis=1, keepdims=True)
        grad = gained * inv - u_f * (inv * inv * inv / D * dot)
        pn[...] += jnp.sum(d_normed * (u_f * inv), axis=0, keepdims=True)
        g_buf[at_b, :] = grad.astype(LOW)
        all_line(lambda to: dx_copy(to, mine, b).start())
        result[0, 2 * b] = u[0:BLOCK, pl.ds(pl.multiple_of(mine * width, LANES), width)]
        result[0, 2 * b + 1] = u[BLOCK:, pl.ds(pl.multiple_of(mine * width, LANES), width)]

    @pl.when((turn >= 0) & (turn < blocks))
    def _():
        after[...] = d_conv[jnp.where(turn == 0, 1, 0), 0:EDGE, :]

    @pl.when(turn == blocks)
    def _():
        own_copies["dx"].start()
        dw_low[:, :inner] = dw[:, :inner].astype(LOW)
        dw_low[:, inner:] = dw[:, wide:].astype(LOW)
        da_low[...] = dw[:, inner:wide].astype(LOW)
        w_start(3)
        w_start(2)
        own_copies["dw"].start()
        da_got[me] = da_low[rows_of(me), :]

        for z in range(line):
            slab = z * size // LANES * LANES
            zs_send[z] = jnp.zeros(zs_send.shape[1:], WIDE)
            zs_send[z, 0:1, :] = pn[:, z * width : (z + 1) * width]
            zs_send[z, EDGE : EDGE + TAPS, :LANES] = taps_g[0:TAPS, inner + slab : inner + slab + LANES]
            zs_send[z, EDGE + TAPS : EDGE + TAPS + 1, :LANES] = bias_g[:, inner + slab : inner + slab + LANES]
        zs_got[mine] = zs_send[mine]
        all_line(lambda to: zs_copy(to, mine).start())

        all_line(lambda other: out_copy(other, other).wait())
        own_copies["out"].wait()

        def fetch(src, n):
            return pltpu.make_async_copy(src, out_part, load_sem.at[n])

        fetch(out_got, 0).start()
        fetch(out_got, 0).wait()

        @pl.loop(0, blocks)
        def _(b):
            inv, _ = row_stats(b)
            total = out_part[0, group_rows(b)].astype(WIDE)
            for z in range(1, line):
                total = total + out_part[z, group_rows(b)].astype(WIDE)
            total = total * inv
            result[0, 2 * b] = (result[0, 2 * b].astype(WIDE) + total[:BLOCK]).astype(LOW)
            result[0, 2 * b + 1] = (result[0, 2 * b + 1].astype(WIDE) + total[BLOCK:]).astype(LOW)

        route(0)
        all_line(lambda other: zs_copy(other, other).wait())
        from_line = jnp.sum(zs_got[...], axis=0)
        small[...] = jnp.zeros_like(small)
        small[0:TAPS, :inner] = taps_g[0:TAPS, :inner]
        small[0:TAPS, inner:] = from_line[EDGE : EDGE + TAPS, :LANES]
        small[4:5, :inner] = bias_g[:, :inner]
        small[4:5, inner:] = from_line[EDGE + TAPS : EDGE + TAPS + 1, :LANES]
        small[5:6, :inner] = gpost[...]
        small[6:7, :width] = from_line[0:1]
        for n in range(3):
            small[7:8, n * LANES : (n + 1) * LANES] = tiny[n : n + 1, :]
        own_copies["small"].start()
        all_seq(lambda to: small_copy(to, me).start())

        w_wait(3)
        from_plane = da_got[0].astype(WIDE)
        for n in range(1, seqs):
            from_plane = from_plane + da_got[n].astype(WIDE)
        for z in range(line):
            slab = z * size // LANES * LANES
            da_send[z] = from_plane[:, slab : slab + LANES]
        own_copies["addr"].start()
        all_line(lambda to: da_copy(to, mine).start())

        @pl.loop(0, blocks)
        def _(b):
            all_line(lambda other: dx_copy(other, other, b).wait())

        own_copies["dx"].wait()
        fetch(dx_got, 1).start()
        fetch(dx_got, 1).wait()

        @pl.loop(0, blocks)
        def _(b):
            total = out_part[0, group_rows(b)].astype(WIDE)
            for z in range(1, line):
                total = total + out_part[z, group_rows(b)].astype(WIDE)
            done = (g_own[group_rows(b), :].astype(WIDE) + total).astype(LOW)
            result[1, 2 * b] = done[:BLOCK]
            result[1, 2 * b + 1] = done[BLOCK:]

        route(1)
        for which in range(3):
            w_wait(which)
        all_line(lambda other: da_copy(other, other).wait())
        all_seq(lambda other: small_copy(other, other).wait())
        all_seq(lambda other: fin_copy(0, other, other).wait())
        all_seq(lambda other: fin_copy(1, other, other).wait())
        for name in ("gread", "ggate", "dw", "addr", "small", "fin0", "fin1"):
            own_copies[name].wait()


def core(
    flags, give, gate, part, act, cum, raw, local, conv, pre, normed, u, g_part, state_in, r_t, w_all, postnorm, vec,
    prenorm, kernels, filters, rim,
):
    seqs, line = lax.axis_size("seq"), lax.axis_size("head")
    rows, inner = gate.shape
    wide = act.shape[1]
    total = g_part.shape[1]
    width = total // line
    depth = total // seqs
    blocks, tiles = rows // GROUP, rows // BLOCK
    heads = inner // HDIM
    steps = 4 * blocks + 1

    def scan_block(i):
        return jnp.clip(4 * blocks - 1 - i, 0, blocks - 1)

    def late_block(i):
        return jnp.where(i == steps - 1, blocks - 1, jnp.clip(4 * blocks - 1 - i, 0, max(blocks - 2, 0)))

    def place(early, late=None):
        def at(i):
            index = jnp.int32(0)
            for n in range(3):
                if n in early:
                    now = i - n * blocks
                elif any(m > n for m in early):
                    now = jnp.int32(0)
                elif late is not None:
                    now = late(jnp.int32(3 * blocks))
                else:
                    now = jnp.int32(blocks - 1)
                index = jnp.where((i >= n * blocks) & (i < (n + 1) * blocks), now, index)
            return jnp.where(i >= 3 * blocks, late(i) if late is not None else blocks - 1, index)

        return at

    def by_rows(columns, at, column=0):
        return blockwise((GROUP, columns), lambda i: (at(i), column))

    local_at = place((0,))
    pre_at = place((), late_block)
    message = (inner + HALO, STATE)
    sums = (blocks, EDGE, GROUP)
    whole = (state_in, r_t, w_all, postnorm, vec, prenorm, kernels, filters, rim)
    gather = (line, rows, width)
    small = (EDGE, inner + LANES)
    return pl.pallas_call(
        functools.partial(core_kernel, seqs, line, heads, blocks),
        grid=(steps,),
        out_shape=(
            shape((seqs, BLOCK, width), LOW), shape((seqs, BLOCK, width), LOW), shape(gather, LOW), shape(gather, LOW),
            shape((seqs, depth, inner), LOW), shape((seqs, depth, inner), LOW), shape((seqs, depth, inner + LANES), LOW),
            shape((line, depth, LANES), WIDE), shape((seqs,) + small, WIDE),
        ),
        in_specs=[
            SMEM_SPEC, SMEM_SPEC,
            by_rows(inner, place((0, 1, 2))), by_rows(inner, place((0,))),
            by_rows(STATE, place((0, 2)), (inner + STATE) // STATE), by_rows(wide, place((), scan_block)),
            by_rows(LANES, place((0, 2), scan_block)), by_rows(LANES, place((), scan_block)),
            blockwise((1, inner, STATE), lambda i: (local_at(i), 0, 0)), by_rows(wide, place((), scan_block)),
            by_rows(wide, pre_at),
            blockwise((HALO, wide), lambda i: (jnp.maximum(pre_at(i) * (GROUP // HALO) - 1, 0), 0)),
            by_rows(total, place((2,), late_block)), by_rows(total, pre_at), ANY_SPEC,
        ] + [fixed(a.shape) for a in whole],
        out_specs=(ANY_SPEC,) * 9,
        scratch_shapes=[
            pltpu.VMEM((rows, inner), WIDE), pltpu.VMEM((rows, inner), WIDE), pltpu.VMEM((rows, inner), LOW),
            pltpu.VMEM((rows, inner), LOW), pltpu.VMEM((blocks, inner, STATE), WIDE),
            pltpu.VMEM((blocks, inner, STATE), WIDE), pltpu.VMEM((inner, STATE), WIDE), pltpu.VMEM((LANES, 1), WIDE),
            pltpu.VMEM((rows, total), LOW), pltpu.VMEM((rows, width), LOW), pltpu.VMEM(gather, LOW),
            pltpu.VMEM((seqs,) + message, LOW), pltpu.VMEM(message, LOW),
            pltpu.VMEM((line,) + sums, WIDE), pltpu.VMEM(sums, WIDE),
            pltpu.VMEM((total, inner), WIDE), pltpu.VMEM((total, inner), WIDE), pltpu.VMEM((total, inner), LOW),
            pltpu.VMEM((total, inner), LOW), pltpu.VMEM((1, inner), WIDE), pltpu.VMEM((EDGE, LANES), WIDE),
            pltpu.VMEM((2, GROUP, wide), WIDE), pltpu.VMEM((2, GROUP, LANES), LOW), pltpu.VMEM((EDGE, wide), WIDE),
            pltpu.VMEM((EDGE, wide), WIDE), pltpu.VMEM((EDGE, wide), WIDE), pltpu.VMEM((BLOCK + EDGE, wide), WIDE),
            pltpu.VMEM((EDGE, wide), WIDE), pltpu.VMEM((1, wide), WIDE), pltpu.VMEM((total, wide + LANES), WIDE),
            pltpu.VMEM((total, inner + LANES), LOW), pltpu.VMEM((total, wide - inner), LOW),
            pltpu.VMEM((seqs, depth, wide - inner), LOW), pltpu.VMEM((line, depth, LANES), WIDE),
            pltpu.VMEM((1, total), WIDE), pltpu.VMEM((line, 2 * EDGE, width), WIDE),
            pltpu.VMEM((line, 2 * EDGE, width), WIDE), pltpu.VMEM(small, WIDE),
            pltpu.VMEM((2, tiles, BLOCK, width), LOW), pltpu.VMEM((2, seqs, BLOCK, width), LOW),
            DMA((seqs,)), DMA((seqs,)), DMA((seqs,)), DMA((line,)), DMA((line,)), DMA((2, line)), DMA((line,)), DMA((4,)),
            DMA((line,)), DMA((line,)), DMA((4, seqs)), DMA((4, seqs)), DMA((line, blocks)), DMA((line, blocks)), DMA, DMA,
            DMA((line,)), DMA((line,)), DMA((line,)), DMA((line,)), DMA((seqs,)), DMA((seqs,)), DMA((2, seqs)),
            DMA((2, seqs)), DMA((9,)),
        ],
        compiler_params=pltpu.CompilerParams(
            collective_id=1, has_side_effects=True, vmem_limit_bytes=VMEM_LIMIT, dimension_semantics=("arbitrary",)
        ),
        name="core",
    )(
        flags, give, gate, part, act, act, cum, raw, local, conv, pre, pre, normed, u, g_part, *whole
    )


def finish_kernel(
    take, out_recv, grad_recv, gread_got, ggate_got, dw_got, addr_got, small_got,
    out_o, dx_o, prenorm_o, gate_o, pay_o, addr_o, step_o, kernels_o, offsets_o, filters_o, shifts_o,
    stepbias_o, decays_o, through_o, post_o, read_o,
):
    inner, size, heads, width = gate_o.shape[1], addr_o.shape[1], step_o.shape[0], prenorm_o.shape[1]
    offset = lax.rem(lax.axis_index("head") * size, LANES)
    back_turn = lax.rem(LANES - offset, LANES)
    for k in range(out_o.shape[0]):
        out_o[k] = out_recv[take[k]]
        dx_o[k] = grad_recv[take[k]]

    def summed(ref):
        total = ref[0].astype(WIDE)
        for n in range(1, ref.shape[0]):
            total = total + ref[n].astype(WIDE)
        return total

    read_o[...] = summed(gread_got).T
    gate_o[...] = summed(ggate_got)
    grads = summed(dw_got)
    pay_o[...] = grads[:, :inner]
    step_o[...] = grads[:, inner:].T[:heads]
    addr_o[...] = pltpu.roll(summed(addr_got), back_turn, 1)[:, :size]
    totals = jnp.sum(small_got[...], axis=0)
    kernels_o[...] = totals[0:TAPS, :inner]
    offsets_o[...] = totals[4:5, :inner]
    turned = pltpu.roll(totals[:, inner:], back_turn, 1)
    filters_o[...] = turned[0:TAPS, :size]
    shifts_o[...] = turned[4:5, :size]
    post_o[...] = totals[5:6, :inner]
    prenorm_o[...] = totals[6:7, :width]
    for n, ref in enumerate((stepbias_o, decays_o, through_o)):
        ref[...] = totals[7:8, n * LANES : n * LANES + heads]


def finish(take, out_recv, grad_recv, gread_got, ggate_got, dw_got, addr_got, small_got):
    seqs, _, width = out_recv.shape
    tiles = take.shape[0]
    _, depth, inner = gread_got.shape
    heads = inner // HDIM
    size = 2 * STATE // addr_got.shape[0]
    operands = (out_recv, grad_recv, gread_got, ggate_got, dw_got, addr_got, small_got)
    outs = (
        shape((tiles, BLOCK, width), LOW), shape((tiles, BLOCK, width), LOW), shape((1, width), WIDE),
        shape((depth, inner), WIDE), shape((depth, inner), WIDE), shape((depth, size), WIDE),
        shape((heads, depth), WIDE), shape((TAPS, inner), WIDE), shape((1, inner), WIDE),
        shape((TAPS, size), WIDE), shape((1, size), WIDE), shape((1, heads), WIDE), shape((1, heads), WIDE),
        shape((1, heads), WIDE), shape((1, inner), WIDE), shape((inner, depth), WIDE),
    )
    return pl.pallas_call(
        finish_kernel,
        grid=(1,),
        out_shape=outs,
        in_specs=[SMEM_SPEC] + [fixed(a.shape) for a in operands],
        out_specs=tuple(fixed(a.shape) for a in outs),
        compiler_params=pltpu.CompilerParams(vmem_limit_bytes=VMEM_LIMIT, dimension_semantics=("arbitrary",)),
        name="finish",
    )(take, *operands)


def on_device(
    inputs,
    cotangent,
    lengths,
    placement,
    prenorm,
    gating,
    payload,
    address,
    stepping,
    kernels,
    offsets,
    filters,
    shifts,
    stepbias,
    decays,
    through,
    postnorm,
    readout,
):
    rows, width = inputs.shape
    heads = stepbias.shape[0]
    tiles = rows // BLOCK
    give_in, take_in, give_out, take_out, flags, vec = index(placement, lengths, stepbias, decays, through, tiles)
    gain, post = prenorm[None, :], postnorm[None, :]
    (
        u, normed, gate, pre, conv, act, raw, cum, part, local, state_in, rim, g_part, w_all, r_t
    ) = front(
        give_in, take_in, flags, inputs, cotangent, gating, payload, address, stepping, readout, vec, gain, kernels,
        filters, offsets[None, :], shifts[None, :]
    )
    out_recv, grad_recv, _, _, gread_got, ggate_got, dw_got, addr_got, small_got = core(
        flags, give_out, gate, part, act, cum, raw, local, conv, pre, normed, u, g_part, state_in, r_t, w_all, post, vec,
        gain, kernels, filters, rim
    )
    (
        out, dx, prenorm_g, gate_g, pay_g, addr_g, step_g, kernels_g, offsets_g, filters_g, shifts_g, stepbias_g,
        decays_g, through_g, post_g, read_g,
    ) = finish(take_out, out_recv, grad_recv, gread_got, ggate_got, dw_got, addr_got, small_got)
    return (
        out.reshape(rows, width),
        dx.reshape(rows, width),
        prenorm_g.reshape(-1),
        gate_g,
        pay_g,
        addr_g,
        step_g.T,
        kernels_g,
        offsets_g.reshape(-1),
        filters_g,
        shifts_g.reshape(-1),
        stepbias_g.reshape(-1),
        decays_g.reshape(-1),
        through_g.reshape(-1),
        post_g.reshape(-1),
        read_g,
    )


def solution(mesh):
    in_specs = (
        P("seq", "head"),
        P("seq", "head"),
        P(),
        P(),
        P(),
        P("seq", "head"),
        P("seq", "head"),
        P("seq", None),
        P("seq", "head"),
        P(None, "head"),
        P("head"),
        P(),
        P(),
        P("head"),
        P("head"),
        P("head"),
        P("head"),
        P("head", "seq"),
    )
    out_specs = (
        P("seq", "head"),
        P("seq", "head"),
        P("head"),
        P("seq", "head"),
        P("seq", "head"),
        P("seq", "head"),
        P("seq", "head"),
        P(None, "head"),
        P("head"),
        P(None, "head"),
        P("head"),
        P("head"),
        P("head"),
        P("head"),
        P("head"),
        P("head", "seq"),
    )
    return jax.shard_map(
        on_device, mesh=mesh, in_specs=in_specs, out_specs=out_specs, check_vma=False
    )
```

```python
import functools

import jax
import jax.numpy as jnp
from jax import lax
from jax.experimental import pallas as pl
from jax.experimental.pallas import tpu as pltpu
from jax.sharding import PartitionSpec as P

D = 1024
GROUP = 256
BLOCK = 128
INNER = 2048
HDIM = 64
STATE = 128
TAPS = 4
HALO = 16
EDGE = 8
LANES = 128
EPS = 1e-05
MESH = pl.DeviceIdType.MESH
VMEM = pltpu.MemorySpace.VMEM
SMEM = pltpu.MemorySpace.SMEM
DMA = pltpu.SemaphoreType.DMA
VMEM_LIMIT = 63 << 20
LOW = jnp.bfloat16
WIDE = jnp.float32


def shape(dims, kind):
    return jax.ShapeDtypeStruct(dims, kind)


def nn(a, b):
    return jnp.dot(a, b, preferred_element_type=WIDE)


def nt(a, b):
    return lax.dot_general(a, b, (((1,), (1,)), ((), ())), preferred_element_type=WIDE)


def tn(a, b):
    return lax.dot_general(a, b, (((0,), (0,)), ((), ())), preferred_element_type=WIDE)


def halves(x):
    high = x.astype(LOW)
    return high, (x - high.astype(WIDE)).astype(LOW)


def thirds(x):
    high = x.astype(LOW)
    rest = x - high.astype(WIDE)
    middle = rest.astype(LOW)
    return high, middle, (rest - middle.astype(WIDE)).astype(LOW)


def head_rows(inner):
    row = lax.broadcasted_iota(jnp.int32, (LANES, inner), 0)
    column = lax.broadcasted_iota(jnp.int32, (LANES, inner), 1)
    return jnp.where(column // HDIM == row, 1.0, 0.0).astype(LOW)


def head_columns(inner):
    row = lax.broadcasted_iota(jnp.int32, (inner, LANES), 0)
    column = lax.broadcasted_iota(jnp.int32, (inner, LANES), 1)
    return jnp.where(row // HDIM == column, 1.0, 0.0).astype(LOW)


def to_columns(x, spread):
    high, rest = halves(x)
    return nn(high, spread) + nn(rest, spread)


def to_heads(x, collect):
    high, rest = halves(x)
    return nn(high, collect) + nn(rest, collect)


def ones_before(count):
    row = lax.broadcasted_iota(jnp.int32, (count, count), 0)
    column = lax.broadcasted_iota(jnp.int32, (count, count), 1)
    return row >= column


def sum_before(x):
    matrix = jnp.where(ones_before(x.shape[0]), 1.0, 0.0).astype(LOW)
    high, middle, low = thirds(x)
    return nn(matrix, high) + (nn(matrix, middle) + nn(matrix, low))


def sum_after(x):
    count = x.shape[0]
    row = lax.broadcasted_iota(jnp.int32, (count, count), 0)
    column = lax.broadcasted_iota(jnp.int32, (count, count), 1)
    matrix = jnp.where(row <= column, 1.0, 0.0).astype(LOW)
    high, middle, low = thirds(x)
    return nn(matrix, high) + (nn(matrix, middle) + nn(matrix, low))


def sigmoid(x):
    return 0.5 * jnp.tanh(0.5 * x) + 0.5


def step_terms(raw, heads):
    z = jnp.exp(-jnp.abs(raw))
    series = 1.0 - z * (0.5 - z * (1.0 / 3.0 - z * (0.25 - z * 0.2)))
    small = z < 0.03
    log1p = jnp.where(small, z * series, jnp.log(1.0 + z))
    soft = jnp.maximum(raw, 0.0) + log1p
    one = 1.0 / (1.0 + z)
    sig = jnp.where(raw >= 0, one, z * one)
    ratio = jnp.where(small & (raw < 0), one / series, sig / jnp.maximum(soft, 1e-20))
    lane = lax.broadcasted_iota(jnp.int32, raw.shape, 1)
    return jnp.where(lane < heads, soft, 0.0), sig, ratio


def greet(seq_peers, head_peers, corners=False):
    barrier = pltpu.get_barrier_semaphore()
    count = 0
    if seq_peers > 1:
        me = lax.axis_index("seq")

        @pl.loop(1, seq_peers)
        def _(i):
            pl.semaphore_signal(
                barrier, inc=1, device_id={"seq": lax.rem(me + i, seq_peers)}, device_id_type=MESH
            )

        count += seq_peers - 1
    if head_peers > 1:
        mine = lax.axis_index("head")

        @pl.loop(1, head_peers)
        def _(i):
            pl.semaphore_signal(
                barrier, inc=1, device_id={"head": lax.rem(mine + i, head_peers)}, device_id_type=MESH
            )

        count += head_peers - 1
    if corners and head_peers > 1:
        me, mine = lax.axis_index("seq"), lax.axis_index("head")
        for side in (1, seq_peers - 1):

            @pl.loop(1, head_peers)
            def _(i):
                where = {"seq": lax.rem(me + side, seq_peers), "head": lax.rem(mine + i, head_peers)}
                pl.semaphore_signal(barrier, inc=1, device_id=where, device_id_type=MESH)

        count += 2 * (head_peers - 1)
    pl.semaphore_wait(barrier, count)


def remote(src, dst, send_sem, recv_sem, where):
    return pltpu.make_async_remote_copy(
        src_ref=src, dst_ref=dst, send_sem=send_sem, recv_sem=recv_sem, device_id=where, device_id_type=MESH
    )


class Line:
    def __init__(self, count, out, width, send, recv):
        self.count, self.out, self.width, self.send, self.recv = count, out, width, send, recv
        self.me = lax.axis_index("head")

    def view(self, shard):
        return self.out.at[:, pl.ds(pl.multiple_of(shard * self.width, LANES), self.width)]

    def copy(self, src, shard, way, step):
        return remote(
            src, self.view(shard), self.send.at[way, step], self.recv.at[shard], {"head": self.me + (1 - 2 * way)}
        )

    def first(self, own):
        self.pass_on(own, self.me, 0, 0)
        self.pass_on(own, self.me, 1, 0)

    def pass_on(self, src, shard, way, step):
        reach = (self.me < self.count - 1) if way == 0 else (self.me > 0)

        @pl.when(reach)
        def _():
            self.copy(src, shard, way, step).start()

    def hop(self, step, take=True, give=True, source=None):
        for way in (0, 1):
            shard = self.me - step if way == 0 else self.me + step
            there = (shard >= 0) if way == 0 else (shard < self.count)

            @pl.when(there)
            def _():
                if take:
                    self.copy(self.view(shard), shard, way, step).wait_recv()
                if give and step < self.count - 1:
                    self.pass_on(self.view(shard) if source is None else source(shard), shard, way, step)

    def finish(self, own, steps=None):
        for way in (0, 1):
            reach = (self.me < self.count - 1) if way == 0 else (self.me > 0)
            for step in range(self.count - 1) if steps is None else steps:
                shard = self.me - step if way == 0 else self.me + step
                there = (shard >= 0) if way == 0 else (shard < self.count)

                @pl.when(reach & there)
                def _():
                    src = own if step == 0 else self.view(shard)
                    self.copy(src, shard, way, step).wait_send()


class Plane:
    def __init__(self, seqs, view, sent, got, passed, way=0):
        self.chips, self.view, self.sent, self.got, self.passed, self.way = seqs // 2, view, sent, got, passed, way
        self.me = lax.axis_index("seq")
        self.core = lax.rem(self.me, 2)
        self.chip = self.me // 2
        self.mate = self.me + 1 - 2 * self.core

    def forward(self, chip):
        return (chip > self.chip) if self.way == 1 else (chip < self.chip) if self.way == -1 else (chip >= 0)

    def backward(self, chip):
        return (chip < self.chip) if self.way == 1 else (chip > self.chip) if self.way == -1 else (chip >= 0)

    def each_chip(self, body):
        @pl.loop(1, self.chips)
        def _(i):
            body(lax.rem(self.chip + i, self.chips))

    def copy(self, src, source, to, sem):
        return remote(src, self.view(source), sem, self.got.at[source], {"seq": to})

    def start(self, own):
        def send(chip):
            to = 2 * chip + self.core

            @pl.when(self.forward(chip))
            def _():
                self.copy(own, self.me, to, self.sent.at[to]).start()

        self.each_chip(send)
        self.copy(own, self.me, self.mate, self.sent.at[self.mate]).start()

    def relay(self):
        def take(chip):
            source = 2 * chip + self.core

            @pl.when(self.backward(chip))
            def _():
                landed = self.view(source)
                self.copy(landed, source, self.mate, self.passed.at[source]).wait_recv()
                self.copy(landed, source, self.mate, self.passed.at[source]).start()

        self.each_chip(take)

    def finish(self, own):
        def take(chip):
            source = 2 * chip + 1 - self.core

            @pl.when(self.backward(chip))
            def _():
                self.copy(self.view(source), source, self.mate, self.passed.at[source]).wait_recv()

        self.each_chip(take)
        self.copy(self.view(self.mate), self.mate, self.mate, self.sent.at[self.mate]).wait_recv()
        self.copy(own, self.me, self.mate, self.sent.at[self.mate]).wait_send()

        def drain(chip):
            same = 2 * chip + self.core

            @pl.when(self.forward(chip))
            def _():
                self.copy(own, self.me, same, self.sent.at[same]).wait_send()

            @pl.when(self.backward(chip))
            def _():
                self.copy(self.view(same), same, self.mate, self.passed.at[same]).wait_send()

        self.each_chip(drain)


ANY_SPEC = pl.BlockSpec(memory_space=pl.ANY)
VMEM_SPEC = pl.BlockSpec(memory_space=VMEM)
SMEM_SPEC = pl.BlockSpec(memory_space=SMEM)


def index_kernel(
    seqs, tiles, place, lengths, stepbias, decays, through, give_in, take_in, give_out, take_out, flags, vec
):
    me = lax.axis_index("seq")

    @pl.loop(0, seqs * tiles)
    def _(j):
        block = place[j]

        @pl.when(lax.div(block, tiles) == me)
        def _():
            to = lax.div(j, tiles)
            give_in[to] = lax.rem(block, tiles)
            take_out[lax.rem(block, tiles)] = to

    @pl.loop(0, tiles)
    def _(k):
        source = lax.div(place[me * tiles + k], tiles)
        take_in[k] = source
        give_out[source] = k

    @pl.loop(0, tiles + 1)
    def _(k):
        position = (me * tiles + k) * BLOCK
        end = jnp.int32(0)
        border = position == 0
        for n in range(lengths.shape[0]):
            end = end + lengths[n]
            border = border | (position == end)
        flags[k] = jnp.where(border, 0.0, 1.0)

    heads = stepbias.shape[1]
    vec[...] = jnp.zeros_like(vec)
    vec[0:1, :heads] = stepbias[...]
    vec[1:2, :heads] = decays[...]
    vec[2:3, :heads] = through[...]


def index(place, lengths, stepbias, decays, through, tiles):
    seqs = lax.axis_size("seq")
    whole = jnp.int32
    return pl.pallas_call(
        functools.partial(index_kernel, seqs, tiles),
        out_shape=(
            shape((seqs,), whole), shape((tiles,), whole), shape((seqs,), whole), shape((tiles,), whole),
            shape((tiles + 1,), WIDE), shape((EDGE, LANES), WIDE),
        ),
        in_specs=[SMEM_SPEC] * 2 + [VMEM_SPEC] * 3,
        out_specs=(SMEM_SPEC,) * 5 + (VMEM_SPEC,),
        compiler_params=pltpu.CompilerParams(vmem_limit_bytes=VMEM_LIMIT),
        name="index",
    )(place, lengths, stepbias[None, :], decays[None, :], through[None, :])


def blockwise(dims, index):
    return pl.BlockSpec(dims, index)


def fixed(dims):
    return pl.BlockSpec(dims, lambda i: (0,) * len(dims), pipeline_mode=pl.Buffered(1))


def carry_columns(carry_row_t, collect):
    high, middle, low = thirds(jnp.broadcast_to(carry_row_t, (LANES, LANES)))
    return nn(collect, high) + (nn(collect, middle) + nn(collect, low))


def pair_lanes(slab):
    lane = lax.broadcasted_iota(jnp.int32, slab.shape, 1)
    zero = jnp.zeros_like(slab)
    return jnp.where(lane < HDIM, slab, zero), jnp.where(lane >= HDIM, slab, zero)


def fold_states(slots, collect, inner, first, last, step, start):
    def hop(n, state):
        message = slots[first + n * step]
        carry = nn(collect[:, :HALO], message[inner:])
        return carry * state + message[:inner].astype(WIDE)

    return lax.fori_loop(0, (last - first) * step, hop, start)


def front_kernel(
    seqs, line, heads, blocks, chunks, give, take, flags,
    x_in, g_in, gating_in, payload_in, address_in, stepping_in, readout_in,
    vec, prenorm, kernels, filters, offsets, shifts,
    u_o, normed_o, gate_o, pre_o, conv_o, act_o, raw_o, cum_o, part_o, local_o, state_o, rim_o, g_o, w_o, r_o,
    x, g, gating, payload, address, stepping, readout, square,
    send_x, send_g, recv_x, recv_g, work_x, work_g, w_own, r_own, u, w, msg, slots,
    ext, prev, state, prod,
    sent, got, w_sent, w_got, w_passed, r_sent, r_got, r_passed, s_sent, s_got, s_passed, rim_sent, rim_got, own_sem,
    load_sem, line_sent, line_got, g_sent, g_got,
):
    i = pl.program_id(0)
    me, mine = lax.axis_index("seq"), lax.axis_index("head")
    tiles, _, width = x.shape
    rows = tiles * BLOCK
    depth, inner = gating.shape
    wide = pre_o.shape[1]
    part = rows // chunks
    per = blocks // chunks

    def rows_of(device):
        return pl.ds(pl.multiple_of(device * depth, depth), depth)

    def piece(n):
        if isinstance(n, int):
            return pl.ds(n * part, part)
        return pl.ds(pl.multiple_of(n * part, part), part)

    def u_line(n):
        return Line(line, u.at[piece(n)], width, line_sent.at[n], line_got.at[n])

    def own_columns(ref):
        return ref.at[:, pl.ds(pl.multiple_of(mine * width, LANES), width)]

    w_plane = Plane(seqs, lambda s: w.at[rows_of(s)], w_sent, w_got, w_passed)
    r_plane = Plane(seqs, lambda s: r_o.at[rows_of(s)], r_sent, r_got, r_passed)
    s_plane = Plane(seqs, lambda s: slots.at[s], s_sent, s_got, s_passed, way=1)
    g_line = Line(line, g_o, width, g_sent, g_got)
    own_r = pltpu.make_async_copy(r_own, r_o.at[rows_of(me)], own_sem.at[0])
    own_g = pltpu.make_async_copy(work_g, g_line.view(mine), own_sem.at[1])
    save_w = pltpu.make_async_copy(w, w_o, own_sem.at[2])

    def rim_copy(to, shard):
        columns = pl.ds(pl.multiple_of(shard * width, LANES), width)
        return remote(
            work_x.at[pl.ds(rows - HALO, HALO)], u.at[pl.ds(rows, HALO), columns], rim_sent.at[to], rim_got.at[shard],
            {"seq": lax.rem(me + 1, seqs), "head": to},
        )

    def arrange(which, received, work):
        @pl.loop(1, seqs)
        def _(n):
            source = lax.rem(me + n, seqs)
            remote(
                received.at[source], received.at[source], sent.at[which, source], got.at[which, source], {"seq": source}
            ).wait_recv()

        for k in range(tiles):
            work[pl.ds(k * BLOCK, BLOCK), :] = received[take[k]]

    @pl.when(i == 0)
    def _():
        pairs = (
            (x_in, x), (g_in, g), (gating_in, gating), (payload_in, payload), (address_in, address),
            (stepping_in, stepping), (readout_in, readout),
        )
        loads = [pltpu.make_async_copy(src, dst, load_sem.at[n]) for n, (src, dst) in enumerate(pairs)]
        for load in loads:
            load.start()
        greet(seqs, line, corners=True)

        def post(which, source, outgoing, incoming):
            @pl.loop(1, seqs)
            def _(n):
                to = lax.rem(me + n, seqs)
                outgoing[to] = source[give[to]]
                remote(outgoing.at[to], incoming.at[me], sent.at[which, to], got.at[which, me], {"seq": to}).start()

            incoming[me] = source[give[me]]

        loads[0].wait()
        post(0, x, send_x, recv_x)
        for load in loads[1:]:
            load.wait()

        w_own[:, :inner] = gating[...].astype(LOW)
        w_own[:, inner : 2 * inner] = payload[...].astype(LOW)
        state2 = address.shape[1]
        w_own[:, 2 * inner : 2 * inner + state2] = address[...].astype(LOW)
        square[...] = jnp.zeros_like(square)
        square[: stepping.shape[0], :depth] = stepping[...]
        w_own[:, 2 * inner + state2 :] = square[...].T[:depth].astype(LOW)
        r_own[...] = readout[...].T.astype(LOW)
        w[rows_of(me), :] = w_own[...]
        own_r.start()

        arrange(0, recv_x, work_x)

        @pl.loop(0, line)
        def _(n):
            rim_copy(lax.rem(mine + n, line), mine).start()

        for n in range(chunks):
            u_line(n).first(work_x.at[piece(n)])
        w_plane.start(w_own)
        own = pltpu.make_async_copy(work_x, own_columns(u.at[pl.ds(0, rows)]), own_sem.at[3])
        own.start()
        post(1, g, send_g, recv_g)
        r_plane.start(r_own)
        for step in range(1, line - 1):
            for n in range(chunks):
                u_line(n).hop(step)
            if step == 1:
                w_plane.relay()
        own.wait()

        @pl.loop(0, line)
        def _(n):
            rim_copy(n, n).wait_recv()

        w_plane.finish(w_own)
        save_w.start()

    if line > 1:

        @pl.when(lax.rem(i, per) == 0)
        def _():
            u_line(lax.div(i, per)).hop(line - 1)

    @pl.when(i == blocks - 1)
    def _():
        arrange(1, recv_g, work_g)
        g_line.first(work_g)
        own_g.start()

    taps = jnp.concatenate([kernels[...], filters[...]], axis=1)
    bias = jnp.concatenate([offsets[...], shifts[...]], axis=1)
    spread_m, collect = head_rows(inner), head_columns(inner)

    def normalize(block):
        wide_rows = block.astype(WIDE)
        scale = lax.rsqrt(jnp.mean(wide_rows * wide_rows, axis=1, keepdims=True) + EPS)
        return (wide_rows * scale * prenorm[...]).astype(LOW)

    @pl.when(i == 0)
    def _():
        before = nn(normalize(u[pl.ds(rows, HALO), :]), w[:, inner : inner + wide]).astype(LOW).astype(WIDE)
        prev[...] = before[HALO - EDGE :]
        rim_o[...] = before[HALO - EDGE :]
        state[...] = jnp.zeros_like(state)
        prod[...] = jnp.ones_like(prod)

    u_v = u[pl.ds(pl.multiple_of(i * GROUP, GROUP), GROUP), :]
    u_o[...] = u_v
    normed = normalize(u_v)
    normed_o[...] = normed
    gate_o[...] = nn(normed, w[:, :inner])
    pre = nn(normed, w[:, inner : inner + wide]).astype(LOW)
    pre_o[...] = pre
    lane = lax.broadcasted_iota(jnp.int32, (GROUP, LANES), 1)
    raw = jnp.where(lane < heads, nn(normed, w[:, inner + wide :]) + vec[0:1, :], 0.0)
    raw_o[...] = raw
    first, second = flags[2 * i], flags[2 * i + 1]
    same = (first, second)
    for half in range(2):
        at = pl.ds(half * BLOCK, BLOCK)
        ext[0:EDGE, :] = prev[...] * same[half]
        ext[EDGE:, :] = pre[half * BLOCK : (half + 1) * BLOCK].astype(WIDE)
        prev[...] = ext[BLOCK:, :]
        total = bias + taps[TAPS - 1 : TAPS] * ext[EDGE:, :]
        for tap in range(TAPS - 1):
            total = total + taps[tap : tap + 1] * ext[pl.ds(EDGE - (TAPS - 1) + tap, BLOCK), :]
        conv_o[at, :] = total
        act_o[at, :] = (total * sigmoid(total)).astype(LOW)

    steps, _, _ = step_terms(raw, heads)
    scale = -jnp.exp(vec[1:2, :])
    cum = sum_before(steps * scale)
    cum_o[...] = cum
    cum_t, steps_t = cum.T, steps.T
    write = act_o[:, inner : inner + STATE]
    read = act_o[:, inner + STATE :]
    lower = ones_before(BLOCK)
    top, low = slice(0, BLOCK), slice(BLOCK, GROUP)
    s00 = jnp.where(lower, nt(read[top], write[top]), 0.0)
    s10 = nt(read[low], write[top]) * second
    s11 = jnp.where(lower, nt(read[low], write[low]), 0.0)

    def mix(scores, head, t, s):
        decay = jnp.exp(jnp.minimum(cum[t, head : head + 1] - cum_t[head : head + 1, s], 0.0))
        return (scores * (decay * steps_t[head : head + 1, s])).astype(LOW)

    last = cum[GROUP - 1 : GROUP, :]
    row = lax.broadcasted_iota(jnp.int32, (GROUP, LANES), 0)
    weight = steps * jnp.exp(last - cum) * jnp.where(row < BLOCK, second, 1.0)
    weight_w = to_columns(weight, spread_m)
    skip = to_columns(jnp.broadcast_to(vec[2:3, :], (EDGE, LANES)), spread_m)[0:1]
    packed = []
    for pair in range(inner // LANES):
        columns = slice(pair * LANES, (pair + 1) * LANES)
        slab = act_o[:, columns]
        slab_f = slab.astype(WIDE)
        ones = pair_lanes(slab)
        h0, h1 = 2 * pair, 2 * pair + 1
        y0 = nn(
            jnp.concatenate([mix(s00, h0, top, top), mix(s00, h1, top, top)], axis=1),
            jnp.concatenate([ones[0][top], ones[1][top]], axis=0),
        )
        y1 = nn(
            jnp.concatenate(
                [mix(s10, h0, low, top), mix(s11, h0, low, low), mix(s10, h1, low, top), mix(s11, h1, low, low)], axis=1
            ),
            jnp.concatenate([ones[0], ones[1]], axis=0),
        )
        part_o[top, columns] = y0 + skip[:, columns] * slab_f[top]
        part_o[low, columns] = y1 + skip[:, columns] * slab_f[low]
        packed.append((slab_f * weight_w[:, columns]).astype(LOW))
    local = tn(jnp.concatenate(packed, axis=1), write)
    local_o[0] = local
    carry = jnp.exp(cum_t[:, GROUP - 1 : GROUP]) * (first * second)
    state[...] = carry_columns(carry, collect) * state[...] + local
    prod[...] = jnp.broadcast_to(carry[:HALO], (HALO, STATE)) * prod[...]

    @pl.when(i == blocks - 1)
    def _():
        msg[:inner, :] = state[...].astype(LOW)
        msg[inner:, :] = prod[...].astype(LOW)
        s_plane.start(msg)
        s_plane.relay()
        s_plane.finish(msg)
        state_o[...] = fold_states(slots, collect, inner, 0, me, 1, jnp.zeros((inner, STATE), WIDE))
        r_plane.relay()
        r_plane.finish(r_own)
        if line > 1:
            g_line.hop(1, give=False)
        g_line.finish(work_g, (0,))
        for n in range(chunks):
            u_line(n).finish(work_x.at[piece(n)])

        @pl.loop(0, line)
        def _(n):
            rim_copy(n, mine).wait_send()


        @pl.loop(1, seqs)
        def _(n):
            other = lax.rem(me + n, seqs)
            for which, buffer in ((0, send_x), (1, send_g)):
                remote(
                    buffer.at[other], buffer.at[other], sent.at[which, other], got.at[which, other], {"seq": other}
                ).wait_send()

        own_r.wait()
        own_g.wait()
        save_w.wait()


def front(give, take, flags, x, g, gating, payload, address, stepping, readout, vec, prenorm, kernels, filters, offsets, shifts):
    seqs, line = lax.axis_size("seq"), lax.axis_size("head")
    rows, width = x.shape
    depth, inner = gating.shape
    total = depth * seqs
    wide = inner + address.shape[1]
    columns = inner + wide + LANES
    blocks = rows // GROUP
    chunks = min(blocks, 4)
    heads = stepping.shape[1]
    routed = (seqs, BLOCK, width)
    given = (rows // BLOCK, BLOCK, width)
    message = (inner + HALO, STATE)
    operands = (x.reshape(given), g.reshape(given), gating, payload, address, stepping.T, readout)
    small = (vec, prenorm, kernels, filters, offsets, shifts)

    def by_rows(size):
        return blockwise((GROUP, size), lambda i: (i, 0))

    return pl.pallas_call(
        functools.partial(front_kernel, seqs, line, heads, blocks, chunks),
        grid=(blocks,),
        out_shape=(
            shape((rows, total), LOW), shape((rows, total), LOW), shape((rows, inner), WIDE), shape((rows, wide), LOW),
            shape((rows, wide), WIDE), shape((rows, wide), LOW), shape((rows, LANES), WIDE), shape((rows, LANES), WIDE),
            shape((rows, inner), WIDE), shape((blocks, inner, STATE), WIDE), shape((inner, STATE), WIDE),
            shape((EDGE, wide), WIDE), shape((rows, total), LOW), shape((total, columns), LOW),
            shape((total, inner), LOW),
        ),
        in_specs=[SMEM_SPEC] * 3 + [ANY_SPEC] * 7 + [fixed(a.shape) for a in small],
        out_specs=(
            by_rows(total), by_rows(total), by_rows(inner), by_rows(wide), by_rows(wide), by_rows(wide), by_rows(LANES),
            by_rows(LANES), by_rows(inner), blockwise((1, inner, STATE), lambda i: (i, 0, 0)), fixed((inner, STATE)),
            fixed((EDGE, wide)), ANY_SPEC, ANY_SPEC, ANY_SPEC,
        ),
        scratch_shapes=[pltpu.VMEM(a.shape, a.dtype) for a in operands] + [
            pltpu.VMEM((LANES, LANES), WIDE),
            pltpu.VMEM(routed, LOW), pltpu.VMEM(routed, LOW), pltpu.VMEM(routed, LOW), pltpu.VMEM(routed, LOW),
            pltpu.VMEM((rows, width), LOW), pltpu.VMEM((rows, width), LOW),
            pltpu.VMEM((depth, columns), LOW), pltpu.VMEM((depth, inner), LOW),
            pltpu.VMEM((rows + HALO, total), LOW), pltpu.VMEM((total, columns), LOW),
            pltpu.VMEM(message, LOW), pltpu.VMEM((seqs,) + message, LOW),
            pltpu.VMEM((EDGE + BLOCK, wide), WIDE), pltpu.VMEM((EDGE, wide), WIDE),
            pltpu.VMEM((inner, STATE), WIDE), pltpu.VMEM((HALO, STATE), WIDE),
            DMA((2, seqs)), DMA((2, seqs)),
            DMA((seqs,)), DMA((seqs,)), DMA((seqs,)), DMA((seqs,)), DMA((seqs,)), DMA((seqs,)),
            DMA((seqs,)), DMA((seqs,)), DMA((seqs,)), DMA((line,)), DMA((line,)), DMA((4,)), DMA((7,)),
            DMA((chunks, 2, line)), DMA((chunks, line)), DMA((2, line)), DMA((line,)),
        ],
        compiler_params=pltpu.CompilerParams(
            collective_id=0, has_side_effects=True, vmem_limit_bytes=VMEM_LIMIT, dimension_semantics=("arbitrary",)
        ),
        name="front",
    )(give, take, flags, *operands, *small)


def conv_grad(d_act, conv):
    sig = sigmoid(conv)
    return d_act * (sig * (1.0 + conv * (1.0 - sig)))


def core_kernel(
    seqs, line, heads, blocks, flags, give,
    gate, part, read, act, cum, raw, local, conv, pre, pre_before, normed, u, g_part,
    r_in, w_in, state_in, postnorm, vec, prenorm, kernels, filters, rim,
    out_recv, grad_recv, out_got, dx_got, gread_got, ggate_got, dw_got, addr_got, small_got,
    r_t, w, ssd_s, din_s, dssd_s, dgate_s, starts, q, state, prod, g_buf, g_own, out_part, back_slots, back_msg, relay, dx_relay, sums,
    totals, gread, ggate, gread_low, ggate_low, gpost, tiny, d_conv, d_step, after, edge_own, edge_got, ext,
    taps_g, bias_g, dw, dw_low, da_low, da_got, da_send, pn, zs_send, zs_got, small, result, fin_send,
    back_sent, back_sem, back_passed, sum_sent, sum_sem, line_sent, line_sem, load_sem, out_sent, out_sem,
    w_sent, w_sem, dx_sent, dx_sem, edge_sent, edge_sem, zs_sent, zs_sem, da_sent, da_sem, small_sent, small_sem,
    fin_sent, fin_sem, own_sem, weight_sem, relay_sent, relay_sem, dx_relay_sent, dx_relay_sem,
):
    i = pl.program_id(0)
    me, mine = lax.axis_index("seq"), lax.axis_index("head")
    inner = gate.shape[1]
    wide = act.shape[1]
    width = out_part.shape[2]
    depth = gread_got.shape[1]
    size = 2 * STATE // line
    phase = jnp.minimum(lax.div(i, blocks), 3)
    turn = i - 3 * blocks
    block = jnp.where(phase == 3, jnp.maximum(blocks - 1 - turn, 0), lax.rem(i, blocks))
    first, second = flags[2 * block], flags[2 * block + 1]
    g_line = Line(line, g_buf, width, line_sent, line_sem)
    back_plane = Plane(seqs, lambda s: back_slots.at[s], back_sent, back_sem, back_passed, way=-1)

    def group_rows(b):
        return pl.ds(pl.multiple_of(b * GROUP, GROUP), GROUP)

    here = group_rows(block)

    def rows_of(device):
        return pl.ds(pl.multiple_of(device * depth, depth), depth)

    def shard_of(ref, shard):
        return ref.at[:, pl.ds(pl.multiple_of(shard * width, LANES), width)]

    def all_line(body):
        if line > 1:

            @pl.loop(1, line)
            def _(n):
                body(lax.rem(mine + n, line))

    def all_seq(body):
        @pl.loop(1, seqs)
        def _(n):
            body(lax.rem(me + n, seqs))

    def each_load(body):
        def load(shard, n):
            return pltpu.make_async_copy(shard_of(g_part, shard), shard_of(g_buf, shard), load_sem.at[n])

        body(load(mine, 0))
        body(pltpu.make_async_copy(shard_of(g_part, mine), g_own, load_sem.at[3]))
        if line > 1:
            pl.when(mine > 0)(lambda: body(load(mine - 1, 1)))
            pl.when(mine < line - 1)(lambda: body(load(mine + 1, 2)))

    def sum_copy(to, slot):
        return remote(sums.at[mine], sums.at[slot], sum_sent.at[to], sum_sem.at[slot], {"head": to})

    def out_copy(to, slot):
        return remote(out_part.at[to], out_got.at[slot], out_sent.at[to], out_sem.at[slot], {"head": to})

    weights = ((gread_low, gread_got), (ggate_low, ggate_got), (dw_low, dw_got), (da_low, da_got))

    def w_copy(which, to, slot):
        src, dst = weights[which]
        return remote(src.at[rows_of(to)], dst.at[slot], w_sent.at[which, to], w_sem.at[which, slot], {"seq": to})

    def w_start(which):
        all_seq(lambda to: w_copy(which, to, me).start())

    def w_wait(which):
        all_seq(lambda other: w_copy(which, other, other).wait())

    def dx_copy(to, slot, b):
        return remote(
            shard_of(g_buf.at[group_rows(b)], to), dx_got.at[slot, group_rows(b)], dx_sent.at[to, b],
            dx_sem.at[slot, b], {"head": to},
        )

    merge = line == 4
    is_end = (mine == 0) | (mine == line - 1)
    low_side = mine < 2
    mid = jnp.where(low_side, 1, 2)
    far = jnp.where(low_side, 3, 0)

    def relay_copy():
        return remote(out_part.at[far], relay, relay_sent, relay_sem, {"head": mid})

    def dx_relay_copy(b):
        return remote(
            shard_of(g_buf.at[group_rows(b)], far), dx_relay.at[group_rows(b)], dx_relay_sent.at[b],
            dx_relay_sem.at[b], {"head": mid},
        )

    def all_direct(body, received=False):
        if not merge:
            all_line(body)
            return

        @pl.loop(1, line)
        def _(n):
            other = lax.rem(mine + n, line)
            skipped = (is_end & (other == far)) if received else (other == far)
            pl.when(jnp.logical_not(skipped))(lambda: body(other))

    def send_out():
        if merge:
            pl.when(is_end)(lambda: relay_copy().start())
        all_direct(lambda to: out_copy(to, mine).start())

    def merge_out():
        if merge:

            @pl.when(jnp.logical_not(is_end))
            def _():
                relay_copy().wait_recv()

                @pl.loop(0, blocks)
                def _(b):
                    at = group_rows(b)
                    out_part[far, at] = (out_part[far, at].astype(WIDE) + relay[at].astype(WIDE)).astype(LOW)

                out_copy(far, mine).start()

    def wait_out():
        all_direct(lambda other: out_copy(other, mine).wait_send())
        all_direct(lambda other: out_copy(other, other).wait_recv(), received=True)
        if merge:
            pl.when(is_end)(lambda: relay_copy().wait_send())
            pl.when(jnp.logical_not(is_end))(lambda: out_copy(far, mine).wait_send())

    def send_dx(b):
        if merge:
            pl.when(is_end)(lambda: dx_relay_copy(b).start())
        all_direct(lambda to: dx_copy(to, mine, b).start())

    def merge_dx(b):
        if merge:

            @pl.when(jnp.logical_not(is_end))
            def _():
                at = group_rows(b)
                columns = pl.ds(pl.multiple_of(far * width, LANES), width)
                dx_relay_copy(b).wait_recv()
                g_buf[at, columns] = (g_buf[at, columns].astype(WIDE) + dx_relay[at].astype(WIDE)).astype(LOW)
                dx_copy(far, mine, b).start()

    def wait_dx(b):
        all_direct(lambda other: dx_copy(other, mine, b).wait_send())
        all_direct(lambda other: dx_copy(other, other, b).wait_recv(), received=True)
        if merge:
            pl.when(is_end)(lambda: dx_relay_copy(b).wait_send())
            pl.when(jnp.logical_not(is_end))(lambda: dx_copy(far, mine, b).wait_send())

    def from_line_of(b):
        total = jnp.zeros((GROUP, width), WIDE)
        for z in range(line):
            block_z = out_part[z, group_rows(b)].astype(WIDE)
            total = total + (jnp.where(is_end & (far == z), 0.0, block_z) if merge else block_z)
        return total

    def edge_copy(to):
        return remote(edge_own, edge_got, edge_sent, edge_sem, {"seq": to})

    def zs_copy(to, slot):
        return remote(zs_send.at[to], zs_got.at[slot], zs_sent.at[to], zs_sem.at[slot], {"head": to})

    def da_copy(to, slot):
        return remote(da_send.at[to], addr_got.at[slot], da_sent.at[to], da_sem.at[slot], {"head": to})

    def small_copy(to, slot):
        return remote(small, small_got.at[slot], small_sent.at[to], small_sem.at[slot], {"seq": to})

    arrivals = (out_recv, grad_recv)

    def fin_copy(which, to, slot):
        return remote(
            fin_send.at[which, to], arrivals[which].at[slot], fin_sent.at[which, to], fin_sem.at[which, slot],
            {"seq": to},
        )

    own_copies = {
        "out": pltpu.make_async_copy(out_part.at[mine], out_got.at[mine], own_sem.at[0]),
        "gread": pltpu.make_async_copy(gread_low.at[rows_of(me)], gread_got.at[me], own_sem.at[1]),
        "ggate": pltpu.make_async_copy(ggate_low.at[rows_of(me)], ggate_got.at[me], own_sem.at[2]),
        "dw": pltpu.make_async_copy(dw_low.at[rows_of(me)], dw_got.at[me], own_sem.at[3]),
        "dx": pltpu.make_async_copy(shard_of(g_buf, mine), dx_got.at[mine], own_sem.at[4]),
        "addr": pltpu.make_async_copy(da_send.at[mine], addr_got.at[mine], own_sem.at[5]),
        "small": pltpu.make_async_copy(small, small_got.at[me], own_sem.at[6]),
        "fin0": pltpu.make_async_copy(fin_send.at[0, me], out_recv.at[me], own_sem.at[7]),
        "fin1": pltpu.make_async_copy(fin_send.at[1, me], grad_recv.at[me], own_sem.at[8]),
    }

    def route(which):
        def send(to):
            fin_send[which, to] = result[which, give[to]]
            fin_copy(which, to, me).start()

        all_seq(send)
        fin_send[which, me] = result[which, give[me]]
        own_copies["fin%d" % which].start()

    row = lax.broadcasted_iota(jnp.int32, (GROUP, LANES), 0)
    lane = lax.broadcasted_iota(jnp.int32, (GROUP, LANES), 1)

    def entry_of(cum_v, spread_m):
        return to_columns(jnp.exp(cum_v) * (first * jnp.where(row < BLOCK, 1.0, second)), spread_m)

    def row_stats(b):
        stats = jnp.concatenate([totals[b], jnp.zeros((LANES - EDGE, GROUP), WIDE)], axis=0).T
        return lax.rsqrt(stats[:, 0:1] / INNER + EPS), stats[:, 1:2]

    def gated_of(ssd):
        gate_v = gate[...]
        return ssd * (gate_v * sigmoid(gate_v))

    fetch_r = pltpu.make_async_copy(r_in, r_t, weight_sem.at[0])
    fetch_w = pltpu.make_async_copy(w_in, w, weight_sem.at[1])

    @pl.when(i == 0)
    def _():
        fetch_r.start()
        greet(seqs, line)
        g_line.hop(1, take=False, source=lambda shard: shard_of(g_part, shard))
        each_load(lambda copy: copy.start())
        fetch_w.start()
        state[...] = state_in[...]
        fetch_r.wait()

    @pl.when(phase == 0)
    def _():
        spread_m, collect = head_rows(inner), head_columns(inner)
        cum_v = cum[...]
        carry = jnp.exp(cum_v.T[:, GROUP - 1 : GROUP]) * (first * second)
        start = state[...]
        starts[block] = start
        ssd = part[...] + entry_of(cum_v, spread_m) * nt(read[...], start.astype(LOW))
        ssd_s[here, :] = ssd
        state[...] = carry_columns(carry, collect) * start + local[0]
        out = nt((gated_of(ssd) * postnorm[...]).astype(LOW), r_t[...])
        for z in range(line):
            out_part[z, here] = out[:, z * width : (z + 1) * width].astype(LOW)

    @pl.when(i == blocks - 1)
    def _():
        for step in range(2, line):
            g_line.hop(step)
        each_load(lambda copy: copy.wait())
        g_line.finish(None, range(1, line - 1))
        fetch_w.wait()
    @pl.when(phase == 1)
    def _():
        gated = gated_of(ssd_s[here, :])
        d_inner = nn(g_buf[here, :], r_t[...])
        din_s[here, :] = d_inner
        squares = jnp.sum(gated * gated, axis=1, keepdims=True)
        dots = jnp.sum(gated * postnorm[...] * d_inner, axis=1, keepdims=True)
        both = jnp.where(lane == 0, squares, jnp.where(lane == 1, dots, 0.0)).T
        sums[mine, block] = both[:EDGE]

    @pl.when(i == 2 * blocks - 1)
    def _():
        all_line(lambda to: sum_copy(to, mine).start())
        gread[...] = jnp.zeros_like(gread)
        ggate[...] = jnp.zeros_like(ggate)
        gpost[...] = jnp.zeros_like(gpost)
        state[...] = jnp.zeros_like(state)
        prod[...] = jnp.ones_like(prod)
        all_line(lambda other: sum_copy(other, other).wait())
        totals[...] = jnp.sum(sums[...], axis=0)
        send_out()
        own_copies["out"].start()

    @pl.when(phase == 2)
    def _():
        spread_m, collect = head_rows(inner), head_columns(inner)
        cum_v = cum[...]
        carry = jnp.exp(cum_v.T[:, GROUP - 1 : GROUP]) * (first * second)
        inv, dot = row_stats(block)
        gate_v = gate[...]
        sig = sigmoid(gate_v)
        ssd = ssd_s[here, :]
        d_inner = din_s[here, :]
        gated = ssd * (gate_v * sig)
        gated_inv = gated * inv
        inner_normed = (gated_inv * postnorm[...]).astype(LOW)
        d_gated = (inv * postnorm[...]) * d_inner - gated * (inv * inv * inv / INNER * dot)
        gpost[...] += jnp.sum(d_inner * gated_inv, axis=0, keepdims=True)
        d_ssd = (d_gated * (gate_v * sig)).astype(LOW)
        d_gate = (d_gated * ssd * sig * (1.0 + gate_v * (1.0 - sig))).astype(LOW)
        dssd_s[here, :] = d_ssd
        dgate_s[here, :] = d_gate
        gread[...] += tn(g_buf[here, :], inner_normed)
        ggate[...] += tn(normed[...], d_gate)
        query_grad = (d_ssd.astype(WIDE) * entry_of(cum_v, spread_m)).astype(LOW)
        found = tn(query_grad, read[...])
        q[block] = found
        state[...] += carry_columns(prod[...], collect) * found
        prod[...] = prod[...] * carry

    @pl.when(i == 3 * blocks - 1)
    def _():
        back_msg[:inner, :] = state[...].astype(LOW)
        back_msg[inner:, :] = jnp.broadcast_to(prod[:HALO], (HALO, STATE)).astype(LOW)
        back_plane.start(back_msg)
        gread_low[...] = gread[...].astype(LOW)
        ggate_low[...] = ggate[...].astype(LOW)
        for ref in (tiny, taps_g, bias_g, dw, pn):
            ref[...] = jnp.zeros_like(ref)
        back_plane.relay()
        back_plane.finish(back_msg)
        w_start(0)
        w_start(1)
        own_copies["gread"].start()
        own_copies["ggate"].start()
        state[...] = fold_states(
            back_slots, head_columns(inner), inner, seqs - 1, me, -1, jnp.zeros((inner, STATE), WIDE)
        )
        merge_out()

    @pl.when((phase == 3) & (turn < blocks))
    def _():
        slot = jnp.where(turn == 0, 1, 0)
        spread_m, collect = head_rows(inner), head_columns(inner)
        lower_mask = ones_before(BLOCK)
        top, low = slice(0, BLOCK), slice(BLOCK, GROUP)
        cum_v = cum[...]
        cum_t = cum_v.T
        steps, sig, ratio = step_terms(raw[...], heads)
        steps_t = steps.T
        scale = -jnp.exp(vec[1:2, :])
        last = cum_v[GROUP - 1 : GROUP, :]
        write = act[:, inner : inner + STATE]
        read_v = act[:, inner + STATE :]
        s00 = jnp.where(lower_mask, nt(read_v[top], write[top]), 0.0)
        s10 = nt(read_v[low], write[top]) * second
        s11 = jnp.where(lower_mask, nt(read_v[low], write[low]), 0.0)

        end = state[...]
        end_low = end.astype(LOW)
        start = starts[block]
        carry = jnp.exp(cum_t[:, GROUP - 1 : GROUP]) * (first * second)
        state[...] = carry_columns(carry, collect) * end + q[block]
        weight = steps * jnp.exp(last - cum_v) * jnp.where(row < BLOCK, second, 1.0)
        weight_w = to_columns(weight, spread_m)
        d_ssd = dssd_s[here, :]
        d_query = (d_ssd.astype(WIDE) * entry_of(cum_v, spread_m)).astype(LOW)
        through_w = to_columns(jnp.broadcast_to(vec[2:3, :], (EDGE, LANES)), spread_m)[0:1]

        def decay_of(head, t, s):
            decay = jnp.exp(jnp.minimum(cum_v[t, head : head + 1] - cum_t[head : head + 1, s], 0.0))
            return decay * steps_t[head : head + 1, s]

        ds00 = jnp.zeros((BLOCK, BLOCK), WIDE)
        ds10 = jnp.zeros((BLOCK, BLOCK), WIDE)
        ds11 = jnp.zeros((BLOCK, BLOCK), WIDE)
        packed, value_parts, tails = [], [], []
        d_packed = nt(write, end_low)
        for pair in range(inner // LANES):
            columns = slice(pair * LANES, (pair + 1) * LANES)
            values = act[:, columns]
            values_f = values.astype(WIDE)
            dy = d_ssd[:, columns]
            dys = pair_lanes(dy)
            m00, m10, m11 = [], [], []
            for k in range(2):
                head = 2 * pair + k
                l00, l10, l11 = decay_of(head, top, top), decay_of(head, low, top), decay_of(head, low, low)
                m00.append((s00 * l00).astype(LOW))
                m10.append((s10 * l10).astype(LOW))
                m11.append((s11 * l11).astype(LOW))
                ds00 = ds00 + nt(dys[k][top], values[top]) * l00
                ds10 = ds10 + nt(dys[k][low], values[top]) * l10
                ds11 = ds11 + nt(dys[k][low], values[low]) * l11
            v0 = tn(
                jnp.concatenate([m00[0], m10[0], m00[1], m10[1]], axis=0), jnp.concatenate([dys[0], dys[1]], axis=0)
            )
            v1 = tn(
                jnp.concatenate([m11[0], m11[1]], axis=0), jnp.concatenate([dys[0][low], dys[1][low]], axis=0)
            )
            tail = d_packed[:, columns] * weight_w[:, columns]
            whole = jnp.concatenate([v0, v1], axis=0) + tail
            d_conv[slot, :, columns] = conv_grad(
                whole + through_w[:, columns] * dy.astype(WIDE), conv[:, columns]
            )
            value_parts.append(values_f * whole)
            tails.append(jnp.sum(tail * values_f, axis=0, keepdims=True))
            packed.append((values_f * weight_w[:, columns]).astype(LOW))

        ds = jnp.concatenate(
            [
                jnp.concatenate([jnp.where(lower_mask, ds00, 0.0), jnp.zeros((BLOCK, BLOCK), WIDE)], axis=1),
                jnp.concatenate([ds10 * second, jnp.where(lower_mask, ds11, 0.0)], axis=1),
            ],
            axis=0,
        ).astype(LOW)
        d_read = nn(ds, write) + nn(d_query, start.astype(LOW))
        d_write = tn(ds, read_v) + nn(jnp.concatenate(packed, axis=1), end_low)
        d_conv[slot, :, inner : inner + STATE] = conv_grad(d_write, conv[:, inner : inner + STATE])
        d_conv[slot, :, inner + STATE :] = conv_grad(d_read, conv[:, inner + STATE :])

        dy_f = d_ssd.astype(WIDE)
        own = to_heads(dy_f * act[:, :inner].astype(WIDE), collect)
        r1 = to_heads(dy_f * ssd_s[here, :], collect) - vec[2:3, :] * own
        by_value = to_heads(jnp.concatenate(value_parts, axis=1), collect)
        tail_row = to_heads(jnp.broadcast_to(jnp.concatenate(tails, axis=1), (EDGE, inner)), collect)[0:1]
        high, rest = halves(end * start)
        ones = jnp.ones((EDGE, STATE), LOW)
        carry_grad = to_heads(nt(ones, high) + nt(ones, rest), collect)[0:1]
        d_last = tail_row + carry_grad * (jnp.exp(last) * (first * second))
        d_cum = r1 - by_value + jnp.where(row == GROUP - 1, d_last, 0.0)
        d_rate = sum_after(d_cum)
        d_raw = d_rate * scale * sig + by_value * ratio
        d_step[slot] = d_raw.astype(LOW)
        tiny[0:1, :] += jnp.sum(d_raw, axis=0, keepdims=True)
        tiny[1:2, :] += jnp.sum(d_rate * steps, axis=0, keepdims=True) * scale
        tiny[2:3, :] += jnp.sum(own, axis=0, keepdims=True)

    @pl.when(turn == blocks - 1)
    def _():
        edge_own[...] = d_conv[jnp.where(turn == 0, 1, 0), 0:EDGE, :]
        edge_copy(lax.rem(me + seqs - 1, seqs)).start()

    @pl.when(turn == blocks)
    def _():
        edge_copy(lax.rem(me + 1, seqs)).wait()
        after[...] = edge_got[...]

    @pl.when(turn >= 1)
    def _():
        final = turn == blocks
        slot = jnp.where(final, 1, 0)
        b = jnp.where(final, blocks - 1, blocks - 1 - turn)
        at_b = group_rows(b)
        taps = jnp.concatenate([kernels[...], filters[...]], axis=1)
        grad_c = d_conv[slot]
        pre_v = pre[...].astype(WIDE)
        before = jnp.where(b == 0, rim[...], pre_before[HALO - EDGE :, :].astype(WIDE))
        bias_g[...] += jnp.sum(grad_c, axis=0, keepdims=True)
        d_pre = []
        for half in range(2):
            part_rows = slice(half * BLOCK, (half + 1) * BLOCK)
            tile = grad_c[part_rows]
            ext[0:EDGE, :] = (before if half == 0 else pre_v[BLOCK - EDGE : BLOCK]) * flags[2 * b + half]
            ext[EDGE:, :] = pre_v[part_rows]
            for tap in range(TAPS):
                taps_g[tap : tap + 1, :] += jnp.sum(
                    tile * ext[pl.ds(EDGE - (TAPS - 1) + tap, BLOCK), :], axis=0, keepdims=True
                )
            ext[:BLOCK, :] = tile
            ext[BLOCK:, :] = (grad_c[BLOCK : BLOCK + EDGE] if half == 0 else after[...]) * flags[2 * b + half + 1]
            total = taps[TAPS - 1 : TAPS] * ext[:BLOCK, :]
            for tap in range(TAPS - 1):
                total = total + taps[tap : tap + 1] * ext[pl.ds(TAPS - 1 - tap, BLOCK), :]
            d_pre.append(total.astype(LOW))
        d_pre = jnp.concatenate(d_pre, axis=0)
        step_grad = d_step[slot]
        normed_v = normed[...]
        dw[:, :wide] += tn(normed_v, d_pre)
        dw[:, wide:] += tn(normed_v, step_grad)
        d_normed = (
            nt(dgate_s[at_b, :], w[:, :inner])
            + nt(d_pre, w[:, inner : inner + wide])
            + nt(step_grad, w[:, inner + wide :])
        )
        u_f = u[...].astype(WIDE)
        inv = lax.rsqrt(jnp.mean(u_f * u_f, axis=1, keepdims=True) + EPS)
        gained = d_normed * prenorm[...]
        dot = jnp.sum(gained * u_f, axis=1, keepdims=True)
        grad = gained * inv - u_f * (inv * inv * inv / D * dot)
        pn[...] += jnp.sum(d_normed * (u_f * inv), axis=0, keepdims=True)
        g_buf[at_b, :] = grad.astype(LOW)
        send_dx(b)
        result[0, 2 * b] = u[0:BLOCK, pl.ds(pl.multiple_of(mine * width, LANES), width)]
        result[0, 2 * b + 1] = u[BLOCK:, pl.ds(pl.multiple_of(mine * width, LANES), width)]

    @pl.when((turn >= 2) & (turn < blocks))
    def _():
        merge_dx(blocks - turn)

    @pl.when((turn >= 0) & (turn < blocks))
    def _():
        after[...] = d_conv[jnp.where(turn == 0, 1, 0), 0:EDGE, :]

    @pl.when(turn == blocks)
    def _():
        own_copies["dx"].start()
        dw_low[:, :inner] = dw[:, :inner].astype(LOW)
        dw_low[:, inner:] = dw[:, wide:].astype(LOW)
        da_low[...] = dw[:, inner:wide].astype(LOW)
        w_start(3)
        w_start(2)
        own_copies["dw"].start()
        da_got[me] = da_low[rows_of(me), :]

        if blocks > 1:
            merge_dx(0)

        for z in range(line):
            slab = z * size // LANES * LANES
            zs_send[z] = jnp.zeros(zs_send.shape[1:], WIDE)
            zs_send[z, 0:1, :] = pn[:, z * width : (z + 1) * width]
            zs_send[z, EDGE : EDGE + TAPS, :LANES] = taps_g[0:TAPS, inner + slab : inner + slab + LANES]
            zs_send[z, EDGE + TAPS : EDGE + TAPS + 1, :LANES] = bias_g[:, inner + slab : inner + slab + LANES]
        zs_got[mine] = zs_send[mine]
        all_line(lambda to: zs_copy(to, mine).start())

        wait_out()
        own_copies["out"].wait()

        def fetch(src, n):
            return pltpu.make_async_copy(src, out_part, load_sem.at[n])

        fetch(out_got, 0).start()
        fetch(out_got, 0).wait()

        @pl.loop(0, blocks)
        def _(b):
            inv, _ = row_stats(b)
            total = from_line_of(b) * inv
            result[0, 2 * b] = (result[0, 2 * b].astype(WIDE) + total[:BLOCK]).astype(LOW)
            result[0, 2 * b + 1] = (result[0, 2 * b + 1].astype(WIDE) + total[BLOCK:]).astype(LOW)

        route(0)
        merge_dx(blocks - 1)
        all_line(lambda other: zs_copy(other, other).wait())
        from_line = jnp.sum(zs_got[...], axis=0)
        small[...] = jnp.zeros_like(small)
        small[0:TAPS, :inner] = taps_g[0:TAPS, :inner]
        small[0:TAPS, inner:] = from_line[EDGE : EDGE + TAPS, :LANES]
        small[4:5, :inner] = bias_g[:, :inner]
        small[4:5, inner:] = from_line[EDGE + TAPS : EDGE + TAPS + 1, :LANES]
        small[5:6, :inner] = gpost[...]
        small[6:7, :width] = from_line[0:1]
        for n in range(3):
            small[7:8, n * LANES : (n + 1) * LANES] = tiny[n : n + 1, :]
        own_copies["small"].start()
        all_seq(lambda to: small_copy(to, me).start())

        w_wait(3)
        from_plane = da_got[0].astype(WIDE)
        for n in range(1, seqs):
            from_plane = from_plane + da_got[n].astype(WIDE)
        for z in range(line):
            slab = z * size // LANES * LANES
            da_send[z] = from_plane[:, slab : slab + LANES]
        own_copies["addr"].start()
        all_line(lambda to: da_copy(to, mine).start())

        @pl.loop(0, blocks)
        def _(b):
            wait_dx(b)

        own_copies["dx"].wait()
        fetch(dx_got, 1).start()
        fetch(dx_got, 1).wait()

        @pl.loop(0, blocks)
        def _(b):
            done = (g_own[group_rows(b), :].astype(WIDE) + from_line_of(b)).astype(LOW)
            result[1, 2 * b] = done[:BLOCK]
            result[1, 2 * b + 1] = done[BLOCK:]

        route(1)
        for which in range(3):
            w_wait(which)
        all_line(lambda other: da_copy(other, other).wait())
        all_seq(lambda other: small_copy(other, other).wait())
        all_seq(lambda other: fin_copy(0, other, other).wait())
        all_seq(lambda other: fin_copy(1, other, other).wait())
        for name in ("gread", "ggate", "dw", "addr", "small", "fin0", "fin1"):
            own_copies[name].wait()


def core(
    flags, give, gate, part, act, cum, raw, local, conv, pre, normed, u, g_part, state_in, r_t, w_all, postnorm, vec,
    prenorm, kernels, filters, rim,
):
    seqs, line = lax.axis_size("seq"), lax.axis_size("head")
    rows, inner = gate.shape
    wide = act.shape[1]
    total = g_part.shape[1]
    width = total // line
    depth = total // seqs
    blocks, tiles = rows // GROUP, rows // BLOCK
    heads = inner // HDIM
    steps = 4 * blocks + 1

    def scan_block(i):
        return jnp.clip(4 * blocks - 1 - i, 0, blocks - 1)

    def late_block(i):
        return jnp.where(i == steps - 1, blocks - 1, jnp.clip(4 * blocks - 1 - i, 0, max(blocks - 2, 0)))

    def place(early, late=None):
        def at(i):
            index = jnp.int32(0)
            for n in range(3):
                if n in early:
                    now = i - n * blocks
                elif any(m > n for m in early):
                    now = jnp.int32(0)
                elif late is not None:
                    now = late(jnp.int32(3 * blocks))
                else:
                    now = jnp.int32(blocks - 1)
                index = jnp.where((i >= n * blocks) & (i < (n + 1) * blocks), now, index)
            return jnp.where(i >= 3 * blocks, late(i) if late is not None else blocks - 1, index)

        return at

    def by_rows(columns, at, column=0):
        return blockwise((GROUP, columns), lambda i: (at(i), column))

    local_at = place((0,))
    pre_at = place((), late_block)
    message = (inner + HALO, STATE)
    sums = (blocks, EDGE, GROUP)
    whole = (state_in, postnorm, vec, prenorm, kernels, filters, rim)
    gather = (line, rows, width)
    small = (EDGE, inner + LANES)
    return pl.pallas_call(
        functools.partial(core_kernel, seqs, line, heads, blocks),
        grid=(steps,),
        out_shape=(
            shape((seqs, BLOCK, width), LOW), shape((seqs, BLOCK, width), LOW), shape(gather, LOW), shape(gather, LOW),
            shape((seqs, depth, inner), LOW), shape((seqs, depth, inner), LOW), shape((seqs, depth, inner + LANES), LOW),
            shape((line, depth, LANES), WIDE), shape((seqs,) + small, WIDE),
        ),
        in_specs=[
            SMEM_SPEC, SMEM_SPEC,
            by_rows(inner, place((0, 1, 2))), by_rows(inner, place((0,))),
            by_rows(STATE, place((0, 2)), (inner + STATE) // STATE), by_rows(wide, place((), scan_block)),
            by_rows(LANES, place((0, 2), scan_block)), by_rows(LANES, place((), scan_block)),
            blockwise((1, inner, STATE), lambda i: (local_at(i), 0, 0)), by_rows(wide, place((), scan_block)),
            by_rows(wide, pre_at),
            blockwise((HALO, wide), lambda i: (jnp.maximum(pre_at(i) * (GROUP // HALO) - 1, 0), 0)),
            by_rows(total, place((2,), late_block)), by_rows(total, pre_at), ANY_SPEC, ANY_SPEC, ANY_SPEC,
        ] + [fixed(a.shape) for a in whole],
        out_specs=(ANY_SPEC,) * 9,
        scratch_shapes=[
            pltpu.VMEM(r_t.shape, LOW), pltpu.VMEM(w_all.shape, LOW),
            pltpu.VMEM((rows, inner), WIDE), pltpu.VMEM((rows, inner), WIDE), pltpu.VMEM((rows, inner), LOW),
            pltpu.VMEM((rows, inner), LOW), pltpu.VMEM((blocks, inner, STATE), WIDE),
            pltpu.VMEM((blocks, inner, STATE), WIDE), pltpu.VMEM((inner, STATE), WIDE), pltpu.VMEM((LANES, 1), WIDE),
            pltpu.VMEM((rows, total), LOW), pltpu.VMEM((rows, width), LOW), pltpu.VMEM(gather, LOW),
            pltpu.VMEM((seqs,) + message, LOW), pltpu.VMEM(message, LOW),
            pltpu.VMEM((rows if line == 4 else GROUP, width), LOW), pltpu.VMEM((rows if line == 4 else GROUP, width), LOW),
            pltpu.VMEM((line,) + sums, WIDE), pltpu.VMEM(sums, WIDE),
            pltpu.VMEM((total, inner), WIDE), pltpu.VMEM((total, inner), WIDE), pltpu.VMEM((total, inner), LOW),
            pltpu.VMEM((total, inner), LOW), pltpu.VMEM((1, inner), WIDE), pltpu.VMEM((EDGE, LANES), WIDE),
            pltpu.VMEM((2, GROUP, wide), WIDE), pltpu.VMEM((2, GROUP, LANES), LOW), pltpu.VMEM((EDGE, wide), WIDE),
            pltpu.VMEM((EDGE, wide), WIDE), pltpu.VMEM((EDGE, wide), WIDE), pltpu.VMEM((BLOCK + EDGE, wide), WIDE),
            pltpu.VMEM((EDGE, wide), WIDE), pltpu.VMEM((1, wide), WIDE), pltpu.VMEM((total, wide + LANES), WIDE),
            pltpu.VMEM((total, inner + LANES), LOW), pltpu.VMEM((total, wide - inner), LOW),
            pltpu.VMEM((seqs, depth, wide - inner), LOW), pltpu.VMEM((line, depth, LANES), WIDE),
            pltpu.VMEM((1, total), WIDE), pltpu.VMEM((line, 2 * EDGE, width), WIDE),
            pltpu.VMEM((line, 2 * EDGE, width), WIDE), pltpu.VMEM(small, WIDE),
            pltpu.VMEM((2, tiles, BLOCK, width), LOW), pltpu.VMEM((2, seqs, BLOCK, width), LOW),
            DMA((seqs,)), DMA((seqs,)), DMA((seqs,)), DMA((line,)), DMA((line,)), DMA((2, line)), DMA((line,)), DMA((4,)),
            DMA((line,)), DMA((line,)), DMA((4, seqs)), DMA((4, seqs)), DMA((line, blocks)), DMA((line, blocks)), DMA, DMA,
            DMA((line,)), DMA((line,)), DMA((line,)), DMA((line,)), DMA((seqs,)), DMA((seqs,)), DMA((2, seqs)),
            DMA((2, seqs)), DMA((9,)), DMA((2,)), DMA, DMA, DMA((blocks,)), DMA((blocks,)),
        ],
        compiler_params=pltpu.CompilerParams(
            collective_id=1, has_side_effects=True, vmem_limit_bytes=VMEM_LIMIT, dimension_semantics=("arbitrary",)
        ),
        name="core",
    )(
        flags, give, gate, part, act, act, cum, raw, local, conv, pre, pre, normed, u, g_part, r_t, w_all, *whole
    )


def finish_kernel(
    take, out_recv, grad_recv, gread_got, ggate_got, dw_got, addr_got, small_got,
    out_o, dx_o, prenorm_o, gate_o, pay_o, addr_o, step_o, kernels_o, offsets_o, filters_o, shifts_o,
    stepbias_o, decays_o, through_o, post_o, read_o,
):
    inner, size, heads, width = gate_o.shape[1], addr_o.shape[1], step_o.shape[0], prenorm_o.shape[1]
    offset = lax.rem(lax.axis_index("head") * size, LANES)
    back_turn = lax.rem(LANES - offset, LANES)
    for k in range(out_o.shape[0]):
        out_o[k] = out_recv[take[k]]
        dx_o[k] = grad_recv[take[k]]

    def summed(ref):
        total = ref[0].astype(WIDE)
        for n in range(1, ref.shape[0]):
            total = total + ref[n].astype(WIDE)
        return total

    read_o[...] = summed(gread_got).T
    gate_o[...] = summed(ggate_got)
    grads = summed(dw_got)
    pay_o[...] = grads[:, :inner]
    step_o[...] = grads[:, inner:].T[:heads]
    addr_o[...] = pltpu.roll(summed(addr_got), back_turn, 1)[:, :size]
    totals = jnp.sum(small_got[...], axis=0)
    kernels_o[...] = totals[0:TAPS, :inner]
    offsets_o[...] = totals[4:5, :inner]
    turned = pltpu.roll(totals[:, inner:], back_turn, 1)
    filters_o[...] = turned[0:TAPS, :size]
    shifts_o[...] = turned[4:5, :size]
    post_o[...] = totals[5:6, :inner]
    prenorm_o[...] = totals[6:7, :width]
    for n, ref in enumerate((stepbias_o, decays_o, through_o)):
        ref[...] = totals[7:8, n * LANES : n * LANES + heads]


def finish(take, out_recv, grad_recv, gread_got, ggate_got, dw_got, addr_got, small_got):
    seqs, _, width = out_recv.shape
    tiles = take.shape[0]
    _, depth, inner = gread_got.shape
    heads = inner // HDIM
    size = 2 * STATE // addr_got.shape[0]
    operands = (out_recv, grad_recv, gread_got, ggate_got, dw_got, addr_got, small_got)
    outs = (
        shape((tiles, BLOCK, width), LOW), shape((tiles, BLOCK, width), LOW), shape((1, width), WIDE),
        shape((depth, inner), WIDE), shape((depth, inner), WIDE), shape((depth, size), WIDE),
        shape((heads, depth), WIDE), shape((TAPS, inner), WIDE), shape((1, inner), WIDE),
        shape((TAPS, size), WIDE), shape((1, size), WIDE), shape((1, heads), WIDE), shape((1, heads), WIDE),
        shape((1, heads), WIDE), shape((1, inner), WIDE), shape((inner, depth), WIDE),
    )
    return pl.pallas_call(
        finish_kernel,
        grid=(1,),
        out_shape=outs,
        in_specs=[SMEM_SPEC] + [fixed(a.shape) for a in operands],
        out_specs=tuple(fixed(a.shape) for a in outs),
        compiler_params=pltpu.CompilerParams(vmem_limit_bytes=VMEM_LIMIT, dimension_semantics=("arbitrary",)),
        name="finish",
    )(take, *operands)


def on_device(
    inputs,
    cotangent,
    lengths,
    placement,
    prenorm,
    gating,
    payload,
    address,
    stepping,
    kernels,
    offsets,
    filters,
    shifts,
    stepbias,
    decays,
    through,
    postnorm,
    readout,
):
    rows, width = inputs.shape
    heads = stepbias.shape[0]
    tiles = rows // BLOCK
    give_in, take_in, give_out, take_out, flags, vec = index(placement, lengths, stepbias, decays, through, tiles)
    gain, post = prenorm[None, :], postnorm[None, :]
    (
        u, normed, gate, pre, conv, act, raw, cum, part, local, state_in, rim, g_part, w_all, r_t
    ) = front(
        give_in, take_in, flags, inputs, cotangent, gating, payload, address, stepping, readout, vec, gain, kernels,
        filters, offsets[None, :], shifts[None, :]
    )
    out_recv, grad_recv, _, _, gread_got, ggate_got, dw_got, addr_got, small_got = core(
        flags, give_out, gate, part, act, cum, raw, local, conv, pre, normed, u, g_part, state_in, r_t, w_all, post, vec,
        gain, kernels, filters, rim
    )
    (
        out, dx, prenorm_g, gate_g, pay_g, addr_g, step_g, kernels_g, offsets_g, filters_g, shifts_g, stepbias_g,
        decays_g, through_g, post_g, read_g,
    ) = finish(take_out, out_recv, grad_recv, gread_got, ggate_got, dw_got, addr_got, small_got)
    return (
        out.reshape(rows, width),
        dx.reshape(rows, width),
        prenorm_g.reshape(-1),
        gate_g,
        pay_g,
        addr_g,
        step_g.T,
        kernels_g,
        offsets_g.reshape(-1),
        filters_g,
        shifts_g.reshape(-1),
        stepbias_g.reshape(-1),
        decays_g.reshape(-1),
        through_g.reshape(-1),
        post_g.reshape(-1),
        read_g,
    )


def solution(mesh):
    in_specs = (
        P("seq", "head"),
        P("seq", "head"),
        P(),
        P(),
        P(),
        P("seq", "head"),
        P("seq", "head"),
        P("seq", None),
        P("seq", "head"),
        P(None, "head"),
        P("head"),
        P(),
        P(),
        P("head"),
        P("head"),
        P("head"),
        P("head"),
        P("head", "seq"),
    )
    out_specs = (
        P("seq", "head"),
        P("seq", "head"),
        P("head"),
        P("seq", "head"),
        P("seq", "head"),
        P("seq", "head"),
        P("seq", "head"),
        P(None, "head"),
        P("head"),
        P(None, "head"),
        P("head"),
        P("head"),
        P("head"),
        P("head"),
        P("head"),
        P("head", "seq"),
    )
    return jax.shard_map(
        on_device, mesh=mesh, in_specs=in_specs, out_specs=out_specs, check_vma=False
    )
```

```python
import functools

import jax
import jax.numpy as jnp
from jax import lax
from jax.experimental import pallas as pl
from jax.experimental.pallas import tpu as pltpu
from jax.sharding import PartitionSpec as P

D = 1024
GROUP = 256
BLOCK = 128
INNER = 2048
HDIM = 64
STATE = 128
TAPS = 4
HALO = 16
EDGE = 8
LANES = 128
EPS = 1e-05
MESH = pl.DeviceIdType.MESH
VMEM = pltpu.MemorySpace.VMEM
SMEM = pltpu.MemorySpace.SMEM
DMA = pltpu.SemaphoreType.DMA
VMEM_LIMIT = 63 << 20
LOW = jnp.bfloat16
WIDE = jnp.float32


def shape(dims, kind):
    return jax.ShapeDtypeStruct(dims, kind)


def nn(a, b):
    return jnp.dot(a, b, preferred_element_type=WIDE)


def nt(a, b):
    return lax.dot_general(a, b, (((1,), (1,)), ((), ())), preferred_element_type=WIDE)


def tn(a, b):
    return lax.dot_general(a, b, (((0,), (0,)), ((), ())), preferred_element_type=WIDE)


def halves(x):
    high = x.astype(LOW)
    return high, (x - high.astype(WIDE)).astype(LOW)


def thirds(x):
    high = x.astype(LOW)
    rest = x - high.astype(WIDE)
    middle = rest.astype(LOW)
    return high, middle, (rest - middle.astype(WIDE)).astype(LOW)


def head_rows(inner):
    row = lax.broadcasted_iota(jnp.int32, (LANES, inner), 0)
    column = lax.broadcasted_iota(jnp.int32, (LANES, inner), 1)
    return jnp.where(column // HDIM == row, 1.0, 0.0).astype(LOW)


def head_columns(inner):
    row = lax.broadcasted_iota(jnp.int32, (inner, LANES), 0)
    column = lax.broadcasted_iota(jnp.int32, (inner, LANES), 1)
    return jnp.where(row // HDIM == column, 1.0, 0.0).astype(LOW)


def to_columns(x, spread):
    high, rest = halves(x)
    return nn(high, spread) + nn(rest, spread)


def to_heads(x, collect):
    high, rest = halves(x)
    return nn(high, collect) + nn(rest, collect)


def ones_before(count):
    row = lax.broadcasted_iota(jnp.int32, (count, count), 0)
    column = lax.broadcasted_iota(jnp.int32, (count, count), 1)
    return row >= column


def sum_before(x):
    matrix = jnp.where(ones_before(x.shape[0]), 1.0, 0.0).astype(LOW)
    high, middle, low = thirds(x)
    return nn(matrix, high) + (nn(matrix, middle) + nn(matrix, low))


def sum_after(x):
    count = x.shape[0]
    row = lax.broadcasted_iota(jnp.int32, (count, count), 0)
    column = lax.broadcasted_iota(jnp.int32, (count, count), 1)
    matrix = jnp.where(row <= column, 1.0, 0.0).astype(LOW)
    high, middle, low = thirds(x)
    return nn(matrix, high) + (nn(matrix, middle) + nn(matrix, low))


def sigmoid(x):
    return 0.5 * jnp.tanh(0.5 * x) + 0.5


def step_terms(raw, heads):
    z = jnp.exp(-jnp.abs(raw))
    series = 1.0 - z * (0.5 - z * (1.0 / 3.0 - z * (0.25 - z * 0.2)))
    small = z < 0.03
    log1p = jnp.where(small, z * series, jnp.log(1.0 + z))
    soft = jnp.maximum(raw, 0.0) + log1p
    one = 1.0 / (1.0 + z)
    sig = jnp.where(raw >= 0, one, z * one)
    ratio = jnp.where(small & (raw < 0), one / series, sig / jnp.maximum(soft, 1e-20))
    lane = lax.broadcasted_iota(jnp.int32, raw.shape, 1)
    return jnp.where(lane < heads, soft, 0.0), sig, ratio


def greet(seq_peers, head_peers, corners=False):
    barrier = pltpu.get_barrier_semaphore()
    count = 0
    if seq_peers > 1:
        me = lax.axis_index("seq")

        @pl.loop(1, seq_peers)
        def _(i):
            pl.semaphore_signal(
                barrier, inc=1, device_id={"seq": lax.rem(me + i, seq_peers)}, device_id_type=MESH
            )

        count += seq_peers - 1
    if head_peers > 1:
        mine = lax.axis_index("head")

        @pl.loop(1, head_peers)
        def _(i):
            pl.semaphore_signal(
                barrier, inc=1, device_id={"head": lax.rem(mine + i, head_peers)}, device_id_type=MESH
            )

        count += head_peers - 1
    if corners and head_peers > 1:
        me, mine = lax.axis_index("seq"), lax.axis_index("head")
        for side in (1, seq_peers - 1):

            @pl.loop(1, head_peers)
            def _(i):
                where = {"seq": lax.rem(me + side, seq_peers), "head": lax.rem(mine + i, head_peers)}
                pl.semaphore_signal(barrier, inc=1, device_id=where, device_id_type=MESH)

        count += 2 * (head_peers - 1)
    pl.semaphore_wait(barrier, count)


def remote(src, dst, send_sem, recv_sem, where):
    return pltpu.make_async_remote_copy(
        src_ref=src, dst_ref=dst, send_sem=send_sem, recv_sem=recv_sem, device_id=where, device_id_type=MESH
    )


class Line:
    def __init__(self, count, out, width, send, recv):
        self.count, self.out, self.width, self.send, self.recv = count, out, width, send, recv
        self.me = lax.axis_index("head")

    def view(self, shard):
        return self.out.at[:, pl.ds(pl.multiple_of(shard * self.width, LANES), self.width)]

    def copy(self, src, shard, way, step):
        return remote(
            src, self.view(shard), self.send.at[way, step], self.recv.at[shard], {"head": self.me + (1 - 2 * way)}
        )

    def first(self, own):
        self.pass_on(own, self.me, 0, 0)
        self.pass_on(own, self.me, 1, 0)

    def pass_on(self, src, shard, way, step):
        reach = (self.me < self.count - 1) if way == 0 else (self.me > 0)

        @pl.when(reach)
        def _():
            self.copy(src, shard, way, step).start()

    def hop(self, step, take=True, give=True, source=None):
        for way in (0, 1):
            shard = self.me - step if way == 0 else self.me + step
            there = (shard >= 0) if way == 0 else (shard < self.count)

            @pl.when(there)
            def _():
                if take:
                    self.copy(self.view(shard), shard, way, step).wait_recv()
                if give and step < self.count - 1:
                    self.pass_on(self.view(shard) if source is None else source(shard), shard, way, step)

    def finish(self, own, steps=None):
        for way in (0, 1):
            reach = (self.me < self.count - 1) if way == 0 else (self.me > 0)
            for step in range(self.count - 1) if steps is None else steps:
                shard = self.me - step if way == 0 else self.me + step
                there = (shard >= 0) if way == 0 else (shard < self.count)

                @pl.when(reach & there)
                def _():
                    src = own if step == 0 else self.view(shard)
                    self.copy(src, shard, way, step).wait_send()


class Plane:
    def __init__(self, seqs, view, sent, got, passed, way=0):
        self.chips, self.view, self.sent, self.got, self.passed, self.way = seqs // 2, view, sent, got, passed, way
        self.me = lax.axis_index("seq")
        self.core = lax.rem(self.me, 2)
        self.chip = self.me // 2
        self.mate = self.me + 1 - 2 * self.core

    def forward(self, chip):
        return (chip > self.chip) if self.way == 1 else (chip < self.chip) if self.way == -1 else (chip >= 0)

    def backward(self, chip):
        return (chip < self.chip) if self.way == 1 else (chip > self.chip) if self.way == -1 else (chip >= 0)

    def each_chip(self, body):
        @pl.loop(1, self.chips)
        def _(i):
            body(lax.rem(self.chip + i, self.chips))

    def copy(self, src, source, to, sem):
        return remote(src, self.view(source), sem, self.got.at[source], {"seq": to})

    def start(self, own):
        def send(chip):
            to = 2 * chip + self.core

            @pl.when(self.forward(chip))
            def _():
                self.copy(own, self.me, to, self.sent.at[to]).start()

        self.each_chip(send)
        self.copy(own, self.me, self.mate, self.sent.at[self.mate]).start()

    def relay(self):
        def take(chip):
            source = 2 * chip + self.core

            @pl.when(self.backward(chip))
            def _():
                landed = self.view(source)
                self.copy(landed, source, self.mate, self.passed.at[source]).wait_recv()
                self.copy(landed, source, self.mate, self.passed.at[source]).start()

        self.each_chip(take)

    def finish(self, own):
        def take(chip):
            source = 2 * chip + 1 - self.core

            @pl.when(self.backward(chip))
            def _():
                self.copy(self.view(source), source, self.mate, self.passed.at[source]).wait_recv()

        self.each_chip(take)
        self.copy(self.view(self.mate), self.mate, self.mate, self.sent.at[self.mate]).wait_recv()
        self.copy(own, self.me, self.mate, self.sent.at[self.mate]).wait_send()

        def drain(chip):
            same = 2 * chip + self.core

            @pl.when(self.forward(chip))
            def _():
                self.copy(own, self.me, same, self.sent.at[same]).wait_send()

            @pl.when(self.backward(chip))
            def _():
                self.copy(self.view(same), same, self.mate, self.passed.at[same]).wait_send()

        self.each_chip(drain)


ANY_SPEC = pl.BlockSpec(memory_space=pl.ANY)
VMEM_SPEC = pl.BlockSpec(memory_space=VMEM)
SMEM_SPEC = pl.BlockSpec(memory_space=SMEM)


def index_kernel(
    seqs, tiles, place, lengths, stepbias, decays, through, give_in, take_in, give_out, take_out, flags, vec
):
    me = lax.axis_index("seq")

    @pl.loop(0, seqs * tiles)
    def _(j):
        block = place[j]

        @pl.when(lax.div(block, tiles) == me)
        def _():
            to = lax.div(j, tiles)
            give_in[to] = lax.rem(block, tiles)
            take_out[lax.rem(block, tiles)] = to

    @pl.loop(0, tiles)
    def _(k):
        source = lax.div(place[me * tiles + k], tiles)
        take_in[k] = source
        give_out[source] = k

    @pl.loop(0, tiles + 1)
    def _(k):
        position = (me * tiles + k) * BLOCK
        end = jnp.int32(0)
        border = position == 0
        for n in range(lengths.shape[0]):
            end = end + lengths[n]
            border = border | (position == end)
        flags[k] = jnp.where(border, 0.0, 1.0)

    heads = stepbias.shape[1]
    vec[...] = jnp.zeros_like(vec)
    vec[0:1, :heads] = stepbias[...]
    vec[1:2, :heads] = decays[...]
    vec[2:3, :heads] = through[...]


def index(place, lengths, stepbias, decays, through, tiles):
    seqs = lax.axis_size("seq")
    whole = jnp.int32
    return pl.pallas_call(
        functools.partial(index_kernel, seqs, tiles),
        out_shape=(
            shape((seqs,), whole), shape((tiles,), whole), shape((seqs,), whole), shape((tiles,), whole),
            shape((tiles + 1,), WIDE), shape((EDGE, LANES), WIDE),
        ),
        in_specs=[SMEM_SPEC] * 2 + [VMEM_SPEC] * 3,
        out_specs=(SMEM_SPEC,) * 5 + (VMEM_SPEC,),
        compiler_params=pltpu.CompilerParams(vmem_limit_bytes=VMEM_LIMIT),
        name="index",
    )(place, lengths, stepbias[None, :], decays[None, :], through[None, :])


def blockwise(dims, index):
    return pl.BlockSpec(dims, index)


def fixed(dims):
    return pl.BlockSpec(dims, lambda i: (0,) * len(dims), pipeline_mode=pl.Buffered(1))


def carry_columns(carry_row_t, collect):
    high, middle, low = thirds(jnp.broadcast_to(carry_row_t, (LANES, LANES)))
    return nn(collect, high) + (nn(collect, middle) + nn(collect, low))


def pair_lanes(slab):
    lane = lax.broadcasted_iota(jnp.int32, slab.shape, 1)
    zero = jnp.zeros_like(slab)
    return jnp.where(lane < HDIM, slab, zero), jnp.where(lane >= HDIM, slab, zero)


def fold_states(slots, collect, inner, first, last, step, start):
    def hop(n, state):
        message = slots[first + n * step]
        carry = nn(collect[:, :HALO], message[inner:])
        return carry * state + message[:inner].astype(WIDE)

    return lax.fori_loop(0, (last - first) * step, hop, start)


def front_kernel(
    seqs, line, heads, blocks, chunks, give, take, flags,
    x_in, g_in, gating_in, payload_in, address_in, stepping_in, readout_in,
    vec, prenorm, kernels, filters, offsets, shifts,
    u_o, normed_o, gate_o, pre_o, conv_o, act_o, raw_o, cum_o, part_o, local_o, state_o, rim_o, g_o, w_o, r_o,
    x, g, gating, payload, address, stepping, readout, square,
    send_x, send_g, recv_x, recv_g, work_x, work_g, w_own, r_own, u, w, msg, slots,
    ext, prev, state, prod,
    sent, got, w_sent, w_got, w_passed, r_sent, r_got, r_passed, s_sent, s_got, s_passed, rim_sent, rim_got, own_sem,
    load_sem, line_sent, line_got, g_sent, g_got,
):
    i = pl.program_id(0)
    me, mine = lax.axis_index("seq"), lax.axis_index("head")
    tiles, _, width = x.shape
    rows = tiles * BLOCK
    depth, inner = gating.shape
    wide = pre_o.shape[1]
    part = rows // chunks
    per = blocks // chunks

    def rows_of(device):
        return pl.ds(pl.multiple_of(device * depth, depth), depth)

    def piece(n):
        if isinstance(n, int):
            return pl.ds(n * part, part)
        return pl.ds(pl.multiple_of(n * part, part), part)

    def u_line(n):
        return Line(line, u.at[piece(n)], width, line_sent.at[n], line_got.at[n])

    def own_columns(ref):
        return ref.at[:, pl.ds(pl.multiple_of(mine * width, LANES), width)]

    w_plane = Plane(seqs, lambda s: w.at[rows_of(s)], w_sent, w_got, w_passed)
    r_plane = Plane(seqs, lambda s: r_o.at[rows_of(s)], r_sent, r_got, r_passed)
    s_plane = Plane(seqs, lambda s: slots.at[s], s_sent, s_got, s_passed, way=1)
    g_line = Line(line, g_o, width, g_sent, g_got)
    own_r = pltpu.make_async_copy(r_own, r_o.at[rows_of(me)], own_sem.at[0])
    own_g = pltpu.make_async_copy(work_g, g_line.view(mine), own_sem.at[1])
    save_w = pltpu.make_async_copy(w, w_o, own_sem.at[2])

    def rim_copy(to, shard):
        columns = pl.ds(pl.multiple_of(shard * width, LANES), width)
        return remote(
            work_x.at[pl.ds(rows - HALO, HALO)], u.at[pl.ds(rows, HALO), columns], rim_sent.at[to], rim_got.at[shard],
            {"seq": lax.rem(me + 1, seqs), "head": to},
        )

    def arrange(which, received, work):
        @pl.loop(1, seqs)
        def _(n):
            source = lax.rem(me + n, seqs)
            remote(
                received.at[source], received.at[source], sent.at[which, source], got.at[which, source], {"seq": source}
            ).wait_recv()

        for k in range(tiles):
            work[pl.ds(k * BLOCK, BLOCK), :] = received[take[k]]

    @pl.when(i == 0)
    def _():
        pairs = (
            (x_in, x), (g_in, g), (gating_in, gating), (payload_in, payload), (address_in, address),
            (stepping_in, stepping), (readout_in, readout),
        )
        loads = [pltpu.make_async_copy(src, dst, load_sem.at[n]) for n, (src, dst) in enumerate(pairs)]
        for load in loads:
            load.start()
        greet(seqs, line, corners=True)

        def post(which, source, outgoing, incoming):
            @pl.loop(1, seqs)
            def _(n):
                to = lax.rem(me + n, seqs)
                outgoing[to] = source[give[to]]
                remote(outgoing.at[to], incoming.at[me], sent.at[which, to], got.at[which, me], {"seq": to}).start()

            incoming[me] = source[give[me]]

        loads[0].wait()
        post(0, x, send_x, recv_x)
        for load in loads[1:]:
            load.wait()

        w_own[:, :inner] = gating[...].astype(LOW)
        w_own[:, inner : 2 * inner] = payload[...].astype(LOW)
        state2 = address.shape[1]
        w_own[:, 2 * inner : 2 * inner + state2] = address[...].astype(LOW)
        square[...] = jnp.zeros_like(square)
        square[: stepping.shape[0], :depth] = stepping[...]
        w_own[:, 2 * inner + state2 :] = square[...].T[:depth].astype(LOW)
        r_own[...] = readout[...].T.astype(LOW)
        w[rows_of(me), :] = w_own[...]
        own_r.start()

        arrange(0, recv_x, work_x)

        @pl.loop(0, line)
        def _(n):
            rim_copy(lax.rem(mine + n, line), mine).start()

        for n in range(chunks):
            u_line(n).first(work_x.at[piece(n)])
        w_plane.start(w_own)
        own = pltpu.make_async_copy(work_x, own_columns(u.at[pl.ds(0, rows)]), own_sem.at[3])
        own.start()
        post(1, g, send_g, recv_g)
        r_plane.start(r_own)
        for step in range(1, line - 1):
            for n in range(chunks):
                u_line(n).hop(step)
            if step == 1:
                w_plane.relay()
        own.wait()

        @pl.loop(0, line)
        def _(n):
            rim_copy(n, n).wait_recv()

        w_plane.finish(w_own)
        save_w.start()

    if line > 1:

        @pl.when(lax.rem(i, per) == 0)
        def _():
            u_line(lax.div(i, per)).hop(line - 1)

    @pl.when(i == blocks - 1)
    def _():
        arrange(1, recv_g, work_g)
        g_line.first(work_g)
        own_g.start()

    taps = jnp.concatenate([kernels[...], filters[...]], axis=1)
    bias = jnp.concatenate([offsets[...], shifts[...]], axis=1)
    spread_m, collect = head_rows(inner), head_columns(inner)

    def normalize(block):
        wide_rows = block.astype(WIDE)
        scale = lax.rsqrt(jnp.mean(wide_rows * wide_rows, axis=1, keepdims=True) + EPS)
        return (wide_rows * scale * prenorm[...]).astype(LOW)

    @pl.when(i == 0)
    def _():
        before = nn(normalize(u[pl.ds(rows, HALO), :]), w[:, inner : inner + wide]).astype(LOW).astype(WIDE)
        prev[...] = before[HALO - EDGE :]
        rim_o[...] = before[HALO - EDGE :]
        state[...] = jnp.zeros_like(state)
        prod[...] = jnp.ones_like(prod)

    u_v = u[pl.ds(pl.multiple_of(i * GROUP, GROUP), GROUP), :]
    u_o[...] = u_v
    normed = normalize(u_v)
    normed_o[...] = normed
    gate_o[...] = nn(normed, w[:, :inner])
    pre = nn(normed, w[:, inner : inner + wide]).astype(LOW)
    pre_o[...] = pre
    lane = lax.broadcasted_iota(jnp.int32, (GROUP, LANES), 1)
    raw = jnp.where(lane < heads, nn(normed, w[:, inner + wide :]) + vec[0:1, :], 0.0)
    raw_o[...] = raw
    first, second = flags[2 * i], flags[2 * i + 1]
    same = (first, second)
    for half in range(2):
        at = pl.ds(half * BLOCK, BLOCK)
        ext[0:EDGE, :] = prev[...] * same[half]
        ext[EDGE:, :] = pre[half * BLOCK : (half + 1) * BLOCK].astype(WIDE)
        prev[...] = ext[BLOCK:, :]
        total = bias + taps[TAPS - 1 : TAPS] * ext[EDGE:, :]
        for tap in range(TAPS - 1):
            total = total + taps[tap : tap + 1] * ext[pl.ds(EDGE - (TAPS - 1) + tap, BLOCK), :]
        conv_o[at, :] = total
        act_o[at, :] = (total * sigmoid(total)).astype(LOW)

    steps, _, _ = step_terms(raw, heads)
    scale = -jnp.exp(vec[1:2, :])
    cum = sum_before(steps * scale)
    cum_o[...] = cum
    cum_t, steps_t = cum.T, steps.T
    write = act_o[:, inner : inner + STATE]
    read = act_o[:, inner + STATE :]
    lower = ones_before(BLOCK)
    top, low = slice(0, BLOCK), slice(BLOCK, GROUP)
    s00 = jnp.where(lower, nt(read[top], write[top]), 0.0)
    s10 = nt(read[low], write[top]) * second
    s11 = jnp.where(lower, nt(read[low], write[low]), 0.0)

    def mix(scores, head, t, s):
        decay = jnp.exp(jnp.minimum(cum[t, head : head + 1] - cum_t[head : head + 1, s], 0.0))
        return (scores * (decay * steps_t[head : head + 1, s])).astype(LOW)

    last = cum[GROUP - 1 : GROUP, :]
    row = lax.broadcasted_iota(jnp.int32, (GROUP, LANES), 0)
    weight = steps * jnp.exp(last - cum) * jnp.where(row < BLOCK, second, 1.0)
    weight_w = to_columns(weight, spread_m)
    skip = to_columns(jnp.broadcast_to(vec[2:3, :], (EDGE, LANES)), spread_m)[0:1]
    packed = []
    for pair in range(inner // LANES):
        columns = slice(pair * LANES, (pair + 1) * LANES)
        slab = act_o[:, columns]
        slab_f = slab.astype(WIDE)
        ones = pair_lanes(slab)
        h0, h1 = 2 * pair, 2 * pair + 1
        y0 = nn(
            jnp.concatenate([mix(s00, h0, top, top), mix(s00, h1, top, top)], axis=1),
            jnp.concatenate([ones[0][top], ones[1][top]], axis=0),
        )
        y1 = nn(
            jnp.concatenate(
                [mix(s10, h0, low, top), mix(s11, h0, low, low), mix(s10, h1, low, top), mix(s11, h1, low, low)], axis=1
            ),
            jnp.concatenate([ones[0], ones[1]], axis=0),
        )
        part_o[top, columns] = y0 + skip[:, columns] * slab_f[top]
        part_o[low, columns] = y1 + skip[:, columns] * slab_f[low]
        packed.append((slab_f * weight_w[:, columns]).astype(LOW))
    local = tn(jnp.concatenate(packed, axis=1), write)
    local_o[0] = local
    carry = jnp.exp(cum_t[:, GROUP - 1 : GROUP]) * (first * second)
    state[...] = carry_columns(carry, collect) * state[...] + local
    prod[...] = jnp.broadcast_to(carry[:HALO], (HALO, STATE)) * prod[...]

    @pl.when(i == blocks - 1)
    def _():
        msg[:inner, :] = state[...].astype(LOW)
        msg[inner:, :] = prod[...].astype(LOW)
        s_plane.start(msg)
        s_plane.relay()
        s_plane.finish(msg)
        state_o[...] = fold_states(slots, collect, inner, 0, me, 1, jnp.zeros((inner, STATE), WIDE))
        r_plane.relay()
        r_plane.finish(r_own)
        if line > 1:
            g_line.hop(1, give=False)
        g_line.finish(work_g, (0,))
        for n in range(chunks):
            u_line(n).finish(work_x.at[piece(n)])

        @pl.loop(0, line)
        def _(n):
            rim_copy(n, mine).wait_send()


        @pl.loop(1, seqs)
        def _(n):
            other = lax.rem(me + n, seqs)
            for which, buffer in ((0, send_x), (1, send_g)):
                remote(
                    buffer.at[other], buffer.at[other], sent.at[which, other], got.at[which, other], {"seq": other}
                ).wait_send()

        own_r.wait()
        own_g.wait()
        save_w.wait()


def front(give, take, flags, x, g, gating, payload, address, stepping, readout, vec, prenorm, kernels, filters, offsets, shifts):
    seqs, line = lax.axis_size("seq"), lax.axis_size("head")
    rows, width = x.shape
    depth, inner = gating.shape
    total = depth * seqs
    wide = inner + address.shape[1]
    columns = inner + wide + LANES
    blocks = rows // GROUP
    chunks = min(blocks, 4)
    heads = stepping.shape[1]
    routed = (seqs, BLOCK, width)
    given = (rows // BLOCK, BLOCK, width)
    message = (inner + HALO, STATE)
    operands = (x.reshape(given), g.reshape(given), gating, payload, address, stepping.T, readout)
    small = (vec, prenorm, kernels, filters, offsets, shifts)

    def by_rows(size):
        return blockwise((GROUP, size), lambda i: (i, 0))

    return pl.pallas_call(
        functools.partial(front_kernel, seqs, line, heads, blocks, chunks),
        grid=(blocks,),
        out_shape=(
            shape((rows, total), LOW), shape((rows, total), LOW), shape((rows, inner), WIDE), shape((rows, wide), LOW),
            shape((rows, wide), WIDE), shape((rows, wide), LOW), shape((rows, LANES), WIDE), shape((rows, LANES), WIDE),
            shape((rows, inner), WIDE), shape((blocks, inner, STATE), WIDE), shape((inner, STATE), WIDE),
            shape((EDGE, wide), WIDE), shape((rows, total), LOW), shape((total, columns), LOW),
            shape((total, inner), LOW),
        ),
        in_specs=[SMEM_SPEC] * 3 + [ANY_SPEC] * 7 + [fixed(a.shape) for a in small],
        out_specs=(
            by_rows(total), by_rows(total), by_rows(inner), by_rows(wide), by_rows(wide), by_rows(wide), by_rows(LANES),
            by_rows(LANES), by_rows(inner), blockwise((1, inner, STATE), lambda i: (i, 0, 0)), fixed((inner, STATE)),
            fixed((EDGE, wide)), ANY_SPEC, ANY_SPEC, ANY_SPEC,
        ),
        scratch_shapes=[pltpu.VMEM(a.shape, a.dtype) for a in operands] + [
            pltpu.VMEM((LANES, LANES), WIDE),
            pltpu.VMEM(routed, LOW), pltpu.VMEM(routed, LOW), pltpu.VMEM(routed, LOW), pltpu.VMEM(routed, LOW),
            pltpu.VMEM((rows, width), LOW), pltpu.VMEM((rows, width), LOW),
            pltpu.VMEM((depth, columns), LOW), pltpu.VMEM((depth, inner), LOW),
            pltpu.VMEM((rows + HALO, total), LOW), pltpu.VMEM((total, columns), LOW),
            pltpu.VMEM(message, LOW), pltpu.VMEM((seqs,) + message, LOW),
            pltpu.VMEM((EDGE + BLOCK, wide), WIDE), pltpu.VMEM((EDGE, wide), WIDE),
            pltpu.VMEM((inner, STATE), WIDE), pltpu.VMEM((HALO, STATE), WIDE),
            DMA((2, seqs)), DMA((2, seqs)),
            DMA((seqs,)), DMA((seqs,)), DMA((seqs,)), DMA((seqs,)), DMA((seqs,)), DMA((seqs,)),
            DMA((seqs,)), DMA((seqs,)), DMA((seqs,)), DMA((line,)), DMA((line,)), DMA((4,)), DMA((7,)),
            DMA((chunks, 2, line)), DMA((chunks, line)), DMA((2, line)), DMA((line,)),
        ],
        compiler_params=pltpu.CompilerParams(
            collective_id=0, has_side_effects=True, vmem_limit_bytes=VMEM_LIMIT, dimension_semantics=("arbitrary",)
        ),
        name="front",
    )(give, take, flags, *operands, *small)


def conv_grad(d_act, conv):
    sig = sigmoid(conv)
    return d_act * (sig * (1.0 + conv * (1.0 - sig)))


class Stream:
    def __init__(self, view, slots, sems):
        self.view, self.slots, self.sems = view, slots, sems

    def copy(self, block, turn):
        slot = lax.rem(turn, 2)
        return pltpu.make_async_copy(self.view(block), self.slots.at[slot], self.sems.at[slot])

    def start(self, block, turn):
        self.copy(block, turn).start()

    def wait(self, block, turn):
        self.copy(block, turn).wait()

    def at(self, turn):
        return self.slots.at[lax.rem(turn, 2)]


class Fold:
    def __init__(self, line, part, got, relay, sent, arrived, relayed):
        self.line, self.part, self.got, self.relay = line, part, got, relay
        self.sent, self.arrived, self.relayed = sent, arrived, relayed
        self.mine = mine = lax.axis_index("head")
        self.merges = line == 4
        low = mine < 2
        self.is_end = (mine == 0) | (mine == line - 1)
        self.end, self.mid = jnp.where(low, 0, 3), jnp.where(low, 1, 2)
        self.next, self.far = jnp.where(low, 2, 1), jnp.where(low, 3, 0)

    def others(self, body):
        @pl.loop(1, self.line)
        def _(n):
            body(lax.rem(self.mine + n, self.line))

    def chunk(self, rows, piece, chunk, to, way):
        return remote(
            self.part(chunk, rows), self.got.at[self.mine, rows], self.sent.at[way, piece],
            self.arrived.at[self.mine, piece], {"head": to},
        )

    def hand(self, rows, piece, chunk, which):
        return remote(
            self.part(chunk, rows), self.relay.at[which, rows], self.sent.at[1 + which, piece],
            self.relayed.at[which, piece], {"head": self.mid},
        )

    def landed(self, rows, piece, source):
        slot = self.got.at[source, rows]
        return remote(slot, slot, self.sent.at[0, piece], self.arrived.at[source, piece], {"head": source})

    def send(self, rows, piece):
        if not self.merges:
            if self.line > 1:
                self.others(lambda to: self.chunk(rows, piece, to, to, to).start())
            return

        @pl.when(self.is_end)
        def _():
            self.hand(rows, piece, self.far, 1).start()
            self.hand(rows, piece, self.next, 0).start()
            self.chunk(rows, piece, self.mid, self.mid, 0).start()

        @pl.when(jnp.logical_not(self.is_end))
        def _():
            self.chunk(rows, piece, self.end, self.end, 0).start()

    def merge(self, rows, piece):
        if self.merges:

            @pl.when(jnp.logical_not(self.is_end))
            def _():
                for which, chunk in ((1, self.far), (0, self.next)):
                    self.hand(rows, piece, chunk, which).wait_recv()
                    own = self.part(chunk, rows)
                    own[...] = (own[...].astype(WIDE) + self.relay[which, rows].astype(WIDE)).astype(LOW)
                    self.chunk(rows, piece, chunk, chunk, 1 + which).start()

    def drain(self, rows, piece):
        if not self.merges:
            if self.line > 1:
                self.others(lambda to: self.chunk(rows, piece, to, to, to).wait_send())
                self.others(lambda source: self.landed(rows, piece, source).wait_recv())
            return
        for way in range(3):
            self.chunk(rows, piece, self.mid, self.mid, way).wait_send()
        for source in (jnp.where(self.is_end, self.mid, self.end), self.next):
            self.landed(rows, piece, source).wait_recv()

    def total(self, rows, ref):
        sum_ = self.part(self.mine, rows)[...].astype(WIDE)
        if self.merges:
            first = jnp.where(self.is_end, self.mid, self.end)
            return sum_ + ref[first, rows].astype(WIDE) + ref[self.next, rows].astype(WIDE)
        for n in range(1, self.line):
            sum_ = sum_ + ref[lax.rem(self.mine + n, self.line), rows].astype(WIDE)
        return sum_


def core_kernel(
    seqs, line, heads, blocks, roomy, flags, give,
    gate_in, part_in, act_in, cum_in, raw_in, local_in, conv_in, pre_in, normed_in, u_in, g_part, r_in, w_in,
    state_in, postnorm, vec, prenorm, kernels, filters, rim,
    out_recv, grad_recv, out_far, dx_far, gread_got, ggate_got, dw_got, addr_got, small_got,
    gate_b, part_b, read_b, cum_b, local_b, normed_b, act_b, raw_b, conv_b, pre_b, before_b, u_b, stream_sems,
    r_t, w, ssd_s, din_s, dssd_s, dgate_s, ds_s, starts, q, state, prod, g_buf, out_part, back_slots, back_msg,
    relay, dx_relay, out_near, dx_near, sums,
    totals, gread, ggate, gread_low, ggate_low, gpost, tiny, d_conv, d_step, after, edge_own, edge_got, ext,
    keep_conv, keep_step, keep_normed, keep_u,
    taps_g, bias_g, dw, dw_low, da_low, da_got, da_send, pn, zs_send, zs_got, small, result, fin_send,
    back_sent, back_sem, back_passed, sum_sent, sum_sem, line_sent, line_sem, load_sem, out_sent, out_sem, out_relayed,
    w_sent, w_sem, dx_sent, dx_sem, dx_relayed, edge_sent, edge_sem, zs_sent, zs_sem, da_sent, da_sem, small_sent,
    small_sem, fin_sent, fin_sem, own_sem, weight_sem,
):
    me, mine = lax.axis_index("seq"), lax.axis_index("head")
    inner = r_t.shape[1]
    wide = act_b.shape[2]
    width = out_part.shape[2]
    depth = gread_got.shape[1]
    rows = ssd_s.shape[0]
    size = 2 * STATE // line
    g_line = Line(line, g_buf, width, line_sent, line_sem)
    back_plane = Plane(seqs, lambda s: back_slots.at[s], back_sent, back_sem, back_passed, way=-1)
    out_got, dx_got = (out_near, dx_near) if roomy else (out_far, dx_far)

    def group_rows(b):
        return pl.ds(pl.multiple_of(b * GROUP, GROUP), GROUP)

    def rows_of(device):
        return pl.ds(pl.multiple_of(device * depth, depth), depth)

    def shard_of(ref, shard):
        return ref.at[:, pl.ds(pl.multiple_of(shard * width, LANES), width)]

    def by_group(ref, first=0, columns=None):
        if columns is None:
            return lambda b: ref.at[group_rows(b)]
        return lambda b: ref.at[group_rows(b), pl.ds(first, columns)]

    def all_line(body):
        if line > 1:

            @pl.loop(1, line)
            def _(n):
                body(lax.rem(mine + n, line))

    def all_seq(body):
        @pl.loop(1, seqs)
        def _(n):
            body(lax.rem(me + n, seqs))

    def before_rows(b):
        start = jnp.maximum(b * GROUP - HALO, 0)
        return pre_in.at[pl.ds(pl.multiple_of(start, HALO), HALO)]

    views = (
        (by_group(gate_in), gate_b), (by_group(part_in), part_b), (by_group(act_in, inner + STATE, STATE), read_b),
        (by_group(cum_in), cum_b), (lambda b: local_in.at[b], local_b), (by_group(normed_in), normed_b),
        (by_group(act_in), act_b), (by_group(raw_in), raw_b), (by_group(conv_in), conv_b), (by_group(pre_in), pre_b),
        (before_rows, before_b), (by_group(u_in), u_b),
    )
    gate_f, part_f, read_f, cum_f, local_f, normed_f, act_f, raw_f, conv_f, pre_f, before_f, u_f = [
        Stream(view, slots, stream_sems.at[n]) for n, (view, slots) in enumerate(views)
    ]

    def forwards(turn):
        return turn

    def backwards(turn):
        return blocks - 1 - turn

    def begin(streams, order):
        for stream in streams:
            stream.start(order(0), 0)

    def step(streams, order, turn, following):
        @pl.when(turn + 1 < blocks)
        def _():
            for stream in streams:
                stream.start(order(turn + 1), turn + 1)

        if following is not None:
            pl.when(turn + 1 == blocks)(lambda: begin(*following))
        for stream in streams:
            stream.wait(order(turn), turn)

    first_phase = ((gate_f, part_f, read_f, cum_f, local_f), forwards)
    norm_phase = ((gate_f,), forwards)
    gate_phase = ((gate_f, normed_f, read_f, cum_f), forwards)
    scan_phase = ((act_f, cum_f, raw_f), forwards)
    last_phase = ((act_f, cum_f, raw_f, conv_f, pre_f, before_f, normed_f, u_f), backwards)

    def each_load(body):
        def load(shard, n):
            return pltpu.make_async_copy(shard_of(g_part, shard), shard_of(g_buf, shard), load_sem.at[n])

        body(load(mine, 0))
        if line > 1:
            pl.when(mine > 0)(lambda: body(load(mine - 1, 1)))
            pl.when(mine < line - 1)(lambda: body(load(mine + 1, 2)))

    def sum_copy(to, slot):
        return remote(sums.at[mine], sums.at[slot], sum_sent.at[to], sum_sem.at[slot], {"head": to})

    weights = ((gread_low, gread_got), (ggate_low, ggate_got), (dw_low, dw_got), (da_low, da_got))

    def w_copy(which, to, slot):
        src, dst = weights[which]
        return remote(src.at[rows_of(to)], dst.at[slot], w_sent.at[which, to], w_sem.at[which, slot], {"seq": to})

    def w_start(which):
        all_seq(lambda to: w_copy(which, to, me).start())

    def w_wait(which):
        all_seq(lambda other: w_copy(which, other, other).wait())

    out_fold = Fold(
        line, lambda z, at: out_part.at[z, at], out_got, relay, out_sent, out_sem, out_relayed
    )
    dx_fold = Fold(
        line, lambda z, at: shard_of(g_buf.at[at], z), dx_got, dx_relay, dx_sent, dx_sem, dx_relayed
    )
    short_piece = (pl.ds(rows - GROUP, GROUP - HALO), blocks - 1)
    edge_piece = (pl.ds(rows - HALO, HALO), blocks)

    def each_piece(body):
        body(*short_piece)

        @pl.loop(1, blocks)
        def _(turn):
            b = blocks - 1 - turn
            body(group_rows(b), b)

        body(*edge_piece)

    def edge_copy(to):
        return remote(edge_own, edge_got, edge_sent, edge_sem, {"seq": to})

    def zs_copy(to, slot):
        return remote(zs_send.at[to], zs_got.at[slot], zs_sent.at[to], zs_sem.at[slot], {"head": to})

    def da_copy(to, slot):
        return remote(da_send.at[to], addr_got.at[slot], da_sent.at[to], da_sem.at[slot], {"head": to})

    def small_copy(to, slot):
        return remote(small, small_got.at[slot], small_sent.at[to], small_sem.at[slot], {"seq": to})

    arrivals = (out_recv, grad_recv)

    def fin_copy(which, to, slot):
        return remote(
            fin_send.at[which, to], arrivals[which].at[slot], fin_sent.at[which, to], fin_sem.at[which, slot],
            {"seq": to},
        )

    own_copies = {
        "gread": pltpu.make_async_copy(gread_low.at[rows_of(me)], gread_got.at[me], own_sem.at[0]),
        "ggate": pltpu.make_async_copy(ggate_low.at[rows_of(me)], ggate_got.at[me], own_sem.at[1]),
        "dw": pltpu.make_async_copy(dw_low.at[rows_of(me)], dw_got.at[me], own_sem.at[2]),
        "addr": pltpu.make_async_copy(da_send.at[mine], addr_got.at[mine], own_sem.at[3]),
        "small": pltpu.make_async_copy(small, small_got.at[me], own_sem.at[4]),
        "fin0": pltpu.make_async_copy(fin_send.at[0, me], out_recv.at[me], own_sem.at[5]),
        "fin1": pltpu.make_async_copy(fin_send.at[1, me], grad_recv.at[me], own_sem.at[6]),
    }

    def route(which):
        def send(to):
            fin_send[which, to] = result[which, give[to]]
            fin_copy(which, to, me).start()

        all_seq(send)
        fin_send[which, me] = result[which, give[me]]
        own_copies["fin%d" % which].start()

    def fetch(src):
        if not roomy:
            all_line(lambda z: pltpu.make_async_copy(src.at[z], out_part.at[z], load_sem.at[0]).start())
            all_line(lambda z: pltpu.make_async_copy(src.at[z], out_part.at[z], load_sem.at[0]).wait())

    row = lax.broadcasted_iota(jnp.int32, (GROUP, LANES), 0)
    lane = lax.broadcasted_iota(jnp.int32, (GROUP, LANES), 1)
    spread_m, collect = head_rows(inner), head_columns(inner)
    lower_mask = ones_before(BLOCK)
    top, low = slice(0, BLOCK), slice(BLOCK, GROUP)

    def entry_of(b, cum_v):
        gone_on = flags[2 * b] * jnp.where(row < BLOCK, 1.0, flags[2 * b + 1])
        return to_columns(jnp.exp(cum_v) * gone_on, spread_m)

    def carry_of(b, cum_t):
        return jnp.exp(cum_t[:, GROUP - 1 : GROUP]) * (flags[2 * b] * flags[2 * b + 1])

    def row_stats(b):
        stats = jnp.concatenate([totals[b], jnp.zeros((LANES - EDGE, GROUP), WIDE)], axis=0).T
        return lax.rsqrt(stats[:, 0:1] / INNER + EPS), stats[:, 1:2]

    def gated_of(ssd, turn):
        gate_v = gate_f.at(turn)[...]
        return ssd * (gate_v * sigmoid(gate_v))

    begin(*first_phase)
    fetch_r = pltpu.make_async_copy(r_in, r_t, weight_sem.at[0])
    fetch_w = pltpu.make_async_copy(w_in, w, weight_sem.at[1])
    fetch_r.start()
    greet(seqs, line)
    g_line.hop(1, take=False, source=lambda shard: shard_of(g_part, shard))
    each_load(lambda copy: copy.start())
    fetch_w.start()
    state[...] = state_in[...]
    fetch_r.wait()

    @pl.loop(0, blocks)
    def _(b):
        step(*first_phase, b, norm_phase)
        here = group_rows(b)
        cum_v = cum_f.at(b)[...]
        start = state[...]
        starts[b] = start
        ssd = part_f.at(b)[...] + entry_of(b, cum_v) * nt(read_f.at(b)[...], start.astype(LOW))
        ssd_s[here, :] = ssd
        state[...] = carry_columns(carry_of(b, cum_v.T), collect) * start + local_f.at(b)[...]
        out = nt((gated_of(ssd, b) * postnorm[...]).astype(LOW), r_t[...])
        for z in range(line):
            out_part[z, here] = out[:, z * width : (z + 1) * width].astype(LOW)
        if out_fold.merges:
            pl.when(out_fold.is_end)(lambda: out_fold.send(here, b))

    for hop in range(2, line):
        g_line.hop(hop)
    each_load(lambda copy: copy.wait())
    g_line.finish(None, range(1, line - 1))
    fetch_w.wait()

    @pl.loop(0, blocks)
    def _(b):
        step(*norm_phase, b, gate_phase)
        here = group_rows(b)
        gated = gated_of(ssd_s[here, :], b)
        d_inner = nn(g_buf[here, :], r_t[...])
        din_s[here, :] = d_inner
        squares = jnp.sum(gated * gated, axis=1, keepdims=True)
        dots = jnp.sum(gated * postnorm[...] * d_inner, axis=1, keepdims=True)
        both = jnp.where(lane == 0, squares, jnp.where(lane == 1, dots, 0.0)).T
        sums[mine, b] = both[:EDGE]

    all_line(lambda to: sum_copy(to, mine).start())
    for ref in (gread, ggate, gpost, state, tiny, taps_g, bias_g, dw, pn):
        ref[...] = jnp.zeros_like(ref)
    prod[...] = jnp.ones_like(prod)
    all_line(lambda other: sum_copy(other, other).wait())
    totals[...] = jnp.sum(sums[...], axis=0)

    @pl.loop(0, blocks)
    def _(b):
        here = group_rows(b)
        if out_fold.merges:
            pl.when(jnp.logical_not(out_fold.is_end))(lambda: out_fold.send(here, b))
        else:
            out_fold.send(here, b)
        out_fold.merge(here, b)

    @pl.loop(0, blocks)
    def _(b):
        step(*gate_phase, b, scan_phase)
        here = group_rows(b)
        cum_v = cum_f.at(b)[...]
        inv, dot = row_stats(b)
        gate_v = gate_f.at(b)[...]
        sig = sigmoid(gate_v)
        ssd = ssd_s[here, :]
        d_inner = din_s[here, :]
        gated = ssd * (gate_v * sig)
        gated_inv = gated * inv
        inner_normed = (gated_inv * postnorm[...]).astype(LOW)
        d_gated = (inv * postnorm[...]) * d_inner - gated * (inv * inv * inv / INNER * dot)
        gpost[...] += jnp.sum(d_inner * gated_inv, axis=0, keepdims=True)
        d_ssd = (d_gated * (gate_v * sig)).astype(LOW)
        d_gate = (d_gated * ssd * sig * (1.0 + gate_v * (1.0 - sig))).astype(LOW)
        dssd_s[here, :] = d_ssd
        dgate_s[here, :] = d_gate
        gread[...] += tn(g_buf[here, :], inner_normed)
        ggate[...] += tn(normed_f.at(b)[...], d_gate)
        query_grad = (d_ssd.astype(WIDE) * entry_of(b, cum_v)).astype(LOW)
        found = tn(query_grad, read_f.at(b)[...])
        q[b] = found
        state[...] += carry_columns(prod[...], collect) * found
        prod[...] = prod[...] * carry_of(b, cum_v.T)

    back_msg[:inner, :] = state[...].astype(LOW)
    back_msg[inner:, :] = jnp.broadcast_to(prod[:HALO], (HALO, STATE)).astype(LOW)
    back_plane.start(back_msg)
    gread_low[...] = gread[...].astype(LOW)
    ggate_low[...] = ggate[...].astype(LOW)
    w_start(0)
    w_start(1)
    own_copies["gread"].start()
    own_copies["ggate"].start()

    @pl.loop(0, blocks)
    def _(b):
        step(*scan_phase, b, last_phase)
        here = group_rows(b)
        second = flags[2 * b + 1]
        act = act_f.at(b)
        cum_v = cum_f.at(b)[...]
        cum_t = cum_v.T
        steps, _, _ = step_terms(raw_f.at(b)[...], heads)
        steps_t = steps.T
        write = act[:, inner : inner + STATE]
        read_v = act[:, inner + STATE :]
        s00 = jnp.where(lower_mask, nt(read_v[top], write[top]), 0.0)
        s10 = nt(read_v[low], write[top]) * second
        s11 = jnp.where(lower_mask, nt(read_v[low], write[low]), 0.0)

        def decay_of(head, t, s):
            decay = jnp.exp(jnp.minimum(cum_v[t, head : head + 1] - cum_t[head : head + 1, s], 0.0))
            return decay * steps_t[head : head + 1, s]

        ds00 = jnp.zeros((BLOCK, BLOCK), WIDE)
        ds10 = jnp.zeros((BLOCK, BLOCK), WIDE)
        ds11 = jnp.zeros((BLOCK, BLOCK), WIDE)
        for pair in range(inner // LANES):
            columns = slice(pair * LANES, (pair + 1) * LANES)
            values = act[:, columns]
            dys = pair_lanes(dssd_s[here, columns])
            m00, m10, m11 = [], [], []
            for k in range(2):
                head = 2 * pair + k
                l00, l10, l11 = decay_of(head, top, top), decay_of(head, low, top), decay_of(head, low, low)
                m00.append((s00 * l00).astype(LOW))
                m10.append((s10 * l10).astype(LOW))
                m11.append((s11 * l11).astype(LOW))
                ds00 = ds00 + nt(dys[k][top], values[top]) * l00
                ds10 = ds10 + nt(dys[k][low], values[top]) * l10
                ds11 = ds11 + nt(dys[k][low], values[low]) * l11
            v0 = tn(
                jnp.concatenate([m00[0], m10[0], m00[1], m10[1]], axis=0), jnp.concatenate([dys[0], dys[1]], axis=0)
            )
            v1 = tn(
                jnp.concatenate([m11[0], m11[1]], axis=0), jnp.concatenate([dys[0][low], dys[1][low]], axis=0)
            )
            din_s[here, columns] = jnp.concatenate([v0, v1], axis=0)
        ds_s[here, :] = jnp.concatenate(
            [
                jnp.concatenate([jnp.where(lower_mask, ds00, 0.0), jnp.zeros((BLOCK, BLOCK), WIDE)], axis=1),
                jnp.concatenate([ds10 * second, jnp.where(lower_mask, ds11, 0.0)], axis=1),
            ],
            axis=0,
        ).astype(LOW)

        @pl.when(b == blocks // 2)
        def _():
            back_plane.relay()

    back_plane.finish(back_msg)
    state[...] = fold_states(back_slots, collect, inner, seqs - 1, me, -1, jnp.zeros((inner, STATE), WIDE))
    taps = jnp.concatenate([kernels[...], filters[...]], axis=1)
    scale = -jnp.exp(vec[1:2, :])
    through_w = to_columns(jnp.broadcast_to(vec[2:3, :], (EDGE, LANES)), spread_m)[0:1]

    def scan_back(b, turn):
        here = group_rows(b)
        first, second = flags[2 * b], flags[2 * b + 1]
        act, conv = act_f.at(turn), conv_f.at(turn)
        cum_v = cum_f.at(turn)[...]
        steps, sig, ratio = step_terms(raw_f.at(turn)[...], heads)
        last = cum_v[GROUP - 1 : GROUP, :]
        write = act[:, inner : inner + STATE]
        read_v = act[:, inner + STATE :]
        end = state[...]
        end_low = end.astype(LOW)
        start = starts[b]
        state[...] = carry_columns(carry_of(b, cum_v.T), collect) * end + q[b]
        weight = steps * jnp.exp(last - cum_v) * jnp.where(row < BLOCK, second, 1.0)
        weight_w = to_columns(weight, spread_m)
        d_ssd = dssd_s[here, :]
        dy_f = d_ssd.astype(WIDE)
        values_f = act[:, :inner].astype(WIDE)
        d_query = (dy_f * entry_of(b, cum_v)).astype(LOW)
        tail = nt(write, end_low) * weight_w
        whole = din_s[here, :] + tail
        d_conv[:, :inner] = conv_grad(whole + through_w * dy_f, conv[:, :inner])
        packed = (values_f * weight_w).astype(LOW)
        ds = ds_s[here, :]
        d_read = nn(ds, write) + nn(d_query, start.astype(LOW))
        d_write = tn(ds, read_v) + nn(packed, end_low)
        d_conv[:, inner : inner + STATE] = conv_grad(d_write, conv[:, inner : inner + STATE])
        d_conv[:, inner + STATE :] = conv_grad(d_read, conv[:, inner + STATE :])

        own = to_heads(dy_f * values_f, collect)
        r1 = to_heads(dy_f * ssd_s[here, :], collect) - vec[2:3, :] * own
        by_value = to_heads(values_f * whole, collect)
        tail_sum = jnp.sum(tail * values_f, axis=0, keepdims=True)
        tail_row = to_heads(jnp.broadcast_to(tail_sum, (EDGE, inner)), collect)[0:1]
        high, rest = halves(end * start)
        ones = jnp.ones((EDGE, STATE), LOW)
        carry_grad = to_heads(nt(ones, high) + nt(ones, rest), collect)[0:1]
        d_last = tail_row + carry_grad * (jnp.exp(last) * (first * second))
        d_cum = r1 - by_value + jnp.where(row == GROUP - 1, d_last, 0.0)
        d_rate = sum_after(d_cum)
        d_raw = d_rate * scale * sig + by_value * ratio
        d_step[...] = d_raw.astype(LOW)
        tiny[0:1, :] += jnp.sum(d_raw, axis=0, keepdims=True)
        tiny[1:2, :] += jnp.sum(d_rate * steps, axis=0, keepdims=True) * scale
        tiny[2:3, :] += jnp.sum(own, axis=0, keepdims=True)

    def conv_back(ref, count):
        total = taps[TAPS - 1 : TAPS] * ref[pl.ds(0, count), :]
        for tap in range(TAPS - 1):
            total = total + taps[tap : tap + 1] * ref[pl.ds(TAPS - 1 - tap, count), :]
        return total.astype(LOW)

    def input_back(d_pre, step_grad, gate_grad, u_rows):
        d_normed = (
            nt(gate_grad, w[:, :inner])
            + nt(d_pre, w[:, inner : inner + wide])
            + nt(step_grad, w[:, inner + wide :])
        )
        rows_f = u_rows.astype(WIDE)
        inv = lax.rsqrt(jnp.mean(rows_f * rows_f, axis=1, keepdims=True) + EPS)
        gained = d_normed * prenorm[...]
        dot = jnp.sum(gained * rows_f, axis=1, keepdims=True)
        grad = gained * inv - rows_f * (inv * inv * inv / D * dot)
        return grad.astype(LOW), d_normed * (rows_f * inv)

    def rows_back(b, turn, final):
        grad_c = d_conv[...]
        pre_v = pre_f.at(turn)[...].astype(WIDE)
        before = jnp.where(b == 0, rim[...], before_f.at(turn)[HALO - EDGE :, :].astype(WIDE))
        bias_g[...] += jnp.sum(grad_c, axis=0, keepdims=True)
        parts = []
        for half in range(2):
            part_rows = slice(half * BLOCK, (half + 1) * BLOCK)
            tile = grad_c[part_rows]
            ext[0:EDGE, :] = (before if half == 0 else pre_v[BLOCK - EDGE : BLOCK]) * flags[2 * b + half]
            ext[EDGE:, :] = pre_v[part_rows]
            for tap in range(TAPS):
                taps_g[tap : tap + 1, :] += jnp.sum(
                    tile * ext[pl.ds(EDGE - (TAPS - 1) + tap, BLOCK), :], axis=0, keepdims=True
                )
            ext[:BLOCK, :] = tile
            if half == 0:
                ext[BLOCK:, :] = grad_c[BLOCK : BLOCK + EDGE] * flags[2 * b + 1]
            elif final:
                ext[BLOCK:, :] = jnp.zeros((EDGE, wide), WIDE)
            else:
                ext[BLOCK:, :] = after[...] * flags[2 * b + 2]
            parts.append(conv_back(ext, BLOCK))
        d_pre = jnp.concatenate(parts, axis=0)
        step_grad = d_step[...]
        normed_v = normed_f.at(turn)[...]
        u_v = u_f.at(turn)
        done = lax.broadcasted_iota(jnp.int32, (GROUP, 1), 0) < GROUP - HALO
        if final:
            d_pre = jnp.where(done, d_pre, jnp.zeros_like(d_pre))
            keep_conv[:HALO, :] = grad_c[GROUP - HALO :]
            keep_step[...] = step_grad[GROUP - HALO :]
            keep_normed[...] = normed_v[GROUP - HALO :]
            keep_u[...] = u_v[GROUP - HALO :, :]
        dw[:, :wide] += tn(normed_v, d_pre)
        dw[:, wide:] += tn(normed_v, step_grad)
        grad, gain = input_back(d_pre, step_grad, dgate_s[group_rows(b), :], u_v[...])
        pn[...] += jnp.sum(jnp.where(done, gain, 0.0) if final else gain, axis=0, keepdims=True)
        g_buf[group_rows(b), :] = grad
        own_columns = pl.ds(pl.multiple_of(mine * width, LANES), width)
        result[0, 2 * b] = u_v[0:BLOCK, own_columns]
        result[0, 2 * b + 1] = u_v[BLOCK:, own_columns]
        after[...] = grad_c[0:EDGE]

    step(*last_phase, 0, None)
    scan_back(blocks - 1, 0)
    rows_back(blocks - 1, 0, True)
    dx_fold.send(*short_piece)

    @pl.loop(1, blocks)
    def _(turn):
        b = blocks - 1 - turn
        step(*last_phase, turn, None)
        scan_back(b, turn)

        @pl.when(b == 0)
        def _():
            edge_own[...] = d_conv[0:EDGE, :]
            edge_copy(lax.rem(me + seqs - 1, seqs)).start()

        rows_back(b, turn, False)
        dx_fold.send(group_rows(b), b)

        @pl.when(turn == 2)
        def _():
            dx_fold.merge(*short_piece)

        @pl.when(turn > 2)
        def _():
            dx_fold.merge(group_rows(b + 2), b + 2)

    edge_copy(lax.rem(me + 1, seqs)).wait()
    keep_conv[HALO:, :] = edge_got[...] * flags[2 * blocks]
    d_edge = conv_back(keep_conv, HALO)
    dw[:, :wide] += tn(keep_normed[...], d_edge)
    grad, gain = input_back(d_edge, keep_step[...], dgate_s[pl.ds(rows - HALO, HALO), :], keep_u[...])
    pn[...] += jnp.sum(gain, axis=0, keepdims=True)
    g_buf[pl.ds(rows - HALO, HALO), :] = grad
    dx_fold.send(*edge_piece)

    da_low[...] = dw[:, inner:wide].astype(LOW)
    w_start(3)
    dw_low[:, :inner] = dw[:, :inner].astype(LOW)
    dw_low[:, inner:] = dw[:, wide:].astype(LOW)
    w_start(2)
    own_copies["dw"].start()
    da_got[me] = da_low[rows_of(me), :]

    for z in range(line):
        slab = z * size // LANES * LANES
        zs_send[z] = jnp.zeros(zs_send.shape[1:], WIDE)
        zs_send[z, 0:1, :] = pn[:, z * width : (z + 1) * width]
        zs_send[z, EDGE : EDGE + TAPS, :LANES] = taps_g[0:TAPS, inner + slab : inner + slab + LANES]
        zs_send[z, EDGE + TAPS : EDGE + TAPS + 1, :LANES] = bias_g[:, inner + slab : inner + slab + LANES]
    zs_got[mine] = zs_send[mine]
    all_line(lambda to: zs_copy(to, mine).start())

    if blocks > 3:

        @pl.loop(0, 2)
        def _(n):
            dx_fold.merge(group_rows(1 - n), 1 - n)

    elif blocks == 2:
        dx_fold.merge(*short_piece)
        dx_fold.merge(group_rows(0), 0)
    dx_fold.merge(*edge_piece)

    @pl.loop(0, blocks)
    def _(b):
        out_fold.drain(group_rows(b), b)

    fetch(out_far)

    @pl.loop(0, blocks)
    def _(b):
        inv, _ = row_stats(b)
        total = out_fold.total(group_rows(b), out_near if roomy else out_part) * inv
        result[0, 2 * b] = (result[0, 2 * b].astype(WIDE) + total[:BLOCK]).astype(LOW)
        result[0, 2 * b + 1] = (result[0, 2 * b + 1].astype(WIDE) + total[BLOCK:]).astype(LOW)

    route(0)
    own_g = pltpu.make_async_copy(shard_of(g_part, mine), out_part.at[mine], load_sem.at[3])
    own_g.start()

    w_wait(3)
    from_plane = da_got[0].astype(WIDE)
    for n in range(1, seqs):
        from_plane = from_plane + da_got[n].astype(WIDE)
    for z in range(line):
        slab = z * size // LANES * LANES
        da_send[z] = from_plane[:, slab : slab + LANES]
    own_copies["addr"].start()
    all_line(lambda to: da_copy(to, mine).start())

    each_piece(dx_fold.drain)
    fetch(dx_far)
    own_g.wait()

    @pl.loop(0, blocks)
    def _(b):
        here = group_rows(b)
        total = dx_fold.total(here, dx_near if roomy else out_part)
        done = (out_part[mine, here].astype(WIDE) + total).astype(LOW)
        result[1, 2 * b] = done[:BLOCK]
        result[1, 2 * b + 1] = done[BLOCK:]

    route(1)
    all_line(lambda other: zs_copy(other, other).wait())
    from_line = jnp.sum(zs_got[...], axis=0)
    small[...] = jnp.zeros_like(small)
    small[0:TAPS, :inner] = taps_g[0:TAPS, :inner]
    small[0:TAPS, inner:] = from_line[EDGE : EDGE + TAPS, :LANES]
    small[4:5, :inner] = bias_g[:, :inner]
    small[4:5, inner:] = from_line[EDGE + TAPS : EDGE + TAPS + 1, :LANES]
    small[5:6, :inner] = gpost[...]
    small[6:7, :width] = from_line[0:1]
    for n in range(3):
        small[7:8, n * LANES : (n + 1) * LANES] = tiny[n : n + 1, :]
    own_copies["small"].start()
    all_seq(lambda to: small_copy(to, me).start())

    for which in range(3):
        w_wait(which)
    all_line(lambda other: da_copy(other, other).wait())
    all_seq(lambda other: fin_copy(0, other, other).wait())
    all_seq(lambda other: fin_copy(1, other, other).wait())
    all_seq(lambda other: small_copy(other, other).wait())
    for copy in own_copies.values():
        copy.wait()


def core(
    flags, give, gate, part, act, cum, raw, local, conv, pre, normed, u, g_part, state_in, r_t, w_all, postnorm, vec,
    prenorm, kernels, filters, rim,
):
    seqs, line = lax.axis_size("seq"), lax.axis_size("head")
    rows, inner = gate.shape
    wide = act.shape[1]
    total = g_part.shape[1]
    width = total // line
    depth = total // seqs
    blocks, tiles = rows // GROUP, rows // BLOCK
    heads = inner // HDIM
    pieces = blocks + 1
    message = (inner + HALO, STATE)
    sums = (blocks, EDGE, GROUP)
    streamed = (gate, part, act, cum, raw, local, conv, pre, normed, u, g_part, r_t, w_all)
    whole = (state_in, postnorm, vec, prenorm, kernels, filters, rim)
    gather = (line, rows, width)
    nothing = (line, HALO, width)
    roomy = rows * total * 2 <= 4 << 20
    near, far = (gather, nothing) if roomy else (nothing, gather)
    relay = (2, rows if line == 4 else HALO, width)
    small = (EDGE, inner + LANES)
    ways = max(line, 3)

    def slots(*dims):
        return (2,) + dims

    buffers = (
        (slots(GROUP, inner), WIDE), (slots(GROUP, inner), WIDE), (slots(GROUP, STATE), LOW),
        (slots(GROUP, LANES), WIDE), (slots(inner, STATE), WIDE), (slots(GROUP, total), LOW),
        (slots(GROUP, wide), LOW), (slots(GROUP, LANES), WIDE), (slots(GROUP, wide), WIDE),
        (slots(GROUP, wide), LOW), (slots(HALO, wide), LOW), (slots(GROUP, total), LOW),
    )
    return pl.pallas_call(
        functools.partial(core_kernel, seqs, line, heads, blocks, roomy),
        grid=(1,),
        out_shape=(
            shape((seqs, BLOCK, width), LOW), shape((seqs, BLOCK, width), LOW), shape(far, LOW), shape(far, LOW),
            shape((seqs, depth, inner), LOW), shape((seqs, depth, inner), LOW), shape((seqs, depth, inner + LANES), LOW),
            shape((line, depth, LANES), WIDE), shape((seqs,) + small, WIDE),
        ),
        in_specs=[SMEM_SPEC] * 2 + [ANY_SPEC] * len(streamed) + [fixed(a.shape) for a in whole],
        out_specs=(ANY_SPEC,) * 9,
        scratch_shapes=[pltpu.VMEM(dims, kind) for dims, kind in buffers] + [
            DMA((len(buffers), 2)),
            pltpu.VMEM(r_t.shape, LOW), pltpu.VMEM(w_all.shape, LOW),
            pltpu.VMEM((rows, inner), WIDE), pltpu.VMEM((rows, inner), WIDE), pltpu.VMEM((rows, inner), LOW),
            pltpu.VMEM((rows, inner), LOW), pltpu.VMEM((rows, GROUP), LOW), pltpu.VMEM((blocks, inner, STATE), WIDE),
            pltpu.VMEM((blocks, inner, STATE), WIDE), pltpu.VMEM((inner, STATE), WIDE), pltpu.VMEM((LANES, 1), WIDE),
            pltpu.VMEM((rows, total), LOW), pltpu.VMEM(gather, LOW),
            pltpu.VMEM((seqs,) + message, LOW), pltpu.VMEM(message, LOW),
            pltpu.VMEM(relay, LOW), pltpu.VMEM(relay, LOW), pltpu.VMEM(near, LOW), pltpu.VMEM(near, LOW),
            pltpu.VMEM((line,) + sums, WIDE), pltpu.VMEM(sums, WIDE),
            pltpu.VMEM((total, inner), WIDE), pltpu.VMEM((total, inner), WIDE), pltpu.VMEM((total, inner), LOW),
            pltpu.VMEM((total, inner), LOW), pltpu.VMEM((1, inner), WIDE), pltpu.VMEM((EDGE, LANES), WIDE),
            pltpu.VMEM((GROUP, wide), WIDE), pltpu.VMEM((GROUP, LANES), LOW), pltpu.VMEM((EDGE, wide), WIDE),
            pltpu.VMEM((EDGE, wide), WIDE), pltpu.VMEM((EDGE, wide), WIDE), pltpu.VMEM((BLOCK + EDGE, wide), WIDE),
            pltpu.VMEM((HALO + EDGE, wide), WIDE), pltpu.VMEM((HALO, LANES), LOW), pltpu.VMEM((HALO, total), LOW),
            pltpu.VMEM((HALO, total), LOW),
            pltpu.VMEM((EDGE, wide), WIDE), pltpu.VMEM((1, wide), WIDE), pltpu.VMEM((total, wide + LANES), WIDE),
            pltpu.VMEM((total, inner + LANES), LOW), pltpu.VMEM((total, wide - inner), LOW),
            pltpu.VMEM((seqs, depth, wide - inner), LOW), pltpu.VMEM((line, depth, LANES), WIDE),
            pltpu.VMEM((1, total), WIDE), pltpu.VMEM((line, 2 * EDGE, width), WIDE),
            pltpu.VMEM((line, 2 * EDGE, width), WIDE), pltpu.VMEM(small, WIDE),
            pltpu.VMEM((2, tiles, BLOCK, width), LOW), pltpu.VMEM((2, seqs, BLOCK, width), LOW),
            DMA((seqs,)), DMA((seqs,)), DMA((seqs,)), DMA((line,)), DMA((line,)), DMA((2, line)), DMA((line,)), DMA((4,)),
            DMA((ways, blocks)), DMA((line, blocks)), DMA((2, blocks)), DMA((4, seqs)), DMA((4, seqs)),
            DMA((ways, pieces)), DMA((line, pieces)), DMA((2, pieces)), DMA, DMA,
            DMA((line,)), DMA((line,)), DMA((line,)), DMA((line,)), DMA((seqs,)), DMA((seqs,)), DMA((2, seqs)),
            DMA((2, seqs)), DMA((7,)), DMA((2,)),
        ],
        compiler_params=pltpu.CompilerParams(
            collective_id=1, has_side_effects=True, vmem_limit_bytes=VMEM_LIMIT, dimension_semantics=("arbitrary",)
        ),
        name="core",
    )(flags, give, *streamed, *whole)


def finish_kernel(
    take, out_recv, grad_recv, gread_got, ggate_got, dw_got, addr_got, small_got,
    out_o, dx_o, prenorm_o, gate_o, pay_o, addr_o, step_o, kernels_o, offsets_o, filters_o, shifts_o,
    stepbias_o, decays_o, through_o, post_o, read_o,
):
    inner, size, heads, width = gate_o.shape[1], addr_o.shape[0], step_o.shape[0], prenorm_o.shape[1]
    offset = lax.rem(lax.axis_index("head") * size, LANES)
    back_turn = lax.rem(LANES - offset, LANES)
    for k in range(out_o.shape[0]):
        out_o[k] = out_recv[take[k]]
        dx_o[k] = grad_recv[take[k]]

    def summed(ref):
        total = ref[0].astype(WIDE)
        for n in range(1, ref.shape[0]):
            total = total + ref[n].astype(WIDE)
        return total

    read_o[...] = summed(gread_got).T
    gate_o[...] = summed(ggate_got)
    grads = summed(dw_got)
    pay_o[...] = grads[:, :inner]
    step_o[...] = grads[:, inner:].T[:heads]
    addr_o[...] = pltpu.roll(summed(addr_got), back_turn, 1).T[:size]
    totals = jnp.sum(small_got[...], axis=0)
    kernels_o[...] = totals[0:TAPS, :inner]
    offsets_o[...] = totals[4:5, :inner]
    turned = pltpu.roll(totals[:, inner:], back_turn, 1)
    filters_o[...] = turned[0:TAPS, :size]
    shifts_o[...] = turned[4:5, :size]
    post_o[...] = totals[5:6, :inner]
    prenorm_o[...] = totals[6:7, :width]
    for n, ref in enumerate((stepbias_o, decays_o, through_o)):
        ref[...] = totals[7:8, n * LANES : n * LANES + heads]


def finish(take, out_recv, grad_recv, gread_got, ggate_got, dw_got, addr_got, small_got):
    seqs, _, width = out_recv.shape
    tiles = take.shape[0]
    _, depth, inner = gread_got.shape
    heads = inner // HDIM
    size = 2 * STATE // addr_got.shape[0]
    operands = (out_recv, grad_recv, gread_got, ggate_got, dw_got, addr_got, small_got)
    outs = (
        shape((tiles, BLOCK, width), LOW), shape((tiles, BLOCK, width), LOW), shape((1, width), WIDE),
        shape((depth, inner), WIDE), shape((depth, inner), WIDE), shape((size, depth), WIDE),
        shape((heads, depth), WIDE), shape((TAPS, inner), WIDE), shape((1, inner), WIDE),
        shape((TAPS, size), WIDE), shape((1, size), WIDE), shape((1, heads), WIDE), shape((1, heads), WIDE),
        shape((1, heads), WIDE), shape((1, inner), WIDE), shape((inner, depth), WIDE),
    )
    return pl.pallas_call(
        finish_kernel,
        grid=(1,),
        out_shape=outs,
        in_specs=[SMEM_SPEC] + [fixed(a.shape) for a in operands],
        out_specs=tuple(fixed(a.shape) for a in outs),
        compiler_params=pltpu.CompilerParams(vmem_limit_bytes=VMEM_LIMIT, dimension_semantics=("arbitrary",)),
        name="finish",
    )(take, *operands)


def on_device(
    inputs,
    cotangent,
    lengths,
    placement,
    prenorm,
    gating,
    payload,
    address,
    stepping,
    kernels,
    offsets,
    filters,
    shifts,
    stepbias,
    decays,
    through,
    postnorm,
    readout,
):
    rows, width = inputs.shape
    heads = stepbias.shape[0]
    tiles = rows // BLOCK
    give_in, take_in, give_out, take_out, flags, vec = index(placement, lengths, stepbias, decays, through, tiles)
    gain, post = prenorm[None, :], postnorm[None, :]
    (
        u, normed, gate, pre, conv, act, raw, cum, part, local, state_in, rim, g_part, w_all, r_t
    ) = front(
        give_in, take_in, flags, inputs, cotangent, gating, payload, address, stepping, readout, vec, gain, kernels,
        filters, offsets[None, :], shifts[None, :]
    )
    out_recv, grad_recv, _, _, gread_got, ggate_got, dw_got, addr_got, small_got = core(
        flags, give_out, gate, part, act, cum, raw, local, conv, pre, normed, u, g_part, state_in, r_t, w_all, post, vec,
        gain, kernels, filters, rim
    )
    (
        out, dx, prenorm_g, gate_g, pay_g, addr_g, step_g, kernels_g, offsets_g, filters_g, shifts_g, stepbias_g,
        decays_g, through_g, post_g, read_g,
    ) = finish(take_out, out_recv, grad_recv, gread_got, ggate_got, dw_got, addr_got, small_got)
    return (
        out.reshape(rows, width),
        dx.reshape(rows, width),
        prenorm_g.reshape(-1),
        gate_g,
        pay_g,
        addr_g.T,
        step_g.T,
        kernels_g,
        offsets_g.reshape(-1),
        filters_g,
        shifts_g.reshape(-1),
        stepbias_g.reshape(-1),
        decays_g.reshape(-1),
        through_g.reshape(-1),
        post_g.reshape(-1),
        read_g,
    )


def solution(mesh):
    in_specs = (
        P("seq", "head"),
        P("seq", "head"),
        P(),
        P(),
        P(),
        P("seq", "head"),
        P("seq", "head"),
        P("seq", None),
        P("seq", "head"),
        P(None, "head"),
        P("head"),
        P(),
        P(),
        P("head"),
        P("head"),
        P("head"),
        P("head"),
        P("head", "seq"),
    )
    out_specs = (
        P("seq", "head"),
        P("seq", "head"),
        P("head"),
        P("seq", "head"),
        P("seq", "head"),
        P("seq", "head"),
        P("seq", "head"),
        P(None, "head"),
        P("head"),
        P(None, "head"),
        P("head"),
        P("head"),
        P("head"),
        P("head"),
        P("head"),
        P("head", "seq"),
    )
    return jax.shard_map(
        on_device, mesh=mesh, in_specs=in_specs, out_specs=out_specs, check_vma=False
    )
```

```python
import functools

import jax
import jax.numpy as jnp
from jax import lax
from jax.experimental import pallas as pl
from jax.experimental.pallas import tpu as pltpu
from jax.sharding import PartitionSpec as P

D = 1024
GROUP = 256
BLOCK = 128
INNER = 2048
HDIM = 64
STATE = 128
TAPS = 4
HALO = 16
EDGE = 8
LANES = 128
EPS = 1e-05
MESH = pl.DeviceIdType.MESH
VMEM = pltpu.MemorySpace.VMEM
SMEM = pltpu.MemorySpace.SMEM
DMA = pltpu.SemaphoreType.DMA
VMEM_LIMIT = 63 << 20
LOW = jnp.bfloat16
WIDE = jnp.float32


def shape(dims, kind):
    return jax.ShapeDtypeStruct(dims, kind)


def nn(a, b):
    return jnp.dot(a, b, preferred_element_type=WIDE)


def nt(a, b):
    return lax.dot_general(a, b, (((1,), (1,)), ((), ())), preferred_element_type=WIDE)


def tn(a, b):
    return lax.dot_general(a, b, (((0,), (0,)), ((), ())), preferred_element_type=WIDE)


def halves(x):
    high = x.astype(LOW)
    return high, (x - high.astype(WIDE)).astype(LOW)


def thirds(x):
    high = x.astype(LOW)
    rest = x - high.astype(WIDE)
    middle = rest.astype(LOW)
    return high, middle, (rest - middle.astype(WIDE)).astype(LOW)


def head_rows(inner):
    row = lax.broadcasted_iota(jnp.int32, (LANES, inner), 0)
    column = lax.broadcasted_iota(jnp.int32, (LANES, inner), 1)
    return jnp.where(column // HDIM == row, 1.0, 0.0).astype(LOW)


def head_columns(inner):
    row = lax.broadcasted_iota(jnp.int32, (inner, LANES), 0)
    column = lax.broadcasted_iota(jnp.int32, (inner, LANES), 1)
    return jnp.where(row // HDIM == column, 1.0, 0.0).astype(LOW)


def to_columns(x, spread):
    high, rest = halves(x)
    return nn(high, spread) + nn(rest, spread)


def to_heads(x, collect):
    high, rest = halves(x)
    return nn(high, collect) + nn(rest, collect)


def ones_before(count):
    row = lax.broadcasted_iota(jnp.int32, (count, count), 0)
    column = lax.broadcasted_iota(jnp.int32, (count, count), 1)
    return row >= column


def sum_before(x):
    matrix = jnp.where(ones_before(x.shape[0]), 1.0, 0.0).astype(LOW)
    high, middle, low = thirds(x)
    return nn(matrix, high) + (nn(matrix, middle) + nn(matrix, low))


def sum_after(x):
    count = x.shape[0]
    row = lax.broadcasted_iota(jnp.int32, (count, count), 0)
    column = lax.broadcasted_iota(jnp.int32, (count, count), 1)
    matrix = jnp.where(row <= column, 1.0, 0.0).astype(LOW)
    high, middle, low = thirds(x)
    return nn(matrix, high) + (nn(matrix, middle) + nn(matrix, low))


def sigmoid(x):
    return 0.5 * jnp.tanh(0.5 * x) + 0.5


def step_terms(raw, heads):
    z = jnp.exp(-jnp.abs(raw))
    series = 1.0 - z * (0.5 - z * (1.0 / 3.0 - z * (0.25 - z * 0.2)))
    small = z < 0.03
    log1p = jnp.where(small, z * series, jnp.log(1.0 + z))
    soft = jnp.maximum(raw, 0.0) + log1p
    one = 1.0 / (1.0 + z)
    sig = jnp.where(raw >= 0, one, z * one)
    ratio = jnp.where(small & (raw < 0), one / series, sig / jnp.maximum(soft, 1e-20))
    lane = lax.broadcasted_iota(jnp.int32, raw.shape, 1)
    return jnp.where(lane < heads, soft, 0.0), sig, ratio


def greet(seq_peers, head_peers, corners=False):
    barrier = pltpu.get_barrier_semaphore()
    count = 0
    if seq_peers > 1:
        me = lax.axis_index("seq")

        @pl.loop(1, seq_peers)
        def _(i):
            pl.semaphore_signal(
                barrier, inc=1, device_id={"seq": lax.rem(me + i, seq_peers)}, device_id_type=MESH
            )

        count += seq_peers - 1
    if head_peers > 1:
        mine = lax.axis_index("head")

        @pl.loop(1, head_peers)
        def _(i):
            pl.semaphore_signal(
                barrier, inc=1, device_id={"head": lax.rem(mine + i, head_peers)}, device_id_type=MESH
            )

        count += head_peers - 1
    if corners and head_peers > 1:
        me, mine = lax.axis_index("seq"), lax.axis_index("head")
        for side in (1, seq_peers - 1):

            @pl.loop(1, head_peers)
            def _(i):
                where = {"seq": lax.rem(me + side, seq_peers), "head": lax.rem(mine + i, head_peers)}
                pl.semaphore_signal(barrier, inc=1, device_id=where, device_id_type=MESH)

        count += 2 * (head_peers - 1)
    pl.semaphore_wait(barrier, count)


def remote(src, dst, send_sem, recv_sem, where):
    return pltpu.make_async_remote_copy(
        src_ref=src, dst_ref=dst, send_sem=send_sem, recv_sem=recv_sem, device_id=where, device_id_type=MESH
    )


class Line:
    def __init__(self, count, out, width, send, recv):
        self.count, self.out, self.width, self.send, self.recv = count, out, width, send, recv
        self.me = lax.axis_index("head")

    def view(self, shard):
        return self.out.at[:, pl.ds(pl.multiple_of(shard * self.width, LANES), self.width)]

    def copy(self, src, shard, way, step):
        return remote(
            src, self.view(shard), self.send.at[way, step], self.recv.at[shard], {"head": self.me + (1 - 2 * way)}
        )

    def first(self, own):
        self.pass_on(own, self.me, 0, 0)
        self.pass_on(own, self.me, 1, 0)

    def pass_on(self, src, shard, way, step):
        reach = (self.me < self.count - 1) if way == 0 else (self.me > 0)

        @pl.when(reach)
        def _():
            self.copy(src, shard, way, step).start()

    def hop(self, step, take=True, give=True, source=None):
        for way in (0, 1):
            shard = self.me - step if way == 0 else self.me + step
            there = (shard >= 0) if way == 0 else (shard < self.count)

            @pl.when(there)
            def _():
                if take:
                    self.copy(self.view(shard), shard, way, step).wait_recv()
                if give and step < self.count - 1:
                    self.pass_on(self.view(shard) if source is None else source(shard), shard, way, step)

    def finish(self, own, steps=None):
        for way in (0, 1):
            reach = (self.me < self.count - 1) if way == 0 else (self.me > 0)
            for step in range(self.count - 1) if steps is None else steps:
                shard = self.me - step if way == 0 else self.me + step
                there = (shard >= 0) if way == 0 else (shard < self.count)

                @pl.when(reach & there)
                def _():
                    src = own if step == 0 else self.view(shard)
                    self.copy(src, shard, way, step).wait_send()


class Plane:
    def __init__(self, seqs, view, sent, got, passed, way=0):
        self.chips, self.view, self.sent, self.got, self.passed, self.way = seqs // 2, view, sent, got, passed, way
        self.me = lax.axis_index("seq")
        self.core = lax.rem(self.me, 2)
        self.chip = self.me // 2
        self.mate = self.me + 1 - 2 * self.core

    def forward(self, chip):
        return (chip > self.chip) if self.way == 1 else (chip < self.chip) if self.way == -1 else (chip >= 0)

    def backward(self, chip):
        return (chip < self.chip) if self.way == 1 else (chip > self.chip) if self.way == -1 else (chip >= 0)

    def each_chip(self, body):
        @pl.loop(1, self.chips)
        def _(i):
            body(lax.rem(self.chip + i, self.chips))

    def copy(self, src, source, to, sem):
        return remote(src, self.view(source), sem, self.got.at[source], {"seq": to})

    def start(self, own):
        def send(chip):
            to = 2 * chip + self.core

            @pl.when(self.forward(chip))
            def _():
                self.copy(own, self.me, to, self.sent.at[to]).start()

        self.each_chip(send)
        self.copy(own, self.me, self.mate, self.sent.at[self.mate]).start()

    def relay(self):
        def take(chip):
            source = 2 * chip + self.core

            @pl.when(self.backward(chip))
            def _():
                landed = self.view(source)
                self.copy(landed, source, self.mate, self.passed.at[source]).wait_recv()
                self.copy(landed, source, self.mate, self.passed.at[source]).start()

        self.each_chip(take)

    def finish(self, own):
        def take(chip):
            source = 2 * chip + 1 - self.core

            @pl.when(self.backward(chip))
            def _():
                self.copy(self.view(source), source, self.mate, self.passed.at[source]).wait_recv()

        self.each_chip(take)
        self.copy(self.view(self.mate), self.mate, self.mate, self.sent.at[self.mate]).wait_recv()
        self.copy(own, self.me, self.mate, self.sent.at[self.mate]).wait_send()

        def drain(chip):
            same = 2 * chip + self.core

            @pl.when(self.forward(chip))
            def _():
                self.copy(own, self.me, same, self.sent.at[same]).wait_send()

            @pl.when(self.backward(chip))
            def _():
                self.copy(self.view(same), same, self.mate, self.passed.at[same]).wait_send()

        self.each_chip(drain)


ANY_SPEC = pl.BlockSpec(memory_space=pl.ANY)
VMEM_SPEC = pl.BlockSpec(memory_space=VMEM)
SMEM_SPEC = pl.BlockSpec(memory_space=SMEM)


def index_kernel(
    seqs, tiles, place, lengths, stepbias, decays, through, give_in, take_in, give_out, take_out, flags, vec
):
    me = lax.axis_index("seq")

    @pl.loop(0, seqs * tiles)
    def _(j):
        block = place[j]

        @pl.when(lax.div(block, tiles) == me)
        def _():
            to = lax.div(j, tiles)
            give_in[to] = lax.rem(block, tiles)
            take_out[lax.rem(block, tiles)] = to

    @pl.loop(0, tiles)
    def _(k):
        source = lax.div(place[me * tiles + k], tiles)
        take_in[k] = source
        give_out[source] = k

    @pl.loop(0, tiles + 1)
    def _(k):
        position = (me * tiles + k) * BLOCK
        end = jnp.int32(0)
        border = position == 0
        for n in range(lengths.shape[0]):
            end = end + lengths[n]
            border = border | (position == end)
        flags[k] = jnp.where(border, 0.0, 1.0)

    heads = stepbias.shape[1]
    vec[...] = jnp.zeros_like(vec)
    vec[0:1, :heads] = stepbias[...]
    vec[1:2, :heads] = decays[...]
    vec[2:3, :heads] = through[...]


def index(place, lengths, stepbias, decays, through, tiles):
    seqs = lax.axis_size("seq")
    whole = jnp.int32
    return pl.pallas_call(
        functools.partial(index_kernel, seqs, tiles),
        out_shape=(
            shape((seqs,), whole), shape((tiles,), whole), shape((seqs,), whole), shape((tiles,), whole),
            shape((tiles + 1,), WIDE), shape((EDGE, LANES), WIDE),
        ),
        in_specs=[SMEM_SPEC] * 2 + [VMEM_SPEC] * 3,
        out_specs=(SMEM_SPEC,) * 5 + (VMEM_SPEC,),
        compiler_params=pltpu.CompilerParams(vmem_limit_bytes=VMEM_LIMIT),
        name="index",
    )(place, lengths, stepbias[None, :], decays[None, :], through[None, :])


def blockwise(dims, index):
    return pl.BlockSpec(dims, index)


def fixed(dims):
    return pl.BlockSpec(dims, lambda i: (0,) * len(dims), pipeline_mode=pl.Buffered(1))


def carry_columns(carry_row_t, collect):
    high, middle, low = thirds(jnp.broadcast_to(carry_row_t, (LANES, LANES)))
    return nn(collect, high) + (nn(collect, middle) + nn(collect, low))


def pair_lanes(slab):
    lane = lax.broadcasted_iota(jnp.int32, slab.shape, 1)
    zero = jnp.zeros_like(slab)
    return jnp.where(lane < HDIM, slab, zero), jnp.where(lane >= HDIM, slab, zero)


def fold_states(slots, collect, inner, first, last, step, start):
    def hop(n, state):
        message = slots[first + n * step]
        carry = nn(collect[:, :HALO], message[inner:])
        return carry * state + message[:inner].astype(WIDE)

    return lax.fori_loop(0, (last - first) * step, hop, start)


def front_kernel(
    seqs, line, heads, blocks, chunks, give, take, flags,
    x_in, g_in, gating_in, payload_in, address_in, stepping_in, readout_in,
    vec, prenorm, kernels, filters, offsets, shifts,
    u_o, normed_o, gate_o, pre_o, conv_o, act_o, raw_o, cum_o, part_o, local_o, state_o, rim_o, g_o, w_o, r_o,
    x, g, gating, payload, address, stepping, readout, square,
    send_x, send_g, recv_x, recv_g, work_x, work_g, w_own, r_own, u, w, msg, slots,
    ext, prev, state, prod,
    sent, got, w_sent, w_got, w_passed, r_sent, r_got, r_passed, s_sent, s_got, s_passed, rim_sent, rim_got, own_sem,
    load_sem, line_sent, line_got, g_sent, g_got,
):
    i = pl.program_id(0)
    me, mine = lax.axis_index("seq"), lax.axis_index("head")
    tiles, _, width = x.shape
    rows = tiles * BLOCK
    depth, inner = gating.shape
    wide = pre_o.shape[1]
    part = rows // chunks
    per = blocks // chunks

    def rows_of(device):
        return pl.ds(pl.multiple_of(device * depth, depth), depth)

    def piece(n):
        if isinstance(n, int):
            return pl.ds(n * part, part)
        return pl.ds(pl.multiple_of(n * part, part), part)

    def u_line(n):
        return Line(line, u.at[piece(n)], width, line_sent.at[n], line_got.at[n])

    def own_columns(ref):
        return ref.at[:, pl.ds(pl.multiple_of(mine * width, LANES), width)]

    w_plane = Plane(seqs, lambda s: w.at[rows_of(s)], w_sent, w_got, w_passed)
    r_plane = Plane(seqs, lambda s: r_o.at[rows_of(s)], r_sent, r_got, r_passed)
    s_plane = Plane(seqs, lambda s: slots.at[s], s_sent, s_got, s_passed, way=1)
    g_line = Line(line, g_o, width, g_sent, g_got)
    own_r = pltpu.make_async_copy(r_own, r_o.at[rows_of(me)], own_sem.at[0])
    own_g = pltpu.make_async_copy(work_g, g_line.view(mine), own_sem.at[1])
    save_w = pltpu.make_async_copy(w, w_o, own_sem.at[2])

    def rim_copy(to, shard):
        columns = pl.ds(pl.multiple_of(shard * width, LANES), width)
        return remote(
            work_x.at[pl.ds(rows - HALO, HALO)], u.at[pl.ds(rows, HALO), columns], rim_sent.at[to], rim_got.at[shard],
            {"seq": lax.rem(me + 1, seqs), "head": to},
        )

    def arrange(which, received, work):
        @pl.loop(1, seqs)
        def _(n):
            source = lax.rem(me + n, seqs)
            remote(
                received.at[source], received.at[source], sent.at[which, source], got.at[which, source], {"seq": source}
            ).wait_recv()

        for k in range(tiles):
            work[pl.ds(k * BLOCK, BLOCK), :] = received[take[k]]

    @pl.when(i == 0)
    def _():
        pairs = (
            (x_in, x), (g_in, g), (gating_in, gating), (payload_in, payload), (address_in, address),
            (stepping_in, stepping), (readout_in, readout),
        )
        loads = [pltpu.make_async_copy(src, dst, load_sem.at[n]) for n, (src, dst) in enumerate(pairs)]
        for load in loads:
            load.start()
        greet(seqs, line, corners=True)

        def post(which, source, outgoing, incoming):
            @pl.loop(1, seqs)
            def _(n):
                to = lax.rem(me + n, seqs)
                outgoing[to] = source[give[to]]
                remote(outgoing.at[to], incoming.at[me], sent.at[which, to], got.at[which, me], {"seq": to}).start()

            incoming[me] = source[give[me]]

        loads[0].wait()
        post(0, x, send_x, recv_x)
        for load in loads[1:]:
            load.wait()

        w_own[:, :inner] = gating[...].astype(LOW)
        w_own[:, inner : 2 * inner] = payload[...].astype(LOW)
        state2 = address.shape[1]
        w_own[:, 2 * inner : 2 * inner + state2] = address[...].astype(LOW)
        square[...] = jnp.zeros_like(square)
        square[: stepping.shape[0], :depth] = stepping[...]
        w_own[:, 2 * inner + state2 :] = square[...].T[:depth].astype(LOW)
        r_own[...] = readout[...].T.astype(LOW)
        w[rows_of(me), :] = w_own[...]
        own_r.start()

        arrange(0, recv_x, work_x)

        @pl.loop(0, line)
        def _(n):
            rim_copy(lax.rem(mine + n, line), mine).start()

        for n in range(chunks):
            u_line(n).first(work_x.at[piece(n)])
        w_plane.start(w_own)
        own = pltpu.make_async_copy(work_x, own_columns(u.at[pl.ds(0, rows)]), own_sem.at[3])
        own.start()
        post(1, g, send_g, recv_g)
        r_plane.start(r_own)
        for step in range(1, line - 1):
            for n in range(chunks):
                u_line(n).hop(step)
            if step == 1:
                w_plane.relay()
        own.wait()

        @pl.loop(0, line)
        def _(n):
            rim_copy(n, n).wait_recv()

        arrange(1, recv_g, work_g)
        g_line.first(work_g)
        own_g.start()
        w_plane.finish(w_own)
        save_w.start()

    if line > 1:

        @pl.when(lax.rem(i, per) == 0)
        def _():
            u_line(lax.div(i, per)).hop(line - 1)

    taps = jnp.concatenate([kernels[...], filters[...]], axis=1)
    bias = jnp.concatenate([offsets[...], shifts[...]], axis=1)
    spread_m, collect = head_rows(inner), head_columns(inner)

    def normalize(block):
        wide_rows = block.astype(WIDE)
        scale = lax.rsqrt(jnp.mean(wide_rows * wide_rows, axis=1, keepdims=True) + EPS)
        return (wide_rows * scale * prenorm[...]).astype(LOW)

    @pl.when(i == 0)
    def _():
        before = nn(normalize(u[pl.ds(rows, HALO), :]), w[:, inner : inner + wide]).astype(LOW).astype(WIDE)
        prev[...] = before[HALO - EDGE :]
        rim_o[...] = before[HALO - EDGE :]
        state[...] = jnp.zeros_like(state)
        prod[...] = jnp.ones_like(prod)

    u_v = u[pl.ds(pl.multiple_of(i * GROUP, GROUP), GROUP), :]
    u_o[...] = u_v
    normed = normalize(u_v)
    normed_o[...] = normed
    gate_o[...] = nn(normed, w[:, :inner])
    pre = nn(normed, w[:, inner : inner + wide]).astype(LOW)
    pre_o[...] = pre
    lane = lax.broadcasted_iota(jnp.int32, (GROUP, LANES), 1)
    raw = jnp.where(lane < heads, nn(normed, w[:, inner + wide :]) + vec[0:1, :], 0.0)
    raw_o[...] = raw
    first, second = flags[2 * i], flags[2 * i + 1]
    same = (first, second)
    for half in range(2):
        at = pl.ds(half * BLOCK, BLOCK)
        ext[0:EDGE, :] = prev[...] * same[half]
        ext[EDGE:, :] = pre[half * BLOCK : (half + 1) * BLOCK].astype(WIDE)
        prev[...] = ext[BLOCK:, :]
        total = bias + taps[TAPS - 1 : TAPS] * ext[EDGE:, :]
        for tap in range(TAPS - 1):
            total = total + taps[tap : tap + 1] * ext[pl.ds(EDGE - (TAPS - 1) + tap, BLOCK), :]
        conv_o[at, :] = total
        act_o[at, :] = (total * sigmoid(total)).astype(LOW)

    steps, _, _ = step_terms(raw, heads)
    scale = -jnp.exp(vec[1:2, :])
    cum = sum_before(steps * scale)
    cum_o[...] = cum
    cum_t, steps_t = cum.T, steps.T
    write = act_o[:, inner : inner + STATE]
    read = act_o[:, inner + STATE :]
    lower = ones_before(BLOCK)
    top, low = slice(0, BLOCK), slice(BLOCK, GROUP)
    s00 = jnp.where(lower, nt(read[top], write[top]), 0.0)
    s10 = nt(read[low], write[top]) * second
    s11 = jnp.where(lower, nt(read[low], write[low]), 0.0)

    def mix(scores, head, t, s):
        decay = jnp.exp(jnp.minimum(cum[t, head : head + 1] - cum_t[head : head + 1, s], 0.0))
        return (scores * (decay * steps_t[head : head + 1, s])).astype(LOW)

    last = cum[GROUP - 1 : GROUP, :]
    row = lax.broadcasted_iota(jnp.int32, (GROUP, LANES), 0)
    weight = steps * jnp.exp(last - cum) * jnp.where(row < BLOCK, second, 1.0)
    weight_w = to_columns(weight, spread_m)
    skip = to_columns(jnp.broadcast_to(vec[2:3, :], (EDGE, LANES)), spread_m)[0:1]
    packed = []
    for pair in range(inner // LANES):
        columns = slice(pair * LANES, (pair + 1) * LANES)
        slab = act_o[:, columns]
        slab_f = slab.astype(WIDE)
        ones = pair_lanes(slab)
        h0, h1 = 2 * pair, 2 * pair + 1
        y0 = nn(
            jnp.concatenate([mix(s00, h0, top, top), mix(s00, h1, top, top)], axis=1),
            jnp.concatenate([ones[0][top], ones[1][top]], axis=0),
        )
        y1 = nn(
            jnp.concatenate(
                [mix(s10, h0, low, top), mix(s11, h0, low, low), mix(s10, h1, low, top), mix(s11, h1, low, low)], axis=1
            ),
            jnp.concatenate([ones[0], ones[1]], axis=0),
        )
        part_o[top, columns] = y0 + skip[:, columns] * slab_f[top]
        part_o[low, columns] = y1 + skip[:, columns] * slab_f[low]
        packed.append((slab_f * weight_w[:, columns]).astype(LOW))
    local = tn(jnp.concatenate(packed, axis=1), write)
    local_o[0] = local
    carry = jnp.exp(cum_t[:, GROUP - 1 : GROUP]) * (first * second)
    state[...] = carry_columns(carry, collect) * state[...] + local
    prod[...] = jnp.broadcast_to(carry[:HALO], (HALO, STATE)) * prod[...]

    @pl.when(i == blocks - 1)
    def _():
        msg[:inner, :] = state[...].astype(LOW)
        msg[inner:, :] = prod[...].astype(LOW)
        s_plane.start(msg)
        s_plane.relay()
        s_plane.finish(msg)
        state_o[...] = fold_states(slots, collect, inner, 0, me, 1, jnp.zeros((inner, STATE), WIDE))
        r_plane.relay()
        r_plane.finish(r_own)
        if line > 1:
            g_line.hop(1, give=False)
        g_line.finish(work_g, (0,))
        for n in range(chunks):
            u_line(n).finish(work_x.at[piece(n)])

        @pl.loop(0, line)
        def _(n):
            rim_copy(n, mine).wait_send()


        @pl.loop(1, seqs)
        def _(n):
            other = lax.rem(me + n, seqs)
            for which, buffer in ((0, send_x), (1, send_g)):
                remote(
                    buffer.at[other], buffer.at[other], sent.at[which, other], got.at[which, other], {"seq": other}
                ).wait_send()

        own_r.wait()
        own_g.wait()
        save_w.wait()


def front(give, take, flags, x, g, gating, payload, address, stepping, readout, vec, prenorm, kernels, filters, offsets, shifts):
    seqs, line = lax.axis_size("seq"), lax.axis_size("head")
    rows, width = x.shape
    depth, inner = gating.shape
    total = depth * seqs
    wide = inner + address.shape[1]
    columns = inner + wide + LANES
    blocks = rows // GROUP
    chunks = min(blocks, 4)
    heads = stepping.shape[1]
    routed = (seqs, BLOCK, width)
    given = (rows // BLOCK, BLOCK, width)
    message = (inner + HALO, STATE)
    operands = (x.reshape(given), g.reshape(given), gating, payload, address, stepping.T, readout)
    small = (vec, prenorm, kernels, filters, offsets, shifts)

    def by_rows(size):
        return blockwise((GROUP, size), lambda i: (i, 0))

    return pl.pallas_call(
        functools.partial(front_kernel, seqs, line, heads, blocks, chunks),
        grid=(blocks,),
        out_shape=(
            shape((rows, total), LOW), shape((rows, total), LOW), shape((rows, inner), WIDE), shape((rows, wide), LOW),
            shape((rows, wide), WIDE), shape((rows, wide), LOW), shape((rows, LANES), WIDE), shape((rows, LANES), WIDE),
            shape((rows, inner), WIDE), shape((blocks, inner, STATE), WIDE), shape((inner, STATE), WIDE),
            shape((EDGE, wide), WIDE), shape((rows, total), LOW), shape((total, columns), LOW),
            shape((total, inner), LOW),
        ),
        in_specs=[SMEM_SPEC] * 3 + [ANY_SPEC] * 7 + [fixed(a.shape) for a in small],
        out_specs=(
            by_rows(total), by_rows(total), by_rows(inner), by_rows(wide), by_rows(wide), by_rows(wide), by_rows(LANES),
            by_rows(LANES), by_rows(inner), blockwise((1, inner, STATE), lambda i: (i, 0, 0)), fixed((inner, STATE)),
            fixed((EDGE, wide)), ANY_SPEC, ANY_SPEC, ANY_SPEC,
        ),
        scratch_shapes=[pltpu.VMEM(a.shape, a.dtype) for a in operands] + [
            pltpu.VMEM((LANES, LANES), WIDE),
            pltpu.VMEM(routed, LOW), pltpu.VMEM(routed, LOW), pltpu.VMEM(routed, LOW), pltpu.VMEM(routed, LOW),
            pltpu.VMEM((rows, width), LOW), pltpu.VMEM((rows, width), LOW),
            pltpu.VMEM((depth, columns), LOW), pltpu.VMEM((depth, inner), LOW),
            pltpu.VMEM((rows + HALO, total), LOW), pltpu.VMEM((total, columns), LOW),
            pltpu.VMEM(message, LOW), pltpu.VMEM((seqs,) + message, LOW),
            pltpu.VMEM((EDGE + BLOCK, wide), WIDE), pltpu.VMEM((EDGE, wide), WIDE),
            pltpu.VMEM((inner, STATE), WIDE), pltpu.VMEM((HALO, STATE), WIDE),
            DMA((2, seqs)), DMA((2, seqs)),
            DMA((seqs,)), DMA((seqs,)), DMA((seqs,)), DMA((seqs,)), DMA((seqs,)), DMA((seqs,)),
            DMA((seqs,)), DMA((seqs,)), DMA((seqs,)), DMA((line,)), DMA((line,)), DMA((4,)), DMA((7,)),
            DMA((chunks, 2, line)), DMA((chunks, line)), DMA((2, line)), DMA((line,)),
        ],
        compiler_params=pltpu.CompilerParams(
            collective_id=0, has_side_effects=True, vmem_limit_bytes=VMEM_LIMIT, dimension_semantics=("arbitrary",)
        ),
        name="front",
    )(give, take, flags, *operands, *small)


def conv_grad(d_act, conv):
    sig = sigmoid(conv)
    return d_act * (sig * (1.0 + conv * (1.0 - sig)))


class Stream:
    def __init__(self, view, slots, sems):
        self.view, self.slots, self.sems = view, slots, sems

    def copy(self, block, turn):
        slot = lax.rem(turn, 2)
        return pltpu.make_async_copy(self.view(block), self.slots.at[slot], self.sems.at[slot])

    def start(self, block, turn):
        self.copy(block, turn).start()

    def wait(self, block, turn):
        self.copy(block, turn).wait()

    def at(self, turn):
        return self.slots.at[lax.rem(turn, 2)]


class Fold:
    def __init__(self, line, part, got, relay, sent, arrived, relayed):
        self.line, self.part, self.got, self.relay = line, part, got, relay
        self.sent, self.arrived, self.relayed = sent, arrived, relayed
        self.mine = mine = lax.axis_index("head")
        self.merges = line == 4
        low = mine < 2
        self.is_end = (mine == 0) | (mine == line - 1)
        self.end, self.mid = jnp.where(low, 0, 3), jnp.where(low, 1, 2)
        self.next, self.far = jnp.where(low, 2, 1), jnp.where(low, 3, 0)

    def others(self, body):
        @pl.loop(1, self.line)
        def _(n):
            body(lax.rem(self.mine + n, self.line))

    def chunk(self, rows, piece, chunk, to, way):
        return remote(
            self.part(chunk, rows), self.got.at[self.mine, rows], self.sent.at[way, piece],
            self.arrived.at[self.mine, piece], {"head": to},
        )

    def hand(self, rows, piece, chunk, which):
        return remote(
            self.part(chunk, rows), self.relay.at[which, rows], self.sent.at[1 + which, piece],
            self.relayed.at[which, piece], {"head": self.mid},
        )

    def landed(self, rows, piece, source):
        slot = self.got.at[source, rows]
        return remote(slot, slot, self.sent.at[0, piece], self.arrived.at[source, piece], {"head": source})

    def send_far(self, rows, piece):
        if not self.merges:
            if self.line > 1:
                self.others(lambda to: self.chunk(rows, piece, to, to, to).start())
            return

        @pl.when(self.is_end)
        def _():
            self.hand(rows, piece, self.far, 1).start()
            self.hand(rows, piece, self.next, 0).start()

    def send_near(self, rows, piece):
        if self.merges:
            near = jnp.where(self.is_end, self.mid, self.end)
            self.chunk(rows, piece, near, near, 0).start()

    def merge(self, rows, piece):
        if self.merges:

            @pl.when(jnp.logical_not(self.is_end))
            def _():
                for which, chunk in ((1, self.far), (0, self.next)):
                    self.hand(rows, piece, chunk, which).wait_recv()
                    own = self.part(chunk, rows)
                    own[...] = (own[...].astype(WIDE) + self.relay[which, rows].astype(WIDE)).astype(LOW)
                    self.chunk(rows, piece, chunk, chunk, 1 + which).start()

    def drain(self, rows, piece):
        if not self.merges:
            if self.line > 1:
                self.others(lambda to: self.chunk(rows, piece, to, to, to).wait_send())
                self.others(lambda source: self.landed(rows, piece, source).wait_recv())
            return
        for way in range(3):
            self.chunk(rows, piece, self.mid, self.mid, way).wait_send()
        for source in (jnp.where(self.is_end, self.mid, self.end), self.next):
            self.landed(rows, piece, source).wait_recv()

    def total(self, rows, ref):
        sum_ = self.part(self.mine, rows)[...].astype(WIDE)
        if self.merges:
            first = jnp.where(self.is_end, self.mid, self.end)
            return sum_ + ref[first, rows].astype(WIDE) + ref[self.next, rows].astype(WIDE)
        for n in range(1, self.line):
            sum_ = sum_ + ref[lax.rem(self.mine + n, self.line), rows].astype(WIDE)
        return sum_


class Halved:
    def __init__(self, seqs, src, pair, got, sems):
        self.chips, self.src, self.pair, self.got = seqs // 2, src, pair, got
        self.depth = pair.shape[1]
        self.pair_sent, self.pair_got, self.sent, self.arrived = [sems.at[n] for n in range(4)]
        self.me = lax.axis_index("seq")
        self.core = lax.rem(self.me, 2)
        self.chip = lax.div(self.me, 2)

    def rows(self, chip, core):
        return pl.ds(pl.multiple_of((2 * chip + core) * self.depth, self.depth), self.depth)

    def give(self, chip):
        return remote(
            self.src.at[self.rows(chip, 1 - self.core)], self.pair.at[chip], self.pair_sent.at[chip],
            self.pair_got.at[chip], {"seq": 2 * self.chip + 1 - self.core},
        )

    def send(self, chip, slot):
        return remote(
            self.src.at[self.rows(chip, self.core)], self.got.at[slot], self.sent.at[chip], self.arrived.at[slot],
            {"seq": 2 * chip + self.core},
        )

    def kept(self):
        return pltpu.make_async_copy(
            self.src.at[self.rows(self.chip, self.core)], self.got.at[self.chip], self.sent.at[self.chip]
        )

    def begin(self):
        pl.loop(0, self.chips)(lambda chip: self.give(chip).start())

    def combine(self):
        def add(chip):
            rows = self.rows(chip, self.core)
            self.give(chip).wait_recv()
            self.src[rows, :] = (self.src[rows, :].astype(WIDE) + self.pair[chip].astype(WIDE)).astype(LOW)

        @pl.loop(1, self.chips)
        def _(n):
            chip = lax.rem(self.chip + n, self.chips)
            add(chip)
            self.send(chip, self.chip).start()

        add(self.chip)
        self.kept().start()

    def drain(self):
        @pl.loop(1, self.chips)
        def _(n):
            other = lax.rem(self.chip + n, self.chips)
            self.send(other, other).wait()

        self.kept().wait()
        pl.loop(0, self.chips)(lambda chip: self.give(chip).wait_send())


def core_kernel(
    seqs, line, heads, blocks, roomy, flags, give,
    gate_in, part_in, act_in, cum_in, raw_in, local_in, conv_in, pre_in, normed_in, u_in, g_part, r_in, w_in,
    state_in, postnorm, vec, prenorm, kernels, filters, rim,
    out_recv, grad_recv, out_far, dx_far, early_got, dw_got, addr_got, small_got,
    gate_b, part_b, read_b, cum_b, local_b, normed_b, act_b, raw_b, conv_b, pre_b, before_b, u_b, stream_sems,
    r_t, w, ssd_s, din_s, dssd_s, dgate_s, ds_s, starts, q, state, prod, g_buf, out_part, back_slots, back_msg,
    relay, dx_relay, out_near, dx_near, sums,
    totals, gread, ggate, early_low, early_pair, gpost, tiny, d_conv, d_step, after, edge_own, edge_got, ext,
    keep_conv, keep_step, keep_normed, keep_u,
    taps_g, bias_g, dw, dw_low, dw_pair, da_low, da_pair, da_got, da_send, pn, zs_send, zs_got, small, result, fin_send,
    back_sent, back_sem, back_passed, sum_sent, sum_sem, line_sent, line_sem, load_sem, out_sent, out_sem, out_relayed,
    early_sems, dw_sems, da_sems, dx_sent, dx_sem, dx_relayed, edge_sent, edge_sem, zs_sent, zs_sem, da_sent, da_sem, small_sent,
    small_sem, fin_sent, fin_sem, own_sem, weight_sem, residual_sem,
):
    me, mine = lax.axis_index("seq"), lax.axis_index("head")
    inner = r_t.shape[1]
    wide = act_b.shape[2]
    width = out_part.shape[2]
    depth = early_got.shape[1]
    rows = ssd_s.shape[0]
    size = 2 * STATE // line
    g_line = Line(line, g_buf, width, line_sent, line_sem)
    back_plane = Plane(seqs, lambda s: back_slots.at[s], back_sent, back_sem, back_passed, way=-1)
    out_got, dx_got = (out_near, dx_near) if roomy else (out_far, dx_far)

    def group_rows(b):
        return pl.ds(pl.multiple_of(b * GROUP, GROUP), GROUP)

    def rows_of(device):
        return pl.ds(pl.multiple_of(device * depth, depth), depth)

    def shard_of(ref, shard):
        return ref.at[:, pl.ds(pl.multiple_of(shard * width, LANES), width)]

    def by_group(ref, first=0, columns=None):
        if columns is None:
            return lambda b: ref.at[group_rows(b)]
        return lambda b: ref.at[group_rows(b), pl.ds(first, columns)]

    def all_line(body):
        if line > 1:

            @pl.loop(1, line)
            def _(n):
                body(lax.rem(mine + n, line))

    def all_seq(body):
        @pl.loop(1, seqs)
        def _(n):
            body(lax.rem(me + n, seqs))

    def before_rows(b):
        start = jnp.maximum(b * GROUP - HALO, 0)
        return pre_in.at[pl.ds(pl.multiple_of(start, HALO), HALO)]

    views = (
        (by_group(gate_in), gate_b), (by_group(part_in), part_b), (by_group(act_in, inner + STATE, STATE), read_b),
        (by_group(cum_in), cum_b), (lambda b: local_in.at[b], local_b), (by_group(normed_in), normed_b),
        (by_group(act_in), act_b), (by_group(raw_in), raw_b), (by_group(conv_in), conv_b), (by_group(pre_in), pre_b),
        (before_rows, before_b), (by_group(u_in), u_b),
    )
    gate_f, part_f, read_f, cum_f, local_f, normed_f, act_f, raw_f, conv_f, pre_f, before_f, u_f = [
        Stream(view, slots, stream_sems.at[n]) for n, (view, slots) in enumerate(views)
    ]

    def forwards(turn):
        return turn

    def backwards(turn):
        return blocks - 1 - turn

    def begin(streams, order):
        for stream in streams:
            stream.start(order(0), 0)

    def step(streams, order, turn, following):
        @pl.when(turn + 1 < blocks)
        def _():
            for stream in streams:
                stream.start(order(turn + 1), turn + 1)

        if following is not None:
            pl.when(turn + 1 == blocks)(lambda: begin(*following))
        for stream in streams:
            stream.wait(order(turn), turn)

    first_phase = ((gate_f, part_f, read_f, cum_f, local_f), forwards)
    norm_phase = ((gate_f,), forwards)
    gate_phase = ((gate_f, read_f, cum_f), forwards)
    scan_phase = ((gate_f, normed_f, act_f, cum_f, raw_f), forwards)
    last_phase = ((act_f, cum_f, raw_f, conv_f, pre_f, before_f, normed_f, u_f), backwards)

    def each_load(body):
        def load(shard, n):
            return pltpu.make_async_copy(shard_of(g_part, shard), shard_of(g_buf, shard), load_sem.at[n])

        body(load(mine, 0))
        if line > 1:
            pl.when(mine > 0)(lambda: body(load(mine - 1, 1)))
            pl.when(mine < line - 1)(lambda: body(load(mine + 1, 2)))

    def sum_copy(to, slot):
        return remote(sums.at[mine], sums.at[slot], sum_sent.at[to], sum_sem.at[slot], {"head": to})

    early_sum = Halved(seqs, early_low, early_pair, early_got, early_sems)
    dw_sum = Halved(seqs, dw_low, dw_pair, dw_got, dw_sems)
    da_sum = Halved(seqs, da_low, da_pair, da_got, da_sems)
    out_fold = Fold(
        line, lambda z, at: out_part.at[z, at], out_got, relay, out_sent, out_sem, out_relayed
    )
    dx_fold = Fold(
        line, lambda z, at: shard_of(g_buf.at[at], z), dx_got, dx_relay, dx_sent, dx_sem, dx_relayed
    )
    short_piece = (pl.ds(rows - GROUP, GROUP - HALO), blocks - 1)
    edge_piece = (pl.ds(rows - HALO, HALO), blocks)

    def each_piece(body):
        body(*short_piece)

        @pl.loop(1, blocks)
        def _(turn):
            b = blocks - 1 - turn
            body(group_rows(b), b)

        body(*edge_piece)

    def edge_copy(to):
        return remote(edge_own, edge_got, edge_sent, edge_sem, {"seq": to})

    def zs_copy(to, slot):
        return remote(zs_send.at[to], zs_got.at[slot], zs_sent.at[to], zs_sem.at[slot], {"head": to})

    def da_copy(to, slot):
        return remote(da_send.at[to], addr_got.at[slot], da_sent.at[to], da_sem.at[slot], {"head": to})

    def small_copy(to, slot):
        return remote(small, small_got.at[slot], small_sent.at[to], small_sem.at[slot], {"seq": to})

    arrivals = (out_recv, grad_recv)

    def fin_copy(which, to, slot):
        return remote(
            fin_send.at[to], arrivals[which].at[slot], fin_sent.at[which, to], fin_sem.at[which, slot],
            {"seq": to},
        )

    own_copies = {
        "addr": pltpu.make_async_copy(da_send.at[mine], addr_got.at[mine], own_sem.at[0]),
        "small": pltpu.make_async_copy(small, small_got.at[me], own_sem.at[1]),
        "fin0": pltpu.make_async_copy(fin_send.at[me], out_recv.at[me], own_sem.at[2]),
        "fin1": pltpu.make_async_copy(fin_send.at[me], grad_recv.at[me], own_sem.at[3]),
    }

    def route(which):
        def send(to):
            fin_send[to] = result[give[to]]
            fin_copy(which, to, me).start()

        all_seq(send)
        fin_send[me] = result[give[me]]
        own_copies["fin%d" % which].start()

    def fetch(src):
        if not roomy:
            all_line(lambda z: pltpu.make_async_copy(src.at[z], out_part.at[z], load_sem.at[0]).start())
            all_line(lambda z: pltpu.make_async_copy(src.at[z], out_part.at[z], load_sem.at[0]).wait())

    row = lax.broadcasted_iota(jnp.int32, (GROUP, LANES), 0)
    lane = lax.broadcasted_iota(jnp.int32, (GROUP, LANES), 1)
    spread_m, collect = head_rows(inner), head_columns(inner)
    lower_mask = ones_before(BLOCK)
    top, low = slice(0, BLOCK), slice(BLOCK, GROUP)

    def entry_of(b, cum_v):
        gone_on = flags[2 * b] * jnp.where(row < BLOCK, 1.0, flags[2 * b + 1])
        return to_columns(jnp.exp(cum_v) * gone_on, spread_m)

    def carry_of(b, cum_t):
        return jnp.exp(cum_t[:, GROUP - 1 : GROUP]) * (flags[2 * b] * flags[2 * b + 1])

    def row_stats(b):
        stats = jnp.concatenate([totals[b], jnp.zeros((LANES - EDGE, GROUP), WIDE)], axis=0).T
        return lax.rsqrt(stats[:, 0:1] / INNER + EPS), stats[:, 1:2]

    def gated_of(ssd, turn):
        gate_v = gate_f.at(turn)[...]
        return ssd * (gate_v * sigmoid(gate_v))

    begin(*first_phase)
    fetch_r = pltpu.make_async_copy(r_in, r_t, weight_sem.at[0])
    fetch_w = pltpu.make_async_copy(w_in, w, weight_sem.at[1])
    fetch_r.start()
    greet(seqs, line)
    g_line.hop(1, take=False, source=lambda shard: shard_of(g_part, shard))
    each_load(lambda copy: copy.start())
    fetch_w.start()
    state[...] = state_in[...]
    fetch_r.wait()

    def out_part_done(b):
        if out_fold.merges:
            out_fold.send_far(group_rows(b), b)

    @pl.loop(0, blocks)
    def _(b):
        step(*first_phase, b, norm_phase)
        here = group_rows(b)
        cum_v = cum_f.at(b)[...]
        start = state[...]
        starts[b] = start
        ssd = part_f.at(b)[...] + entry_of(b, cum_v) * nt(read_f.at(b)[...], start.astype(LOW))
        ssd_s[here, :] = ssd
        state[...] = carry_columns(carry_of(b, cum_v.T), collect) * start + local_f.at(b)[...]
        out = nt((gated_of(ssd, b) * postnorm[...]).astype(LOW), r_t[...])
        for z in range(line):
            out_part[z, here] = out[:, z * width : (z + 1) * width].astype(LOW)
        out_part_done(b)

    if out_fold.merges:

        @pl.when(out_fold.is_end)
        def _():
            pl.loop(0, blocks)(lambda b: out_fold.send_near(group_rows(b), b))

    for hop in range(2, line):
        g_line.hop(hop)
    each_load(lambda copy: copy.wait())
    g_line.finish(None, range(1, line - 1))
    fetch_w.wait()

    @pl.loop(0, blocks)
    def _(b):
        step(*norm_phase, b, gate_phase)
        here = group_rows(b)
        gated = gated_of(ssd_s[here, :], b)
        d_inner = nn(g_buf[here, :], r_t[...])
        din_s[here, :] = d_inner
        squares = jnp.sum(gated * gated, axis=1, keepdims=True)
        dots = jnp.sum(gated * postnorm[...] * d_inner, axis=1, keepdims=True)
        both = jnp.where(lane == 0, squares, jnp.where(lane == 1, dots, 0.0)).T
        sums[mine, b] = both[:EDGE]

    all_line(lambda to: sum_copy(to, mine).start())
    for ref in (gread, ggate, gpost, state, tiny, taps_g, bias_g, dw, pn):
        ref[...] = jnp.zeros_like(ref)
    prod[...] = jnp.ones_like(prod)
    all_line(lambda other: sum_copy(other, other).wait())
    totals[...] = jnp.sum(sums[...], axis=0)

    if out_fold.merges:

        @pl.when(jnp.logical_not(out_fold.is_end))
        def _():
            @pl.loop(0, blocks)
            def _(b):
                out_fold.merge(group_rows(b), b)

            pl.loop(0, blocks)(lambda b: out_fold.send_near(group_rows(b), b))

    else:
        pl.loop(0, blocks)(lambda b: out_fold.send_far(group_rows(b), b))

    def residual(n):
        at = pl.ds(pl.multiple_of(n * BLOCK, BLOCK), BLOCK)
        columns = pl.ds(pl.multiple_of(mine * width, LANES), width)
        return pltpu.make_async_copy(u_in.at[at, columns], result.at[n], residual_sem.at[n])

    pl.loop(0, 2 * blocks)(lambda n: residual(n).start())

    def norm_back(b, turn):
        here = group_rows(b)
        inv, dot = row_stats(b)
        gate_v = gate_f.at(turn)[...]
        sig = sigmoid(gate_v)
        ssd = ssd_s[here, :]
        return gate_v, sig, ssd, ssd * (gate_v * sig), inv, dot

    @pl.loop(0, blocks)
    def _(b):
        step(*gate_phase, b, scan_phase)
        here = group_rows(b)
        cum_v = cum_f.at(b)[...]
        gate_v, sig, ssd, gated, inv, dot = norm_back(b, b)
        d_inner = din_s[here, :]
        d_gated = (inv * postnorm[...]) * d_inner - gated * (inv * inv * inv / INNER * dot)
        gpost[...] += jnp.sum(d_inner * (gated * inv), axis=0, keepdims=True)
        d_ssd = (d_gated * (gate_v * sig)).astype(LOW)
        dssd_s[here, :] = d_ssd
        dgate_s[here, :] = (d_gated * ssd * sig * (1.0 + gate_v * (1.0 - sig))).astype(LOW)
        query_grad = (d_ssd.astype(WIDE) * entry_of(b, cum_v)).astype(LOW)
        found = tn(query_grad, read_f.at(b)[...])
        q[b] = found
        state[...] += carry_columns(prod[...], collect) * found
        prod[...] = prod[...] * carry_of(b, cum_v.T)

    back_msg[:inner, :] = state[...].astype(LOW)
    back_msg[inner:, :] = jnp.broadcast_to(prod[:HALO], (HALO, STATE)).astype(LOW)
    back_plane.start(back_msg)

    @pl.loop(0, blocks)
    def _(b):
        step(*scan_phase, b, last_phase)
        here = group_rows(b)
        second = flags[2 * b + 1]
        act = act_f.at(b)
        cum_v = cum_f.at(b)[...]
        cum_t = cum_v.T
        steps, _, _ = step_terms(raw_f.at(b)[...], heads)
        steps_t = steps.T
        write = act[:, inner : inner + STATE]
        read_v = act[:, inner + STATE :]
        s00 = jnp.where(lower_mask, nt(read_v[top], write[top]), 0.0)
        s10 = nt(read_v[low], write[top]) * second
        s11 = jnp.where(lower_mask, nt(read_v[low], write[low]), 0.0)

        def decay_of(head, t, s):
            decay = jnp.exp(jnp.minimum(cum_v[t, head : head + 1] - cum_t[head : head + 1, s], 0.0))
            return decay * steps_t[head : head + 1, s]

        ds00 = jnp.zeros((BLOCK, BLOCK), WIDE)
        ds10 = jnp.zeros((BLOCK, BLOCK), WIDE)
        ds11 = jnp.zeros((BLOCK, BLOCK), WIDE)
        for pair in range(inner // LANES):
            columns = slice(pair * LANES, (pair + 1) * LANES)
            values = act[:, columns]
            dys = pair_lanes(dssd_s[here, columns])
            m00, m10, m11 = [], [], []
            for k in range(2):
                head = 2 * pair + k
                l00, l10, l11 = decay_of(head, top, top), decay_of(head, low, top), decay_of(head, low, low)
                m00.append((s00 * l00).astype(LOW))
                m10.append((s10 * l10).astype(LOW))
                m11.append((s11 * l11).astype(LOW))
                ds00 = ds00 + nt(dys[k][top], values[top]) * l00
                ds10 = ds10 + nt(dys[k][low], values[top]) * l10
                ds11 = ds11 + nt(dys[k][low], values[low]) * l11
            v0 = tn(
                jnp.concatenate([m00[0], m10[0], m00[1], m10[1]], axis=0), jnp.concatenate([dys[0], dys[1]], axis=0)
            )
            v1 = tn(
                jnp.concatenate([m11[0], m11[1]], axis=0), jnp.concatenate([dys[0][low], dys[1][low]], axis=0)
            )
            din_s[here, columns] = jnp.concatenate([v0, v1], axis=0)
        ds_s[here, :] = jnp.concatenate(
            [
                jnp.concatenate([jnp.where(lower_mask, ds00, 0.0), jnp.zeros((BLOCK, BLOCK), WIDE)], axis=1),
                jnp.concatenate([ds10 * second, jnp.where(lower_mask, ds11, 0.0)], axis=1),
            ],
            axis=0,
        ).astype(LOW)

        gated, inv = norm_back(b, b)[3:5]
        inner_normed = (gated * inv * postnorm[...]).astype(LOW)
        gread[...] += tn(g_buf[here, :], inner_normed)
        ggate[...] += tn(normed_f.at(b)[...], dgate_s[here, :])

        @pl.when(b == blocks // 2)
        def _():
            back_plane.relay()

    early_low[:, :inner] = gread[...].astype(LOW)
    early_low[:, inner:] = ggate[...].astype(LOW)
    early_sum.begin()
    back_plane.finish(back_msg)
    state[...] = fold_states(back_slots, collect, inner, seqs - 1, me, -1, jnp.zeros((inner, STATE), WIDE))

    early_sum.combine()
    taps = jnp.concatenate([kernels[...], filters[...]], axis=1)
    scale = -jnp.exp(vec[1:2, :])
    through_w = to_columns(jnp.broadcast_to(vec[2:3, :], (EDGE, LANES)), spread_m)[0:1]

    def scan_back(b, turn):
        here = group_rows(b)
        first, second = flags[2 * b], flags[2 * b + 1]
        act, conv = act_f.at(turn), conv_f.at(turn)
        cum_v = cum_f.at(turn)[...]
        steps, sig, ratio = step_terms(raw_f.at(turn)[...], heads)
        last = cum_v[GROUP - 1 : GROUP, :]
        write = act[:, inner : inner + STATE]
        read_v = act[:, inner + STATE :]
        end = state[...]
        end_low = end.astype(LOW)
        start = starts[b]
        state[...] = carry_columns(carry_of(b, cum_v.T), collect) * end + q[b]
        weight = steps * jnp.exp(last - cum_v) * jnp.where(row < BLOCK, second, 1.0)
        weight_w = to_columns(weight, spread_m)
        d_ssd = dssd_s[here, :]
        dy_f = d_ssd.astype(WIDE)
        values_f = act[:, :inner].astype(WIDE)
        d_query = (dy_f * entry_of(b, cum_v)).astype(LOW)
        tail = nt(write, end_low) * weight_w
        whole = din_s[here, :] + tail
        d_conv[:, :inner] = conv_grad(whole + through_w * dy_f, conv[:, :inner])
        packed = (values_f * weight_w).astype(LOW)
        ds = ds_s[here, :]
        d_read = nn(ds, write) + nn(d_query, start.astype(LOW))
        d_write = tn(ds, read_v) + nn(packed, end_low)
        d_conv[:, inner : inner + STATE] = conv_grad(d_write, conv[:, inner : inner + STATE])
        d_conv[:, inner + STATE :] = conv_grad(d_read, conv[:, inner + STATE :])

        own = to_heads(dy_f * values_f, collect)
        r1 = to_heads(dy_f * ssd_s[here, :], collect) - vec[2:3, :] * own
        by_value = to_heads(values_f * whole, collect)
        tail_sum = jnp.sum(tail * values_f, axis=0, keepdims=True)
        tail_row = to_heads(jnp.broadcast_to(tail_sum, (EDGE, inner)), collect)[0:1]
        high, rest = halves(end * start)
        ones = jnp.ones((EDGE, STATE), LOW)
        carry_grad = to_heads(nt(ones, high) + nt(ones, rest), collect)[0:1]
        d_last = tail_row + carry_grad * (jnp.exp(last) * (first * second))
        d_cum = r1 - by_value + jnp.where(row == GROUP - 1, d_last, 0.0)
        d_rate = sum_after(d_cum)
        d_raw = d_rate * scale * sig + by_value * ratio
        d_step[...] = d_raw.astype(LOW)
        tiny[0:1, :] += jnp.sum(d_raw, axis=0, keepdims=True)
        tiny[1:2, :] += jnp.sum(d_rate * steps, axis=0, keepdims=True) * scale
        tiny[2:3, :] += jnp.sum(own, axis=0, keepdims=True)

    def conv_back(ref, count):
        total = taps[TAPS - 1 : TAPS] * ref[pl.ds(0, count), :]
        for tap in range(TAPS - 1):
            total = total + taps[tap : tap + 1] * ref[pl.ds(TAPS - 1 - tap, count), :]
        return total.astype(LOW)

    def input_back(d_pre, step_grad, gate_grad, u_rows):
        d_normed = (
            nt(gate_grad, w[:, :inner])
            + nt(d_pre, w[:, inner : inner + wide])
            + nt(step_grad, w[:, inner + wide :])
        )
        rows_f = u_rows.astype(WIDE)
        inv = lax.rsqrt(jnp.mean(rows_f * rows_f, axis=1, keepdims=True) + EPS)
        gained = d_normed * prenorm[...]
        dot = jnp.sum(gained * rows_f, axis=1, keepdims=True)
        grad = gained * inv - rows_f * (inv * inv * inv / D * dot)
        return grad.astype(LOW), d_normed * (rows_f * inv)

    def rows_back(b, turn, final):
        grad_c = d_conv[...]
        pre_v = pre_f.at(turn)[...].astype(WIDE)
        before = jnp.where(b == 0, rim[...], before_f.at(turn)[HALO - EDGE :, :].astype(WIDE))
        bias_g[...] += jnp.sum(grad_c, axis=0, keepdims=True)
        parts = []
        for half in range(2):
            part_rows = slice(half * BLOCK, (half + 1) * BLOCK)
            tile = grad_c[part_rows]
            ext[0:EDGE, :] = (before if half == 0 else pre_v[BLOCK - EDGE : BLOCK]) * flags[2 * b + half]
            ext[EDGE:, :] = pre_v[part_rows]
            for tap in range(TAPS):
                taps_g[tap : tap + 1, :] += jnp.sum(
                    tile * ext[pl.ds(EDGE - (TAPS - 1) + tap, BLOCK), :], axis=0, keepdims=True
                )
            ext[:BLOCK, :] = tile
            if half == 0:
                ext[BLOCK:, :] = grad_c[BLOCK : BLOCK + EDGE] * flags[2 * b + 1]
            elif final:
                ext[BLOCK:, :] = jnp.zeros((EDGE, wide), WIDE)
            else:
                ext[BLOCK:, :] = after[...] * flags[2 * b + 2]
            parts.append(conv_back(ext, BLOCK))
        d_pre = jnp.concatenate(parts, axis=0)
        step_grad = d_step[...]
        normed_v = normed_f.at(turn)[...]
        u_v = u_f.at(turn)
        done = lax.broadcasted_iota(jnp.int32, (GROUP, 1), 0) < GROUP - HALO
        if final:
            d_pre = jnp.where(done, d_pre, jnp.zeros_like(d_pre))
            keep_conv[:HALO, :] = grad_c[GROUP - HALO :]
            keep_step[...] = step_grad[GROUP - HALO :]
            keep_normed[...] = normed_v[GROUP - HALO :]
            keep_u[...] = u_v[GROUP - HALO :, :]
        dw[:, :wide] += tn(normed_v, d_pre)
        dw[:, wide:] += tn(normed_v, step_grad)
        grad, gain = input_back(d_pre, step_grad, dgate_s[group_rows(b), :], u_v[...])
        pn[...] += jnp.sum(jnp.where(done, gain, 0.0) if final else gain, axis=0, keepdims=True)
        g_buf[group_rows(b), :] = grad
        after[...] = grad_c[0:EDGE]

    def outputs_home():
        pl.loop(0, 2 * blocks)(lambda n: residual(n).wait())
        pl.loop(0, blocks)(lambda b: out_fold.drain(group_rows(b), b))
        fetch(out_far)

        @pl.loop(0, blocks)
        def _(b):
            inv, _ = row_stats(b)
            total = out_fold.total(group_rows(b), out_near if roomy else out_part) * inv
            result[2 * b] = (result[2 * b].astype(WIDE) + total[:BLOCK]).astype(LOW)
            result[2 * b + 1] = (result[2 * b + 1].astype(WIDE) + total[BLOCK:]).astype(LOW)

        route(0)
        own_g.start()

    own_g = pltpu.make_async_copy(shard_of(g_part, mine), out_part.at[mine], load_sem.at[3])

    step(*last_phase, 0, None)
    scan_back(blocks - 1, 0)
    rows_back(blocks - 1, 0, True)
    dx_fold.send_far(*short_piece)

    @pl.loop(1, blocks)
    def _(turn):
        b = blocks - 1 - turn
        step(*last_phase, turn, None)
        scan_back(b, turn)

        @pl.when(b == 0)
        def _():
            edge_own[...] = d_conv[0:EDGE, :]
            edge_copy(lax.rem(me + seqs - 1, seqs)).start()

        rows_back(b, turn, False)
        dx_fold.send_far(group_rows(b), b)

        @pl.when(turn == 2)
        def _():
            dx_fold.merge(*short_piece)

        pl.when(turn == max(blocks // 2, 1))(outputs_home)

        @pl.when(turn > 2)
        def _():
            dx_fold.merge(group_rows(b + 2), b + 2)

    edge_copy(lax.rem(me + 1, seqs)).wait()
    keep_conv[HALO:, :] = edge_got[...] * flags[2 * blocks]
    d_edge = conv_back(keep_conv, HALO)
    dw[:, :wide] += tn(keep_normed[...], d_edge)
    grad, gain = input_back(d_edge, keep_step[...], dgate_s[pl.ds(rows - HALO, HALO), :], keep_u[...])
    pn[...] += jnp.sum(gain, axis=0, keepdims=True)
    g_buf[pl.ds(rows - HALO, HALO), :] = grad
    dx_fold.send_far(*edge_piece)
    each_piece(dx_fold.send_near)

    if blocks > 3:
        dx_fold.merge(group_rows(1), 1)

    da_low[...] = dw[:, inner:wide].astype(LOW)
    da_sum.begin()
    dw_low[:, :inner] = dw[:, :inner].astype(LOW)
    dw_low[:, inner:] = dw[:, wide:].astype(LOW)
    dw_sum.begin()

    for z in range(line):
        slab = z * size // LANES * LANES
        zs_send[z] = jnp.zeros(zs_send.shape[1:], WIDE)
        zs_send[z, 0:1, :] = pn[:, z * width : (z + 1) * width]
        zs_send[z, EDGE : EDGE + TAPS, :LANES] = taps_g[0:TAPS, inner + slab : inner + slab + LANES]
        zs_send[z, EDGE + TAPS : EDGE + TAPS + 1, :LANES] = bias_g[:, inner + slab : inner + slab + LANES]
    zs_got[mine] = zs_send[mine]
    all_line(lambda to: zs_copy(to, mine).start())

    if blocks > 3:
        dx_fold.merge(group_rows(0), 0)
    elif blocks == 2:
        dx_fold.merge(*short_piece)
        dx_fold.merge(group_rows(0), 0)
    dx_fold.merge(*edge_piece)
    da_sum.combine()
    dw_sum.combine()

    da_sum.drain()
    from_plane = da_got[0].astype(WIDE)
    for n in range(1, seqs // 2):
        from_plane = from_plane + da_got[n].astype(WIDE)
    for z in range(line):
        slab = z * size // LANES * LANES
        da_send[z] = from_plane[:, slab : slab + LANES]
    own_copies["addr"].start()
    all_line(lambda to: da_copy(to, mine).start())

    all_seq(lambda other: fin_copy(0, other, other).wait())
    own_copies["fin0"].wait()
    each_piece(dx_fold.drain)
    fetch(dx_far)
    own_g.wait()

    @pl.loop(0, blocks)
    def _(b):
        here = group_rows(b)
        total = dx_fold.total(here, dx_near if roomy else out_part)
        done = (out_part[mine, here].astype(WIDE) + total).astype(LOW)
        result[2 * b] = done[:BLOCK]
        result[2 * b + 1] = done[BLOCK:]

    route(1)
    all_line(lambda other: zs_copy(other, other).wait())
    from_line = jnp.sum(zs_got[...], axis=0)
    small[...] = jnp.zeros_like(small)
    small[0:TAPS, :inner] = taps_g[0:TAPS, :inner]
    small[0:TAPS, inner:] = from_line[EDGE : EDGE + TAPS, :LANES]
    small[4:5, :inner] = bias_g[:, :inner]
    small[4:5, inner:] = from_line[EDGE + TAPS : EDGE + TAPS + 1, :LANES]
    small[5:6, :inner] = gpost[...]
    small[6:7, :width] = from_line[0:1]
    for n in range(3):
        small[7:8, n * LANES : (n + 1) * LANES] = tiny[n : n + 1, :]
    own_copies["small"].start()
    all_seq(lambda to: small_copy(to, me).start())

    early_sum.drain()
    dw_sum.drain()
    all_line(lambda other: da_copy(other, other).wait())
    all_seq(lambda other: fin_copy(1, other, other).wait())
    all_seq(lambda other: small_copy(other, other).wait())
    for name in ("addr", "small", "fin1"):
        own_copies[name].wait()


def core(
    flags, give, gate, part, act, cum, raw, local, conv, pre, normed, u, g_part, state_in, r_t, w_all, postnorm, vec,
    prenorm, kernels, filters, rim,
):
    seqs, line = lax.axis_size("seq"), lax.axis_size("head")
    rows, inner = gate.shape
    wide = act.shape[1]
    total = g_part.shape[1]
    width = total // line
    depth = total // seqs
    blocks, tiles = rows // GROUP, rows // BLOCK
    heads = inner // HDIM
    pieces = blocks + 1
    message = (inner + HALO, STATE)
    sums = (blocks, EDGE, GROUP)
    streamed = (gate, part, act, cum, raw, local, conv, pre, normed, u, g_part, r_t, w_all)
    whole = (state_in, postnorm, vec, prenorm, kernels, filters, rim)
    gather = (line, rows, width)
    nothing = (line, HALO, width)
    roomy = rows * total * 2 <= 4 << 20
    near, far = (gather, nothing) if roomy else (nothing, gather)
    relay = (2, rows if line == 4 else HALO, width)
    small = (EDGE, inner + LANES)
    ways = max(line, 3)

    def slots(*dims):
        return (2,) + dims

    buffers = (
        (slots(GROUP, inner), WIDE), (slots(GROUP, inner), WIDE), (slots(GROUP, STATE), LOW),
        (slots(GROUP, LANES), WIDE), (slots(inner, STATE), WIDE), (slots(GROUP, total), LOW),
        (slots(GROUP, wide), LOW), (slots(GROUP, LANES), WIDE), (slots(GROUP, wide), WIDE),
        (slots(GROUP, wide), LOW), (slots(HALO, wide), LOW), (slots(GROUP, total), LOW),
    )
    return pl.pallas_call(
        functools.partial(core_kernel, seqs, line, heads, blocks, roomy),
        grid=(1,),
        out_shape=(
            shape((seqs, BLOCK, width), LOW), shape((seqs, BLOCK, width), LOW), shape(far, LOW), shape(far, LOW),
            shape((seqs // 2, depth, 2 * inner), LOW), shape((seqs // 2, depth, inner + LANES), LOW),
            shape((line, depth, LANES), WIDE), shape((seqs,) + small, WIDE),
        ),
        in_specs=[SMEM_SPEC] * 2 + [ANY_SPEC] * len(streamed) + [fixed(a.shape) for a in whole],
        out_specs=(ANY_SPEC,) * 8,
        scratch_shapes=[pltpu.VMEM(dims, kind) for dims, kind in buffers] + [
            DMA((len(buffers), 2)),
            pltpu.VMEM(r_t.shape, LOW), pltpu.VMEM(w_all.shape, LOW),
            pltpu.VMEM((rows, inner), WIDE), pltpu.VMEM((rows, inner), WIDE), pltpu.VMEM((rows, inner), LOW),
            pltpu.VMEM((rows, inner), LOW), pltpu.VMEM((rows, GROUP), LOW), pltpu.VMEM((blocks, inner, STATE), WIDE),
            pltpu.VMEM((blocks, inner, STATE), WIDE), pltpu.VMEM((inner, STATE), WIDE), pltpu.VMEM((LANES, 1), WIDE),
            pltpu.VMEM((rows, total), LOW), pltpu.VMEM(gather, LOW),
            pltpu.VMEM((seqs,) + message, LOW), pltpu.VMEM(message, LOW),
            pltpu.VMEM(relay, LOW), pltpu.VMEM(relay, LOW), pltpu.VMEM(near, LOW), pltpu.VMEM(near, LOW),
            pltpu.VMEM((line,) + sums, WIDE), pltpu.VMEM(sums, WIDE),
            pltpu.VMEM((total, inner), WIDE), pltpu.VMEM((total, inner), WIDE), pltpu.VMEM((total, 2 * inner), LOW),
            pltpu.VMEM((seqs // 2, depth, 2 * inner), LOW), pltpu.VMEM((1, inner), WIDE), pltpu.VMEM((EDGE, LANES), WIDE),
            pltpu.VMEM((GROUP, wide), WIDE), pltpu.VMEM((GROUP, LANES), LOW), pltpu.VMEM((EDGE, wide), WIDE),
            pltpu.VMEM((EDGE, wide), WIDE), pltpu.VMEM((EDGE, wide), WIDE), pltpu.VMEM((BLOCK + EDGE, wide), WIDE),
            pltpu.VMEM((HALO + EDGE, wide), WIDE), pltpu.VMEM((HALO, LANES), LOW), pltpu.VMEM((HALO, total), LOW),
            pltpu.VMEM((HALO, total), LOW),
            pltpu.VMEM((EDGE, wide), WIDE), pltpu.VMEM((1, wide), WIDE), pltpu.VMEM((total, wide + LANES), WIDE),
            pltpu.VMEM((total, inner + LANES), LOW), pltpu.VMEM((seqs // 2, depth, inner + LANES), LOW),
            pltpu.VMEM((total, wide - inner), LOW), pltpu.VMEM((seqs // 2, depth, wide - inner), LOW),
            pltpu.VMEM((seqs // 2, depth, wide - inner), LOW), pltpu.VMEM((line, depth, LANES), WIDE),
            pltpu.VMEM((1, total), WIDE), pltpu.VMEM((line, 2 * EDGE, width), WIDE),
            pltpu.VMEM((line, 2 * EDGE, width), WIDE), pltpu.VMEM(small, WIDE),
            pltpu.VMEM((tiles, BLOCK, width), LOW), pltpu.VMEM((seqs, BLOCK, width), LOW),
            DMA((seqs,)), DMA((seqs,)), DMA((seqs,)), DMA((line,)), DMA((line,)), DMA((2, line)), DMA((line,)), DMA((4,)),
            DMA((ways, blocks)), DMA((line, blocks)), DMA((2, blocks)), DMA((4, seqs // 2)), DMA((4, seqs // 2)), DMA((4, seqs // 2)),
            DMA((ways, pieces)), DMA((line, pieces)), DMA((2, pieces)), DMA, DMA,
            DMA((line,)), DMA((line,)), DMA((line,)), DMA((line,)), DMA((seqs,)), DMA((seqs,)), DMA((2, seqs)),
            DMA((2, seqs)), DMA((4,)), DMA((2,)), DMA((tiles,)),
        ],
        compiler_params=pltpu.CompilerParams(
            collective_id=1, has_side_effects=True, vmem_limit_bytes=VMEM_LIMIT, dimension_semantics=("arbitrary",)
        ),
        name="core",
    )(flags, give, *streamed, *whole)


def finish_kernel(
    take, out_recv, grad_recv, early_got, dw_got, addr_got, small_got,
    out_o, dx_o, prenorm_o, gate_o, pay_o, addr_o, step_o, kernels_o, offsets_o, filters_o, shifts_o,
    stepbias_o, decays_o, through_o, post_o, read_o,
):
    inner, size, heads, width = gate_o.shape[1], addr_o.shape[0], step_o.shape[0], prenorm_o.shape[1]
    offset = lax.rem(lax.axis_index("head") * size, LANES)
    back_turn = lax.rem(LANES - offset, LANES)
    for k in range(out_o.shape[0]):
        out_o[k] = out_recv[take[k]]
        dx_o[k] = grad_recv[take[k]]

    def summed(ref):
        total = ref[0].astype(WIDE)
        for n in range(1, ref.shape[0]):
            total = total + ref[n].astype(WIDE)
        return total

    early = summed(early_got)
    read_o[...] = early[:, :inner].T
    gate_o[...] = early[:, inner:]
    grads = summed(dw_got)
    pay_o[...] = grads[:, :inner]
    step_o[...] = grads[:, inner:].T[:heads]
    addr_o[...] = pltpu.roll(summed(addr_got), back_turn, 1).T[:size]
    totals = jnp.sum(small_got[...], axis=0)
    kernels_o[...] = totals[0:TAPS, :inner]
    offsets_o[...] = totals[4:5, :inner]
    turned = pltpu.roll(totals[:, inner:], back_turn, 1)
    filters_o[...] = turned[0:TAPS, :size]
    shifts_o[...] = turned[4:5, :size]
    post_o[...] = totals[5:6, :inner]
    prenorm_o[...] = totals[6:7, :width]
    for n, ref in enumerate((stepbias_o, decays_o, through_o)):
        ref[...] = totals[7:8, n * LANES : n * LANES + heads]


def finish(take, out_recv, grad_recv, early_got, dw_got, addr_got, small_got):
    seqs, _, width = out_recv.shape
    tiles = take.shape[0]
    _, depth, inner = early_got.shape
    inner = inner // 2
    heads = inner // HDIM
    size = 2 * STATE // addr_got.shape[0]
    operands = (out_recv, grad_recv, early_got, dw_got, addr_got, small_got)
    outs = (
        shape((tiles, BLOCK, width), LOW), shape((tiles, BLOCK, width), LOW), shape((1, width), WIDE),
        shape((depth, inner), WIDE), shape((depth, inner), WIDE), shape((size, depth), WIDE),
        shape((heads, depth), WIDE), shape((TAPS, inner), WIDE), shape((1, inner), WIDE),
        shape((TAPS, size), WIDE), shape((1, size), WIDE), shape((1, heads), WIDE), shape((1, heads), WIDE),
        shape((1, heads), WIDE), shape((1, inner), WIDE), shape((inner, depth), WIDE),
    )
    return pl.pallas_call(
        finish_kernel,
        grid=(1,),
        out_shape=outs,
        in_specs=[SMEM_SPEC] + [fixed(a.shape) for a in operands],
        out_specs=tuple(fixed(a.shape) for a in outs),
        compiler_params=pltpu.CompilerParams(vmem_limit_bytes=VMEM_LIMIT, dimension_semantics=("arbitrary",)),
        name="finish",
    )(take, *operands)


def on_device(
    inputs,
    cotangent,
    lengths,
    placement,
    prenorm,
    gating,
    payload,
    address,
    stepping,
    kernels,
    offsets,
    filters,
    shifts,
    stepbias,
    decays,
    through,
    postnorm,
    readout,
):
    rows, width = inputs.shape
    heads = stepbias.shape[0]
    tiles = rows // BLOCK
    give_in, take_in, give_out, take_out, flags, vec = index(placement, lengths, stepbias, decays, through, tiles)
    gain, post = prenorm[None, :], postnorm[None, :]
    (
        u, normed, gate, pre, conv, act, raw, cum, part, local, state_in, rim, g_part, w_all, r_t
    ) = front(
        give_in, take_in, flags, inputs, cotangent, gating, payload, address, stepping, readout, vec, gain, kernels,
        filters, offsets[None, :], shifts[None, :]
    )
    out_recv, grad_recv, _, _, early_got, dw_got, addr_got, small_got = core(
        flags, give_out, gate, part, act, cum, raw, local, conv, pre, normed, u, g_part, state_in, r_t, w_all, post, vec,
        gain, kernels, filters, rim
    )
    (
        out, dx, prenorm_g, gate_g, pay_g, addr_g, step_g, kernels_g, offsets_g, filters_g, shifts_g, stepbias_g,
        decays_g, through_g, post_g, read_g,
    ) = finish(take_out, out_recv, grad_recv, early_got, dw_got, addr_got, small_got)
    return (
        out.reshape(rows, width),
        dx.reshape(rows, width),
        prenorm_g.reshape(-1),
        gate_g,
        pay_g,
        addr_g.T,
        step_g.T,
        kernels_g,
        offsets_g.reshape(-1),
        filters_g,
        shifts_g.reshape(-1),
        stepbias_g.reshape(-1),
        decays_g.reshape(-1),
        through_g.reshape(-1),
        post_g.reshape(-1),
        read_g,
    )


def solution(mesh):
    in_specs = (
        P("seq", "head"),
        P("seq", "head"),
        P(),
        P(),
        P(),
        P("seq", "head"),
        P("seq", "head"),
        P("seq", None),
        P("seq", "head"),
        P(None, "head"),
        P("head"),
        P(),
        P(),
        P("head"),
        P("head"),
        P("head"),
        P("head"),
        P("head", "seq"),
    )
    out_specs = (
        P("seq", "head"),
        P("seq", "head"),
        P("head"),
        P("seq", "head"),
        P("seq", "head"),
        P("seq", "head"),
        P("seq", "head"),
        P(None, "head"),
        P("head"),
        P(None, "head"),
        P("head"),
        P("head"),
        P("head"),
        P("head"),
        P("head"),
        P("head", "seq"),
    )
    return jax.shard_map(
        on_device, mesh=mesh, in_specs=in_specs, out_specs=out_specs, check_vma=False
    )
```

```python
import functools

import jax
import jax.numpy as jnp
from jax import lax
from jax.experimental import pallas as pl
from jax.experimental.pallas import tpu as pltpu
from jax.sharding import PartitionSpec as P

D = 1024
GROUP = 256
BLOCK = 128
INNER = 2048
HDIM = 64
STATE = 128
TAPS = 4
HALO = 16
EDGE = 8
LANES = 128
EPS = 1e-05
MESH = pl.DeviceIdType.MESH
VMEM = pltpu.MemorySpace.VMEM
SMEM = pltpu.MemorySpace.SMEM
DMA = pltpu.SemaphoreType.DMA
VMEM_LIMIT = 63 << 20
LOW = jnp.bfloat16
WIDE = jnp.float32


def shape(dims, kind):
    return jax.ShapeDtypeStruct(dims, kind)


def nn(a, b):
    return jnp.dot(a, b, preferred_element_type=WIDE)


def nt(a, b):
    return lax.dot_general(a, b, (((1,), (1,)), ((), ())), preferred_element_type=WIDE)


def tn(a, b):
    return lax.dot_general(a, b, (((0,), (0,)), ((), ())), preferred_element_type=WIDE)


def halves(x):
    high = x.astype(LOW)
    return high, (x - high.astype(WIDE)).astype(LOW)


def thirds(x):
    high = x.astype(LOW)
    rest = x - high.astype(WIDE)
    middle = rest.astype(LOW)
    return high, middle, (rest - middle.astype(WIDE)).astype(LOW)


def head_rows(inner):
    row = lax.broadcasted_iota(jnp.int32, (LANES, inner), 0)
    column = lax.broadcasted_iota(jnp.int32, (LANES, inner), 1)
    return jnp.where(column // HDIM == row, 1.0, 0.0).astype(LOW)


def head_columns(inner):
    row = lax.broadcasted_iota(jnp.int32, (inner, LANES), 0)
    column = lax.broadcasted_iota(jnp.int32, (inner, LANES), 1)
    return jnp.where(row // HDIM == column, 1.0, 0.0).astype(LOW)


def to_columns(x, spread):
    high, rest = halves(x)
    return nn(high, spread) + nn(rest, spread)


def to_heads(x, collect):
    high, rest = halves(x)
    return nn(high, collect) + nn(rest, collect)


def ones_before(count):
    row = lax.broadcasted_iota(jnp.int32, (count, count), 0)
    column = lax.broadcasted_iota(jnp.int32, (count, count), 1)
    return row >= column


def sum_before(x):
    matrix = jnp.where(ones_before(x.shape[0]), 1.0, 0.0).astype(LOW)
    high, middle, low = thirds(x)
    return nn(matrix, high) + (nn(matrix, middle) + nn(matrix, low))


def sum_after(x):
    count = x.shape[0]
    row = lax.broadcasted_iota(jnp.int32, (count, count), 0)
    column = lax.broadcasted_iota(jnp.int32, (count, count), 1)
    matrix = jnp.where(row <= column, 1.0, 0.0).astype(LOW)
    high, middle, low = thirds(x)
    return nn(matrix, high) + (nn(matrix, middle) + nn(matrix, low))


def sigmoid(x):
    return 0.5 * jnp.tanh(0.5 * x) + 0.5


def step_terms(raw, heads):
    z = jnp.exp(-jnp.abs(raw))
    series = 1.0 - z * (0.5 - z * (1.0 / 3.0 - z * (0.25 - z * 0.2)))
    small = z < 0.03
    log1p = jnp.where(small, z * series, jnp.log(1.0 + z))
    soft = jnp.maximum(raw, 0.0) + log1p
    one = 1.0 / (1.0 + z)
    sig = jnp.where(raw >= 0, one, z * one)
    ratio = jnp.where(small & (raw < 0), one / series, sig / jnp.maximum(soft, 1e-20))
    lane = lax.broadcasted_iota(jnp.int32, raw.shape, 1)
    return jnp.where(lane < heads, soft, 0.0), sig, ratio


def greet(seq_peers, head_peers, corners=False):
    barrier = pltpu.get_barrier_semaphore()
    count = 0
    if seq_peers > 1:
        me = lax.axis_index("seq")

        @pl.loop(1, seq_peers)
        def _(i):
            pl.semaphore_signal(
                barrier, inc=1, device_id={"seq": lax.rem(me + i, seq_peers)}, device_id_type=MESH
            )

        count += seq_peers - 1
    if head_peers > 1:
        mine = lax.axis_index("head")

        @pl.loop(1, head_peers)
        def _(i):
            pl.semaphore_signal(
                barrier, inc=1, device_id={"head": lax.rem(mine + i, head_peers)}, device_id_type=MESH
            )

        count += head_peers - 1
    if corners and head_peers > 1:
        me, mine = lax.axis_index("seq"), lax.axis_index("head")
        for side in (1, seq_peers - 1):

            @pl.loop(1, head_peers)
            def _(i):
                where = {"seq": lax.rem(me + side, seq_peers), "head": lax.rem(mine + i, head_peers)}
                pl.semaphore_signal(barrier, inc=1, device_id=where, device_id_type=MESH)

        count += 2 * (head_peers - 1)
    pl.semaphore_wait(barrier, count)


def remote(src, dst, send_sem, recv_sem, where):
    return pltpu.make_async_remote_copy(
        src_ref=src, dst_ref=dst, send_sem=send_sem, recv_sem=recv_sem, device_id=where, device_id_type=MESH
    )


class Line:
    def __init__(self, count, out, width, send, recv):
        self.count, self.out, self.width, self.send, self.recv = count, out, width, send, recv
        self.me = lax.axis_index("head")

    def view(self, shard):
        return self.out.at[:, pl.ds(pl.multiple_of(shard * self.width, LANES), self.width)]

    def copy(self, src, shard, way, step):
        return remote(
            src, self.view(shard), self.send.at[way, step], self.recv.at[shard], {"head": self.me + (1 - 2 * way)}
        )

    def first(self, own):
        self.pass_on(own, self.me, 0, 0)
        self.pass_on(own, self.me, 1, 0)

    def pass_on(self, src, shard, way, step):
        reach = (self.me < self.count - 1) if way == 0 else (self.me > 0)

        @pl.when(reach)
        def _():
            self.copy(src, shard, way, step).start()

    def hop(self, step, take=True, give=True, source=None):
        for way in (0, 1):
            shard = self.me - step if way == 0 else self.me + step
            there = (shard >= 0) if way == 0 else (shard < self.count)

            @pl.when(there)
            def _():
                if take:
                    self.copy(self.view(shard), shard, way, step).wait_recv()
                if give and step < self.count - 1:
                    self.pass_on(self.view(shard) if source is None else source(shard), shard, way, step)

    def finish(self, own, steps=None):
        for way in (0, 1):
            reach = (self.me < self.count - 1) if way == 0 else (self.me > 0)
            for step in range(self.count - 1) if steps is None else steps:
                shard = self.me - step if way == 0 else self.me + step
                there = (shard >= 0) if way == 0 else (shard < self.count)

                @pl.when(reach & there)
                def _():
                    src = own if step == 0 else self.view(shard)
                    self.copy(src, shard, way, step).wait_send()


class Plane:
    def __init__(self, seqs, view, sent, got, passed, way=0):
        self.chips, self.view, self.sent, self.got, self.passed, self.way = seqs // 2, view, sent, got, passed, way
        self.me = lax.axis_index("seq")
        self.core = lax.rem(self.me, 2)
        self.chip = self.me // 2
        self.mate = self.me + 1 - 2 * self.core

    def forward(self, chip):
        return (chip > self.chip) if self.way == 1 else (chip < self.chip) if self.way == -1 else (chip >= 0)

    def backward(self, chip):
        return (chip < self.chip) if self.way == 1 else (chip > self.chip) if self.way == -1 else (chip >= 0)

    def each_chip(self, body):
        @pl.loop(1, self.chips)
        def _(i):
            body(lax.rem(self.chip + i, self.chips))

    def copy(self, src, source, to, sem):
        return remote(src, self.view(source), sem, self.got.at[source], {"seq": to})

    def start(self, own):
        def send(chip):
            to = 2 * chip + self.core

            @pl.when(self.forward(chip))
            def _():
                self.copy(own, self.me, to, self.sent.at[to]).start()

        self.each_chip(send)
        self.copy(own, self.me, self.mate, self.sent.at[self.mate]).start()

    def relay(self):
        def take(chip):
            source = 2 * chip + self.core

            @pl.when(self.backward(chip))
            def _():
                landed = self.view(source)
                self.copy(landed, source, self.mate, self.passed.at[source]).wait_recv()
                self.copy(landed, source, self.mate, self.passed.at[source]).start()

        self.each_chip(take)

    def finish(self, own):
        def take(chip):
            source = 2 * chip + 1 - self.core

            @pl.when(self.backward(chip))
            def _():
                self.copy(self.view(source), source, self.mate, self.passed.at[source]).wait_recv()

        self.each_chip(take)
        self.copy(self.view(self.mate), self.mate, self.mate, self.sent.at[self.mate]).wait_recv()
        self.copy(own, self.me, self.mate, self.sent.at[self.mate]).wait_send()

        def drain(chip):
            same = 2 * chip + self.core

            @pl.when(self.forward(chip))
            def _():
                self.copy(own, self.me, same, self.sent.at[same]).wait_send()

            @pl.when(self.backward(chip))
            def _():
                self.copy(self.view(same), same, self.mate, self.passed.at[same]).wait_send()

        self.each_chip(drain)


ANY_SPEC = pl.BlockSpec(memory_space=pl.ANY)
VMEM_SPEC = pl.BlockSpec(memory_space=VMEM)
SMEM_SPEC = pl.BlockSpec(memory_space=SMEM)


def index_kernel(
    seqs, tiles, place, lengths, stepbias, decays, through, give_in, take_in, give_out, take_out, flags, vec
):
    me = lax.axis_index("seq")

    @pl.loop(0, seqs * tiles)
    def _(j):
        block = place[j]

        @pl.when(lax.div(block, tiles) == me)
        def _():
            to = lax.div(j, tiles)
            give_in[to] = lax.rem(block, tiles)
            take_out[lax.rem(block, tiles)] = to

    @pl.loop(0, tiles)
    def _(k):
        source = lax.div(place[me * tiles + k], tiles)
        take_in[k] = source
        give_out[source] = k

    @pl.loop(0, tiles + 1)
    def _(k):
        position = (me * tiles + k) * BLOCK
        end = jnp.int32(0)
        border = position == 0
        for n in range(lengths.shape[0]):
            end = end + lengths[n]
            border = border | (position == end)
        flags[k] = jnp.where(border, 0.0, 1.0)

    heads = stepbias.shape[1]
    vec[...] = jnp.zeros_like(vec)
    vec[0:1, :heads] = stepbias[...]
    vec[1:2, :heads] = decays[...]
    vec[2:3, :heads] = through[...]


def index(place, lengths, stepbias, decays, through, tiles):
    seqs = lax.axis_size("seq")
    whole = jnp.int32
    return pl.pallas_call(
        functools.partial(index_kernel, seqs, tiles),
        out_shape=(
            shape((seqs,), whole), shape((tiles,), whole), shape((seqs,), whole), shape((tiles,), whole),
            shape((tiles + 1,), WIDE), shape((EDGE, LANES), WIDE),
        ),
        in_specs=[SMEM_SPEC] * 2 + [VMEM_SPEC] * 3,
        out_specs=(SMEM_SPEC,) * 5 + (VMEM_SPEC,),
        compiler_params=pltpu.CompilerParams(vmem_limit_bytes=VMEM_LIMIT),
        name="index",
    )(place, lengths, stepbias[None, :], decays[None, :], through[None, :])


def blockwise(dims, index):
    return pl.BlockSpec(dims, index)


def fixed(dims):
    return pl.BlockSpec(dims, lambda i: (0,) * len(dims), pipeline_mode=pl.Buffered(1))


def carry_columns(carry_row_t, collect):
    high, middle, low = thirds(jnp.broadcast_to(carry_row_t, (LANES, LANES)))
    return nn(collect, high) + (nn(collect, middle) + nn(collect, low))


def pair_lanes(slab):
    lane = lax.broadcasted_iota(jnp.int32, slab.shape, 1)
    zero = jnp.zeros_like(slab)
    return jnp.where(lane < HDIM, slab, zero), jnp.where(lane >= HDIM, slab, zero)


def fold_states(slots, collect, inner, first, last, step, start):
    def hop(n, state):
        message = slots[first + n * step]
        carry = nn(collect[:, :HALO], message[inner:])
        return carry * state + message[:inner].astype(WIDE)

    return lax.fori_loop(0, (last - first) * step, hop, start)


def front_kernel(
    seqs, line, heads, blocks, chunks, give, take, flags,
    x_in, g_in, gating_in, payload_in, address_in, stepping_in, readout_in,
    vec, prenorm, kernels, filters, offsets, shifts,
    u_o, normed_o, gate_o, pre_o, conv_o, act_o, raw_o, cum_o, part_o, local_o, state_o, rim_o, g_o, w_o, r_o,
    x, g, gating, payload, address, stepping, readout, square,
    send_x, send_g, recv_x, recv_g, work_x, work_g, w_own, r_own, u, w, msg, slots,
    ext, prev, state, prod,
    sent, got, w_sent, w_got, w_passed, r_sent, r_got, r_passed, s_sent, s_got, s_passed, rim_sent, rim_got, own_sem,
    load_sem, line_sent, line_got, g_sent, g_got,
):
    i = pl.program_id(0)
    me, mine = lax.axis_index("seq"), lax.axis_index("head")
    tiles, _, width = x.shape
    rows = tiles * BLOCK
    depth, inner = gating.shape
    wide = pre_o.shape[1]
    part = rows // chunks
    per = blocks // chunks

    def rows_of(device):
        return pl.ds(pl.multiple_of(device * depth, depth), depth)

    def piece(n):
        if isinstance(n, int):
            return pl.ds(n * part, part)
        return pl.ds(pl.multiple_of(n * part, part), part)

    def u_line(n):
        return Line(line, u.at[piece(n)], width, line_sent.at[n], line_got.at[n])

    def own_columns(ref):
        return ref.at[:, pl.ds(pl.multiple_of(mine * width, LANES), width)]

    w_plane = Plane(seqs, lambda s: w.at[rows_of(s)], w_sent, w_got, w_passed)
    r_plane = Plane(seqs, lambda s: r_o.at[rows_of(s)], r_sent, r_got, r_passed)
    s_plane = Plane(seqs, lambda s: slots.at[s], s_sent, s_got, s_passed, way=1)
    g_line = Line(line, g_o, width, g_sent, g_got)
    own_r = pltpu.make_async_copy(r_own, r_o.at[rows_of(me)], own_sem.at[0])
    own_g = pltpu.make_async_copy(work_g, g_line.view(mine), own_sem.at[1])
    save_w = pltpu.make_async_copy(w, w_o, own_sem.at[2])

    def rim_copy(to, shard):
        columns = pl.ds(pl.multiple_of(shard * width, LANES), width)
        return remote(
            work_x.at[pl.ds(rows - HALO, HALO)], u.at[pl.ds(rows, HALO), columns], rim_sent.at[to], rim_got.at[shard],
            {"seq": lax.rem(me + 1, seqs), "head": to},
        )

    def arrange(which, received, work):
        @pl.loop(1, seqs)
        def _(n):
            source = lax.rem(me + n, seqs)
            remote(
                received.at[source], received.at[source], sent.at[which, source], got.at[which, source], {"seq": source}
            ).wait_recv()

        for k in range(tiles):
            work[pl.ds(k * BLOCK, BLOCK), :] = received[take[k]]

    @pl.when(i == 0)
    def _():
        pairs = (
            (x_in, x), (g_in, g), (gating_in, gating), (payload_in, payload), (address_in, address),
            (stepping_in, stepping), (readout_in, readout),
        )
        loads = [pltpu.make_async_copy(src, dst, load_sem.at[n]) for n, (src, dst) in enumerate(pairs)]
        for load in loads:
            load.start()
        greet(seqs, line, corners=True)

        def post(which, source, outgoing, incoming):
            @pl.loop(1, seqs)
            def _(n):
                to = lax.rem(me + n, seqs)
                outgoing[to] = source[give[to]]
                remote(outgoing.at[to], incoming.at[me], sent.at[which, to], got.at[which, me], {"seq": to}).start()

            incoming[me] = source[give[me]]

        loads[0].wait()
        post(0, x, send_x, recv_x)
        for load in loads[1:]:
            load.wait()

        w_own[:, :inner] = gating[...].astype(LOW)
        w_own[:, inner : 2 * inner] = payload[...].astype(LOW)
        state2 = address.shape[1]
        w_own[:, 2 * inner : 2 * inner + state2] = address[...].astype(LOW)
        square[...] = jnp.zeros_like(square)
        square[: stepping.shape[0], :depth] = stepping[...]
        w_own[:, 2 * inner + state2 :] = square[...].T[:depth].astype(LOW)
        r_own[...] = readout[...].T.astype(LOW)
        w[rows_of(me), :] = w_own[...]
        own_r.start()

        arrange(0, recv_x, work_x)

        @pl.loop(0, line)
        def _(n):
            rim_copy(lax.rem(mine + n, line), mine).start()

        for n in range(chunks):
            u_line(n).first(work_x.at[piece(n)])
        w_plane.start(w_own)
        own = pltpu.make_async_copy(work_x, own_columns(u.at[pl.ds(0, rows)]), own_sem.at[3])
        own.start()
        post(1, g, send_g, recv_g)
        r_plane.start(r_own)
        for step in range(1, line - 1):
            for n in range(chunks):
                u_line(n).hop(step)
            if step == 1:
                w_plane.relay()
        own.wait()

        @pl.loop(0, line)
        def _(n):
            rim_copy(n, n).wait_recv()

        arrange(1, recv_g, work_g)
        g_line.first(work_g)
        own_g.start()
        w_plane.finish(w_own)
        save_w.start()

    if line > 1:

        @pl.when(lax.rem(i, per) == 0)
        def _():
            u_line(lax.div(i, per)).hop(line - 1)

    taps = jnp.concatenate([kernels[...], filters[...]], axis=1)
    bias = jnp.concatenate([offsets[...], shifts[...]], axis=1)
    spread_m, collect = head_rows(inner), head_columns(inner)

    def normalize(block):
        wide_rows = block.astype(WIDE)
        scale = lax.rsqrt(jnp.mean(wide_rows * wide_rows, axis=1, keepdims=True) + EPS)
        return (wide_rows * scale * prenorm[...]).astype(LOW)

    @pl.when(i == 0)
    def _():
        before = nn(normalize(u[pl.ds(rows, HALO), :]), w[:, inner : inner + wide]).astype(LOW).astype(WIDE)
        prev[...] = before[HALO - EDGE :]
        rim_o[...] = before[HALO - EDGE :]
        state[...] = jnp.zeros_like(state)
        prod[...] = jnp.ones_like(prod)

    u_v = u[pl.ds(pl.multiple_of(i * GROUP, GROUP), GROUP), :]
    u_o[...] = u_v
    normed = normalize(u_v)
    normed_o[...] = normed
    gate_o[...] = nn(normed, w[:, :inner])
    pre = nn(normed, w[:, inner : inner + wide]).astype(LOW)
    pre_o[...] = pre
    lane = lax.broadcasted_iota(jnp.int32, (GROUP, LANES), 1)
    raw = jnp.where(lane < heads, nn(normed, w[:, inner + wide :]) + vec[0:1, :], 0.0)
    raw_o[...] = raw
    first, second = flags[2 * i], flags[2 * i + 1]
    same = (first, second)
    for half in range(2):
        at = pl.ds(half * BLOCK, BLOCK)
        ext[0:EDGE, :] = prev[...] * same[half]
        ext[EDGE:, :] = pre[half * BLOCK : (half + 1) * BLOCK].astype(WIDE)
        prev[...] = ext[BLOCK:, :]
        total = bias + taps[TAPS - 1 : TAPS] * ext[EDGE:, :]
        for tap in range(TAPS - 1):
            total = total + taps[tap : tap + 1] * ext[pl.ds(EDGE - (TAPS - 1) + tap, BLOCK), :]
        conv_o[at, :] = total
        act_o[at, :] = (total * sigmoid(total)).astype(LOW)

    steps, _, _ = step_terms(raw, heads)
    scale = -jnp.exp(vec[1:2, :])
    cum = sum_before(steps * scale)
    cum_o[...] = cum
    cum_t, steps_t = cum.T, steps.T
    write = act_o[:, inner : inner + STATE]
    read = act_o[:, inner + STATE :]
    lower = ones_before(BLOCK)
    top, low = slice(0, BLOCK), slice(BLOCK, GROUP)
    s00 = jnp.where(lower, nt(read[top], write[top]), 0.0)
    s10 = nt(read[low], write[top]) * second
    s11 = jnp.where(lower, nt(read[low], write[low]), 0.0)

    def mix(scores, head, t, s):
        decay = jnp.exp(jnp.minimum(cum[t, head : head + 1] - cum_t[head : head + 1, s], 0.0))
        return (scores * (decay * steps_t[head : head + 1, s])).astype(LOW)

    last = cum[GROUP - 1 : GROUP, :]
    row = lax.broadcasted_iota(jnp.int32, (GROUP, LANES), 0)
    weight = steps * jnp.exp(last - cum) * jnp.where(row < BLOCK, second, 1.0)
    weight_w = to_columns(weight, spread_m)
    skip = to_columns(jnp.broadcast_to(vec[2:3, :], (EDGE, LANES)), spread_m)[0:1]
    packed = []
    for pair in range(inner // LANES):
        columns = slice(pair * LANES, (pair + 1) * LANES)
        slab = act_o[:, columns]
        slab_f = slab.astype(WIDE)
        ones = pair_lanes(slab)
        h0, h1 = 2 * pair, 2 * pair + 1
        y0 = nn(
            jnp.concatenate([mix(s00, h0, top, top), mix(s00, h1, top, top)], axis=1),
            jnp.concatenate([ones[0][top], ones[1][top]], axis=0),
        )
        y1 = nn(
            jnp.concatenate(
                [mix(s10, h0, low, top), mix(s11, h0, low, low), mix(s10, h1, low, top), mix(s11, h1, low, low)], axis=1
            ),
            jnp.concatenate([ones[0], ones[1]], axis=0),
        )
        part_o[top, columns] = y0 + skip[:, columns] * slab_f[top]
        part_o[low, columns] = y1 + skip[:, columns] * slab_f[low]
        packed.append((slab_f * weight_w[:, columns]).astype(LOW))
    local = tn(jnp.concatenate(packed, axis=1), write)
    local_o[0] = local
    carry = jnp.exp(cum_t[:, GROUP - 1 : GROUP]) * (first * second)
    state[...] = carry_columns(carry, collect) * state[...] + local
    prod[...] = jnp.broadcast_to(carry[:HALO], (HALO, STATE)) * prod[...]

    @pl.when(i == blocks - 1)
    def _():
        msg[:inner, :] = state[...].astype(LOW)
        msg[inner:, :] = prod[...].astype(LOW)
        s_plane.start(msg)
        s_plane.relay()
        s_plane.finish(msg)
        state_o[...] = fold_states(slots, collect, inner, 0, me, 1, jnp.zeros((inner, STATE), WIDE))
        r_plane.relay()
        r_plane.finish(r_own)
        if line > 1:
            g_line.hop(1, give=False)
        g_line.finish(work_g, (0,))
        for n in range(chunks):
            u_line(n).finish(work_x.at[piece(n)])

        @pl.loop(0, line)
        def _(n):
            rim_copy(n, mine).wait_send()


        @pl.loop(1, seqs)
        def _(n):
            other = lax.rem(me + n, seqs)
            for which, buffer in ((0, send_x), (1, send_g)):
                remote(
                    buffer.at[other], buffer.at[other], sent.at[which, other], got.at[which, other], {"seq": other}
                ).wait_send()

        own_r.wait()
        own_g.wait()
        save_w.wait()


def front(give, take, flags, x, g, gating, payload, address, stepping, readout, vec, prenorm, kernels, filters, offsets, shifts):
    seqs, line = lax.axis_size("seq"), lax.axis_size("head")
    rows, width = x.shape
    depth, inner = gating.shape
    total = depth * seqs
    wide = inner + address.shape[1]
    columns = inner + wide + LANES
    blocks = rows // GROUP
    chunks = min(blocks, 4)
    heads = stepping.shape[1]
    routed = (seqs, BLOCK, width)
    given = (rows // BLOCK, BLOCK, width)
    message = (inner + HALO, STATE)
    operands = (x.reshape(given), g.reshape(given), gating, payload, address, stepping.T, readout)
    small = (vec, prenorm, kernels, filters, offsets, shifts)

    def by_rows(size):
        return blockwise((GROUP, size), lambda i: (i, 0))

    return pl.pallas_call(
        functools.partial(front_kernel, seqs, line, heads, blocks, chunks),
        grid=(blocks,),
        out_shape=(
            shape((rows, total), LOW), shape((rows, total), LOW), shape((rows, inner), WIDE), shape((rows, wide), LOW),
            shape((rows, wide), WIDE), shape((rows, wide), LOW), shape((rows, LANES), WIDE), shape((rows, LANES), WIDE),
            shape((rows, inner), WIDE), shape((blocks, inner, STATE), WIDE), shape((inner, STATE), WIDE),
            shape((EDGE, wide), WIDE), shape((rows, total), LOW), shape((total, columns), LOW),
            shape((total, inner), LOW),
        ),
        in_specs=[SMEM_SPEC] * 3 + [ANY_SPEC] * 7 + [fixed(a.shape) for a in small],
        out_specs=(
            by_rows(total), by_rows(total), by_rows(inner), by_rows(wide), by_rows(wide), by_rows(wide), by_rows(LANES),
            by_rows(LANES), by_rows(inner), blockwise((1, inner, STATE), lambda i: (i, 0, 0)), fixed((inner, STATE)),
            fixed((EDGE, wide)), ANY_SPEC, ANY_SPEC, ANY_SPEC,
        ),
        scratch_shapes=[pltpu.VMEM(a.shape, a.dtype) for a in operands] + [
            pltpu.VMEM((LANES, LANES), WIDE),
            pltpu.VMEM(routed, LOW), pltpu.VMEM(routed, LOW), pltpu.VMEM(routed, LOW), pltpu.VMEM(routed, LOW),
            pltpu.VMEM((rows, width), LOW), pltpu.VMEM((rows, width), LOW),
            pltpu.VMEM((depth, columns), LOW), pltpu.VMEM((depth, inner), LOW),
            pltpu.VMEM((rows + HALO, total), LOW), pltpu.VMEM((total, columns), LOW),
            pltpu.VMEM(message, LOW), pltpu.VMEM((seqs,) + message, LOW),
            pltpu.VMEM((EDGE + BLOCK, wide), WIDE), pltpu.VMEM((EDGE, wide), WIDE),
            pltpu.VMEM((inner, STATE), WIDE), pltpu.VMEM((HALO, STATE), WIDE),
            DMA((2, seqs)), DMA((2, seqs)),
            DMA((seqs,)), DMA((seqs,)), DMA((seqs,)), DMA((seqs,)), DMA((seqs,)), DMA((seqs,)),
            DMA((seqs,)), DMA((seqs,)), DMA((seqs,)), DMA((line,)), DMA((line,)), DMA((4,)), DMA((7,)),
            DMA((chunks, 2, line)), DMA((chunks, line)), DMA((2, line)), DMA((line,)),
        ],
        compiler_params=pltpu.CompilerParams(
            collective_id=0, has_side_effects=True, vmem_limit_bytes=VMEM_LIMIT, dimension_semantics=("arbitrary",)
        ),
        name="front",
    )(give, take, flags, *operands, *small)


def conv_grad(d_act, conv):
    sig = sigmoid(conv)
    return d_act * (sig * (1.0 + conv * (1.0 - sig)))


class Stream:
    def __init__(self, view, slots, sems):
        self.view, self.slots, self.sems = view, slots, sems

    def copy(self, block, turn):
        slot = lax.rem(turn, 2)
        return pltpu.make_async_copy(self.view(block), self.slots.at[slot], self.sems.at[slot])

    def start(self, block, turn):
        self.copy(block, turn).start()

    def wait(self, block, turn):
        self.copy(block, turn).wait()

    def at(self, turn):
        return self.slots.at[lax.rem(turn, 2)]


class Fold:
    def __init__(self, line, part, got, relay, sent, arrived, relayed):
        self.line, self.part, self.got, self.relay = line, part, got, relay
        self.sent, self.arrived, self.relayed = sent, arrived, relayed
        self.mine = mine = lax.axis_index("head")
        self.merges = line == 4
        low = mine < 2
        self.is_end = (mine == 0) | (mine == line - 1)
        self.end, self.mid = jnp.where(low, 0, 3), jnp.where(low, 1, 2)
        self.next, self.far = jnp.where(low, 2, 1), jnp.where(low, 3, 0)

    def others(self, body):
        @pl.loop(1, self.line)
        def _(n):
            body(lax.rem(self.mine + n, self.line))

    def chunk(self, rows, piece, chunk, to, way):
        return remote(
            self.part(chunk, rows), self.got.at[self.mine, rows], self.sent.at[way, piece],
            self.arrived.at[self.mine, piece], {"head": to},
        )

    def hand(self, rows, piece, chunk, which):
        return remote(
            self.part(chunk, rows), self.relay.at[which, rows], self.sent.at[1 + which, piece],
            self.relayed.at[which, piece], {"head": self.mid},
        )

    def landed(self, rows, piece, source):
        slot = self.got.at[source, rows]
        return remote(slot, slot, self.sent.at[0, piece], self.arrived.at[source, piece], {"head": source})

    def send_far(self, rows, piece):
        if not self.merges:
            if self.line > 1:
                self.others(lambda to: self.chunk(rows, piece, to, to, to).start())
            return

        @pl.when(self.is_end)
        def _():
            self.hand(rows, piece, self.far, 1).start()
            self.hand(rows, piece, self.next, 0).start()

    def send_near(self, rows, piece):
        if self.merges:
            near = jnp.where(self.is_end, self.mid, self.end)
            self.chunk(rows, piece, near, near, 0).start()

    def merge(self, rows, piece):
        if self.merges:

            @pl.when(jnp.logical_not(self.is_end))
            def _():
                for which, chunk in ((1, self.far), (0, self.next)):
                    self.hand(rows, piece, chunk, which).wait_recv()
                    own = self.part(chunk, rows)
                    own[...] = (own[...].astype(WIDE) + self.relay[which, rows].astype(WIDE)).astype(LOW)
                    self.chunk(rows, piece, chunk, chunk, 1 + which).start()

    def drain(self, rows, piece):
        if not self.merges:
            if self.line > 1:
                self.others(lambda to: self.chunk(rows, piece, to, to, to).wait_send())
                self.others(lambda source: self.landed(rows, piece, source).wait_recv())
            return
        for way in range(3):
            self.chunk(rows, piece, self.mid, self.mid, way).wait_send()
        for source in (jnp.where(self.is_end, self.mid, self.end), self.next):
            self.landed(rows, piece, source).wait_recv()

    def total(self, rows, ref):
        sum_ = self.part(self.mine, rows)[...].astype(WIDE)
        if self.merges:
            first = jnp.where(self.is_end, self.mid, self.end)
            return sum_ + ref[first, rows].astype(WIDE) + ref[self.next, rows].astype(WIDE)
        for n in range(1, self.line):
            sum_ = sum_ + ref[lax.rem(self.mine + n, self.line), rows].astype(WIDE)
        return sum_


class Halved:
    def __init__(self, seqs, src, pair, got, sems):
        self.chips, self.src, self.pair, self.got = seqs // 2, src, pair, got
        self.depth = pair.shape[1]
        self.pair_sent, self.pair_got, self.sent, self.arrived = [sems.at[n] for n in range(4)]
        self.me = lax.axis_index("seq")
        self.core = lax.rem(self.me, 2)
        self.chip = lax.div(self.me, 2)

    def rows(self, chip, core):
        return pl.ds(pl.multiple_of((2 * chip + core) * self.depth, self.depth), self.depth)

    def give(self, chip):
        return remote(
            self.src.at[self.rows(chip, 1 - self.core)], self.pair.at[chip], self.pair_sent.at[chip],
            self.pair_got.at[chip], {"seq": 2 * self.chip + 1 - self.core},
        )

    def send(self, chip, slot):
        return remote(
            self.src.at[self.rows(chip, self.core)], self.got.at[slot], self.sent.at[chip], self.arrived.at[slot],
            {"seq": 2 * chip + self.core},
        )

    def kept(self):
        return pltpu.make_async_copy(
            self.src.at[self.rows(self.chip, self.core)], self.got.at[self.chip], self.sent.at[self.chip]
        )

    def begin(self):
        pl.loop(0, self.chips)(lambda chip: self.give(chip).start())

    def combine(self):
        def add(chip):
            rows = self.rows(chip, self.core)
            self.give(chip).wait_recv()
            self.src[rows, :] = (self.src[rows, :].astype(WIDE) + self.pair[chip].astype(WIDE)).astype(LOW)

        @pl.loop(1, self.chips)
        def _(n):
            chip = lax.rem(self.chip + n, self.chips)
            add(chip)
            self.send(chip, self.chip).start()

        add(self.chip)
        self.kept().start()

    def drain(self):
        @pl.loop(1, self.chips)
        def _(n):
            other = lax.rem(self.chip + n, self.chips)
            self.send(other, other).wait()

        self.kept().wait()
        pl.loop(0, self.chips)(lambda chip: self.give(chip).wait_send())


def core_kernel(
    seqs, line, heads, blocks, roomy, flags, give,
    gate_in, part_in, act_in, cum_in, raw_in, local_in, conv_in, pre_in, normed_in, u_in, g_part, r_in, w_in,
    state_in, postnorm, vec, prenorm, kernels, filters, rim,
    out_recv, grad_recv, out_far, dx_far, early_got, dw_got, addr_got, small_got,
    gate_b, part_b, read_b, cum_b, local_b, normed_b, act_b, raw_b, conv_b, pre_b, before_b, u_b, stream_sems,
    r_t, w, ssd_s, din_s, dssd_s, dgate_s, ds_s, starts, q, state, prod, g_buf, out_part, back_slots, back_msg,
    relay, dx_relay, out_near, dx_near, sums,
    totals, gread, ggate, early_low, early_pair, gpost, tiny, d_conv, d_step, after, edge_own, edge_got, ext,
    keep_conv, keep_step, keep_normed, keep_u,
    taps_g, bias_g, dw, dw_low, dw_pair, da_low, da_pair, da_got, da_send, pn, zs_send, zs_got, small, result, fin_send,
    back_sent, back_sem, back_passed, sum_sent, sum_sem, line_sent, line_sem, load_sem, out_sent, out_sem, out_relayed,
    early_sems, dw_sems, da_sems, dx_sent, dx_sem, dx_relayed, edge_sent, edge_sem, zs_sent, zs_sem, da_sent, da_sem, small_sent,
    small_sem, fin_sent, fin_sem, own_sem, weight_sem, residual_sem,
):
    me, mine = lax.axis_index("seq"), lax.axis_index("head")
    inner = r_t.shape[1]
    wide = act_b.shape[2]
    width = out_part.shape[2]
    depth = early_got.shape[1]
    rows = ssd_s.shape[0]
    size = 2 * STATE // line
    g_line = Line(line, g_buf, width, line_sent, line_sem)
    back_plane = Plane(seqs, lambda s: back_slots.at[s], back_sent, back_sem, back_passed, way=-1)
    out_got, dx_got = (out_near, dx_near) if roomy else (out_far, dx_far)

    def group_rows(b):
        return pl.ds(pl.multiple_of(b * GROUP, GROUP), GROUP)

    def rows_of(device):
        return pl.ds(pl.multiple_of(device * depth, depth), depth)

    def shard_of(ref, shard):
        return ref.at[:, pl.ds(pl.multiple_of(shard * width, LANES), width)]

    def by_group(ref, first=0, columns=None):
        if columns is None:
            return lambda b: ref.at[group_rows(b)]
        return lambda b: ref.at[group_rows(b), pl.ds(first, columns)]

    def all_line(body):
        if line > 1:

            @pl.loop(1, line)
            def _(n):
                body(lax.rem(mine + n, line))

    def all_seq(body):
        @pl.loop(1, seqs)
        def _(n):
            body(lax.rem(me + n, seqs))

    def before_rows(b):
        start = jnp.maximum(b * GROUP - HALO, 0)
        return pre_in.at[pl.ds(pl.multiple_of(start, HALO), HALO)]

    views = (
        (by_group(gate_in), gate_b), (by_group(part_in), part_b), (by_group(act_in, inner + STATE, STATE), read_b),
        (by_group(cum_in), cum_b), (lambda b: local_in.at[b], local_b), (by_group(normed_in), normed_b),
        (by_group(act_in), act_b), (by_group(raw_in), raw_b), (by_group(conv_in), conv_b), (by_group(pre_in), pre_b),
        (before_rows, before_b), (by_group(u_in), u_b),
    )
    gate_f, part_f, read_f, cum_f, local_f, normed_f, act_f, raw_f, conv_f, pre_f, before_f, u_f = [
        Stream(view, slots, stream_sems.at[n]) for n, (view, slots) in enumerate(views)
    ]

    def forwards(turn):
        return turn

    def backwards(turn):
        return blocks - 1 - turn

    def begin(streams, order):
        for stream in streams:
            stream.start(order(0), 0)

    def step(streams, order, turn, following):
        @pl.when(turn + 1 < blocks)
        def _():
            for stream in streams:
                stream.start(order(turn + 1), turn + 1)

        if following is not None:
            pl.when(turn + 1 == blocks)(lambda: begin(*following))
        for stream in streams:
            stream.wait(order(turn), turn)

    first_phase = ((gate_f, part_f, read_f, cum_f, local_f), forwards)
    norm_phase = ((gate_f,), forwards)
    gate_phase = ((gate_f, read_f, cum_f), forwards)
    scan_phase = ((gate_f, normed_f, act_f, cum_f, raw_f), forwards)
    last_phase = ((act_f, cum_f, raw_f, conv_f, pre_f, before_f, normed_f, u_f), backwards)

    def each_load(body):
        def load(shard, n):
            return pltpu.make_async_copy(shard_of(g_part, shard), shard_of(g_buf, shard), load_sem.at[n])

        for n, away in enumerate((0, -1, 1)):
            if abs(away) < line:
                there = (mine + away >= 0) & (mine + away < line)
                pl.when(there)(lambda: body(load(mine + away, n)))

    def sum_copy(to, slot):
        return remote(sums.at[mine], sums.at[slot], sum_sent.at[to], sum_sem.at[slot], {"head": to})

    early_sum = Halved(seqs, early_low, early_pair, early_got, early_sems)
    dw_sum = Halved(seqs, dw_low, dw_pair, dw_got, dw_sems)
    da_sum = Halved(seqs, da_low, da_pair, da_got, da_sems)
    out_fold = Fold(
        line, lambda z, at: out_part.at[z, at], out_got, relay, out_sent, out_sem, out_relayed
    )
    dx_fold = Fold(
        line, lambda z, at: shard_of(g_buf.at[at], z), dx_got, dx_relay, dx_sent, dx_sem, dx_relayed
    )
    short_piece = (pl.ds(rows - GROUP, GROUP - HALO), blocks - 1)
    edge_piece = (pl.ds(rows - HALO, HALO), blocks)

    def each_piece(body):
        body(*short_piece)

        @pl.loop(1, blocks)
        def _(turn):
            b = blocks - 1 - turn
            body(group_rows(b), b)

        body(*edge_piece)

    def edge_copy(to):
        return remote(edge_own, edge_got, edge_sent, edge_sem, {"seq": to})

    def zs_copy(to, slot):
        return remote(zs_send.at[to], zs_got.at[slot], zs_sent.at[to], zs_sem.at[slot], {"head": to})

    def da_copy(to, slot):
        return remote(da_send.at[to], addr_got.at[slot], da_sent.at[to], da_sem.at[slot], {"head": to})

    def small_copy(to, slot):
        return remote(small, small_got.at[slot], small_sent.at[to], small_sem.at[slot], {"seq": to})

    arrivals = (out_recv, grad_recv)

    def fin_copy(which, to, slot):
        return remote(
            fin_send.at[to], arrivals[which].at[slot], fin_sent.at[which, to], fin_sem.at[which, slot],
            {"seq": to},
        )

    own_copies = {
        "addr": pltpu.make_async_copy(da_send.at[mine], addr_got.at[mine], own_sem.at[0]),
        "small": pltpu.make_async_copy(small, small_got.at[me], own_sem.at[1]),
        "fin0": pltpu.make_async_copy(fin_send.at[me], out_recv.at[me], own_sem.at[2]),
        "fin1": pltpu.make_async_copy(fin_send.at[me], grad_recv.at[me], own_sem.at[3]),
    }

    def route(which):
        def send(to):
            fin_send[to] = result[give[to]]
            fin_copy(which, to, me).start()

        all_seq(send)
        fin_send[me] = result[give[me]]
        own_copies["fin%d" % which].start()

    def fetch(src):
        if not roomy:
            all_line(lambda z: pltpu.make_async_copy(src.at[z], out_part.at[z], load_sem.at[0]).start())
            all_line(lambda z: pltpu.make_async_copy(src.at[z], out_part.at[z], load_sem.at[0]).wait())

    row = lax.broadcasted_iota(jnp.int32, (GROUP, LANES), 0)
    lane = lax.broadcasted_iota(jnp.int32, (GROUP, LANES), 1)
    spread_m, collect = head_rows(inner), head_columns(inner)
    lower_mask = ones_before(BLOCK)
    top, low = slice(0, BLOCK), slice(BLOCK, GROUP)

    def entry_of(b, cum_v):
        gone_on = flags[2 * b] * jnp.where(row < BLOCK, 1.0, flags[2 * b + 1])
        return to_columns(jnp.exp(cum_v) * gone_on, spread_m)

    def carry_of(b, cum_t):
        return jnp.exp(cum_t[:, GROUP - 1 : GROUP]) * (flags[2 * b] * flags[2 * b + 1])

    def row_stats(b):
        stats = jnp.concatenate([totals[b], jnp.zeros((LANES - EDGE, GROUP), WIDE)], axis=0).T
        return lax.rsqrt(stats[:, 0:1] / INNER + EPS), stats[:, 1:2]

    def gated_of(ssd, turn):
        gate_v = gate_f.at(turn)[...]
        return ssd * (gate_v * sigmoid(gate_v))

    begin(*first_phase)
    fetch_r = pltpu.make_async_copy(r_in, r_t, weight_sem.at[0])
    fetch_w = pltpu.make_async_copy(w_in, w, weight_sem.at[1])
    fetch_r.start()
    greet(seqs, line)
    g_line.hop(1, take=False, source=lambda shard: shard_of(g_part, shard))
    each_load(lambda copy: copy.start())
    fetch_w.start()
    state[...] = state_in[...]
    fetch_r.wait()

    def out_part_done(b):
        if out_fold.merges:
            out_fold.send_far(group_rows(b), b)

    @pl.loop(0, blocks)
    def _(b):
        step(*first_phase, b, norm_phase)
        here = group_rows(b)
        cum_v = cum_f.at(b)[...]
        start = state[...]
        starts[b] = start
        ssd = part_f.at(b)[...] + entry_of(b, cum_v) * nt(read_f.at(b)[...], start.astype(LOW))
        ssd_s[here, :] = ssd
        state[...] = carry_columns(carry_of(b, cum_v.T), collect) * start + local_f.at(b)[...]
        out = nt((gated_of(ssd, b) * postnorm[...]).astype(LOW), r_t[...])
        for z in range(line):
            out_part[z, here] = out[:, z * width : (z + 1) * width].astype(LOW)
        out_part_done(b)

    for hop in range(2, line):
        g_line.hop(hop)
    each_load(lambda copy: copy.wait())
    g_line.finish(None, range(1, line - 1))
    fetch_w.wait()

    @pl.loop(0, blocks)
    def _(b):
        step(*norm_phase, b, gate_phase)
        here = group_rows(b)
        gated = gated_of(ssd_s[here, :], b)
        d_inner = nn(g_buf[here, :], r_t[...])
        din_s[here, :] = d_inner
        squares = jnp.sum(gated * gated, axis=1, keepdims=True)
        dots = jnp.sum(gated * postnorm[...] * d_inner, axis=1, keepdims=True)
        both = jnp.where(lane == 0, squares, jnp.where(lane == 1, dots, 0.0)).T
        sums[mine, b] = both[:EDGE]

    all_line(lambda to: sum_copy(to, mine).start())
    for ref in (gread, ggate, gpost, state, tiny, taps_g, bias_g, dw, pn):
        ref[...] = jnp.zeros_like(ref)
    prod[...] = jnp.ones_like(prod)
    all_line(lambda other: sum_copy(other, other).wait())
    totals[...] = jnp.sum(sums[...], axis=0)

    if out_fold.merges:
        pl.loop(0, blocks)(lambda b: out_fold.send_near(group_rows(b), b))

    def residual(n):
        at = pl.ds(pl.multiple_of(n * BLOCK, BLOCK), BLOCK)
        columns = pl.ds(pl.multiple_of(mine * width, LANES), width)
        return pltpu.make_async_copy(u_in.at[at, columns], result.at[n], residual_sem.at[n])

    pl.loop(0, 2 * blocks)(lambda n: residual(n).start())

    def norm_back(b, turn):
        here = group_rows(b)
        inv, dot = row_stats(b)
        gate_v = gate_f.at(turn)[...]
        sig = sigmoid(gate_v)
        ssd = ssd_s[here, :]
        return gate_v, sig, ssd, ssd * (gate_v * sig), inv, dot

    @pl.loop(0, blocks)
    def _(b):
        step(*gate_phase, b, scan_phase)
        here = group_rows(b)
        cum_v = cum_f.at(b)[...]
        gate_v, sig, ssd, gated, inv, dot = norm_back(b, b)
        d_inner = din_s[here, :]
        d_gated = (inv * postnorm[...]) * d_inner - gated * (inv * inv * inv / INNER * dot)
        gpost[...] += jnp.sum(d_inner * (gated * inv), axis=0, keepdims=True)
        d_ssd = (d_gated * (gate_v * sig)).astype(LOW)
        dssd_s[here, :] = d_ssd
        dgate_s[here, :] = (d_gated * ssd * sig * (1.0 + gate_v * (1.0 - sig))).astype(LOW)
        query_grad = (d_ssd.astype(WIDE) * entry_of(b, cum_v)).astype(LOW)
        found = tn(query_grad, read_f.at(b)[...])
        q[b] = found
        state[...] += carry_columns(prod[...], collect) * found
        prod[...] = prod[...] * carry_of(b, cum_v.T)

    back_msg[:inner, :] = state[...].astype(LOW)
    back_msg[inner:, :] = jnp.broadcast_to(prod[:HALO], (HALO, STATE)).astype(LOW)
    back_plane.start(back_msg)

    if out_fold.merges:

        @pl.when(jnp.logical_not(out_fold.is_end))
        def _():
            @pl.loop(0, blocks)
            def _(b):
                out_fold.merge(group_rows(b), b)

    else:
        pl.loop(0, blocks)(lambda b: out_fold.send_far(group_rows(b), b))

    @pl.loop(0, blocks)
    def _(b):
        step(*scan_phase, b, last_phase)
        here = group_rows(b)
        second = flags[2 * b + 1]
        act = act_f.at(b)
        cum_v = cum_f.at(b)[...]
        cum_t = cum_v.T
        steps, _, _ = step_terms(raw_f.at(b)[...], heads)
        steps_t = steps.T
        write = act[:, inner : inner + STATE]
        read_v = act[:, inner + STATE :]
        s00 = jnp.where(lower_mask, nt(read_v[top], write[top]), 0.0)
        s10 = nt(read_v[low], write[top]) * second
        s11 = jnp.where(lower_mask, nt(read_v[low], write[low]), 0.0)

        def decay_of(head, t, s):
            decay = jnp.exp(jnp.minimum(cum_v[t, head : head + 1] - cum_t[head : head + 1, s], 0.0))
            return decay * steps_t[head : head + 1, s]

        ds00 = jnp.zeros((BLOCK, BLOCK), WIDE)
        ds10 = jnp.zeros((BLOCK, BLOCK), WIDE)
        ds11 = jnp.zeros((BLOCK, BLOCK), WIDE)
        for pair in range(inner // LANES):
            columns = slice(pair * LANES, (pair + 1) * LANES)
            values = act[:, columns]
            dys = pair_lanes(dssd_s[here, columns])
            m00, m10, m11 = [], [], []
            for k in range(2):
                head = 2 * pair + k
                l00, l10, l11 = decay_of(head, top, top), decay_of(head, low, top), decay_of(head, low, low)
                m00.append((s00 * l00).astype(LOW))
                m10.append((s10 * l10).astype(LOW))
                m11.append((s11 * l11).astype(LOW))
                ds00 = ds00 + nt(dys[k][top], values[top]) * l00
                ds10 = ds10 + nt(dys[k][low], values[top]) * l10
                ds11 = ds11 + nt(dys[k][low], values[low]) * l11
            v0 = tn(
                jnp.concatenate([m00[0], m10[0], m00[1], m10[1]], axis=0), jnp.concatenate([dys[0], dys[1]], axis=0)
            )
            v1 = tn(
                jnp.concatenate([m11[0], m11[1]], axis=0), jnp.concatenate([dys[0][low], dys[1][low]], axis=0)
            )
            din_s[here, columns] = jnp.concatenate([v0, v1], axis=0)
        ds_s[here, :] = jnp.concatenate(
            [
                jnp.concatenate([jnp.where(lower_mask, ds00, 0.0), jnp.zeros((BLOCK, BLOCK), WIDE)], axis=1),
                jnp.concatenate([ds10 * second, jnp.where(lower_mask, ds11, 0.0)], axis=1),
            ],
            axis=0,
        ).astype(LOW)

        gated, inv = norm_back(b, b)[3:5]
        inner_normed = (gated * inv * postnorm[...]).astype(LOW)
        gread[...] += tn(g_buf[here, :], inner_normed)
        ggate[...] += tn(normed_f.at(b)[...], dgate_s[here, :])

        @pl.when(b == blocks // 2)
        def _():
            back_plane.relay()

    early_low[:, :inner] = gread[...].astype(LOW)
    early_low[:, inner:] = ggate[...].astype(LOW)
    early_sum.begin()
    back_plane.finish(back_msg)
    state[...] = fold_states(back_slots, collect, inner, seqs - 1, me, -1, jnp.zeros((inner, STATE), WIDE))

    early_sum.combine()
    taps = jnp.concatenate([kernels[...], filters[...]], axis=1)
    scale = -jnp.exp(vec[1:2, :])
    through_w = to_columns(jnp.broadcast_to(vec[2:3, :], (EDGE, LANES)), spread_m)[0:1]

    def scan_back(b, turn):
        here = group_rows(b)
        first, second = flags[2 * b], flags[2 * b + 1]
        act, conv = act_f.at(turn), conv_f.at(turn)
        cum_v = cum_f.at(turn)[...]
        steps, sig, ratio = step_terms(raw_f.at(turn)[...], heads)
        last = cum_v[GROUP - 1 : GROUP, :]
        write = act[:, inner : inner + STATE]
        read_v = act[:, inner + STATE :]
        end = state[...]
        end_low = end.astype(LOW)
        start = starts[b]
        state[...] = carry_columns(carry_of(b, cum_v.T), collect) * end + q[b]
        weight = steps * jnp.exp(last - cum_v) * jnp.where(row < BLOCK, second, 1.0)
        weight_w = to_columns(weight, spread_m)
        d_ssd = dssd_s[here, :]
        dy_f = d_ssd.astype(WIDE)
        values_f = act[:, :inner].astype(WIDE)
        d_query = (dy_f * entry_of(b, cum_v)).astype(LOW)
        tail = nt(write, end_low) * weight_w
        whole = din_s[here, :] + tail
        d_conv[:, :inner] = conv_grad(whole + through_w * dy_f, conv[:, :inner])
        packed = (values_f * weight_w).astype(LOW)
        ds = ds_s[here, :]
        d_read = nn(ds, write) + nn(d_query, start.astype(LOW))
        d_write = tn(ds, read_v) + nn(packed, end_low)
        d_conv[:, inner : inner + STATE] = conv_grad(d_write, conv[:, inner : inner + STATE])
        d_conv[:, inner + STATE :] = conv_grad(d_read, conv[:, inner + STATE :])

        own = to_heads(dy_f * values_f, collect)
        r1 = to_heads(dy_f * ssd_s[here, :], collect) - vec[2:3, :] * own
        by_value = to_heads(values_f * whole, collect)
        tail_sum = jnp.sum(tail * values_f, axis=0, keepdims=True)
        tail_row = to_heads(jnp.broadcast_to(tail_sum, (EDGE, inner)), collect)[0:1]
        high, rest = halves(end * start)
        ones = jnp.ones((EDGE, STATE), LOW)
        carry_grad = to_heads(nt(ones, high) + nt(ones, rest), collect)[0:1]
        d_last = tail_row + carry_grad * (jnp.exp(last) * (first * second))
        d_cum = r1 - by_value + jnp.where(row == GROUP - 1, d_last, 0.0)
        d_rate = sum_after(d_cum)
        d_raw = d_rate * scale * sig + by_value * ratio
        d_step[...] = d_raw.astype(LOW)
        tiny[0:1, :] += jnp.sum(d_raw, axis=0, keepdims=True)
        tiny[1:2, :] += jnp.sum(d_rate * steps, axis=0, keepdims=True) * scale
        tiny[2:3, :] += jnp.sum(own, axis=0, keepdims=True)

    def conv_back(ref, count):
        total = taps[TAPS - 1 : TAPS] * ref[pl.ds(0, count), :]
        for tap in range(TAPS - 1):
            total = total + taps[tap : tap + 1] * ref[pl.ds(TAPS - 1 - tap, count), :]
        return total.astype(LOW)

    def input_back(d_pre, step_grad, gate_grad, u_rows):
        d_normed = (
            nt(gate_grad, w[:, :inner])
            + nt(d_pre, w[:, inner : inner + wide])
            + nt(step_grad, w[:, inner + wide :])
        )
        rows_f = u_rows.astype(WIDE)
        inv = lax.rsqrt(jnp.mean(rows_f * rows_f, axis=1, keepdims=True) + EPS)
        gained = d_normed * prenorm[...]
        dot = jnp.sum(gained * rows_f, axis=1, keepdims=True)
        grad = gained * inv - rows_f * (inv * inv * inv / D * dot)
        return grad.astype(LOW), d_normed * (rows_f * inv)

    def rows_back(b, turn, final):
        grad_c = d_conv[...]
        pre_v = pre_f.at(turn)[...].astype(WIDE)
        before = jnp.where(b == 0, rim[...], before_f.at(turn)[HALO - EDGE :, :].astype(WIDE))
        bias_g[...] += jnp.sum(grad_c, axis=0, keepdims=True)
        parts = []
        for half in range(2):
            part_rows = slice(half * BLOCK, (half + 1) * BLOCK)
            tile = grad_c[part_rows]
            ext[0:EDGE, :] = (before if half == 0 else pre_v[BLOCK - EDGE : BLOCK]) * flags[2 * b + half]
            ext[EDGE:, :] = pre_v[part_rows]
            for tap in range(TAPS):
                taps_g[tap : tap + 1, :] += jnp.sum(
                    tile * ext[pl.ds(EDGE - (TAPS - 1) + tap, BLOCK), :], axis=0, keepdims=True
                )
            ext[:BLOCK, :] = tile
            if half == 0:
                ext[BLOCK:, :] = grad_c[BLOCK : BLOCK + EDGE] * flags[2 * b + 1]
            elif final:
                ext[BLOCK:, :] = jnp.zeros((EDGE, wide), WIDE)
            else:
                ext[BLOCK:, :] = after[...] * flags[2 * b + 2]
            parts.append(conv_back(ext, BLOCK))
        d_pre = jnp.concatenate(parts, axis=0)
        step_grad = d_step[...]
        normed_v = normed_f.at(turn)[...]
        u_v = u_f.at(turn)
        done = lax.broadcasted_iota(jnp.int32, (GROUP, 1), 0) < GROUP - HALO
        if final:
            d_pre = jnp.where(done, d_pre, jnp.zeros_like(d_pre))
            keep_conv[:HALO, :] = grad_c[GROUP - HALO :]
            keep_step[...] = step_grad[GROUP - HALO :]
            keep_normed[...] = normed_v[GROUP - HALO :]
            keep_u[...] = u_v[GROUP - HALO :, :]
        dw[:, :wide] += tn(normed_v, d_pre)
        dw[:, wide:] += tn(normed_v, step_grad)
        grad, gain = input_back(d_pre, step_grad, dgate_s[group_rows(b), :], u_v[...])
        pn[...] += jnp.sum(jnp.where(done, gain, 0.0) if final else gain, axis=0, keepdims=True)
        g_buf[group_rows(b), :] = grad
        after[...] = grad_c[0:EDGE]

    def outputs_home():
        pl.loop(0, 2 * blocks)(lambda n: residual(n).wait())
        pl.loop(0, blocks)(lambda b: out_fold.drain(group_rows(b), b))
        fetch(out_far)

        @pl.loop(0, blocks)
        def _(b):
            inv, _ = row_stats(b)
            total = out_fold.total(group_rows(b), out_near if roomy else out_part) * inv
            result[2 * b] = (result[2 * b].astype(WIDE) + total[:BLOCK]).astype(LOW)
            result[2 * b + 1] = (result[2 * b + 1].astype(WIDE) + total[BLOCK:]).astype(LOW)

        route(0)
        own_g.start()

    own_g = pltpu.make_async_copy(shard_of(g_part, mine), out_part.at[mine], load_sem.at[5])

    step(*last_phase, 0, None)
    scan_back(blocks - 1, 0)
    rows_back(blocks - 1, 0, True)
    dx_fold.send_far(*short_piece)

    @pl.loop(1, blocks)
    def _(turn):
        b = blocks - 1 - turn
        step(*last_phase, turn, None)
        scan_back(b, turn)

        @pl.when(b == 0)
        def _():
            edge_own[...] = d_conv[0:EDGE, :]
            edge_copy(lax.rem(me + seqs - 1, seqs)).start()

        rows_back(b, turn, False)
        dx_fold.send_far(group_rows(b), b)

        @pl.when(turn == 2)
        def _():
            dx_fold.merge(*short_piece)

        pl.when(turn == max(blocks // 2, 1))(outputs_home)

        @pl.when(turn > 2)
        def _():
            dx_fold.merge(group_rows(b + 2), b + 2)

    edge_copy(lax.rem(me + 1, seqs)).wait()
    keep_conv[HALO:, :] = edge_got[...] * flags[2 * blocks]
    d_edge = conv_back(keep_conv, HALO)
    dw[:, :wide] += tn(keep_normed[...], d_edge)
    grad, gain = input_back(d_edge, keep_step[...], dgate_s[pl.ds(rows - HALO, HALO), :], keep_u[...])
    pn[...] += jnp.sum(gain, axis=0, keepdims=True)
    g_buf[pl.ds(rows - HALO, HALO), :] = grad
    dx_fold.send_far(*edge_piece)

    for z in range(line):
        slab = z * size // LANES * LANES
        zs_send[z] = jnp.zeros(zs_send.shape[1:], WIDE)
        zs_send[z, 0:1, :] = pn[:, z * width : (z + 1) * width]
        zs_send[z, EDGE : EDGE + TAPS, :LANES] = taps_g[0:TAPS, inner + slab : inner + slab + LANES]
        zs_send[z, EDGE + TAPS : EDGE + TAPS + 1, :LANES] = bias_g[:, inner + slab : inner + slab + LANES]
    zs_got[mine] = zs_send[mine]
    all_line(lambda to: zs_copy(to, mine).start())

    each_piece(dx_fold.send_near)

    if blocks > 3:
        dx_fold.merge(group_rows(1), 1)

    da_low[...] = dw[:, inner:wide].astype(LOW)
    da_sum.begin()
    dw_low[:, :inner] = dw[:, :inner].astype(LOW)
    dw_low[:, inner:] = dw[:, wide:].astype(LOW)
    dw_sum.begin()

    if blocks > 3:
        dx_fold.merge(group_rows(0), 0)
    elif blocks == 2:
        dx_fold.merge(*short_piece)
        dx_fold.merge(group_rows(0), 0)
    dx_fold.merge(*edge_piece)
    da_sum.combine()
    dw_sum.combine()

    all_line(lambda other: zs_copy(other, other).wait())
    from_line = jnp.sum(zs_got[...], axis=0)
    small[...] = jnp.zeros_like(small)
    small[0:TAPS, :inner] = taps_g[0:TAPS, :inner]
    small[0:TAPS, inner:] = from_line[EDGE : EDGE + TAPS, :LANES]
    small[4:5, :inner] = bias_g[:, :inner]
    small[4:5, inner:] = from_line[EDGE + TAPS : EDGE + TAPS + 1, :LANES]
    small[5:6, :inner] = gpost[...]
    small[6:7, :width] = from_line[0:1]
    for n in range(3):
        small[7:8, n * LANES : (n + 1) * LANES] = tiny[n : n + 1, :]
    own_copies["small"].start()
    all_seq(lambda to: small_copy(to, me).start())

    da_sum.drain()
    from_plane = da_got[0].astype(WIDE)
    for n in range(1, seqs // 2):
        from_plane = from_plane + da_got[n].astype(WIDE)
    for z in range(line):
        slab = z * size // LANES * LANES
        da_send[z] = from_plane[:, slab : slab + LANES]
    own_copies["addr"].start()
    all_line(lambda to: da_copy(to, mine).start())

    all_seq(lambda other: fin_copy(0, other, other).wait())
    own_copies["fin0"].wait()
    each_piece(dx_fold.drain)
    fetch(dx_far)
    own_g.wait()

    @pl.loop(0, blocks)
    def _(b):
        here = group_rows(b)
        total = dx_fold.total(here, dx_near if roomy else out_part)
        done = (out_part[mine, here].astype(WIDE) + total).astype(LOW)
        result[2 * b] = done[:BLOCK]
        result[2 * b + 1] = done[BLOCK:]

    route(1)
    early_sum.drain()
    dw_sum.drain()
    all_line(lambda other: da_copy(other, other).wait())
    all_seq(lambda other: fin_copy(1, other, other).wait())
    all_seq(lambda other: small_copy(other, other).wait())
    for name in ("addr", "small", "fin1"):
        own_copies[name].wait()


def core(
    flags, give, gate, part, act, cum, raw, local, conv, pre, normed, u, g_part, state_in, r_t, w_all, postnorm, vec,
    prenorm, kernels, filters, rim,
):
    seqs, line = lax.axis_size("seq"), lax.axis_size("head")
    rows, inner = gate.shape
    wide = act.shape[1]
    total = g_part.shape[1]
    width = total // line
    depth = total // seqs
    blocks, tiles = rows // GROUP, rows // BLOCK
    heads = inner // HDIM
    pieces = blocks + 1
    message = (inner + HALO, STATE)
    sums = (blocks, EDGE, GROUP)
    streamed = (gate, part, act, cum, raw, local, conv, pre, normed, u, g_part, r_t, w_all)
    whole = (state_in, postnorm, vec, prenorm, kernels, filters, rim)
    gather = (line, rows, width)
    nothing = (line, HALO, width)
    roomy = rows * total * 2 <= 4 << 20
    near, far = (gather, nothing) if roomy else (nothing, gather)
    relay = (2, rows if line == 4 else HALO, width)
    small = (EDGE, inner + LANES)
    ways = max(line, 3)

    def slots(*dims):
        return (2,) + dims

    buffers = (
        (slots(GROUP, inner), WIDE), (slots(GROUP, inner), WIDE), (slots(GROUP, STATE), LOW),
        (slots(GROUP, LANES), WIDE), (slots(inner, STATE), WIDE), (slots(GROUP, total), LOW),
        (slots(GROUP, wide), LOW), (slots(GROUP, LANES), WIDE), (slots(GROUP, wide), WIDE),
        (slots(GROUP, wide), LOW), (slots(HALO, wide), LOW), (slots(GROUP, total), LOW),
    )
    return pl.pallas_call(
        functools.partial(core_kernel, seqs, line, heads, blocks, roomy),
        grid=(1,),
        out_shape=(
            shape((seqs, BLOCK, width), LOW), shape((seqs, BLOCK, width), LOW), shape(far, LOW), shape(far, LOW),
            shape((seqs // 2, depth, 2 * inner), LOW), shape((seqs // 2, depth, inner + LANES), LOW),
            shape((line, depth, LANES), WIDE), shape((seqs,) + small, WIDE),
        ),
        in_specs=[SMEM_SPEC] * 2 + [ANY_SPEC] * len(streamed) + [fixed(a.shape) for a in whole],
        out_specs=(ANY_SPEC,) * 8,
        scratch_shapes=[pltpu.VMEM(dims, kind) for dims, kind in buffers] + [
            DMA((len(buffers), 2)),
            pltpu.VMEM(r_t.shape, LOW), pltpu.VMEM(w_all.shape, LOW),
            pltpu.VMEM((rows, inner), WIDE), pltpu.VMEM((rows, inner), WIDE), pltpu.VMEM((rows, inner), LOW),
            pltpu.VMEM((rows, inner), LOW), pltpu.VMEM((rows, GROUP), LOW), pltpu.VMEM((blocks, inner, STATE), WIDE),
            pltpu.VMEM((blocks, inner, STATE), WIDE), pltpu.VMEM((inner, STATE), WIDE), pltpu.VMEM((LANES, 1), WIDE),
            pltpu.VMEM((rows, total), LOW), pltpu.VMEM(gather, LOW),
            pltpu.VMEM((seqs,) + message, LOW), pltpu.VMEM(message, LOW),
            pltpu.VMEM(relay, LOW), pltpu.VMEM(relay, LOW), pltpu.VMEM(near, LOW), pltpu.VMEM(near, LOW),
            pltpu.VMEM((line,) + sums, WIDE), pltpu.VMEM(sums, WIDE),
            pltpu.VMEM((total, inner), WIDE), pltpu.VMEM((total, inner), WIDE), pltpu.VMEM((total, 2 * inner), LOW),
            pltpu.VMEM((seqs // 2, depth, 2 * inner), LOW), pltpu.VMEM((1, inner), WIDE), pltpu.VMEM((EDGE, LANES), WIDE),
            pltpu.VMEM((GROUP, wide), WIDE), pltpu.VMEM((GROUP, LANES), LOW), pltpu.VMEM((EDGE, wide), WIDE),
            pltpu.VMEM((EDGE, wide), WIDE), pltpu.VMEM((EDGE, wide), WIDE), pltpu.VMEM((BLOCK + EDGE, wide), WIDE),
            pltpu.VMEM((HALO + EDGE, wide), WIDE), pltpu.VMEM((HALO, LANES), LOW), pltpu.VMEM((HALO, total), LOW),
            pltpu.VMEM((HALO, total), LOW),
            pltpu.VMEM((EDGE, wide), WIDE), pltpu.VMEM((1, wide), WIDE), pltpu.VMEM((total, wide + LANES), WIDE),
            pltpu.VMEM((total, inner + LANES), LOW), pltpu.VMEM((seqs // 2, depth, inner + LANES), LOW),
            pltpu.VMEM((total, wide - inner), LOW), pltpu.VMEM((seqs // 2, depth, wide - inner), LOW),
            pltpu.VMEM((seqs // 2, depth, wide - inner), LOW), pltpu.VMEM((line, depth, LANES), WIDE),
            pltpu.VMEM((1, total), WIDE), pltpu.VMEM((line, 2 * EDGE, width), WIDE),
            pltpu.VMEM((line, 2 * EDGE, width), WIDE), pltpu.VMEM(small, WIDE),
            pltpu.VMEM((tiles, BLOCK, width), LOW), pltpu.VMEM((seqs, BLOCK, width), LOW),
            DMA((seqs,)), DMA((seqs,)), DMA((seqs,)), DMA((line,)), DMA((line,)), DMA((2, line)), DMA((line,)), DMA((6,)),
            DMA((ways, blocks)), DMA((line, blocks)), DMA((2, blocks)), DMA((4, seqs // 2)), DMA((4, seqs // 2)), DMA((4, seqs // 2)),
            DMA((ways, pieces)), DMA((line, pieces)), DMA((2, pieces)), DMA, DMA,
            DMA((line,)), DMA((line,)), DMA((line,)), DMA((line,)), DMA((seqs,)), DMA((seqs,)), DMA((2, seqs)),
            DMA((2, seqs)), DMA((4,)), DMA((2,)), DMA((tiles,)),
        ],
        compiler_params=pltpu.CompilerParams(
            collective_id=1, has_side_effects=True, vmem_limit_bytes=VMEM_LIMIT, dimension_semantics=("arbitrary",)
        ),
        name="core",
    )(flags, give, *streamed, *whole)


def finish_kernel(
    take, out_recv, grad_recv, early_got, dw_got, addr_got, small_got,
    out_o, dx_o, prenorm_o, gate_o, pay_o, addr_o, step_o, kernels_o, offsets_o, filters_o, shifts_o,
    stepbias_o, decays_o, through_o, post_o, read_o,
):
    inner, size, heads, width = gate_o.shape[1], addr_o.shape[0], step_o.shape[0], prenorm_o.shape[1]
    offset = lax.rem(lax.axis_index("head") * size, LANES)
    back_turn = lax.rem(LANES - offset, LANES)
    for k in range(out_o.shape[0]):
        out_o[k] = out_recv[take[k]]
        dx_o[k] = grad_recv[take[k]]

    def summed(ref):
        total = ref[0].astype(WIDE)
        for n in range(1, ref.shape[0]):
            total = total + ref[n].astype(WIDE)
        return total

    early = summed(early_got)
    read_o[...] = early[:, :inner].T
    gate_o[...] = early[:, inner:]
    grads = summed(dw_got)
    pay_o[...] = grads[:, :inner]
    step_o[...] = grads[:, inner:].T[:heads]
    addr_o[...] = pltpu.roll(summed(addr_got), back_turn, 1).T[:size]
    totals = jnp.sum(small_got[...], axis=0)
    kernels_o[...] = totals[0:TAPS, :inner]
    offsets_o[...] = totals[4:5, :inner]
    turned = pltpu.roll(totals[:, inner:], back_turn, 1)
    filters_o[...] = turned[0:TAPS, :size]
    shifts_o[...] = turned[4:5, :size]
    post_o[...] = totals[5:6, :inner]
    prenorm_o[...] = totals[6:7, :width]
    for n, ref in enumerate((stepbias_o, decays_o, through_o)):
        ref[...] = totals[7:8, n * LANES : n * LANES + heads]


def finish(take, out_recv, grad_recv, early_got, dw_got, addr_got, small_got):
    seqs, _, width = out_recv.shape
    tiles = take.shape[0]
    _, depth, inner = early_got.shape
    inner = inner // 2
    heads = inner // HDIM
    size = 2 * STATE // addr_got.shape[0]
    operands = (out_recv, grad_recv, early_got, dw_got, addr_got, small_got)
    outs = (
        shape((tiles, BLOCK, width), LOW), shape((tiles, BLOCK, width), LOW), shape((1, width), WIDE),
        shape((depth, inner), WIDE), shape((depth, inner), WIDE), shape((size, depth), WIDE),
        shape((heads, depth), WIDE), shape((TAPS, inner), WIDE), shape((1, inner), WIDE),
        shape((TAPS, size), WIDE), shape((1, size), WIDE), shape((1, heads), WIDE), shape((1, heads), WIDE),
        shape((1, heads), WIDE), shape((1, inner), WIDE), shape((inner, depth), WIDE),
    )
    return pl.pallas_call(
        finish_kernel,
        grid=(1,),
        out_shape=outs,
        in_specs=[SMEM_SPEC] + [fixed(a.shape) for a in operands],
        out_specs=tuple(fixed(a.shape) for a in outs),
        compiler_params=pltpu.CompilerParams(vmem_limit_bytes=VMEM_LIMIT, dimension_semantics=("arbitrary",)),
        name="finish",
    )(take, *operands)


def on_device(
    inputs,
    cotangent,
    lengths,
    placement,
    prenorm,
    gating,
    payload,
    address,
    stepping,
    kernels,
    offsets,
    filters,
    shifts,
    stepbias,
    decays,
    through,
    postnorm,
    readout,
):
    rows, width = inputs.shape
    heads = stepbias.shape[0]
    tiles = rows // BLOCK
    give_in, take_in, give_out, take_out, flags, vec = index(placement, lengths, stepbias, decays, through, tiles)
    gain, post = prenorm[None, :], postnorm[None, :]
    (
        u, normed, gate, pre, conv, act, raw, cum, part, local, state_in, rim, g_part, w_all, r_t
    ) = front(
        give_in, take_in, flags, inputs, cotangent, gating, payload, address, stepping, readout, vec, gain, kernels,
        filters, offsets[None, :], shifts[None, :]
    )
    out_recv, grad_recv, _, _, early_got, dw_got, addr_got, small_got = core(
        flags, give_out, gate, part, act, cum, raw, local, conv, pre, normed, u, g_part, state_in, r_t, w_all, post, vec,
        gain, kernels, filters, rim
    )
    (
        out, dx, prenorm_g, gate_g, pay_g, addr_g, step_g, kernels_g, offsets_g, filters_g, shifts_g, stepbias_g,
        decays_g, through_g, post_g, read_g,
    ) = finish(take_out, out_recv, grad_recv, early_got, dw_got, addr_got, small_got)
    return (
        out.reshape(rows, width),
        dx.reshape(rows, width),
        prenorm_g.reshape(-1),
        gate_g,
        pay_g,
        addr_g.T,
        step_g.T,
        kernels_g,
        offsets_g.reshape(-1),
        filters_g,
        shifts_g.reshape(-1),
        stepbias_g.reshape(-1),
        decays_g.reshape(-1),
        through_g.reshape(-1),
        post_g.reshape(-1),
        read_g,
    )


def solution(mesh):
    in_specs = (
        P("seq", "head"),
        P("seq", "head"),
        P(),
        P(),
        P(),
        P("seq", "head"),
        P("seq", "head"),
        P("seq", None),
        P("seq", "head"),
        P(None, "head"),
        P("head"),
        P(),
        P(),
        P("head"),
        P("head"),
        P("head"),
        P("head"),
        P("head", "seq"),
    )
    out_specs = (
        P("seq", "head"),
        P("seq", "head"),
        P("head"),
        P("seq", "head"),
        P("seq", "head"),
        P("seq", "head"),
        P("seq", "head"),
        P(None, "head"),
        P("head"),
        P(None, "head"),
        P("head"),
        P("head"),
        P("head"),
        P("head"),
        P("head"),
        P("head", "seq"),
    )
    return jax.shard_map(
        on_device, mesh=mesh, in_specs=in_specs, out_specs=out_specs, check_vma=False
    )
```

```python
import functools

import jax
import jax.numpy as jnp
from jax import lax
from jax.experimental import pallas as pl
from jax.experimental.pallas import tpu as pltpu
from jax.sharding import PartitionSpec as P

D = 1024
GROUP = 256
BLOCK = 128
INNER = 2048
HDIM = 64
STATE = 128
TAPS = 4
HALO = 16
EDGE = 8
LANES = 128
EPS = 1e-05
MESH = pl.DeviceIdType.MESH
VMEM = pltpu.MemorySpace.VMEM
SMEM = pltpu.MemorySpace.SMEM
DMA = pltpu.SemaphoreType.DMA
VMEM_LIMIT = 63 << 20
LOW = jnp.bfloat16
WIDE = jnp.float32


def shape(dims, kind):
    return jax.ShapeDtypeStruct(dims, kind)


def nn(a, b):
    return jnp.dot(a, b, preferred_element_type=WIDE)


def nt(a, b):
    return lax.dot_general(a, b, (((1,), (1,)), ((), ())), preferred_element_type=WIDE)


def tn(a, b):
    return lax.dot_general(a, b, (((0,), (0,)), ((), ())), preferred_element_type=WIDE)


def halves(x):
    high = x.astype(LOW)
    return high, (x - high.astype(WIDE)).astype(LOW)


def thirds(x):
    high = x.astype(LOW)
    rest = x - high.astype(WIDE)
    middle = rest.astype(LOW)
    return high, middle, (rest - middle.astype(WIDE)).astype(LOW)


def head_rows(inner):
    row = lax.broadcasted_iota(jnp.int32, (LANES, inner), 0)
    column = lax.broadcasted_iota(jnp.int32, (LANES, inner), 1)
    return jnp.where(column // HDIM == row, 1.0, 0.0).astype(LOW)


def head_columns(inner):
    row = lax.broadcasted_iota(jnp.int32, (inner, LANES), 0)
    column = lax.broadcasted_iota(jnp.int32, (inner, LANES), 1)
    return jnp.where(row // HDIM == column, 1.0, 0.0).astype(LOW)


def to_columns(x, spread):
    high, rest = halves(x)
    return nn(high, spread) + nn(rest, spread)


def to_heads(x, collect):
    high, rest = halves(x)
    return nn(high, collect) + nn(rest, collect)


def ones_before(count):
    row = lax.broadcasted_iota(jnp.int32, (count, count), 0)
    column = lax.broadcasted_iota(jnp.int32, (count, count), 1)
    return row >= column


def sum_before(x):
    matrix = jnp.where(ones_before(x.shape[0]), 1.0, 0.0).astype(LOW)
    high, middle, low = thirds(x)
    return nn(matrix, high) + (nn(matrix, middle) + nn(matrix, low))


def sum_after(x):
    count = x.shape[0]
    row = lax.broadcasted_iota(jnp.int32, (count, count), 0)
    column = lax.broadcasted_iota(jnp.int32, (count, count), 1)
    matrix = jnp.where(row <= column, 1.0, 0.0).astype(LOW)
    high, middle, low = thirds(x)
    return nn(matrix, high) + (nn(matrix, middle) + nn(matrix, low))


def sigmoid(x):
    return 0.5 * jnp.tanh(0.5 * x) + 0.5


def step_terms(raw, heads):
    z = jnp.exp(-jnp.abs(raw))
    series = 1.0 - z * (0.5 - z * (1.0 / 3.0 - z * (0.25 - z * 0.2)))
    small = z < 0.03
    log1p = jnp.where(small, z * series, jnp.log(1.0 + z))
    soft = jnp.maximum(raw, 0.0) + log1p
    one = 1.0 / (1.0 + z)
    sig = jnp.where(raw >= 0, one, z * one)
    ratio = jnp.where(small & (raw < 0), one / series, sig / jnp.maximum(soft, 1e-20))
    lane = lax.broadcasted_iota(jnp.int32, raw.shape, 1)
    return jnp.where(lane < heads, soft, 0.0), sig, ratio


def greet(seq_peers, head_peers, corners=False):
    barrier = pltpu.get_barrier_semaphore()
    count = 0
    if seq_peers > 1:
        me = lax.axis_index("seq")

        @pl.loop(1, seq_peers)
        def _(i):
            pl.semaphore_signal(
                barrier, inc=1, device_id={"seq": lax.rem(me + i, seq_peers)}, device_id_type=MESH
            )

        count += seq_peers - 1
    if head_peers > 1:
        mine = lax.axis_index("head")

        @pl.loop(1, head_peers)
        def _(i):
            pl.semaphore_signal(
                barrier, inc=1, device_id={"head": lax.rem(mine + i, head_peers)}, device_id_type=MESH
            )

        count += head_peers - 1
    if corners and head_peers > 1:
        me, mine = lax.axis_index("seq"), lax.axis_index("head")
        for side in (1, seq_peers - 1):

            @pl.loop(1, head_peers)
            def _(i):
                where = {"seq": lax.rem(me + side, seq_peers), "head": lax.rem(mine + i, head_peers)}
                pl.semaphore_signal(barrier, inc=1, device_id=where, device_id_type=MESH)

        count += 2 * (head_peers - 1)
    pl.semaphore_wait(barrier, count)


def remote(src, dst, send_sem, recv_sem, where):
    return pltpu.make_async_remote_copy(
        src_ref=src, dst_ref=dst, send_sem=send_sem, recv_sem=recv_sem, device_id=where, device_id_type=MESH
    )


class Line:
    def __init__(self, count, out, width, send, recv):
        self.count, self.out, self.width, self.send, self.recv = count, out, width, send, recv
        self.me = lax.axis_index("head")

    def view(self, shard):
        return self.out.at[:, pl.ds(pl.multiple_of(shard * self.width, LANES), self.width)]

    def copy(self, src, shard, way, step):
        return remote(
            src, self.view(shard), self.send.at[way, step], self.recv.at[shard], {"head": self.me + (1 - 2 * way)}
        )

    def first(self, own):
        self.pass_on(own, self.me, 0, 0)
        self.pass_on(own, self.me, 1, 0)

    def pass_on(self, src, shard, way, step):
        reach = (self.me < self.count - 1) if way == 0 else (self.me > 0)

        @pl.when(reach)
        def _():
            self.copy(src, shard, way, step).start()

    def hop(self, step, take=True, give=True, source=None):
        for way in (0, 1):
            shard = self.me - step if way == 0 else self.me + step
            there = (shard >= 0) if way == 0 else (shard < self.count)

            @pl.when(there)
            def _():
                if take:
                    self.copy(self.view(shard), shard, way, step).wait_recv()
                if give and step < self.count - 1:
                    self.pass_on(self.view(shard) if source is None else source(shard), shard, way, step)

    def finish(self, own, steps=None):
        for way in (0, 1):
            reach = (self.me < self.count - 1) if way == 0 else (self.me > 0)
            for step in range(self.count - 1) if steps is None else steps:
                shard = self.me - step if way == 0 else self.me + step
                there = (shard >= 0) if way == 0 else (shard < self.count)

                @pl.when(reach & there)
                def _():
                    src = own if step == 0 else self.view(shard)
                    self.copy(src, shard, way, step).wait_send()


class Plane:
    def __init__(self, seqs, view, sent, got, passed, way=0):
        self.chips, self.view, self.sent, self.got, self.passed, self.way = seqs // 2, view, sent, got, passed, way
        self.me = lax.axis_index("seq")
        self.core = lax.rem(self.me, 2)
        self.chip = self.me // 2
        self.mate = self.me + 1 - 2 * self.core

    def forward(self, chip):
        return (chip > self.chip) if self.way == 1 else (chip < self.chip) if self.way == -1 else (chip >= 0)

    def backward(self, chip):
        return (chip < self.chip) if self.way == 1 else (chip > self.chip) if self.way == -1 else (chip >= 0)

    def each_chip(self, body):
        @pl.loop(1, self.chips)
        def _(i):
            body(lax.rem(self.chip + i, self.chips))

    def copy(self, src, source, to, sem):
        return remote(src, self.view(source), sem, self.got.at[source], {"seq": to})

    def start(self, own):
        def send(chip):
            to = 2 * chip + self.core

            @pl.when(self.forward(chip))
            def _():
                self.copy(own, self.me, to, self.sent.at[to]).start()

        self.each_chip(send)
        self.copy(own, self.me, self.mate, self.sent.at[self.mate]).start()

    def relay(self):
        def take(chip):
            source = 2 * chip + self.core

            @pl.when(self.backward(chip))
            def _():
                landed = self.view(source)
                self.copy(landed, source, self.mate, self.passed.at[source]).wait_recv()
                self.copy(landed, source, self.mate, self.passed.at[source]).start()

        self.each_chip(take)

    def finish(self, own):
        def take(chip):
            source = 2 * chip + 1 - self.core

            @pl.when(self.backward(chip))
            def _():
                self.copy(self.view(source), source, self.mate, self.passed.at[source]).wait_recv()

        self.each_chip(take)
        self.copy(self.view(self.mate), self.mate, self.mate, self.sent.at[self.mate]).wait_recv()
        self.copy(own, self.me, self.mate, self.sent.at[self.mate]).wait_send()

        def drain(chip):
            same = 2 * chip + self.core

            @pl.when(self.forward(chip))
            def _():
                self.copy(own, self.me, same, self.sent.at[same]).wait_send()

            @pl.when(self.backward(chip))
            def _():
                self.copy(self.view(same), same, self.mate, self.passed.at[same]).wait_send()

        self.each_chip(drain)


ANY_SPEC = pl.BlockSpec(memory_space=pl.ANY)
VMEM_SPEC = pl.BlockSpec(memory_space=VMEM)
SMEM_SPEC = pl.BlockSpec(memory_space=SMEM)


def index_kernel(
    seqs, tiles, place, lengths, stepbias, decays, through, give_in, take_in, give_out, take_out, flags, vec
):
    me = lax.axis_index("seq")

    @pl.loop(0, seqs * tiles)
    def _(j):
        block = place[j]

        @pl.when(lax.div(block, tiles) == me)
        def _():
            to = lax.div(j, tiles)
            give_in[to] = lax.rem(block, tiles)
            take_out[lax.rem(block, tiles)] = to

    @pl.loop(0, tiles)
    def _(k):
        source = lax.div(place[me * tiles + k], tiles)
        take_in[k] = source
        give_out[source] = k

    @pl.loop(0, tiles + 1)
    def _(k):
        position = (me * tiles + k) * BLOCK
        end = jnp.int32(0)
        border = position == 0
        for n in range(lengths.shape[0]):
            end = end + lengths[n]
            border = border | (position == end)
        flags[k] = jnp.where(border, 0.0, 1.0)

    heads = stepbias.shape[1]
    vec[...] = jnp.zeros_like(vec)
    vec[0:1, :heads] = stepbias[...]
    vec[1:2, :heads] = decays[...]
    vec[2:3, :heads] = through[...]


def index(place, lengths, stepbias, decays, through, tiles):
    seqs = lax.axis_size("seq")
    whole = jnp.int32
    return pl.pallas_call(
        functools.partial(index_kernel, seqs, tiles),
        out_shape=(
            shape((seqs,), whole), shape((tiles,), whole), shape((seqs,), whole), shape((tiles,), whole),
            shape((tiles + 1,), WIDE), shape((EDGE, LANES), WIDE),
        ),
        in_specs=[SMEM_SPEC] * 2 + [VMEM_SPEC] * 3,
        out_specs=(SMEM_SPEC,) * 5 + (VMEM_SPEC,),
        compiler_params=pltpu.CompilerParams(vmem_limit_bytes=VMEM_LIMIT),
        name="index",
    )(place, lengths, stepbias[None, :], decays[None, :], through[None, :])


def blockwise(dims, index):
    return pl.BlockSpec(dims, index)


def fixed(dims):
    return pl.BlockSpec(dims, lambda i: (0,) * len(dims), pipeline_mode=pl.Buffered(1))


def carry_columns(carry_row_t, collect):
    high, middle, low = thirds(jnp.broadcast_to(carry_row_t, (LANES, LANES)))
    return nn(collect, high) + (nn(collect, middle) + nn(collect, low))


def pair_lanes(slab):
    lane = lax.broadcasted_iota(jnp.int32, slab.shape, 1)
    zero = jnp.zeros_like(slab)
    return jnp.where(lane < HDIM, slab, zero), jnp.where(lane >= HDIM, slab, zero)


def fold_states(slots, collect, inner, first, last, step, start):
    def hop(n, state):
        message = slots[first + n * step]
        carry = nn(collect[:, :HALO], message[inner:])
        return carry * state + message[:inner].astype(WIDE)

    return lax.fori_loop(0, (last - first) * step, hop, start)


def front_kernel(
    seqs, line, heads, blocks, chunks, give, take, flags,
    x_in, g_in, gating_in, payload_in, address_in, stepping_in, readout_in,
    vec, prenorm, kernels, filters, offsets, shifts,
    u_o, normed_o, gate_o, pre_o, conv_o, act_o, raw_o, cum_o, part_o, local_o, state_o, rim_o, g_o, w_o, r_o,
    x, g, gating, payload, address, stepping, readout, square,
    send_x, send_g, recv_x, recv_g, work_x, work_g, w_own, r_own, u, w, msg, slots,
    ext, prev, state, prod,
    sent, got, w_sent, w_got, w_passed, r_sent, r_got, r_passed, s_sent, s_got, s_passed, rim_sent, rim_got, own_sem,
    load_sem, line_sent, line_got, g_sent, g_got,
):
    i = pl.program_id(0)
    me, mine = lax.axis_index("seq"), lax.axis_index("head")
    tiles, _, width = x.shape
    rows = tiles * BLOCK
    depth, inner = gating.shape
    wide = pre_o.shape[1]
    part = rows // chunks
    per = blocks // chunks

    def rows_of(device):
        return pl.ds(pl.multiple_of(device * depth, depth), depth)

    def piece(n):
        if isinstance(n, int):
            return pl.ds(n * part, part)
        return pl.ds(pl.multiple_of(n * part, part), part)

    def u_line(n):
        return Line(line, u.at[piece(n)], width, line_sent.at[n], line_got.at[n])

    hops = sorted(((step, n) for step in range(1, line - 1) for n in range(chunks)), key=lambda hop: (sum(hop), hop))
    late_hops = [(step, n) for step, n in hops if step == line - 2 and n >= 2]
    early_hops = [hop for hop in hops if hop not in late_hops]

    def own_columns(ref):
        return ref.at[:, pl.ds(pl.multiple_of(mine * width, LANES), width)]

    w_plane = Plane(seqs, lambda s: w.at[rows_of(s)], w_sent, w_got, w_passed)
    r_plane = Plane(seqs, lambda s: r_o.at[rows_of(s)], r_sent, r_got, r_passed)
    s_plane = Plane(seqs, lambda s: slots.at[s], s_sent, s_got, s_passed, way=1)
    g_line = Line(line, g_o, width, g_sent, g_got)
    own_r = pltpu.make_async_copy(r_own, r_o.at[rows_of(me)], own_sem.at[0])
    own_g = pltpu.make_async_copy(work_g, g_line.view(mine), own_sem.at[1])
    save_w = pltpu.make_async_copy(w, w_o, own_sem.at[2])

    def rim_copy(to, shard):
        columns = pl.ds(pl.multiple_of(shard * width, LANES), width)
        return remote(
            work_x.at[pl.ds(rows - HALO, HALO)], u.at[pl.ds(rows, HALO), columns], rim_sent.at[to], rim_got.at[shard],
            {"seq": lax.rem(me + 1, seqs), "head": to},
        )

    def arrange(which, received, work):
        @pl.loop(1, seqs)
        def _(n):
            source = lax.rem(me + n, seqs)
            remote(
                received.at[source], received.at[source], sent.at[which, source], got.at[which, source], {"seq": source}
            ).wait_recv()

        for k in range(tiles):
            work[pl.ds(k * BLOCK, BLOCK), :] = received[take[k]]

    @pl.when(i == 0)
    def _():
        pairs = (
            (x_in, x), (g_in, g), (gating_in, gating), (payload_in, payload), (address_in, address),
            (stepping_in, stepping), (readout_in, readout),
        )
        loads = [pltpu.make_async_copy(src, dst, load_sem.at[n]) for n, (src, dst) in enumerate(pairs)]
        for load in loads:
            load.start()
        greet(seqs, line, corners=True)

        def post(which, source, outgoing, incoming):
            @pl.loop(1, seqs)
            def _(n):
                to = lax.rem(me + n, seqs)
                outgoing[to] = source[give[to]]
                remote(outgoing.at[to], incoming.at[me], sent.at[which, to], got.at[which, me], {"seq": to}).start()

            incoming[me] = source[give[me]]

        loads[0].wait()
        post(0, x, send_x, recv_x)
        for load in loads[1:]:
            load.wait()

        w_own[:, :inner] = gating[...].astype(LOW)
        w_own[:, inner : 2 * inner] = payload[...].astype(LOW)
        state2 = address.shape[1]
        w_own[:, 2 * inner : 2 * inner + state2] = address[...].astype(LOW)
        square[...] = jnp.zeros_like(square)
        square[: stepping.shape[0], :depth] = stepping[...]
        w_own[:, 2 * inner + state2 :] = square[...].T[:depth].astype(LOW)
        r_own[...] = readout[...].T.astype(LOW)
        w[rows_of(me), :] = w_own[...]
        own_r.start()

        arrange(0, recv_x, work_x)

        @pl.loop(0, line)
        def _(n):
            rim_copy(lax.rem(mine + n, line), mine).start()

        for n in range(chunks):
            u_line(n).first(work_x.at[piece(n)])
        w_plane.start(w_own)
        own = pltpu.make_async_copy(work_x, own_columns(u.at[pl.ds(0, rows)]), own_sem.at[3])
        own.start()
        post(1, g, send_g, recv_g)
        r_plane.start(r_own)
        for step, n in early_hops:
            u_line(n).hop(step)
        w_plane.relay()
        own.wait()

        @pl.loop(0, line)
        def _(n):
            rim_copy(n, n).wait_recv()

        w_plane.finish(w_own)
        save_w.start()

    for step, n in late_hops:

        @pl.when(i == (n - 1) * per)
        def _():
            u_line(n).hop(step)

    @pl.when(i == blocks // 2)
    def _():
        arrange(1, recv_g, work_g)
        g_line.first(work_g)
        own_g.start()

    if line > 1:

        @pl.when(lax.rem(i, per) == 0)
        def _():
            u_line(lax.div(i, per)).hop(line - 1)

    taps = jnp.concatenate([kernels[...], filters[...]], axis=1)
    bias = jnp.concatenate([offsets[...], shifts[...]], axis=1)
    spread_m, collect = head_rows(inner), head_columns(inner)

    def normalize(block):
        wide_rows = block.astype(WIDE)
        scale = lax.rsqrt(jnp.mean(wide_rows * wide_rows, axis=1, keepdims=True) + EPS)
        return (wide_rows * scale * prenorm[...]).astype(LOW)

    @pl.when(i == 0)
    def _():
        before = nn(normalize(u[pl.ds(rows, HALO), :]), w[:, inner : inner + wide]).astype(LOW).astype(WIDE)
        prev[...] = before[HALO - EDGE :]
        rim_o[...] = before[HALO - EDGE :]
        state[...] = jnp.zeros_like(state)
        prod[...] = jnp.ones_like(prod)

    u_v = u[pl.ds(pl.multiple_of(i * GROUP, GROUP), GROUP), :]
    u_o[...] = u_v
    normed = normalize(u_v)
    normed_o[...] = normed
    gate_o[...] = nn(normed, w[:, :inner])
    pre = nn(normed, w[:, inner : inner + wide]).astype(LOW)
    pre_o[...] = pre
    lane = lax.broadcasted_iota(jnp.int32, (GROUP, LANES), 1)
    raw = jnp.where(lane < heads, nn(normed, w[:, inner + wide :]) + vec[0:1, :], 0.0)
    raw_o[...] = raw
    first, second = flags[2 * i], flags[2 * i + 1]
    same = (first, second)
    for half in range(2):
        at = pl.ds(half * BLOCK, BLOCK)
        ext[0:EDGE, :] = prev[...] * same[half]
        ext[EDGE:, :] = pre[half * BLOCK : (half + 1) * BLOCK].astype(WIDE)
        prev[...] = ext[BLOCK:, :]
        total = bias + taps[TAPS - 1 : TAPS] * ext[EDGE:, :]
        for tap in range(TAPS - 1):
            total = total + taps[tap : tap + 1] * ext[pl.ds(EDGE - (TAPS - 1) + tap, BLOCK), :]
        conv_o[at, :] = total
        act_o[at, :] = (total * sigmoid(total)).astype(LOW)

    steps, _, _ = step_terms(raw, heads)
    scale = -jnp.exp(vec[1:2, :])
    cum = sum_before(steps * scale)
    cum_o[...] = cum
    cum_t, steps_t = cum.T, steps.T
    write = act_o[:, inner : inner + STATE]
    read = act_o[:, inner + STATE :]
    lower = ones_before(BLOCK)
    top, low = slice(0, BLOCK), slice(BLOCK, GROUP)
    s00 = jnp.where(lower, nt(read[top], write[top]), 0.0)
    s10 = nt(read[low], write[top]) * second
    s11 = jnp.where(lower, nt(read[low], write[low]), 0.0)

    def mix(scores, head, t, s):
        decay = jnp.exp(jnp.minimum(cum[t, head : head + 1] - cum_t[head : head + 1, s], 0.0))
        return (scores * (decay * steps_t[head : head + 1, s])).astype(LOW)

    last = cum[GROUP - 1 : GROUP, :]
    row = lax.broadcasted_iota(jnp.int32, (GROUP, LANES), 0)
    weight = steps * jnp.exp(last - cum) * jnp.where(row < BLOCK, second, 1.0)
    weight_w = to_columns(weight, spread_m)
    skip = to_columns(jnp.broadcast_to(vec[2:3, :], (EDGE, LANES)), spread_m)[0:1]
    packed = []
    for pair in range(inner // LANES):
        columns = slice(pair * LANES, (pair + 1) * LANES)
        slab = act_o[:, columns]
        slab_f = slab.astype(WIDE)
        ones = pair_lanes(slab)
        h0, h1 = 2 * pair, 2 * pair + 1
        y0 = nn(
            jnp.concatenate([mix(s00, h0, top, top), mix(s00, h1, top, top)], axis=1),
            jnp.concatenate([ones[0][top], ones[1][top]], axis=0),
        )
        y1 = nn(
            jnp.concatenate(
                [mix(s10, h0, low, top), mix(s11, h0, low, low), mix(s10, h1, low, top), mix(s11, h1, low, low)], axis=1
            ),
            jnp.concatenate([ones[0], ones[1]], axis=0),
        )
        part_o[top, columns] = y0 + skip[:, columns] * slab_f[top]
        part_o[low, columns] = y1 + skip[:, columns] * slab_f[low]
        packed.append((slab_f * weight_w[:, columns]).astype(LOW))
    local = tn(jnp.concatenate(packed, axis=1), write)
    local_o[0] = local
    carry = jnp.exp(cum_t[:, GROUP - 1 : GROUP]) * (first * second)
    state[...] = carry_columns(carry, collect) * state[...] + local
    prod[...] = jnp.broadcast_to(carry[:HALO], (HALO, STATE)) * prod[...]

    @pl.when(i == blocks - 1)
    def _():
        msg[:inner, :] = state[...].astype(LOW)
        msg[inner:, :] = prod[...].astype(LOW)
        s_plane.start(msg)
        s_plane.relay()
        s_plane.finish(msg)
        state_o[...] = fold_states(slots, collect, inner, 0, me, 1, jnp.zeros((inner, STATE), WIDE))
        r_plane.relay()
        r_plane.finish(r_own)
        if line > 1:
            g_line.hop(1, give=False)
        g_line.finish(work_g, (0,))
        for n in range(chunks):
            u_line(n).finish(work_x.at[piece(n)])

        @pl.loop(0, line)
        def _(n):
            rim_copy(n, mine).wait_send()


        @pl.loop(1, seqs)
        def _(n):
            other = lax.rem(me + n, seqs)
            for which, buffer in ((0, send_x), (1, send_g)):
                remote(
                    buffer.at[other], buffer.at[other], sent.at[which, other], got.at[which, other], {"seq": other}
                ).wait_send()

        own_r.wait()
        own_g.wait()
        save_w.wait()


def front(give, take, flags, x, g, gating, payload, address, stepping, readout, vec, prenorm, kernels, filters, offsets, shifts):
    seqs, line = lax.axis_size("seq"), lax.axis_size("head")
    rows, width = x.shape
    depth, inner = gating.shape
    total = depth * seqs
    wide = inner + address.shape[1]
    columns = inner + wide + LANES
    blocks = rows // GROUP
    chunks = min(blocks, 4)
    heads = stepping.shape[1]
    routed = (seqs, BLOCK, width)
    given = (rows // BLOCK, BLOCK, width)
    message = (inner + HALO, STATE)
    operands = (x.reshape(given), g.reshape(given), gating, payload, address, stepping.T, readout)
    small = (vec, prenorm, kernels, filters, offsets, shifts)

    def by_rows(size):
        return blockwise((GROUP, size), lambda i: (i, 0))

    return pl.pallas_call(
        functools.partial(front_kernel, seqs, line, heads, blocks, chunks),
        grid=(blocks,),
        out_shape=(
            shape((rows, total), LOW), shape((rows, total), LOW), shape((rows, inner), WIDE), shape((rows, wide), LOW),
            shape((rows, wide), WIDE), shape((rows, wide), LOW), shape((rows, LANES), WIDE), shape((rows, LANES), WIDE),
            shape((rows, inner), WIDE), shape((blocks, inner, STATE), WIDE), shape((inner, STATE), WIDE),
            shape((EDGE, wide), WIDE), shape((rows, total), LOW), shape((total, columns), LOW),
            shape((total, inner), LOW),
        ),
        in_specs=[SMEM_SPEC] * 3 + [ANY_SPEC] * 7 + [fixed(a.shape) for a in small],
        out_specs=(
            by_rows(total), by_rows(total), by_rows(inner), by_rows(wide), by_rows(wide), by_rows(wide), by_rows(LANES),
            by_rows(LANES), by_rows(inner), blockwise((1, inner, STATE), lambda i: (i, 0, 0)), fixed((inner, STATE)),
            fixed((EDGE, wide)), ANY_SPEC, ANY_SPEC, ANY_SPEC,
        ),
        scratch_shapes=[pltpu.VMEM(a.shape, a.dtype) for a in operands] + [
            pltpu.VMEM((LANES, LANES), WIDE),
            pltpu.VMEM(routed, LOW), pltpu.VMEM(routed, LOW), pltpu.VMEM(routed, LOW), pltpu.VMEM(routed, LOW),
            pltpu.VMEM((rows, width), LOW), pltpu.VMEM((rows, width), LOW),
            pltpu.VMEM((depth, columns), LOW), pltpu.VMEM((depth, inner), LOW),
            pltpu.VMEM((rows + HALO, total), LOW), pltpu.VMEM((total, columns), LOW),
            pltpu.VMEM(message, LOW), pltpu.VMEM((seqs,) + message, LOW),
            pltpu.VMEM((EDGE + BLOCK, wide), WIDE), pltpu.VMEM((EDGE, wide), WIDE),
            pltpu.VMEM((inner, STATE), WIDE), pltpu.VMEM((HALO, STATE), WIDE),
            DMA((2, seqs)), DMA((2, seqs)),
            DMA((seqs,)), DMA((seqs,)), DMA((seqs,)), DMA((seqs,)), DMA((seqs,)), DMA((seqs,)),
            DMA((seqs,)), DMA((seqs,)), DMA((seqs,)), DMA((line,)), DMA((line,)), DMA((4,)), DMA((7,)),
            DMA((chunks, 2, line)), DMA((chunks, line)), DMA((2, line)), DMA((line,)),
        ],
        compiler_params=pltpu.CompilerParams(
            collective_id=0, has_side_effects=True, vmem_limit_bytes=VMEM_LIMIT, dimension_semantics=("arbitrary",)
        ),
        name="front",
    )(give, take, flags, *operands, *small)


def conv_grad(d_act, conv):
    sig = sigmoid(conv)
    return d_act * (sig * (1.0 + conv * (1.0 - sig)))


class Stream:
    def __init__(self, view, slots, sems):
        self.view, self.slots, self.sems = view, slots, sems

    def copy(self, block, turn):
        slot = lax.rem(turn, 2)
        return pltpu.make_async_copy(self.view(block), self.slots.at[slot], self.sems.at[slot])

    def start(self, block, turn):
        self.copy(block, turn).start()

    def wait(self, block, turn):
        self.copy(block, turn).wait()

    def at(self, turn):
        return self.slots.at[lax.rem(turn, 2)]


class Fold:
    def __init__(self, line, part, got, relay, sent, arrived, relayed):
        self.line, self.part, self.got, self.relay = line, part, got, relay
        self.sent, self.arrived, self.relayed = sent, arrived, relayed
        self.mine = mine = lax.axis_index("head")
        self.merges = line == 4
        low = mine < 2
        self.is_end = (mine == 0) | (mine == line - 1)
        self.end, self.mid = jnp.where(low, 0, 3), jnp.where(low, 1, 2)
        self.next, self.far = jnp.where(low, 2, 1), jnp.where(low, 3, 0)

    def others(self, body):
        @pl.loop(1, self.line)
        def _(n):
            body(lax.rem(self.mine + n, self.line))

    def chunk(self, rows, piece, chunk, to, way):
        return remote(
            self.part(chunk, rows), self.got.at[self.mine, rows], self.sent.at[way, piece],
            self.arrived.at[self.mine, piece], {"head": to},
        )

    def hand(self, rows, piece, chunk, which):
        return remote(
            self.part(chunk, rows), self.relay.at[which, rows], self.sent.at[1 + which, piece],
            self.relayed.at[which, piece], {"head": self.mid},
        )

    def landed(self, rows, piece, source):
        slot = self.got.at[source, rows]
        return remote(slot, slot, self.sent.at[0, piece], self.arrived.at[source, piece], {"head": source})

    def send_far(self, rows, piece):
        if not self.merges:
            if self.line > 1:
                self.others(lambda to: self.chunk(rows, piece, to, to, to).start())
            return

        @pl.when(self.is_end)
        def _():
            self.hand(rows, piece, self.far, 1).start()
            self.hand(rows, piece, self.next, 0).start()

    def send_near(self, rows, piece):
        if self.merges:
            near = jnp.where(self.is_end, self.mid, self.end)
            self.chunk(rows, piece, near, near, 0).start()

    def merge(self, rows, piece):
        if self.merges:

            @pl.when(jnp.logical_not(self.is_end))
            def _():
                for which, chunk in ((1, self.far), (0, self.next)):
                    self.hand(rows, piece, chunk, which).wait_recv()
                    own = self.part(chunk, rows)
                    own[...] = (own[...].astype(WIDE) + self.relay[which, rows].astype(WIDE)).astype(LOW)
                    self.chunk(rows, piece, chunk, chunk, 1 + which).start()

    def drain(self, rows, piece):
        if not self.merges:
            if self.line > 1:
                self.others(lambda to: self.chunk(rows, piece, to, to, to).wait_send())
                self.others(lambda source: self.landed(rows, piece, source).wait_recv())
            return
        for way in range(3):
            self.chunk(rows, piece, self.mid, self.mid, way).wait_send()
        for source in (jnp.where(self.is_end, self.mid, self.end), self.next):
            self.landed(rows, piece, source).wait_recv()

    def total(self, rows, ref):
        sum_ = self.part(self.mine, rows)[...].astype(WIDE)
        if self.merges:
            first = jnp.where(self.is_end, self.mid, self.end)
            return sum_ + ref[first, rows].astype(WIDE) + ref[self.next, rows].astype(WIDE)
        for n in range(1, self.line):
            sum_ = sum_ + ref[lax.rem(self.mine + n, self.line), rows].astype(WIDE)
        return sum_


class Halved:
    def __init__(self, seqs, src, pair, got, sems):
        self.chips, self.src, self.pair, self.got = seqs // 2, src, pair, got
        self.depth = pair.shape[1]
        self.pair_sent, self.pair_got, self.sent, self.arrived = [sems.at[n] for n in range(4)]
        self.me = lax.axis_index("seq")
        self.core = lax.rem(self.me, 2)
        self.chip = lax.div(self.me, 2)

    def rows(self, chip, core):
        return pl.ds(pl.multiple_of((2 * chip + core) * self.depth, self.depth), self.depth)

    def give(self, chip):
        return remote(
            self.src.at[self.rows(chip, 1 - self.core)], self.pair.at[chip], self.pair_sent.at[chip],
            self.pair_got.at[chip], {"seq": 2 * self.chip + 1 - self.core},
        )

    def send(self, chip, slot):
        return remote(
            self.src.at[self.rows(chip, self.core)], self.got.at[slot], self.sent.at[chip], self.arrived.at[slot],
            {"seq": 2 * chip + self.core},
        )

    def kept(self):
        return pltpu.make_async_copy(
            self.src.at[self.rows(self.chip, self.core)], self.got.at[self.chip], self.sent.at[self.chip]
        )

    def begin(self):
        pl.loop(0, self.chips)(lambda chip: self.give(chip).start())

    def combine(self):
        def add(chip):
            rows = self.rows(chip, self.core)
            self.give(chip).wait_recv()
            self.src[rows, :] = (self.src[rows, :].astype(WIDE) + self.pair[chip].astype(WIDE)).astype(LOW)

        @pl.loop(1, self.chips)
        def _(n):
            chip = lax.rem(self.chip + n, self.chips)
            add(chip)
            self.send(chip, self.chip).start()

        add(self.chip)
        self.kept().start()

    def drain(self):
        @pl.loop(1, self.chips)
        def _(n):
            other = lax.rem(self.chip + n, self.chips)
            self.send(other, other).wait()

        self.kept().wait()
        pl.loop(0, self.chips)(lambda chip: self.give(chip).wait_send())


def core_kernel(
    seqs, line, heads, blocks, roomy, flags, give,
    gate_in, part_in, act_in, cum_in, raw_in, local_in, conv_in, pre_in, normed_in, u_in, g_part, r_in, w_in,
    state_in, postnorm, vec, prenorm, kernels, filters, rim,
    out_recv, grad_recv, out_far, dx_far, early_got, dw_got, addr_got, small_got,
    gate_b, part_b, read_b, cum_b, local_b, normed_b, act_b, raw_b, conv_b, pre_b, before_b, u_b, stream_sems,
    r_t, w, ssd_s, din_s, dssd_s, dgate_s, ds_s, starts, q, state, prod, g_buf, out_part, back_slots, back_msg,
    relay, dx_relay, out_near, dx_near, sums,
    totals, gread, ggate, early_low, early_pair, gpost, tiny, d_conv, d_step, after, edge_own, edge_got, ext,
    keep_conv, keep_step, keep_normed, keep_u,
    taps_g, bias_g, dw, dw_low, dw_pair, da_low, da_pair, da_got, da_send, pn, zs_send, zs_got, small, result, fin_send,
    back_sent, back_sem, back_passed, sum_sent, sum_sem, line_sent, line_sem, load_sem, out_sent, out_sem, out_relayed,
    early_sems, dw_sems, da_sems, dx_sent, dx_sem, dx_relayed, edge_sent, edge_sem, zs_sent, zs_sem, da_sent, da_sem, small_sent,
    small_sem, fin_sent, fin_sem, own_sem, weight_sem, residual_sem,
):
    me, mine = lax.axis_index("seq"), lax.axis_index("head")
    inner = r_t.shape[1]
    wide = act_b.shape[2]
    width = out_part.shape[2]
    depth = early_got.shape[1]
    rows = ssd_s.shape[0]
    size = 2 * STATE // line
    chunks = line_sem.shape[0]
    per = blocks // chunks
    back_plane = Plane(seqs, lambda s: back_slots.at[s], back_sent, back_sem, back_passed, way=-1)
    out_got, dx_got = (out_near, dx_near) if roomy else (out_far, dx_far)

    def group_rows(b):
        return pl.ds(pl.multiple_of(b * GROUP, GROUP), GROUP)

    def rows_of(device):
        return pl.ds(pl.multiple_of(device * depth, depth), depth)

    def shard_of(ref, shard):
        return ref.at[:, pl.ds(pl.multiple_of(shard * width, LANES), width)]

    def chunk_rows(n):
        return pl.ds(pl.multiple_of(n * (rows // chunks), rows // chunks), rows // chunks)

    def g_line(n):
        return Line(line, g_buf.at[chunk_rows(n)], width, line_sent.at[n], line_sem.at[n])

    def by_group(ref, first=0, columns=None):
        if columns is None:
            return lambda b: ref.at[group_rows(b)]
        return lambda b: ref.at[group_rows(b), pl.ds(first, columns)]

    def all_line(body):
        if line > 1:

            @pl.loop(1, line)
            def _(n):
                body(lax.rem(mine + n, line))

    def all_seq(body):
        @pl.loop(1, seqs)
        def _(n):
            body(lax.rem(me + n, seqs))

    def before_rows(b):
        start = jnp.maximum(b * GROUP - HALO, 0)
        return pre_in.at[pl.ds(pl.multiple_of(start, HALO), HALO)]

    views = (
        (by_group(gate_in), gate_b), (by_group(part_in), part_b), (by_group(act_in, inner + STATE, STATE), read_b),
        (by_group(cum_in), cum_b), (lambda b: local_in.at[b], local_b), (by_group(normed_in), normed_b),
        (by_group(act_in), act_b), (by_group(raw_in), raw_b), (by_group(conv_in), conv_b), (by_group(pre_in), pre_b),
        (before_rows, before_b), (by_group(u_in), u_b),
    )
    gate_f, part_f, read_f, cum_f, local_f, normed_f, act_f, raw_f, conv_f, pre_f, before_f, u_f = [
        Stream(view, slots, stream_sems.at[n]) for n, (view, slots) in enumerate(views)
    ]

    def forwards(turn):
        return turn

    def backwards(turn):
        return blocks - 1 - turn

    def begin(streams, order):
        for stream in streams:
            stream.start(order(0), 0)

    def step(streams, order, turn, following):
        @pl.when(turn + 1 < blocks)
        def _():
            for stream in streams:
                stream.start(order(turn + 1), turn + 1)

        if following is not None:
            pl.when(turn + 1 == blocks)(lambda: begin(*following))
        for stream in streams:
            stream.wait(order(turn), turn)

    first_phase = ((gate_f, part_f, read_f, cum_f, local_f), forwards)
    norm_phase = ((gate_f,), forwards)
    gate_phase = ((gate_f, read_f, cum_f), forwards)
    scan_phase = ((gate_f, normed_f, act_f, cum_f, raw_f), forwards)
    last_phase = ((act_f, cum_f, raw_f, conv_f, pre_f, before_f, normed_f, u_f), backwards)

    def each_load(body):
        def load(shard, n):
            return pltpu.make_async_copy(shard_of(g_part, shard), shard_of(g_buf, shard), load_sem.at[n])

        for n, away in enumerate((0, -1, 1)):
            if abs(away) < line:
                there = (mine + away >= 0) & (mine + away < line)
                pl.when(there)(lambda: body(load(mine + away, n)))

    def sum_copy(to, slot):
        return remote(sums.at[mine], sums.at[slot], sum_sent.at[to], sum_sem.at[slot], {"head": to})

    early_sum = Halved(seqs, early_low, early_pair, early_got, early_sems)
    dw_sum = Halved(seqs, dw_low, dw_pair, dw_got, dw_sems)
    da_sum = Halved(seqs, da_low, da_pair, da_got, da_sems)
    out_fold = Fold(
        line, lambda z, at: out_part.at[z, at], out_got, relay, out_sent, out_sem, out_relayed
    )
    dx_fold = Fold(
        line, lambda z, at: shard_of(g_buf.at[at], z), dx_got, dx_relay, dx_sent, dx_sem, dx_relayed
    )
    short_piece = (pl.ds(rows - GROUP, GROUP - HALO), blocks - 1)
    edge_piece = (pl.ds(rows - HALO, HALO), blocks)

    def each_piece(body):
        body(*short_piece)

        @pl.loop(1, blocks)
        def _(turn):
            b = blocks - 1 - turn
            body(group_rows(b), b)

        body(*edge_piece)

    def edge_copy(to):
        return remote(edge_own, edge_got, edge_sent, edge_sem, {"seq": to})

    def zs_copy(to, slot):
        return remote(zs_send.at[to], zs_got.at[slot], zs_sent.at[to], zs_sem.at[slot], {"head": to})

    def da_copy(to, slot):
        return remote(da_send.at[to], addr_got.at[slot], da_sent.at[to], da_sem.at[slot], {"head": to})

    def small_copy(to, slot):
        return remote(small, small_got.at[slot], small_sent.at[to], small_sem.at[slot], {"seq": to})

    arrivals = (out_recv, grad_recv)

    def fin_copy(which, to, slot):
        return remote(
            fin_send.at[to], arrivals[which].at[slot], fin_sent.at[which, to], fin_sem.at[which, slot],
            {"seq": to},
        )

    own_copies = {
        "addr": pltpu.make_async_copy(da_send.at[mine], addr_got.at[mine], own_sem.at[0]),
        "small": pltpu.make_async_copy(small, small_got.at[me], own_sem.at[1]),
        "fin0": pltpu.make_async_copy(fin_send.at[me], out_recv.at[me], own_sem.at[2]),
        "fin1": pltpu.make_async_copy(fin_send.at[me], grad_recv.at[me], own_sem.at[3]),
    }

    def route(which):
        def send(to):
            fin_send[to] = result[give[to]]
            fin_copy(which, to, me).start()

        all_seq(send)
        fin_send[me] = result[give[me]]
        own_copies["fin%d" % which].start()

    def fetch(src):
        if not roomy:
            all_line(lambda z: pltpu.make_async_copy(src.at[z], out_part.at[z], load_sem.at[0]).start())
            all_line(lambda z: pltpu.make_async_copy(src.at[z], out_part.at[z], load_sem.at[0]).wait())

    row = lax.broadcasted_iota(jnp.int32, (GROUP, LANES), 0)
    lane = lax.broadcasted_iota(jnp.int32, (GROUP, LANES), 1)
    spread_m, collect = head_rows(inner), head_columns(inner)
    lower_mask = ones_before(BLOCK)
    top, low = slice(0, BLOCK), slice(BLOCK, GROUP)

    def entry_of(b, cum_v):
        gone_on = flags[2 * b] * jnp.where(row < BLOCK, 1.0, flags[2 * b + 1])
        return to_columns(jnp.exp(cum_v) * gone_on, spread_m)

    def carry_of(b, cum_t):
        return jnp.exp(cum_t[:, GROUP - 1 : GROUP]) * (flags[2 * b] * flags[2 * b + 1])

    def row_stats(b):
        stats = jnp.concatenate([totals[b], jnp.zeros((LANES - EDGE, GROUP), WIDE)], axis=0).T
        return lax.rsqrt(stats[:, 0:1] / INNER + EPS), stats[:, 1:2]

    def gated_of(ssd, turn):
        gate_v = gate_f.at(turn)[...]
        return ssd * (gate_v * sigmoid(gate_v))

    begin(*first_phase)
    fetch_r = pltpu.make_async_copy(r_in, r_t, weight_sem.at[0])
    fetch_w = pltpu.make_async_copy(w_in, w, weight_sem.at[1])
    fetch_r.start()
    greet(seqs, line)
    for n in range(chunks):
        g_line(n).hop(1, take=False, source=lambda shard: shard_of(g_part.at[chunk_rows(n)], shard))
    each_load(lambda copy: copy.start())
    fetch_w.start()
    state[...] = state_in[...]
    fetch_r.wait()

    def out_part_done(b):
        if out_fold.merges:
            pl.when(b < blocks - 1)(lambda: out_fold.send_far(group_rows(b), b))

    @pl.loop(0, blocks)
    def _(b):
        step(*first_phase, b, norm_phase)
        here = group_rows(b)
        cum_v = cum_f.at(b)[...]
        start = state[...]
        starts[b] = start
        ssd = part_f.at(b)[...] + entry_of(b, cum_v) * nt(read_f.at(b)[...], start.astype(LOW))
        ssd_s[here, :] = ssd
        state[...] = carry_columns(carry_of(b, cum_v.T), collect) * start + local_f.at(b)[...]
        out = nt((gated_of(ssd, b) * postnorm[...]).astype(LOW), r_t[...])
        for z in range(line):
            out_part[z, here] = out[:, z * width : (z + 1) * width].astype(LOW)
        out_part_done(b)

    for hop in range(2, line - 1):
        for n in range(chunks):
            g_line(n).hop(hop)
    each_load(lambda copy: copy.wait())
    fetch_w.wait()

    @pl.loop(0, blocks)
    def _(b):
        step(*norm_phase, b, gate_phase)
        here = group_rows(b)
        if line > 1:
            pl.when(lax.rem(b, per) == 0)(lambda: g_line(lax.div(b, per)).hop(line - 1))
        gated = gated_of(ssd_s[here, :], b)
        d_inner = nn(g_buf[here, :], r_t[...])
        din_s[here, :] = d_inner
        squares = jnp.sum(gated * gated, axis=1, keepdims=True)
        dots = jnp.sum(gated * postnorm[...] * d_inner, axis=1, keepdims=True)
        both = jnp.where(lane == 0, squares, jnp.where(lane == 1, dots, 0.0)).T
        sums[mine, b] = both[:EDGE]

    all_line(lambda to: sum_copy(to, mine).start())
    for n in range(chunks):
        g_line(n).finish(None, range(1, line - 1))
    for ref in (gread, ggate, gpost, state, tiny, taps_g, bias_g, dw, pn):
        ref[...] = jnp.zeros_like(ref)
    prod[...] = jnp.ones_like(prod)
    all_line(lambda other: sum_copy(other, other).wait())
    totals[...] = jnp.sum(sums[...], axis=0)

    if out_fold.merges:
        out_fold.send_far(group_rows(blocks - 1), blocks - 1)
        pl.loop(0, blocks)(lambda b: out_fold.send_near(group_rows(b), b))

    def residual(n):
        at = pl.ds(pl.multiple_of(n * BLOCK, BLOCK), BLOCK)
        columns = pl.ds(pl.multiple_of(mine * width, LANES), width)
        return pltpu.make_async_copy(u_in.at[at, columns], result.at[n], residual_sem.at[n])

    pl.loop(0, 2 * blocks)(lambda n: residual(n).start())

    def norm_back(b, turn):
        here = group_rows(b)
        inv, dot = row_stats(b)
        gate_v = gate_f.at(turn)[...]
        sig = sigmoid(gate_v)
        ssd = ssd_s[here, :]
        return gate_v, sig, ssd, ssd * (gate_v * sig), inv, dot

    @pl.loop(0, blocks)
    def _(b):
        step(*gate_phase, b, scan_phase)
        here = group_rows(b)
        cum_v = cum_f.at(b)[...]
        gate_v, sig, ssd, gated, inv, dot = norm_back(b, b)
        d_inner = din_s[here, :]
        d_gated = (inv * postnorm[...]) * d_inner - gated * (inv * inv * inv / INNER * dot)
        gpost[...] += jnp.sum(d_inner * (gated * inv), axis=0, keepdims=True)
        d_ssd = (d_gated * (gate_v * sig)).astype(LOW)
        dssd_s[here, :] = d_ssd
        dgate_s[here, :] = (d_gated * ssd * sig * (1.0 + gate_v * (1.0 - sig))).astype(LOW)
        query_grad = (d_ssd.astype(WIDE) * entry_of(b, cum_v)).astype(LOW)
        found = tn(query_grad, read_f.at(b)[...])
        q[b] = found
        state[...] += carry_columns(prod[...], collect) * found
        prod[...] = prod[...] * carry_of(b, cum_v.T)

    back_msg[:inner, :] = state[...].astype(LOW)
    back_msg[inner:, :] = jnp.broadcast_to(prod[:HALO], (HALO, STATE)).astype(LOW)
    back_plane.start(back_msg)

    if out_fold.merges:

        @pl.when(jnp.logical_not(out_fold.is_end))
        def _():
            @pl.loop(0, blocks - 1)
            def _(b):
                out_fold.merge(group_rows(b), b)

    else:
        pl.loop(0, blocks)(lambda b: out_fold.send_far(group_rows(b), b))

    @pl.loop(0, blocks)
    def _(b):
        step(*scan_phase, b, last_phase)
        here = group_rows(b)
        second = flags[2 * b + 1]
        act = act_f.at(b)
        cum_v = cum_f.at(b)[...]
        cum_t = cum_v.T
        steps, _, _ = step_terms(raw_f.at(b)[...], heads)
        steps_t = steps.T
        write = act[:, inner : inner + STATE]
        read_v = act[:, inner + STATE :]
        s00 = jnp.where(lower_mask, nt(read_v[top], write[top]), 0.0)
        s10 = nt(read_v[low], write[top]) * second
        s11 = jnp.where(lower_mask, nt(read_v[low], write[low]), 0.0)

        def decay_of(head, t, s):
            decay = jnp.exp(jnp.minimum(cum_v[t, head : head + 1] - cum_t[head : head + 1, s], 0.0))
            return decay * steps_t[head : head + 1, s]

        ds00 = jnp.zeros((BLOCK, BLOCK), WIDE)
        ds10 = jnp.zeros((BLOCK, BLOCK), WIDE)
        ds11 = jnp.zeros((BLOCK, BLOCK), WIDE)
        for pair in range(inner // LANES):
            columns = slice(pair * LANES, (pair + 1) * LANES)
            values = act[:, columns]
            dys = pair_lanes(dssd_s[here, columns])
            m00, m10, m11 = [], [], []
            for k in range(2):
                head = 2 * pair + k
                l00, l10, l11 = decay_of(head, top, top), decay_of(head, low, top), decay_of(head, low, low)
                m00.append((s00 * l00).astype(LOW))
                m10.append((s10 * l10).astype(LOW))
                m11.append((s11 * l11).astype(LOW))
                ds00 = ds00 + nt(dys[k][top], values[top]) * l00
                ds10 = ds10 + nt(dys[k][low], values[top]) * l10
                ds11 = ds11 + nt(dys[k][low], values[low]) * l11
            v0 = tn(
                jnp.concatenate([m00[0], m10[0], m00[1], m10[1]], axis=0), jnp.concatenate([dys[0], dys[1]], axis=0)
            )
            v1 = tn(
                jnp.concatenate([m11[0], m11[1]], axis=0), jnp.concatenate([dys[0][low], dys[1][low]], axis=0)
            )
            din_s[here, columns] = jnp.concatenate([v0, v1], axis=0)
        ds_s[here, :] = jnp.concatenate(
            [
                jnp.concatenate([jnp.where(lower_mask, ds00, 0.0), jnp.zeros((BLOCK, BLOCK), WIDE)], axis=1),
                jnp.concatenate([ds10 * second, jnp.where(lower_mask, ds11, 0.0)], axis=1),
            ],
            axis=0,
        ).astype(LOW)

        gated, inv = norm_back(b, b)[3:5]
        inner_normed = (gated * inv * postnorm[...]).astype(LOW)
        gread[...] += tn(g_buf[here, :], inner_normed)
        ggate[...] += tn(normed_f.at(b)[...], dgate_s[here, :])

        @pl.when(b == blocks // 2)
        def _():
            back_plane.relay()

    early_low[:, :inner] = gread[...].astype(LOW)
    early_low[:, inner:] = ggate[...].astype(LOW)
    early_sum.begin()
    out_fold.merge(group_rows(blocks - 1), blocks - 1)
    back_plane.finish(back_msg)
    state[...] = fold_states(back_slots, collect, inner, seqs - 1, me, -1, jnp.zeros((inner, STATE), WIDE))

    taps = jnp.concatenate([kernels[...], filters[...]], axis=1)
    scale = -jnp.exp(vec[1:2, :])
    through_w = to_columns(jnp.broadcast_to(vec[2:3, :], (EDGE, LANES)), spread_m)[0:1]

    def scan_back(b, turn):
        here = group_rows(b)
        first, second = flags[2 * b], flags[2 * b + 1]
        act, conv = act_f.at(turn), conv_f.at(turn)
        cum_v = cum_f.at(turn)[...]
        steps, sig, ratio = step_terms(raw_f.at(turn)[...], heads)
        last = cum_v[GROUP - 1 : GROUP, :]
        write = act[:, inner : inner + STATE]
        read_v = act[:, inner + STATE :]
        end = state[...]
        end_low = end.astype(LOW)
        start = starts[b]
        state[...] = carry_columns(carry_of(b, cum_v.T), collect) * end + q[b]
        weight = steps * jnp.exp(last - cum_v) * jnp.where(row < BLOCK, second, 1.0)
        weight_w = to_columns(weight, spread_m)
        d_ssd = dssd_s[here, :]
        dy_f = d_ssd.astype(WIDE)
        values_f = act[:, :inner].astype(WIDE)
        d_query = (dy_f * entry_of(b, cum_v)).astype(LOW)
        tail = nt(write, end_low) * weight_w
        whole = din_s[here, :] + tail
        d_conv[:, :inner] = conv_grad(whole + through_w * dy_f, conv[:, :inner])
        packed = (values_f * weight_w).astype(LOW)
        ds = ds_s[here, :]
        d_read = nn(ds, write) + nn(d_query, start.astype(LOW))
        d_write = tn(ds, read_v) + nn(packed, end_low)
        d_conv[:, inner : inner + STATE] = conv_grad(d_write, conv[:, inner : inner + STATE])
        d_conv[:, inner + STATE :] = conv_grad(d_read, conv[:, inner + STATE :])

        own = to_heads(dy_f * values_f, collect)
        r1 = to_heads(dy_f * ssd_s[here, :], collect) - vec[2:3, :] * own
        by_value = to_heads(values_f * whole, collect)
        tail_sum = jnp.sum(tail * values_f, axis=0, keepdims=True)
        tail_row = to_heads(jnp.broadcast_to(tail_sum, (EDGE, inner)), collect)[0:1]
        high, rest = halves(end * start)
        ones = jnp.ones((EDGE, STATE), LOW)
        carry_grad = to_heads(nt(ones, high) + nt(ones, rest), collect)[0:1]
        d_last = tail_row + carry_grad * (jnp.exp(last) * (first * second))
        d_cum = r1 - by_value + jnp.where(row == GROUP - 1, d_last, 0.0)
        d_rate = sum_after(d_cum)
        d_raw = d_rate * scale * sig + by_value * ratio
        d_step[...] = d_raw.astype(LOW)
        tiny[0:1, :] += jnp.sum(d_raw, axis=0, keepdims=True)
        tiny[1:2, :] += jnp.sum(d_rate * steps, axis=0, keepdims=True) * scale
        tiny[2:3, :] += jnp.sum(own, axis=0, keepdims=True)

    def conv_back(ref, count):
        total = taps[TAPS - 1 : TAPS] * ref[pl.ds(0, count), :]
        for tap in range(TAPS - 1):
            total = total + taps[tap : tap + 1] * ref[pl.ds(TAPS - 1 - tap, count), :]
        return total.astype(LOW)

    def input_back(d_pre, step_grad, gate_grad, u_rows):
        d_normed = (
            nt(gate_grad, w[:, :inner])
            + nt(d_pre, w[:, inner : inner + wide])
            + nt(step_grad, w[:, inner + wide :])
        )
        rows_f = u_rows.astype(WIDE)
        inv = lax.rsqrt(jnp.mean(rows_f * rows_f, axis=1, keepdims=True) + EPS)
        gained = d_normed * prenorm[...]
        dot = jnp.sum(gained * rows_f, axis=1, keepdims=True)
        grad = gained * inv - rows_f * (inv * inv * inv / D * dot)
        return grad.astype(LOW), d_normed * (rows_f * inv)

    def rows_back(b, turn, final):
        grad_c = d_conv[...]
        pre_v = pre_f.at(turn)[...].astype(WIDE)
        before = jnp.where(b == 0, rim[...], before_f.at(turn)[HALO - EDGE :, :].astype(WIDE))
        bias_g[...] += jnp.sum(grad_c, axis=0, keepdims=True)
        parts = []
        for half in range(2):
            part_rows = slice(half * BLOCK, (half + 1) * BLOCK)
            tile = grad_c[part_rows]
            ext[0:EDGE, :] = (before if half == 0 else pre_v[BLOCK - EDGE : BLOCK]) * flags[2 * b + half]
            ext[EDGE:, :] = pre_v[part_rows]
            for tap in range(TAPS):
                taps_g[tap : tap + 1, :] += jnp.sum(
                    tile * ext[pl.ds(EDGE - (TAPS - 1) + tap, BLOCK), :], axis=0, keepdims=True
                )
            ext[:BLOCK, :] = tile
            if half == 0:
                ext[BLOCK:, :] = grad_c[BLOCK : BLOCK + EDGE] * flags[2 * b + 1]
            elif final:
                ext[BLOCK:, :] = jnp.zeros((EDGE, wide), WIDE)
            else:
                ext[BLOCK:, :] = after[...] * flags[2 * b + 2]
            parts.append(conv_back(ext, BLOCK))
        d_pre = jnp.concatenate(parts, axis=0)
        step_grad = d_step[...]
        normed_v = normed_f.at(turn)[...]
        u_v = u_f.at(turn)
        done = lax.broadcasted_iota(jnp.int32, (GROUP, 1), 0) < GROUP - HALO
        if final:
            d_pre = jnp.where(done, d_pre, jnp.zeros_like(d_pre))
            keep_conv[:HALO, :] = grad_c[GROUP - HALO :]
            keep_step[...] = step_grad[GROUP - HALO :]
            keep_normed[...] = normed_v[GROUP - HALO :]
            keep_u[...] = u_v[GROUP - HALO :, :]
        dw[:, :wide] += tn(normed_v, d_pre)
        dw[:, wide:] += tn(normed_v, step_grad)
        grad, gain = input_back(d_pre, step_grad, dgate_s[group_rows(b), :], u_v[...])
        pn[...] += jnp.sum(jnp.where(done, gain, 0.0) if final else gain, axis=0, keepdims=True)
        g_buf[group_rows(b), :] = grad
        after[...] = grad_c[0:EDGE]

    def outputs_home():
        pl.loop(0, 2 * blocks)(lambda n: residual(n).wait())
        pl.loop(0, blocks)(lambda b: out_fold.drain(group_rows(b), b))
        fetch(out_far)

        @pl.loop(0, blocks)
        def _(b):
            inv, _ = row_stats(b)
            total = out_fold.total(group_rows(b), out_near if roomy else out_part) * inv
            result[2 * b] = (result[2 * b].astype(WIDE) + total[:BLOCK]).astype(LOW)
            result[2 * b + 1] = (result[2 * b + 1].astype(WIDE) + total[BLOCK:]).astype(LOW)

        route(0)
        own_g.start()

    own_g = pltpu.make_async_copy(shard_of(g_part, mine), out_part.at[mine], load_sem.at[5])

    step(*last_phase, 0, None)
    scan_back(blocks - 1, 0)
    rows_back(blocks - 1, 0, True)
    dx_fold.send_far(*short_piece)
    early_sum.combine()

    @pl.loop(1, blocks)
    def _(turn):
        b = blocks - 1 - turn
        step(*last_phase, turn, None)
        scan_back(b, turn)

        @pl.when(b == 0)
        def _():
            edge_own[...] = d_conv[0:EDGE, :]
            edge_copy(lax.rem(me + seqs - 1, seqs)).start()

        rows_back(b, turn, False)
        dx_fold.send_far(group_rows(b), b)

        @pl.when(turn == 2)
        def _():
            dx_fold.merge(*short_piece)

        pl.when(turn == max(blocks // 2, 1))(outputs_home)

        @pl.when(turn > 2)
        def _():
            dx_fold.merge(group_rows(b + 2), b + 2)

    edge_copy(lax.rem(me + 1, seqs)).wait()
    keep_conv[HALO:, :] = edge_got[...] * flags[2 * blocks]
    d_edge = conv_back(keep_conv, HALO)
    dw[:, :wide] += tn(keep_normed[...], d_edge)
    grad, gain = input_back(d_edge, keep_step[...], dgate_s[pl.ds(rows - HALO, HALO), :], keep_u[...])
    pn[...] += jnp.sum(gain, axis=0, keepdims=True)
    g_buf[pl.ds(rows - HALO, HALO), :] = grad
    dx_fold.send_far(*edge_piece)

    for z in range(line):
        slab = z * size // LANES * LANES
        zs_send[z] = jnp.zeros(zs_send.shape[1:], WIDE)
        zs_send[z, 0:1, :] = pn[:, z * width : (z + 1) * width]
        zs_send[z, EDGE : EDGE + TAPS, :LANES] = taps_g[0:TAPS, inner + slab : inner + slab + LANES]
        zs_send[z, EDGE + TAPS : EDGE + TAPS + 1, :LANES] = bias_g[:, inner + slab : inner + slab + LANES]
    zs_got[mine] = zs_send[mine]
    all_line(lambda to: zs_copy(to, mine).start())

    each_piece(dx_fold.send_near)

    if blocks > 3:
        dx_fold.merge(group_rows(1), 1)

    da_low[...] = dw[:, inner:wide].astype(LOW)
    da_sum.begin()
    dw_low[:, :inner] = dw[:, :inner].astype(LOW)
    dw_low[:, inner:] = dw[:, wide:].astype(LOW)
    dw_sum.begin()

    if blocks > 3:
        dx_fold.merge(group_rows(0), 0)
    elif blocks == 2:
        dx_fold.merge(*short_piece)
        dx_fold.merge(group_rows(0), 0)
    dx_fold.merge(*edge_piece)
    da_sum.combine()
    dw_sum.combine()

    all_line(lambda other: zs_copy(other, other).wait())
    from_line = jnp.sum(zs_got[...], axis=0)
    small[...] = jnp.zeros_like(small)
    small[0:TAPS, :inner] = taps_g[0:TAPS, :inner]
    small[0:TAPS, inner:] = from_line[EDGE : EDGE + TAPS, :LANES]
    small[4:5, :inner] = bias_g[:, :inner]
    small[4:5, inner:] = from_line[EDGE + TAPS : EDGE + TAPS + 1, :LANES]
    small[5:6, :inner] = gpost[...]
    small[6:7, :width] = from_line[0:1]
    for n in range(3):
        small[7:8, n * LANES : (n + 1) * LANES] = tiny[n : n + 1, :]
    own_copies["small"].start()
    all_seq(lambda to: small_copy(to, me).start())

    da_sum.drain()
    from_plane = da_got[0].astype(WIDE)
    for n in range(1, seqs // 2):
        from_plane = from_plane + da_got[n].astype(WIDE)
    for z in range(line):
        slab = z * size // LANES * LANES
        da_send[z] = from_plane[:, slab : slab + LANES]
    own_copies["addr"].start()
    all_line(lambda to: da_copy(to, mine).start())

    all_seq(lambda other: fin_copy(0, other, other).wait())
    own_copies["fin0"].wait()
    each_piece(dx_fold.drain)
    fetch(dx_far)
    own_g.wait()

    @pl.loop(0, blocks)
    def _(b):
        here = group_rows(b)
        total = dx_fold.total(here, dx_near if roomy else out_part)
        done = (out_part[mine, here].astype(WIDE) + total).astype(LOW)
        result[2 * b] = done[:BLOCK]
        result[2 * b + 1] = done[BLOCK:]

    route(1)
    early_sum.drain()
    dw_sum.drain()
    all_line(lambda other: da_copy(other, other).wait())
    all_seq(lambda other: fin_copy(1, other, other).wait())
    all_seq(lambda other: small_copy(other, other).wait())
    for name in ("addr", "small", "fin1"):
        own_copies[name].wait()


def core(
    flags, give, gate, part, act, cum, raw, local, conv, pre, normed, u, g_part, state_in, r_t, w_all, postnorm, vec,
    prenorm, kernels, filters, rim,
):
    seqs, line = lax.axis_size("seq"), lax.axis_size("head")
    rows, inner = gate.shape
    wide = act.shape[1]
    total = g_part.shape[1]
    width = total // line
    depth = total // seqs
    blocks, tiles = rows // GROUP, rows // BLOCK
    heads = inner // HDIM
    pieces = blocks + 1
    chunks = min(blocks, 4)
    message = (inner + HALO, STATE)
    sums = (blocks, EDGE, GROUP)
    streamed = (gate, part, act, cum, raw, local, conv, pre, normed, u, g_part, r_t, w_all)
    whole = (state_in, postnorm, vec, prenorm, kernels, filters, rim)
    gather = (line, rows, width)
    nothing = (line, HALO, width)
    roomy = rows * total * 2 <= 4 << 20
    near, far = (gather, nothing) if roomy else (nothing, gather)
    relay = (2, rows if line == 4 else HALO, width)
    small = (EDGE, inner + LANES)
    ways = max(line, 3)

    def slots(*dims):
        return (2,) + dims

    buffers = (
        (slots(GROUP, inner), WIDE), (slots(GROUP, inner), WIDE), (slots(GROUP, STATE), LOW),
        (slots(GROUP, LANES), WIDE), (slots(inner, STATE), WIDE), (slots(GROUP, total), LOW),
        (slots(GROUP, wide), LOW), (slots(GROUP, LANES), WIDE), (slots(GROUP, wide), WIDE),
        (slots(GROUP, wide), LOW), (slots(HALO, wide), LOW), (slots(GROUP, total), LOW),
    )
    return pl.pallas_call(
        functools.partial(core_kernel, seqs, line, heads, blocks, roomy),
        grid=(1,),
        out_shape=(
            shape((seqs, BLOCK, width), LOW), shape((seqs, BLOCK, width), LOW), shape(far, LOW), shape(far, LOW),
            shape((seqs // 2, depth, 2 * inner), LOW), shape((seqs // 2, depth, inner + LANES), LOW),
            shape((line, depth, LANES), WIDE), shape((seqs,) + small, WIDE),
        ),
        in_specs=[SMEM_SPEC] * 2 + [ANY_SPEC] * len(streamed) + [fixed(a.shape) for a in whole],
        out_specs=(ANY_SPEC,) * 8,
        scratch_shapes=[pltpu.VMEM(dims, kind) for dims, kind in buffers] + [
            DMA((len(buffers), 2)),
            pltpu.VMEM(r_t.shape, LOW), pltpu.VMEM(w_all.shape, LOW),
            pltpu.VMEM((rows, inner), WIDE), pltpu.VMEM((rows, inner), WIDE), pltpu.VMEM((rows, inner), LOW),
            pltpu.VMEM((rows, inner), LOW), pltpu.VMEM((rows, GROUP), LOW), pltpu.VMEM((blocks, inner, STATE), WIDE),
            pltpu.VMEM((blocks, inner, STATE), WIDE), pltpu.VMEM((inner, STATE), WIDE), pltpu.VMEM((LANES, 1), WIDE),
            pltpu.VMEM((rows, total), LOW), pltpu.VMEM(gather, LOW),
            pltpu.VMEM((seqs,) + message, LOW), pltpu.VMEM(message, LOW),
            pltpu.VMEM(relay, LOW), pltpu.VMEM(relay, LOW), pltpu.VMEM(near, LOW), pltpu.VMEM(near, LOW),
            pltpu.VMEM((line,) + sums, WIDE), pltpu.VMEM(sums, WIDE),
            pltpu.VMEM((total, inner), WIDE), pltpu.VMEM((total, inner), WIDE), pltpu.VMEM((total, 2 * inner), LOW),
            pltpu.VMEM((seqs // 2, depth, 2 * inner), LOW), pltpu.VMEM((1, inner), WIDE), pltpu.VMEM((EDGE, LANES), WIDE),
            pltpu.VMEM((GROUP, wide), WIDE), pltpu.VMEM((GROUP, LANES), LOW), pltpu.VMEM((EDGE, wide), WIDE),
            pltpu.VMEM((EDGE, wide), WIDE), pltpu.VMEM((EDGE, wide), WIDE), pltpu.VMEM((BLOCK + EDGE, wide), WIDE),
            pltpu.VMEM((HALO + EDGE, wide), WIDE), pltpu.VMEM((HALO, LANES), LOW), pltpu.VMEM((HALO, total), LOW),
            pltpu.VMEM((HALO, total), LOW),
            pltpu.VMEM((EDGE, wide), WIDE), pltpu.VMEM((1, wide), WIDE), pltpu.VMEM((total, wide + LANES), WIDE),
            pltpu.VMEM((total, inner + LANES), LOW), pltpu.VMEM((seqs // 2, depth, inner + LANES), LOW),
            pltpu.VMEM((total, wide - inner), LOW), pltpu.VMEM((seqs // 2, depth, wide - inner), LOW),
            pltpu.VMEM((seqs // 2, depth, wide - inner), LOW), pltpu.VMEM((line, depth, LANES), WIDE),
            pltpu.VMEM((1, total), WIDE), pltpu.VMEM((line, 2 * EDGE, width), WIDE),
            pltpu.VMEM((line, 2 * EDGE, width), WIDE), pltpu.VMEM(small, WIDE),
            pltpu.VMEM((tiles, BLOCK, width), LOW), pltpu.VMEM((seqs, BLOCK, width), LOW),
            DMA((seqs,)), DMA((seqs,)), DMA((seqs,)), DMA((line,)), DMA((line,)), DMA((chunks, 2, line)), DMA((chunks, line)),
            DMA((6,)),
            DMA((ways, blocks)), DMA((line, blocks)), DMA((2, blocks)), DMA((4, seqs // 2)), DMA((4, seqs // 2)), DMA((4, seqs // 2)),
            DMA((ways, pieces)), DMA((line, pieces)), DMA((2, pieces)), DMA, DMA,
            DMA((line,)), DMA((line,)), DMA((line,)), DMA((line,)), DMA((seqs,)), DMA((seqs,)), DMA((2, seqs)),
            DMA((2, seqs)), DMA((4,)), DMA((2,)), DMA((tiles,)),
        ],
        compiler_params=pltpu.CompilerParams(
            collective_id=1, has_side_effects=True, vmem_limit_bytes=VMEM_LIMIT, dimension_semantics=("arbitrary",)
        ),
        name="core",
    )(flags, give, *streamed, *whole)


def finish_kernel(
    take, out_recv, grad_recv, early_got, dw_got, addr_got, small_got,
    out_o, dx_o, prenorm_o, gate_o, pay_o, addr_o, step_o, kernels_o, offsets_o, filters_o, shifts_o,
    stepbias_o, decays_o, through_o, post_o, read_o,
):
    inner, size, heads, width = gate_o.shape[1], addr_o.shape[0], step_o.shape[0], prenorm_o.shape[1]
    offset = lax.rem(lax.axis_index("head") * size, LANES)
    back_turn = lax.rem(LANES - offset, LANES)
    for k in range(out_o.shape[0]):
        out_o[k] = out_recv[take[k]]
        dx_o[k] = grad_recv[take[k]]

    def summed(ref):
        total = ref[0].astype(WIDE)
        for n in range(1, ref.shape[0]):
            total = total + ref[n].astype(WIDE)
        return total

    early = summed(early_got)
    read_o[...] = early[:, :inner].T
    gate_o[...] = early[:, inner:]
    grads = summed(dw_got)
    pay_o[...] = grads[:, :inner]
    step_o[...] = grads[:, inner:].T[:heads]
    addr_o[...] = pltpu.roll(summed(addr_got), back_turn, 1).T[:size]
    totals = jnp.sum(small_got[...], axis=0)
    kernels_o[...] = totals[0:TAPS, :inner]
    offsets_o[...] = totals[4:5, :inner]
    turned = pltpu.roll(totals[:, inner:], back_turn, 1)
    filters_o[...] = turned[0:TAPS, :size]
    shifts_o[...] = turned[4:5, :size]
    post_o[...] = totals[5:6, :inner]
    prenorm_o[...] = totals[6:7, :width]
    for n, ref in enumerate((stepbias_o, decays_o, through_o)):
        ref[...] = totals[7:8, n * LANES : n * LANES + heads]


def finish(take, out_recv, grad_recv, early_got, dw_got, addr_got, small_got):
    seqs, _, width = out_recv.shape
    tiles = take.shape[0]
    _, depth, inner = early_got.shape
    inner = inner // 2
    heads = inner // HDIM
    size = 2 * STATE // addr_got.shape[0]
    operands = (out_recv, grad_recv, early_got, dw_got, addr_got, small_got)
    outs = (
        shape((tiles, BLOCK, width), LOW), shape((tiles, BLOCK, width), LOW), shape((1, width), WIDE),
        shape((depth, inner), WIDE), shape((depth, inner), WIDE), shape((size, depth), WIDE),
        shape((heads, depth), WIDE), shape((TAPS, inner), WIDE), shape((1, inner), WIDE),
        shape((TAPS, size), WIDE), shape((1, size), WIDE), shape((1, heads), WIDE), shape((1, heads), WIDE),
        shape((1, heads), WIDE), shape((1, inner), WIDE), shape((inner, depth), WIDE),
    )
    return pl.pallas_call(
        finish_kernel,
        grid=(1,),
        out_shape=outs,
        in_specs=[SMEM_SPEC] + [fixed(a.shape) for a in operands],
        out_specs=tuple(fixed(a.shape) for a in outs),
        compiler_params=pltpu.CompilerParams(vmem_limit_bytes=VMEM_LIMIT, dimension_semantics=("arbitrary",)),
        name="finish",
    )(take, *operands)


def on_device(
    inputs,
    cotangent,
    lengths,
    placement,
    prenorm,
    gating,
    payload,
    address,
    stepping,
    kernels,
    offsets,
    filters,
    shifts,
    stepbias,
    decays,
    through,
    postnorm,
    readout,
):
    rows, width = inputs.shape
    heads = stepbias.shape[0]
    tiles = rows // BLOCK
    give_in, take_in, give_out, take_out, flags, vec = index(placement, lengths, stepbias, decays, through, tiles)
    gain, post = prenorm[None, :], postnorm[None, :]
    (
        u, normed, gate, pre, conv, act, raw, cum, part, local, state_in, rim, g_part, w_all, r_t
    ) = front(
        give_in, take_in, flags, inputs, cotangent, gating, payload, address, stepping, readout, vec, gain, kernels,
        filters, offsets[None, :], shifts[None, :]
    )
    out_recv, grad_recv, _, _, early_got, dw_got, addr_got, small_got = core(
        flags, give_out, gate, part, act, cum, raw, local, conv, pre, normed, u, g_part, state_in, r_t, w_all, post, vec,
        gain, kernels, filters, rim
    )
    (
        out, dx, prenorm_g, gate_g, pay_g, addr_g, step_g, kernels_g, offsets_g, filters_g, shifts_g, stepbias_g,
        decays_g, through_g, post_g, read_g,
    ) = finish(take_out, out_recv, grad_recv, early_got, dw_got, addr_got, small_got)
    return (
        out.reshape(rows, width),
        dx.reshape(rows, width),
        prenorm_g.reshape(-1),
        gate_g,
        pay_g,
        addr_g.T,
        step_g.T,
        kernels_g,
        offsets_g.reshape(-1),
        filters_g,
        shifts_g.reshape(-1),
        stepbias_g.reshape(-1),
        decays_g.reshape(-1),
        through_g.reshape(-1),
        post_g.reshape(-1),
        read_g,
    )


def solution(mesh):
    in_specs = (
        P("seq", "head"),
        P("seq", "head"),
        P(),
        P(),
        P(),
        P("seq", "head"),
        P("seq", "head"),
        P("seq", None),
        P("seq", "head"),
        P(None, "head"),
        P("head"),
        P(),
        P(),
        P("head"),
        P("head"),
        P("head"),
        P("head"),
        P("head", "seq"),
    )
    out_specs = (
        P("seq", "head"),
        P("seq", "head"),
        P("head"),
        P("seq", "head"),
        P("seq", "head"),
        P("seq", "head"),
        P("seq", "head"),
        P(None, "head"),
        P("head"),
        P(None, "head"),
        P("head"),
        P("head"),
        P("head"),
        P("head"),
        P("head"),
        P("head", "seq"),
    )
    return jax.shard_map(
        on_device, mesh=mesh, in_specs=in_specs, out_specs=out_specs, check_vma=False
    )
```

```python
import functools

import jax
import jax.numpy as jnp
from jax import lax
from jax.experimental import pallas as pl
from jax.experimental.pallas import tpu as pltpu
from jax.sharding import PartitionSpec as P

D = 1024
GROUP = 256
BLOCK = 128
INNER = 2048
HDIM = 64
STATE = 128
TAPS = 4
HALO = 16
EDGE = 8
LANES = 128
EPS = 1e-05
MESH = pl.DeviceIdType.MESH
VMEM = pltpu.MemorySpace.VMEM
SMEM = pltpu.MemorySpace.SMEM
DMA = pltpu.SemaphoreType.DMA
VMEM_LIMIT = 63 << 20
LOW = jnp.bfloat16
WIDE = jnp.float32


def shape(dims, kind):
    return jax.ShapeDtypeStruct(dims, kind)


def nn(a, b):
    return jnp.dot(a, b, preferred_element_type=WIDE)


def nt(a, b):
    return lax.dot_general(a, b, (((1,), (1,)), ((), ())), preferred_element_type=WIDE)


def tn(a, b):
    return lax.dot_general(a, b, (((0,), (0,)), ((), ())), preferred_element_type=WIDE)


def halves(x):
    high = x.astype(LOW)
    return high, (x - high.astype(WIDE)).astype(LOW)


def thirds(x):
    high = x.astype(LOW)
    rest = x - high.astype(WIDE)
    middle = rest.astype(LOW)
    return high, middle, (rest - middle.astype(WIDE)).astype(LOW)


def head_rows(inner):
    row = lax.broadcasted_iota(jnp.int32, (LANES, inner), 0)
    column = lax.broadcasted_iota(jnp.int32, (LANES, inner), 1)
    return jnp.where(column // HDIM == row, 1.0, 0.0).astype(LOW)


def head_columns(inner):
    row = lax.broadcasted_iota(jnp.int32, (inner, LANES), 0)
    column = lax.broadcasted_iota(jnp.int32, (inner, LANES), 1)
    return jnp.where(row // HDIM == column, 1.0, 0.0).astype(LOW)


def to_columns(x, spread):
    high, rest = halves(x)
    return nn(high, spread) + nn(rest, spread)


def to_heads(x, collect):
    high, rest = halves(x)
    return nn(high, collect) + nn(rest, collect)


def ones_before(count):
    row = lax.broadcasted_iota(jnp.int32, (count, count), 0)
    column = lax.broadcasted_iota(jnp.int32, (count, count), 1)
    return row >= column


def sum_before(x):
    matrix = jnp.where(ones_before(x.shape[0]), 1.0, 0.0).astype(LOW)
    high, middle, low = thirds(x)
    return nn(matrix, high) + (nn(matrix, middle) + nn(matrix, low))


def sum_after(x):
    count = x.shape[0]
    row = lax.broadcasted_iota(jnp.int32, (count, count), 0)
    column = lax.broadcasted_iota(jnp.int32, (count, count), 1)
    matrix = jnp.where(row <= column, 1.0, 0.0).astype(LOW)
    high, middle, low = thirds(x)
    return nn(matrix, high) + (nn(matrix, middle) + nn(matrix, low))


def sigmoid(x):
    return 0.5 * jnp.tanh(0.5 * x) + 0.5


def step_terms(raw, heads):
    z = jnp.exp(-jnp.abs(raw))
    series = 1.0 - z * (0.5 - z * (1.0 / 3.0 - z * (0.25 - z * 0.2)))
    small = z < 0.03
    log1p = jnp.where(small, z * series, jnp.log(1.0 + z))
    soft = jnp.maximum(raw, 0.0) + log1p
    one = 1.0 / (1.0 + z)
    sig = jnp.where(raw >= 0, one, z * one)
    ratio = jnp.where(small & (raw < 0), one / series, sig / jnp.maximum(soft, 1e-20))
    lane = lax.broadcasted_iota(jnp.int32, raw.shape, 1)
    return jnp.where(lane < heads, soft, 0.0), sig, ratio


def greet(seq_peers, head_peers, corners=False):
    barrier = pltpu.get_barrier_semaphore()
    count = 0
    if seq_peers > 1:
        me = lax.axis_index("seq")

        @pl.loop(1, seq_peers)
        def _(i):
            pl.semaphore_signal(
                barrier, inc=1, device_id={"seq": lax.rem(me + i, seq_peers)}, device_id_type=MESH
            )

        count += seq_peers - 1
    if head_peers > 1:
        mine = lax.axis_index("head")

        @pl.loop(1, head_peers)
        def _(i):
            pl.semaphore_signal(
                barrier, inc=1, device_id={"head": lax.rem(mine + i, head_peers)}, device_id_type=MESH
            )

        count += head_peers - 1
    if corners and head_peers > 1:
        me, mine = lax.axis_index("seq"), lax.axis_index("head")
        for side in (1, seq_peers - 1):

            @pl.loop(1, head_peers)
            def _(i):
                where = {"seq": lax.rem(me + side, seq_peers), "head": lax.rem(mine + i, head_peers)}
                pl.semaphore_signal(barrier, inc=1, device_id=where, device_id_type=MESH)

        count += 2 * (head_peers - 1)
    pl.semaphore_wait(barrier, count)


def remote(src, dst, send_sem, recv_sem, where):
    return pltpu.make_async_remote_copy(
        src_ref=src, dst_ref=dst, send_sem=send_sem, recv_sem=recv_sem, device_id=where, device_id_type=MESH
    )


class Line:
    def __init__(self, count, out, width, send, recv):
        self.count, self.out, self.width, self.send, self.recv = count, out, width, send, recv
        self.me = lax.axis_index("head")

    def view(self, shard):
        return self.out.at[:, pl.ds(pl.multiple_of(shard * self.width, LANES), self.width)]

    def copy(self, src, shard, way, step):
        return remote(
            src, self.view(shard), self.send.at[way, step], self.recv.at[shard], {"head": self.me + (1 - 2 * way)}
        )

    def first(self, own):
        self.pass_on(own, self.me, 0, 0)
        self.pass_on(own, self.me, 1, 0)

    def pass_on(self, src, shard, way, step):
        reach = (self.me < self.count - 1) if way == 0 else (self.me > 0)

        @pl.when(reach)
        def _():
            self.copy(src, shard, way, step).start()

    def hop(self, step, take=True, give=True, source=None):
        for way in (0, 1):
            shard = self.me - step if way == 0 else self.me + step
            there = (shard >= 0) if way == 0 else (shard < self.count)

            @pl.when(there)
            def _():
                if take:
                    self.copy(self.view(shard), shard, way, step).wait_recv()
                if give and step < self.count - 1:
                    self.pass_on(self.view(shard) if source is None else source(shard), shard, way, step)

    def finish(self, own, steps=None):
        for way in (0, 1):
            reach = (self.me < self.count - 1) if way == 0 else (self.me > 0)
            for step in range(self.count - 1) if steps is None else steps:
                shard = self.me - step if way == 0 else self.me + step
                there = (shard >= 0) if way == 0 else (shard < self.count)

                @pl.when(reach & there)
                def _():
                    src = own if step == 0 else self.view(shard)
                    self.copy(src, shard, way, step).wait_send()


class Plane:
    def __init__(self, seqs, view, sent, got, passed, way=0):
        self.chips, self.view, self.sent, self.got, self.passed, self.way = seqs // 2, view, sent, got, passed, way
        self.me = lax.axis_index("seq")
        self.core = lax.rem(self.me, 2)
        self.chip = self.me // 2
        self.mate = self.me + 1 - 2 * self.core

    def forward(self, chip):
        return (chip > self.chip) if self.way == 1 else (chip < self.chip) if self.way == -1 else (chip >= 0)

    def backward(self, chip):
        return (chip < self.chip) if self.way == 1 else (chip > self.chip) if self.way == -1 else (chip >= 0)

    def each_chip(self, body):
        @pl.loop(1, self.chips)
        def _(i):
            body(lax.rem(self.chip + i, self.chips))

    def copy(self, src, source, to, sem):
        return remote(src, self.view(source), sem, self.got.at[source], {"seq": to})

    def start(self, own):
        def send(chip):
            to = 2 * chip + self.core

            @pl.when(self.forward(chip))
            def _():
                self.copy(own, self.me, to, self.sent.at[to]).start()

        self.each_chip(send)
        self.copy(own, self.me, self.mate, self.sent.at[self.mate]).start()

    def relay(self):
        def take(chip):
            source = 2 * chip + self.core

            @pl.when(self.backward(chip))
            def _():
                landed = self.view(source)
                self.copy(landed, source, self.mate, self.passed.at[source]).wait_recv()
                self.copy(landed, source, self.mate, self.passed.at[source]).start()

        self.each_chip(take)

    def finish(self, own):
        def take(chip):
            source = 2 * chip + 1 - self.core

            @pl.when(self.backward(chip))
            def _():
                self.copy(self.view(source), source, self.mate, self.passed.at[source]).wait_recv()

        self.each_chip(take)
        self.copy(self.view(self.mate), self.mate, self.mate, self.sent.at[self.mate]).wait_recv()
        self.copy(own, self.me, self.mate, self.sent.at[self.mate]).wait_send()

        def drain(chip):
            same = 2 * chip + self.core

            @pl.when(self.forward(chip))
            def _():
                self.copy(own, self.me, same, self.sent.at[same]).wait_send()

            @pl.when(self.backward(chip))
            def _():
                self.copy(self.view(same), same, self.mate, self.passed.at[same]).wait_send()

        self.each_chip(drain)


ANY_SPEC = pl.BlockSpec(memory_space=pl.ANY)
VMEM_SPEC = pl.BlockSpec(memory_space=VMEM)
SMEM_SPEC = pl.BlockSpec(memory_space=SMEM)


def index_kernel(
    seqs, tiles, place, lengths, stepbias, decays, through, give_in, take_in, give_out, take_out, flags, vec
):
    me = lax.axis_index("seq")

    @pl.loop(0, seqs * tiles)
    def _(j):
        block = place[j]

        @pl.when(lax.div(block, tiles) == me)
        def _():
            to = lax.div(j, tiles)
            give_in[to] = lax.rem(block, tiles)
            take_out[lax.rem(block, tiles)] = to

    @pl.loop(0, tiles)
    def _(k):
        source = lax.div(place[me * tiles + k], tiles)
        take_in[k] = source
        give_out[source] = k

    @pl.loop(0, tiles + 1)
    def _(k):
        position = (me * tiles + k) * BLOCK
        end = jnp.int32(0)
        border = position == 0
        for n in range(lengths.shape[0]):
            end = end + lengths[n]
            border = border | (position == end)
        flags[k] = jnp.where(border, 0.0, 1.0)

    heads = stepbias.shape[1]
    vec[...] = jnp.zeros_like(vec)
    vec[0:1, :heads] = stepbias[...]
    vec[1:2, :heads] = decays[...]
    vec[2:3, :heads] = through[...]


def index(place, lengths, stepbias, decays, through, tiles):
    seqs = lax.axis_size("seq")
    whole = jnp.int32
    return pl.pallas_call(
        functools.partial(index_kernel, seqs, tiles),
        out_shape=(
            shape((seqs,), whole), shape((tiles,), whole), shape((seqs,), whole), shape((tiles,), whole),
            shape((tiles + 1,), WIDE), shape((EDGE, LANES), WIDE),
        ),
        in_specs=[SMEM_SPEC] * 2 + [VMEM_SPEC] * 3,
        out_specs=(SMEM_SPEC,) * 5 + (VMEM_SPEC,),
        compiler_params=pltpu.CompilerParams(vmem_limit_bytes=VMEM_LIMIT),
        name="index",
    )(place, lengths, stepbias[None, :], decays[None, :], through[None, :])


def blockwise(dims, index):
    return pl.BlockSpec(dims, index)


def fixed(dims):
    return pl.BlockSpec(dims, lambda i: (0,) * len(dims), pipeline_mode=pl.Buffered(1))


def carry_columns(carry_row_t, collect):
    high, middle, low = thirds(jnp.broadcast_to(carry_row_t, (LANES, LANES)))
    return nn(collect, high) + (nn(collect, middle) + nn(collect, low))


def pair_lanes(slab):
    lane = lax.broadcasted_iota(jnp.int32, slab.shape, 1)
    zero = jnp.zeros_like(slab)
    return jnp.where(lane < HDIM, slab, zero), jnp.where(lane >= HDIM, slab, zero)


def fold_states(slots, collect, inner, first, last, step, start):
    def hop(n, state):
        message = slots[first + n * step]
        carry = nn(collect[:, :HALO], message[inner:])
        return carry * state + message[:inner].astype(WIDE)

    return lax.fori_loop(0, (last - first) * step, hop, start)


def front_kernel(
    seqs, line, heads, blocks, chunks, give, take, flags,
    x_in, g_in, gating_in, payload_in, address_in, stepping_in, readout_in,
    vec, prenorm, kernels, filters, offsets, shifts,
    u_o, normed_o, gate_o, pre_o, conv_o, act_o, raw_o, cum_o, part_o, local_o, state_o, rim_o, g_o, w_o, r_o,
    x, g, gating, payload, address, stepping, readout, square,
    send_x, send_g, recv_x, recv_g, work_x, work_g, w_own, r_own, u, w, msg, slots,
    ext, prev, state, prod,
    sent, got, w_sent, w_got, w_passed, r_sent, r_got, r_passed, s_sent, s_got, s_passed, rim_sent, rim_got, own_sem,
    load_sem, line_sent, line_got, g_sent, g_got,
):
    i = pl.program_id(0)
    me, mine = lax.axis_index("seq"), lax.axis_index("head")
    tiles, _, width = x.shape
    rows = tiles * BLOCK
    depth, inner = gating.shape
    wide = pre_o.shape[1]
    part = rows // chunks
    per = blocks // chunks

    def rows_of(device):
        return pl.ds(pl.multiple_of(device * depth, depth), depth)

    def piece(n):
        if isinstance(n, int):
            return pl.ds(n * part, part)
        return pl.ds(pl.multiple_of(n * part, part), part)

    def u_line(n):
        return Line(line, u.at[piece(n)], width, line_sent.at[n], line_got.at[n])

    hops = sorted(((step, n) for step in range(1, line - 1) for n in range(chunks)), key=lambda hop: (sum(hop), hop))
    late_hops = [(step, n) for step, n in hops if step == line - 2 and n >= 2]
    early_hops = [hop for hop in hops if hop not in late_hops]

    def own_columns(ref):
        return ref.at[:, pl.ds(pl.multiple_of(mine * width, LANES), width)]

    w_plane = Plane(seqs, lambda s: w.at[rows_of(s)], w_sent, w_got, w_passed)
    r_plane = Plane(seqs, lambda s: r_o.at[rows_of(s)], r_sent, r_got, r_passed)
    s_plane = Plane(seqs, lambda s: slots.at[s], s_sent, s_got, s_passed, way=1)
    g_line = Line(line, g_o, width, g_sent, g_got)
    own_r = pltpu.make_async_copy(r_own, r_o.at[rows_of(me)], own_sem.at[0])
    own_g = pltpu.make_async_copy(work_g, g_line.view(mine), own_sem.at[1])
    save_w = pltpu.make_async_copy(w, w_o, own_sem.at[2])

    def rim_copy(to, shard):
        columns = pl.ds(pl.multiple_of(shard * width, LANES), width)
        return remote(
            work_x.at[pl.ds(rows - HALO, HALO)], u.at[pl.ds(rows, HALO), columns], rim_sent.at[to], rim_got.at[shard],
            {"seq": lax.rem(me + 1, seqs), "head": to},
        )

    def arrange(which, received, work):
        @pl.loop(1, seqs)
        def _(n):
            source = lax.rem(me + n, seqs)
            remote(
                received.at[source], received.at[source], sent.at[which, source], got.at[which, source], {"seq": source}
            ).wait_recv()

        for k in range(tiles):
            work[pl.ds(k * BLOCK, BLOCK), :] = received[take[k]]

    @pl.when(i == 0)
    def _():
        pairs = (
            (x_in, x), (g_in, g), (gating_in, gating), (payload_in, payload), (address_in, address),
            (stepping_in, stepping), (readout_in, readout),
        )
        loads = [pltpu.make_async_copy(src, dst, load_sem.at[n]) for n, (src, dst) in enumerate(pairs)]
        for load in loads:
            load.start()
        greet(seqs, line, corners=True)

        def post(which, source, outgoing, incoming):
            @pl.loop(1, seqs)
            def _(n):
                to = lax.rem(me + n, seqs)
                outgoing[to] = source[give[to]]
                remote(outgoing.at[to], incoming.at[me], sent.at[which, to], got.at[which, me], {"seq": to}).start()

            incoming[me] = source[give[me]]

        loads[0].wait()
        post(0, x, send_x, recv_x)
        for load in loads[1:]:
            load.wait()

        w_own[:, :inner] = gating[...].astype(LOW)
        w_own[:, inner : 2 * inner] = payload[...].astype(LOW)
        state2 = address.shape[1]
        w_own[:, 2 * inner : 2 * inner + state2] = address[...].astype(LOW)
        square[...] = jnp.zeros_like(square)
        square[: stepping.shape[0], :depth] = stepping[...]
        w_own[:, 2 * inner + state2 :] = square[...].T[:depth].astype(LOW)
        r_own[...] = readout[...].T.astype(LOW)
        w[rows_of(me), :] = w_own[...]
        own_r.start()

        arrange(0, recv_x, work_x)

        @pl.loop(0, line)
        def _(n):
            rim_copy(lax.rem(mine + n, line), mine).start()

        for n in range(chunks):
            u_line(n).first(work_x.at[piece(n)])
        w_plane.start(w_own)
        own = pltpu.make_async_copy(work_x, own_columns(u.at[pl.ds(0, rows)]), own_sem.at[3])
        own.start()
        post(1, g, send_g, recv_g)
        r_plane.start(r_own)
        for step, n in early_hops:
            u_line(n).hop(step)
        w_plane.relay()
        own.wait()

        @pl.loop(0, line)
        def _(n):
            rim_copy(n, n).wait_recv()

        w_plane.finish(w_own)
        save_w.start()

    for step, n in late_hops:

        @pl.when(i == (n - 1) * per)
        def _():
            u_line(n).hop(step)

    @pl.when(i == blocks // 2)
    def _():
        arrange(1, recv_g, work_g)
        g_line.first(work_g)
        own_g.start()

    if line > 1:

        @pl.when(lax.rem(i, per) == 0)
        def _():
            u_line(lax.div(i, per)).hop(line - 1)

    taps = jnp.concatenate([kernels[...], filters[...]], axis=1)
    bias = jnp.concatenate([offsets[...], shifts[...]], axis=1)
    spread_m, collect = head_rows(inner), head_columns(inner)

    def normalize(block):
        wide_rows = block.astype(WIDE)
        scale = lax.rsqrt(jnp.mean(wide_rows * wide_rows, axis=1, keepdims=True) + EPS)
        return (wide_rows * scale * prenorm[...]).astype(LOW)

    @pl.when(i == 0)
    def _():
        before = nn(normalize(u[pl.ds(rows, HALO), :]), w[:, inner : inner + wide]).astype(LOW).astype(WIDE)
        prev[...] = before[HALO - EDGE :]
        rim_o[...] = before[HALO - EDGE :]
        state[...] = jnp.zeros_like(state)
        prod[...] = jnp.ones_like(prod)

    u_v = u[pl.ds(pl.multiple_of(i * GROUP, GROUP), GROUP), :]
    u_o[...] = u_v
    normed = normalize(u_v)
    normed_o[...] = normed
    gate_o[...] = nn(normed, w[:, :inner])
    pre = nn(normed, w[:, inner : inner + wide]).astype(LOW)
    pre_o[...] = pre
    lane = lax.broadcasted_iota(jnp.int32, (GROUP, LANES), 1)
    raw = jnp.where(lane < heads, nn(normed, w[:, inner + wide :]) + vec[0:1, :], 0.0)
    raw_o[...] = raw
    first, second = flags[2 * i], flags[2 * i + 1]
    same = (first, second)
    for half in range(2):
        at = pl.ds(half * BLOCK, BLOCK)
        ext[0:EDGE, :] = prev[...] * same[half]
        ext[EDGE:, :] = pre[half * BLOCK : (half + 1) * BLOCK].astype(WIDE)
        prev[...] = ext[BLOCK:, :]
        total = bias + taps[TAPS - 1 : TAPS] * ext[EDGE:, :]
        for tap in range(TAPS - 1):
            total = total + taps[tap : tap + 1] * ext[pl.ds(EDGE - (TAPS - 1) + tap, BLOCK), :]
        conv_o[at, :] = total
        act_o[at, :] = (total * sigmoid(total)).astype(LOW)

    steps, _, _ = step_terms(raw, heads)
    scale = -jnp.exp(vec[1:2, :])
    cum = sum_before(steps * scale)
    cum_o[...] = cum
    cum_t, steps_t = cum.T, steps.T
    write = act_o[:, inner : inner + STATE]
    read = act_o[:, inner + STATE :]
    lower = ones_before(BLOCK)
    top, low = slice(0, BLOCK), slice(BLOCK, GROUP)
    s00 = jnp.where(lower, nt(read[top], write[top]), 0.0)
    s10 = nt(read[low], write[top]) * second
    s11 = jnp.where(lower, nt(read[low], write[low]), 0.0)

    def mix(scores, head, t, s):
        decay = jnp.exp(jnp.minimum(cum[t, head : head + 1] - cum_t[head : head + 1, s], 0.0))
        return (scores * (decay * steps_t[head : head + 1, s])).astype(LOW)

    last = cum[GROUP - 1 : GROUP, :]
    row = lax.broadcasted_iota(jnp.int32, (GROUP, LANES), 0)
    weight = steps * jnp.exp(last - cum) * jnp.where(row < BLOCK, second, 1.0)
    weight_w = to_columns(weight, spread_m)
    skip = to_columns(jnp.broadcast_to(vec[2:3, :], (EDGE, LANES)), spread_m)[0:1]
    packed = []
    for pair in range(inner // LANES):
        columns = slice(pair * LANES, (pair + 1) * LANES)
        slab = act_o[:, columns]
        slab_f = slab.astype(WIDE)
        ones = pair_lanes(slab)
        h0, h1 = 2 * pair, 2 * pair + 1
        y0 = nn(
            jnp.concatenate([mix(s00, h0, top, top), mix(s00, h1, top, top)], axis=1),
            jnp.concatenate([ones[0][top], ones[1][top]], axis=0),
        )
        y1 = nn(
            jnp.concatenate(
                [mix(s10, h0, low, top), mix(s11, h0, low, low), mix(s10, h1, low, top), mix(s11, h1, low, low)], axis=1
            ),
            jnp.concatenate([ones[0], ones[1]], axis=0),
        )
        part_o[top, columns] = y0 + skip[:, columns] * slab_f[top]
        part_o[low, columns] = y1 + skip[:, columns] * slab_f[low]
        packed.append((slab_f * weight_w[:, columns]).astype(LOW))
    local = tn(jnp.concatenate(packed, axis=1), write)
    local_o[0] = local
    carry = jnp.exp(cum_t[:, GROUP - 1 : GROUP]) * (first * second)
    state[...] = carry_columns(carry, collect) * state[...] + local
    prod[...] = jnp.broadcast_to(carry[:HALO], (HALO, STATE)) * prod[...]

    @pl.when(i == blocks - 1)
    def _():
        msg[:inner, :] = state[...].astype(LOW)
        msg[inner:, :] = prod[...].astype(LOW)
        s_plane.start(msg)
        s_plane.relay()
        s_plane.finish(msg)
        state_o[...] = fold_states(slots, collect, inner, 0, me, 1, jnp.zeros((inner, STATE), WIDE))
        r_plane.relay()
        r_plane.finish(r_own)
        if line > 1:
            g_line.hop(1, give=False)
        g_line.finish(work_g, (0,))
        for n in range(chunks):
            u_line(n).finish(work_x.at[piece(n)])

        @pl.loop(0, line)
        def _(n):
            rim_copy(n, mine).wait_send()


        @pl.loop(1, seqs)
        def _(n):
            other = lax.rem(me + n, seqs)
            for which, buffer in ((0, send_x), (1, send_g)):
                remote(
                    buffer.at[other], buffer.at[other], sent.at[which, other], got.at[which, other], {"seq": other}
                ).wait_send()

        own_r.wait()
        own_g.wait()
        save_w.wait()


def front(give, take, flags, x, g, gating, payload, address, stepping, readout, vec, prenorm, kernels, filters, offsets, shifts):
    seqs, line = lax.axis_size("seq"), lax.axis_size("head")
    rows, width = x.shape
    depth, inner = gating.shape
    total = depth * seqs
    wide = inner + address.shape[1]
    columns = inner + wide + LANES
    blocks = rows // GROUP
    chunks = min(blocks, 4)
    heads = stepping.shape[1]
    routed = (seqs, BLOCK, width)
    given = (rows // BLOCK, BLOCK, width)
    message = (inner + HALO, STATE)
    operands = (x.reshape(given), g.reshape(given), gating, payload, address, stepping.T, readout)
    small = (vec, prenorm, kernels, filters, offsets, shifts)

    def by_rows(size):
        return blockwise((GROUP, size), lambda i: (i, 0))

    return pl.pallas_call(
        functools.partial(front_kernel, seqs, line, heads, blocks, chunks),
        grid=(blocks,),
        out_shape=(
            shape((rows, total), LOW), shape((rows, total), LOW), shape((rows, inner), WIDE), shape((rows, wide), LOW),
            shape((rows, wide), WIDE), shape((rows, wide), LOW), shape((rows, LANES), WIDE), shape((rows, LANES), WIDE),
            shape((rows, inner), WIDE), shape((blocks, inner, STATE), WIDE), shape((inner, STATE), WIDE),
            shape((EDGE, wide), WIDE), shape((rows, total), LOW), shape((total, columns), LOW),
            shape((total, inner), LOW),
        ),
        in_specs=[SMEM_SPEC] * 3 + [ANY_SPEC] * 7 + [fixed(a.shape) for a in small],
        out_specs=(
            by_rows(total), by_rows(total), by_rows(inner), by_rows(wide), by_rows(wide), by_rows(wide), by_rows(LANES),
            by_rows(LANES), by_rows(inner), blockwise((1, inner, STATE), lambda i: (i, 0, 0)), fixed((inner, STATE)),
            fixed((EDGE, wide)), ANY_SPEC, ANY_SPEC, ANY_SPEC,
        ),
        scratch_shapes=[pltpu.VMEM(a.shape, a.dtype) for a in operands] + [
            pltpu.VMEM((LANES, LANES), WIDE),
            pltpu.VMEM(routed, LOW), pltpu.VMEM(routed, LOW), pltpu.VMEM(routed, LOW), pltpu.VMEM(routed, LOW),
            pltpu.VMEM((rows, width), LOW), pltpu.VMEM((rows, width), LOW),
            pltpu.VMEM((depth, columns), LOW), pltpu.VMEM((depth, inner), LOW),
            pltpu.VMEM((rows + HALO, total), LOW), pltpu.VMEM((total, columns), LOW),
            pltpu.VMEM(message, LOW), pltpu.VMEM((seqs,) + message, LOW),
            pltpu.VMEM((EDGE + BLOCK, wide), WIDE), pltpu.VMEM((EDGE, wide), WIDE),
            pltpu.VMEM((inner, STATE), WIDE), pltpu.VMEM((HALO, STATE), WIDE),
            DMA((2, seqs)), DMA((2, seqs)),
            DMA((seqs,)), DMA((seqs,)), DMA((seqs,)), DMA((seqs,)), DMA((seqs,)), DMA((seqs,)),
            DMA((seqs,)), DMA((seqs,)), DMA((seqs,)), DMA((line,)), DMA((line,)), DMA((4,)), DMA((7,)),
            DMA((chunks, 2, line)), DMA((chunks, line)), DMA((2, line)), DMA((line,)),
        ],
        compiler_params=pltpu.CompilerParams(
            collective_id=0, has_side_effects=True, vmem_limit_bytes=VMEM_LIMIT, dimension_semantics=("arbitrary",)
        ),
        name="front",
    )(give, take, flags, *operands, *small)


def conv_grad(d_act, conv):
    sig = sigmoid(conv)
    return d_act * (sig * (1.0 + conv * (1.0 - sig)))


class Stream:
    def __init__(self, view, slots, sems):
        self.view, self.slots, self.sems = view, slots, sems

    def copy(self, block, turn):
        slot = lax.rem(turn, 2)
        return pltpu.make_async_copy(self.view(block), self.slots.at[slot], self.sems.at[slot])

    def start(self, block, turn):
        self.copy(block, turn).start()

    def wait(self, block, turn):
        self.copy(block, turn).wait()

    def at(self, turn):
        return self.slots.at[lax.rem(turn, 2)]


class Fold:
    def __init__(self, line, part, got, relay, sent, arrived, relayed):
        self.line, self.part, self.got, self.relay = line, part, got, relay
        self.sent, self.arrived, self.relayed = sent, arrived, relayed
        self.mine = mine = lax.axis_index("head")
        self.merges = line == 4
        low = mine < 2
        self.is_end = (mine == 0) | (mine == line - 1)
        self.end, self.mid = jnp.where(low, 0, 3), jnp.where(low, 1, 2)
        self.next, self.far = jnp.where(low, 2, 1), jnp.where(low, 3, 0)

    def others(self, body):
        @pl.loop(1, self.line)
        def _(n):
            body(lax.rem(self.mine + n, self.line))

    def chunk(self, rows, piece, chunk, to, way):
        return remote(
            self.part(chunk, rows), self.got.at[self.mine, rows], self.sent.at[way, piece],
            self.arrived.at[self.mine, piece], {"head": to},
        )

    def hand(self, rows, piece, chunk, which):
        return remote(
            self.part(chunk, rows), self.relay.at[which, rows], self.sent.at[1 + which, piece],
            self.relayed.at[which, piece], {"head": self.mid},
        )

    def landed(self, rows, piece, source):
        slot = self.got.at[source, rows]
        return remote(slot, slot, self.sent.at[0, piece], self.arrived.at[source, piece], {"head": source})

    def send_far(self, rows, piece):
        if not self.merges:
            if self.line > 1:
                self.others(lambda to: self.chunk(rows, piece, to, to, to).start())
            return

        @pl.when(self.is_end)
        def _():
            self.hand(rows, piece, self.far, 1).start()
            self.hand(rows, piece, self.next, 0).start()

    def send_near(self, rows, piece):
        if self.merges:
            near = jnp.where(self.is_end, self.mid, self.end)
            self.chunk(rows, piece, near, near, 0).start()

    def merge(self, rows, piece):
        if self.merges:

            @pl.when(jnp.logical_not(self.is_end))
            def _():
                for which, chunk in ((1, self.far), (0, self.next)):
                    self.hand(rows, piece, chunk, which).wait_recv()
                    own = self.part(chunk, rows)
                    own[...] = (own[...].astype(WIDE) + self.relay[which, rows].astype(WIDE)).astype(LOW)
                    self.chunk(rows, piece, chunk, chunk, 1 + which).start()

    def drain(self, rows, piece):
        if not self.merges:
            if self.line > 1:
                self.others(lambda to: self.chunk(rows, piece, to, to, to).wait_send())
                self.others(lambda source: self.landed(rows, piece, source).wait_recv())
            return
        for way in range(3):
            self.chunk(rows, piece, self.mid, self.mid, way).wait_send()
        for source in (jnp.where(self.is_end, self.mid, self.end), self.next):
            self.landed(rows, piece, source).wait_recv()

    def total(self, rows, ref):
        sum_ = self.part(self.mine, rows)[...].astype(WIDE)
        if self.merges:
            first = jnp.where(self.is_end, self.mid, self.end)
            return sum_ + ref[first, rows].astype(WIDE) + ref[self.next, rows].astype(WIDE)
        for n in range(1, self.line):
            sum_ = sum_ + ref[lax.rem(self.mine + n, self.line), rows].astype(WIDE)
        return sum_


class Halved:
    def __init__(self, seqs, src, pair, got, sems):
        self.chips, self.src, self.pair, self.got = seqs // 2, src, pair, got
        self.depth = pair.shape[1]
        self.pair_sent, self.pair_got, self.sent, self.arrived = [sems.at[n] for n in range(4)]
        self.me = lax.axis_index("seq")
        self.core = lax.rem(self.me, 2)
        self.chip = lax.div(self.me, 2)

    def rows(self, chip, core):
        return pl.ds(pl.multiple_of((2 * chip + core) * self.depth, self.depth), self.depth)

    def give(self, chip):
        return remote(
            self.src.at[self.rows(chip, 1 - self.core)], self.pair.at[chip], self.pair_sent.at[chip],
            self.pair_got.at[chip], {"seq": 2 * self.chip + 1 - self.core},
        )

    def send(self, chip, slot):
        return remote(
            self.src.at[self.rows(chip, self.core)], self.got.at[slot], self.sent.at[chip], self.arrived.at[slot],
            {"seq": 2 * chip + self.core},
        )

    def kept(self):
        return pltpu.make_async_copy(
            self.src.at[self.rows(self.chip, self.core)], self.got.at[self.chip], self.sent.at[self.chip]
        )

    def begin(self):
        pl.loop(0, self.chips)(lambda chip: self.give(chip).start())

    def combine(self):
        def add(chip):
            rows = self.rows(chip, self.core)
            self.give(chip).wait_recv()
            self.src[rows, :] = (self.src[rows, :].astype(WIDE) + self.pair[chip].astype(WIDE)).astype(LOW)

        @pl.loop(1, self.chips)
        def _(n):
            chip = lax.rem(self.chip + n, self.chips)
            add(chip)
            self.send(chip, self.chip).start()

        add(self.chip)
        self.kept().start()

    def drain(self):
        @pl.loop(1, self.chips)
        def _(n):
            other = lax.rem(self.chip + n, self.chips)
            self.send(other, other).wait()

        self.kept().wait()
        pl.loop(0, self.chips)(lambda chip: self.give(chip).wait_send())


def core_kernel(
    seqs, line, heads, blocks, roomy, flags, give,
    gate_in, part_in, act_in, cum_in, raw_in, local_in, conv_in, pre_in, normed_in, u_in, g_part, r_in, w_in,
    state_in, postnorm, vec, prenorm, kernels, filters, rim,
    out_recv, grad_recv, out_far, dx_far, early_got, dw_got, addr_got, small_got,
    gate_b, part_b, read_b, cum_b, local_b, normed_b, act_b, raw_b, conv_b, pre_b, before_b, u_b, stream_sems,
    r_t, w, ssd_s, din_s, dssd_s, dgate_s, ds_s, starts, q, state, prod, g_buf, out_part, back_slots, back_msg,
    relay, dx_relay, out_near, dx_near, sums,
    totals, gread, ggate, early_low, early_pair, gpost, tiny, d_conv, d_step, after, edge_own, edge_got, ext,
    keep_conv, keep_step, keep_normed, keep_u,
    taps_g, bias_g, dw, dw_low, dw_pair, da_low, da_pair, da_got, da_send, pn, zs_send, zs_got, small, result, fin_send,
    back_sent, back_sem, back_passed, sum_sent, sum_sem, line_sent, line_sem, load_sem, out_sent, out_sem, out_relayed,
    early_sems, dw_sems, da_sems, dx_sent, dx_sem, dx_relayed, edge_sent, edge_sem, zs_sent, zs_sem, da_sent, da_sem, small_sent,
    small_sem, fin_sent, fin_sem, own_sem, weight_sem, residual_sem,
):
    me, mine = lax.axis_index("seq"), lax.axis_index("head")
    inner = r_t.shape[1]
    wide = act_b.shape[2]
    width = out_part.shape[2]
    depth = early_got.shape[1]
    rows = ssd_s.shape[0]
    size = 2 * STATE // line
    chunks = line_sem.shape[0]
    per = blocks // chunks
    back_plane = Plane(seqs, lambda s: back_slots.at[s], back_sent, back_sem, back_passed, way=-1)
    out_got, dx_got = (out_near, dx_near) if roomy else (out_far, dx_far)

    def group_rows(b):
        return pl.ds(pl.multiple_of(b * GROUP, GROUP), GROUP)

    def rows_of(device):
        return pl.ds(pl.multiple_of(device * depth, depth), depth)

    def shard_of(ref, shard):
        return ref.at[:, pl.ds(pl.multiple_of(shard * width, LANES), width)]

    def chunk_rows(n):
        return pl.ds(pl.multiple_of(n * (rows // chunks), rows // chunks), rows // chunks)

    def g_line(n):
        return Line(line, g_buf.at[chunk_rows(n)], width, line_sent.at[n], line_sem.at[n])

    def by_group(ref, first=0, columns=None):
        if columns is None:
            return lambda b: ref.at[group_rows(b)]
        return lambda b: ref.at[group_rows(b), pl.ds(first, columns)]

    def all_line(body):
        if line > 1:

            @pl.loop(1, line)
            def _(n):
                body(lax.rem(mine + n, line))

    def all_seq(body):
        @pl.loop(1, seqs)
        def _(n):
            body(lax.rem(me + n, seqs))

    def before_rows(b):
        start = jnp.maximum(b * GROUP - HALO, 0)
        return pre_in.at[pl.ds(pl.multiple_of(start, HALO), HALO)]

    views = (
        (by_group(gate_in), gate_b), (by_group(part_in), part_b), (by_group(act_in, inner + STATE, STATE), read_b),
        (by_group(cum_in), cum_b), (lambda b: local_in.at[b], local_b), (by_group(normed_in), normed_b),
        (by_group(act_in), act_b), (by_group(raw_in), raw_b), (by_group(conv_in), conv_b), (by_group(pre_in), pre_b),
        (before_rows, before_b), (by_group(u_in), u_b),
    )
    gate_f, part_f, read_f, cum_f, local_f, normed_f, act_f, raw_f, conv_f, pre_f, before_f, u_f = [
        Stream(view, slots, stream_sems.at[n]) for n, (view, slots) in enumerate(views)
    ]

    def forwards(turn):
        return turn

    def backwards(turn):
        return blocks - 1 - turn

    def begin(streams, order):
        for stream in streams:
            stream.start(order(0), 0)

    def step(streams, order, turn, following):
        @pl.when(turn + 1 < blocks)
        def _():
            for stream in streams:
                stream.start(order(turn + 1), turn + 1)

        if following is not None:
            pl.when(turn + 1 == blocks)(lambda: begin(*following))
        for stream in streams:
            stream.wait(order(turn), turn)

    first_phase = ((gate_f, part_f, read_f, cum_f, local_f), forwards)
    norm_phase = ((gate_f,), forwards)
    gate_phase = ((gate_f, read_f, cum_f), forwards)
    scan_phase = ((gate_f, normed_f, act_f, cum_f, raw_f), forwards)
    last_phase = ((act_f, cum_f, raw_f, conv_f, pre_f, before_f, normed_f, u_f), backwards)

    def each_load(body):
        def load(shard, n):
            return pltpu.make_async_copy(shard_of(g_part, shard), shard_of(g_buf, shard), load_sem.at[n])

        for n, away in enumerate((0, -1, 1)):
            if abs(away) < line:
                there = (mine + away >= 0) & (mine + away < line)
                pl.when(there)(lambda: body(load(mine + away, n)))

    def sum_copy(to, slot):
        return remote(sums.at[mine], sums.at[slot], sum_sent.at[to], sum_sem.at[slot], {"head": to})

    early_sum = Halved(seqs, early_low, early_pair, early_got, early_sems)
    dw_sum = Halved(seqs, dw_low, dw_pair, dw_got, dw_sems)
    da_sum = Halved(seqs, da_low, da_pair, da_got, da_sems)
    out_fold = Fold(
        line, lambda z, at: out_part.at[z, at], out_got, relay, out_sent, out_sem, out_relayed
    )
    dx_fold = Fold(
        line, lambda z, at: shard_of(g_buf.at[at], z), dx_got, dx_relay, dx_sent, dx_sem, dx_relayed
    )
    short_piece = (pl.ds(rows - GROUP, GROUP - HALO), blocks - 1)
    edge_piece = (pl.ds(rows - HALO, HALO), blocks)

    def each_piece(body):
        body(*short_piece)

        @pl.loop(1, blocks)
        def _(turn):
            b = blocks - 1 - turn
            body(group_rows(b), b)

        body(*edge_piece)

    def edge_copy(to):
        return remote(edge_own, edge_got, edge_sent, edge_sem, {"seq": to})

    def zs_copy(to, slot):
        return remote(zs_send.at[to], zs_got.at[slot], zs_sent.at[to], zs_sem.at[slot], {"head": to})

    def da_copy(to, slot):
        return remote(da_send.at[to], addr_got.at[slot], da_sent.at[to], da_sem.at[slot], {"head": to})

    def small_copy(to, slot):
        return remote(small, small_got.at[slot], small_sent.at[to], small_sem.at[slot], {"seq": to})

    arrivals = (out_recv, grad_recv)

    def fin_copy(which, to, slot):
        return remote(
            fin_send.at[to], arrivals[which].at[slot], fin_sent.at[which, to], fin_sem.at[which, slot],
            {"seq": to},
        )

    own_copies = {
        "addr": pltpu.make_async_copy(da_send.at[mine], addr_got.at[mine], own_sem.at[0]),
        "small": pltpu.make_async_copy(small, small_got.at[me], own_sem.at[1]),
        "fin0": pltpu.make_async_copy(fin_send.at[me], out_recv.at[me], own_sem.at[2]),
        "fin1": pltpu.make_async_copy(fin_send.at[me], grad_recv.at[me], own_sem.at[3]),
    }

    def route(which):
        def send(to):
            fin_send[to] = result[give[to]]
            fin_copy(which, to, me).start()

        all_seq(send)
        fin_send[me] = result[give[me]]
        own_copies["fin%d" % which].start()

    def fetch(src):
        if not roomy:
            all_line(lambda z: pltpu.make_async_copy(src.at[z], out_part.at[z], load_sem.at[0]).start())
            all_line(lambda z: pltpu.make_async_copy(src.at[z], out_part.at[z], load_sem.at[0]).wait())

    row = lax.broadcasted_iota(jnp.int32, (GROUP, LANES), 0)
    lane = lax.broadcasted_iota(jnp.int32, (GROUP, LANES), 1)
    spread_m, collect = head_rows(inner), head_columns(inner)
    lower_mask = ones_before(BLOCK)
    top, low = slice(0, BLOCK), slice(BLOCK, GROUP)

    def entry_of(b, cum_v):
        gone_on = flags[2 * b] * jnp.where(row < BLOCK, 1.0, flags[2 * b + 1])
        return to_columns(jnp.exp(cum_v) * gone_on, spread_m)

    def carry_of(b, cum_t):
        return jnp.exp(cum_t[:, GROUP - 1 : GROUP]) * (flags[2 * b] * flags[2 * b + 1])

    def row_stats(b):
        stats = jnp.concatenate([totals[b], jnp.zeros((LANES - EDGE, GROUP), WIDE)], axis=0).T
        return lax.rsqrt(stats[:, 0:1] / INNER + EPS), stats[:, 1:2]

    def gated_of(ssd, turn):
        gate_v = gate_f.at(turn)[...]
        return ssd * (gate_v * sigmoid(gate_v))

    begin(*first_phase)
    fetch_r = pltpu.make_async_copy(r_in, r_t, weight_sem.at[0])
    fetch_w = pltpu.make_async_copy(w_in, w, weight_sem.at[1])
    fetch_r.start()
    greet(seqs, line)
    for n in range(chunks):
        g_line(n).hop(1, take=False, source=lambda shard: shard_of(g_part.at[chunk_rows(n)], shard))
    each_load(lambda copy: copy.start())
    fetch_w.start()
    state[...] = state_in[...]
    fetch_r.wait()

    def out_part_done(b):
        if out_fold.merges:
            pl.when(b < blocks - 1)(lambda: out_fold.send_far(group_rows(b), b))

    @pl.loop(0, blocks)
    def _(b):
        step(*first_phase, b, norm_phase)
        here = group_rows(b)
        cum_v = cum_f.at(b)[...]
        start = state[...]
        starts[b] = start
        ssd = part_f.at(b)[...] + entry_of(b, cum_v) * nt(read_f.at(b)[...], start.astype(LOW))
        ssd_s[here, :] = ssd
        state[...] = carry_columns(carry_of(b, cum_v.T), collect) * start + local_f.at(b)[...]
        out = nt((gated_of(ssd, b) * postnorm[...]).astype(LOW), r_t[...])
        for z in range(line):
            out_part[z, here] = out[:, z * width : (z + 1) * width].astype(LOW)
        out_part_done(b)

    for hop in range(2, line - 1):
        for n in range(chunks):
            g_line(n).hop(hop)
    each_load(lambda copy: copy.wait())
    fetch_w.wait()

    @pl.loop(0, blocks)
    def _(b):
        step(*norm_phase, b, gate_phase)
        here = group_rows(b)
        if line > 1:
            pl.when(lax.rem(b, per) == 0)(lambda: g_line(lax.div(b, per)).hop(line - 1))
        gated = gated_of(ssd_s[here, :], b)
        d_inner = nn(g_buf[here, :], r_t[...])
        din_s[here, :] = d_inner
        squares = jnp.sum(gated * gated, axis=1, keepdims=True)
        dots = jnp.sum(gated * postnorm[...] * d_inner, axis=1, keepdims=True)
        both = jnp.where(lane == 0, squares, jnp.where(lane == 1, dots, 0.0)).T
        sums[mine, b] = both[:EDGE]

    all_line(lambda to: sum_copy(to, mine).start())
    for n in range(chunks):
        g_line(n).finish(None, range(1, line - 1))
    for ref in (gread, ggate, gpost, state, tiny, taps_g, bias_g, dw, pn):
        ref[...] = jnp.zeros_like(ref)
    prod[...] = jnp.ones_like(prod)
    all_line(lambda other: sum_copy(other, other).wait())
    totals[...] = jnp.sum(sums[...], axis=0)

    if out_fold.merges:
        out_fold.send_far(group_rows(blocks - 1), blocks - 1)
        pl.loop(0, blocks)(lambda b: out_fold.send_near(group_rows(b), b))

    def residual(n):
        at = pl.ds(pl.multiple_of(n * BLOCK, BLOCK), BLOCK)
        columns = pl.ds(pl.multiple_of(mine * width, LANES), width)
        return pltpu.make_async_copy(u_in.at[at, columns], result.at[n], residual_sem.at[n])

    pl.loop(0, 2 * blocks)(lambda n: residual(n).start())

    def norm_back(b, turn):
        here = group_rows(b)
        inv, dot = row_stats(b)
        gate_v = gate_f.at(turn)[...]
        sig = sigmoid(gate_v)
        ssd = ssd_s[here, :]
        return gate_v, sig, ssd, ssd * (gate_v * sig), inv, dot

    @pl.loop(0, blocks)
    def _(b):
        step(*gate_phase, b, scan_phase)
        here = group_rows(b)
        cum_v = cum_f.at(b)[...]
        gate_v, sig, ssd, gated, inv, dot = norm_back(b, b)
        d_inner = din_s[here, :]
        d_gated = (inv * postnorm[...]) * d_inner - gated * (inv * inv * inv / INNER * dot)
        gpost[...] += jnp.sum(d_inner * (gated * inv), axis=0, keepdims=True)
        d_ssd = (d_gated * (gate_v * sig)).astype(LOW)
        dssd_s[here, :] = d_ssd
        dgate_s[here, :] = (d_gated * ssd * sig * (1.0 + gate_v * (1.0 - sig))).astype(LOW)
        query_grad = (d_ssd.astype(WIDE) * entry_of(b, cum_v)).astype(LOW)
        found = tn(query_grad, read_f.at(b)[...])
        q[b] = found
        state[...] += carry_columns(prod[...], collect) * found
        prod[...] = prod[...] * carry_of(b, cum_v.T)

    back_msg[:inner, :] = state[...].astype(LOW)
    back_msg[inner:, :] = jnp.broadcast_to(prod[:HALO], (HALO, STATE)).astype(LOW)
    back_plane.start(back_msg)

    if out_fold.merges:

        @pl.when(jnp.logical_not(out_fold.is_end))
        def _():
            @pl.loop(0, blocks - 1)
            def _(b):
                out_fold.merge(group_rows(b), b)

    else:
        pl.loop(0, blocks)(lambda b: out_fold.send_far(group_rows(b), b))

    @pl.loop(0, blocks)
    def _(b):
        step(*scan_phase, b, last_phase)
        here = group_rows(b)
        second = flags[2 * b + 1]
        act = act_f.at(b)
        cum_v = cum_f.at(b)[...]
        cum_t = cum_v.T
        steps, _, _ = step_terms(raw_f.at(b)[...], heads)
        steps_t = steps.T
        write = act[:, inner : inner + STATE]
        read_v = act[:, inner + STATE :]
        s00 = jnp.where(lower_mask, nt(read_v[top], write[top]), 0.0)
        s10 = nt(read_v[low], write[top]) * second
        s11 = jnp.where(lower_mask, nt(read_v[low], write[low]), 0.0)

        def decay_of(head, t, s):
            decay = jnp.exp(jnp.minimum(cum_v[t, head : head + 1] - cum_t[head : head + 1, s], 0.0))
            return decay * steps_t[head : head + 1, s]

        ds00 = jnp.zeros((BLOCK, BLOCK), WIDE)
        ds10 = jnp.zeros((BLOCK, BLOCK), WIDE)
        ds11 = jnp.zeros((BLOCK, BLOCK), WIDE)
        for pair in range(inner // LANES):
            columns = slice(pair * LANES, (pair + 1) * LANES)
            values = act[:, columns]
            dys = pair_lanes(dssd_s[here, columns])
            m00, m10, m11 = [], [], []
            for k in range(2):
                head = 2 * pair + k
                l00, l10, l11 = decay_of(head, top, top), decay_of(head, low, top), decay_of(head, low, low)
                m00.append((s00 * l00).astype(LOW))
                m10.append((s10 * l10).astype(LOW))
                m11.append((s11 * l11).astype(LOW))
                ds00 = ds00 + nt(dys[k][top], values[top]) * l00
                ds10 = ds10 + nt(dys[k][low], values[top]) * l10
                ds11 = ds11 + nt(dys[k][low], values[low]) * l11
            v0 = tn(
                jnp.concatenate([m00[0], m10[0], m00[1], m10[1]], axis=0), jnp.concatenate([dys[0], dys[1]], axis=0)
            )
            v1 = tn(
                jnp.concatenate([m11[0], m11[1]], axis=0), jnp.concatenate([dys[0][low], dys[1][low]], axis=0)
            )
            din_s[here, columns] = jnp.concatenate([v0, v1], axis=0)
        ds_s[here, :] = jnp.concatenate(
            [
                jnp.concatenate([jnp.where(lower_mask, ds00, 0.0), jnp.zeros((BLOCK, BLOCK), WIDE)], axis=1),
                jnp.concatenate([ds10 * second, jnp.where(lower_mask, ds11, 0.0)], axis=1),
            ],
            axis=0,
        ).astype(LOW)

        gated, inv = norm_back(b, b)[3:5]
        inner_normed = (gated * inv * postnorm[...]).astype(LOW)
        gread[...] += tn(g_buf[here, :], inner_normed)
        ggate[...] += tn(normed_f.at(b)[...], dgate_s[here, :])

        @pl.when(b == blocks // 2)
        def _():
            back_plane.relay()

    early_low[:, :inner] = gread[...].astype(LOW)
    early_low[:, inner:] = ggate[...].astype(LOW)
    early_sum.begin()
    out_fold.merge(group_rows(blocks - 1), blocks - 1)
    back_plane.finish(back_msg)
    state[...] = fold_states(back_slots, collect, inner, seqs - 1, me, -1, jnp.zeros((inner, STATE), WIDE))

    taps = jnp.concatenate([kernels[...], filters[...]], axis=1)
    scale = -jnp.exp(vec[1:2, :])
    through_w = to_columns(jnp.broadcast_to(vec[2:3, :], (EDGE, LANES)), spread_m)[0:1]

    def scan_back(b, turn):
        here = group_rows(b)
        first, second = flags[2 * b], flags[2 * b + 1]
        act, conv = act_f.at(turn), conv_f.at(turn)
        cum_v = cum_f.at(turn)[...]
        steps, sig, ratio = step_terms(raw_f.at(turn)[...], heads)
        last = cum_v[GROUP - 1 : GROUP, :]
        write = act[:, inner : inner + STATE]
        read_v = act[:, inner + STATE :]
        end = state[...]
        end_low = end.astype(LOW)
        start = starts[b]
        state[...] = carry_columns(carry_of(b, cum_v.T), collect) * end + q[b]
        weight = steps * jnp.exp(last - cum_v) * jnp.where(row < BLOCK, second, 1.0)
        weight_w = to_columns(weight, spread_m)
        d_ssd = dssd_s[here, :]
        dy_f = d_ssd.astype(WIDE)
        values_f = act[:, :inner].astype(WIDE)
        d_query = (dy_f * entry_of(b, cum_v)).astype(LOW)
        tail = nt(write, end_low) * weight_w
        whole = din_s[here, :] + tail
        d_conv[:, :inner] = conv_grad(whole + through_w * dy_f, conv[:, :inner])
        packed = (values_f * weight_w).astype(LOW)
        ds = ds_s[here, :]
        d_read = nn(ds, write) + nn(d_query, start.astype(LOW))
        d_write = tn(ds, read_v) + nn(packed, end_low)
        d_conv[:, inner : inner + STATE] = conv_grad(d_write, conv[:, inner : inner + STATE])
        d_conv[:, inner + STATE :] = conv_grad(d_read, conv[:, inner + STATE :])

        own = to_heads(dy_f * values_f, collect)
        r1 = to_heads(dy_f * ssd_s[here, :], collect) - vec[2:3, :] * own
        by_value = to_heads(values_f * whole, collect)
        tail_sum = jnp.sum(tail * values_f, axis=0, keepdims=True)
        tail_row = to_heads(jnp.broadcast_to(tail_sum, (EDGE, inner)), collect)[0:1]
        high, rest = halves(end * start)
        ones = jnp.ones((EDGE, STATE), LOW)
        carry_grad = to_heads(nt(ones, high) + nt(ones, rest), collect)[0:1]
        d_last = tail_row + carry_grad * (jnp.exp(last) * (first * second))
        d_cum = r1 - by_value + jnp.where(row == GROUP - 1, d_last, 0.0)
        d_rate = sum_after(d_cum)
        d_raw = d_rate * scale * sig + by_value * ratio
        d_step[...] = d_raw.astype(LOW)
        tiny[0:1, :] += jnp.sum(d_raw, axis=0, keepdims=True)
        tiny[1:2, :] += jnp.sum(d_rate * steps, axis=0, keepdims=True) * scale
        tiny[2:3, :] += jnp.sum(own, axis=0, keepdims=True)

    def conv_back(ref, count):
        total = taps[TAPS - 1 : TAPS] * ref[pl.ds(0, count), :]
        for tap in range(TAPS - 1):
            total = total + taps[tap : tap + 1] * ref[pl.ds(TAPS - 1 - tap, count), :]
        return total.astype(LOW)

    def input_back(d_pre, step_grad, gate_grad, u_rows):
        d_normed = (
            nt(gate_grad, w[:, :inner])
            + nt(d_pre, w[:, inner : inner + wide])
            + nt(step_grad, w[:, inner + wide :])
        )
        rows_f = u_rows.astype(WIDE)
        inv = lax.rsqrt(jnp.mean(rows_f * rows_f, axis=1, keepdims=True) + EPS)
        gained = d_normed * prenorm[...]
        dot = jnp.sum(gained * rows_f, axis=1, keepdims=True)
        grad = gained * inv - rows_f * (inv * inv * inv / D * dot)
        return grad.astype(LOW), d_normed * (rows_f * inv)

    def rows_back(b, turn, final):
        grad_c = d_conv[...]
        pre_v = pre_f.at(turn)[...].astype(WIDE)
        before = jnp.where(b == 0, rim[...], before_f.at(turn)[HALO - EDGE :, :].astype(WIDE))
        bias_g[...] += jnp.sum(grad_c, axis=0, keepdims=True)
        parts = []
        for half in range(2):
            part_rows = slice(half * BLOCK, (half + 1) * BLOCK)
            tile = grad_c[part_rows]
            ext[0:EDGE, :] = (before if half == 0 else pre_v[BLOCK - EDGE : BLOCK]) * flags[2 * b + half]
            ext[EDGE:, :] = pre_v[part_rows]
            for tap in range(TAPS):
                taps_g[tap : tap + 1, :] += jnp.sum(
                    tile * ext[pl.ds(EDGE - (TAPS - 1) + tap, BLOCK), :], axis=0, keepdims=True
                )
            ext[:BLOCK, :] = tile
            if half == 0:
                ext[BLOCK:, :] = grad_c[BLOCK : BLOCK + EDGE] * flags[2 * b + 1]
            elif final:
                ext[BLOCK:, :] = jnp.zeros((EDGE, wide), WIDE)
            else:
                ext[BLOCK:, :] = after[...] * flags[2 * b + 2]
            parts.append(conv_back(ext, BLOCK))
        d_pre = jnp.concatenate(parts, axis=0)
        step_grad = d_step[...]
        normed_v = normed_f.at(turn)[...]
        u_v = u_f.at(turn)
        done = lax.broadcasted_iota(jnp.int32, (GROUP, 1), 0) < GROUP - HALO
        if final:
            d_pre = jnp.where(done, d_pre, jnp.zeros_like(d_pre))
            keep_conv[:HALO, :] = grad_c[GROUP - HALO :]
            keep_step[...] = step_grad[GROUP - HALO :]
            keep_normed[...] = normed_v[GROUP - HALO :]
            keep_u[...] = u_v[GROUP - HALO :, :]
        dw[:, :wide] += tn(normed_v, d_pre)
        dw[:, wide:] += tn(normed_v, step_grad)
        grad, gain = input_back(d_pre, step_grad, dgate_s[group_rows(b), :], u_v[...])
        pn[...] += jnp.sum(jnp.where(done, gain, 0.0) if final else gain, axis=0, keepdims=True)
        g_buf[group_rows(b), :] = grad
        after[...] = grad_c[0:EDGE]

    def outputs_home():
        pl.loop(0, 2 * blocks)(lambda n: residual(n).wait())
        pl.loop(0, blocks)(lambda b: out_fold.drain(group_rows(b), b))
        fetch(out_far)

        @pl.loop(0, blocks)
        def _(b):
            inv, _ = row_stats(b)
            total = out_fold.total(group_rows(b), out_near if roomy else out_part) * inv
            result[2 * b] = (result[2 * b].astype(WIDE) + total[:BLOCK]).astype(LOW)
            result[2 * b + 1] = (result[2 * b + 1].astype(WIDE) + total[BLOCK:]).astype(LOW)

        route(0)
        own_g.start()

    own_g = pltpu.make_async_copy(shard_of(g_part, mine), out_part.at[mine], load_sem.at[5])

    step(*last_phase, 0, None)
    scan_back(blocks - 1, 0)
    rows_back(blocks - 1, 0, True)
    dx_fold.send_far(*short_piece)
    early_sum.combine()

    @pl.loop(1, blocks)
    def _(turn):
        b = blocks - 1 - turn
        step(*last_phase, turn, None)
        scan_back(b, turn)

        @pl.when(b == 0)
        def _():
            edge_own[...] = d_conv[0:EDGE, :]
            edge_copy(lax.rem(me + seqs - 1, seqs)).start()

        rows_back(b, turn, False)
        dx_fold.send_far(group_rows(b), b)

        @pl.when(turn == 2)
        def _():
            dx_fold.merge(*short_piece)

        pl.when(turn == blocks - 1)(outputs_home)

        @pl.when(turn > 2)
        def _():
            dx_fold.merge(group_rows(b + 2), b + 2)

    edge_copy(lax.rem(me + 1, seqs)).wait()
    keep_conv[HALO:, :] = edge_got[...] * flags[2 * blocks]
    d_edge = conv_back(keep_conv, HALO)
    dw[:, :wide] += tn(keep_normed[...], d_edge)
    grad, gain = input_back(d_edge, keep_step[...], dgate_s[pl.ds(rows - HALO, HALO), :], keep_u[...])
    pn[...] += jnp.sum(gain, axis=0, keepdims=True)
    g_buf[pl.ds(rows - HALO, HALO), :] = grad
    dx_fold.send_far(*edge_piece)

    for z in range(line):
        slab = z * size // LANES * LANES
        zs_send[z] = jnp.zeros(zs_send.shape[1:], WIDE)
        zs_send[z, 0:1, :] = pn[:, z * width : (z + 1) * width]
        zs_send[z, EDGE : EDGE + TAPS, :LANES] = taps_g[0:TAPS, inner + slab : inner + slab + LANES]
        zs_send[z, EDGE + TAPS : EDGE + TAPS + 1, :LANES] = bias_g[:, inner + slab : inner + slab + LANES]
    zs_got[mine] = zs_send[mine]
    all_line(lambda to: zs_copy(to, mine).start())

    each_piece(dx_fold.send_near)

    if blocks > 3:
        dx_fold.merge(group_rows(1), 1)

    da_low[...] = dw[:, inner:wide].astype(LOW)
    da_sum.begin()
    dw_low[:, :inner] = dw[:, :inner].astype(LOW)
    dw_low[:, inner:] = dw[:, wide:].astype(LOW)
    dw_sum.begin()

    if blocks > 3:
        dx_fold.merge(group_rows(0), 0)
    elif blocks == 2:
        dx_fold.merge(*short_piece)
        dx_fold.merge(group_rows(0), 0)
    dx_fold.merge(*edge_piece)
    da_sum.combine()
    dw_sum.combine()

    all_line(lambda other: zs_copy(other, other).wait())
    from_line = jnp.sum(zs_got[...], axis=0)
    small[...] = jnp.zeros_like(small)
    small[0:TAPS, :inner] = taps_g[0:TAPS, :inner]
    small[0:TAPS, inner:] = from_line[EDGE : EDGE + TAPS, :LANES]
    small[4:5, :inner] = bias_g[:, :inner]
    small[4:5, inner:] = from_line[EDGE + TAPS : EDGE + TAPS + 1, :LANES]
    small[5:6, :inner] = gpost[...]
    small[6:7, :width] = from_line[0:1]
    for n in range(3):
        small[7:8, n * LANES : (n + 1) * LANES] = tiny[n : n + 1, :]
    own_copies["small"].start()
    all_seq(lambda to: small_copy(to, me).start())

    da_sum.drain()
    from_plane = da_got[0].astype(WIDE)
    for n in range(1, seqs // 2):
        from_plane = from_plane + da_got[n].astype(WIDE)
    for z in range(line):
        slab = z * size // LANES * LANES
        da_send[z] = from_plane[:, slab : slab + LANES]
    own_copies["addr"].start()
    all_line(lambda to: da_copy(to, mine).start())

    all_seq(lambda other: fin_copy(0, other, other).wait())
    own_copies["fin0"].wait()
    each_piece(dx_fold.drain)
    fetch(dx_far)
    own_g.wait()

    @pl.loop(0, blocks)
    def _(b):
        here = group_rows(b)
        total = dx_fold.total(here, dx_near if roomy else out_part)
        done = (out_part[mine, here].astype(WIDE) + total).astype(LOW)
        result[2 * b] = done[:BLOCK]
        result[2 * b + 1] = done[BLOCK:]

    route(1)
    early_sum.drain()
    dw_sum.drain()
    all_line(lambda other: da_copy(other, other).wait())
    all_seq(lambda other: fin_copy(1, other, other).wait())
    all_seq(lambda other: small_copy(other, other).wait())
    for name in ("addr", "small", "fin1"):
        own_copies[name].wait()


def core(
    flags, give, gate, part, act, cum, raw, local, conv, pre, normed, u, g_part, state_in, r_t, w_all, postnorm, vec,
    prenorm, kernels, filters, rim,
):
    seqs, line = lax.axis_size("seq"), lax.axis_size("head")
    rows, inner = gate.shape
    wide = act.shape[1]
    total = g_part.shape[1]
    width = total // line
    depth = total // seqs
    blocks, tiles = rows // GROUP, rows // BLOCK
    heads = inner // HDIM
    pieces = blocks + 1
    chunks = min(blocks, 4)
    message = (inner + HALO, STATE)
    sums = (blocks, EDGE, GROUP)
    streamed = (gate, part, act, cum, raw, local, conv, pre, normed, u, g_part, r_t, w_all)
    whole = (state_in, postnorm, vec, prenorm, kernels, filters, rim)
    gather = (line, rows, width)
    nothing = (line, HALO, width)
    roomy = rows * total * 2 <= 4 << 20
    near, far = (gather, nothing) if roomy else (nothing, gather)
    relay = (2, rows if line == 4 else HALO, width)
    small = (EDGE, inner + LANES)
    ways = max(line, 3)

    def slots(*dims):
        return (2,) + dims

    buffers = (
        (slots(GROUP, inner), WIDE), (slots(GROUP, inner), WIDE), (slots(GROUP, STATE), LOW),
        (slots(GROUP, LANES), WIDE), (slots(inner, STATE), WIDE), (slots(GROUP, total), LOW),
        (slots(GROUP, wide), LOW), (slots(GROUP, LANES), WIDE), (slots(GROUP, wide), WIDE),
        (slots(GROUP, wide), LOW), (slots(HALO, wide), LOW), (slots(GROUP, total), LOW),
    )
    return pl.pallas_call(
        functools.partial(core_kernel, seqs, line, heads, blocks, roomy),
        grid=(1,),
        out_shape=(
            shape((seqs, BLOCK, width), LOW), shape((seqs, BLOCK, width), LOW), shape(far, LOW), shape(far, LOW),
            shape((seqs // 2, depth, 2 * inner), LOW), shape((seqs // 2, depth, inner + LANES), LOW),
            shape((line, depth, LANES), WIDE), shape((seqs,) + small, WIDE),
        ),
        in_specs=[SMEM_SPEC] * 2 + [ANY_SPEC] * len(streamed) + [fixed(a.shape) for a in whole],
        out_specs=(ANY_SPEC,) * 8,
        scratch_shapes=[pltpu.VMEM(dims, kind) for dims, kind in buffers] + [
            DMA((len(buffers), 2)),
            pltpu.VMEM(r_t.shape, LOW), pltpu.VMEM(w_all.shape, LOW),
            pltpu.VMEM((rows, inner), WIDE), pltpu.VMEM((rows, inner), WIDE), pltpu.VMEM((rows, inner), LOW),
            pltpu.VMEM((rows, inner), LOW), pltpu.VMEM((rows, GROUP), LOW), pltpu.VMEM((blocks, inner, STATE), WIDE),
            pltpu.VMEM((blocks, inner, STATE), WIDE), pltpu.VMEM((inner, STATE), WIDE), pltpu.VMEM((LANES, 1), WIDE),
            pltpu.VMEM((rows, total), LOW), pltpu.VMEM(gather, LOW),
            pltpu.VMEM((seqs,) + message, LOW), pltpu.VMEM(message, LOW),
            pltpu.VMEM(relay, LOW), pltpu.VMEM(relay, LOW), pltpu.VMEM(near, LOW), pltpu.VMEM(near, LOW),
            pltpu.VMEM((line,) + sums, WIDE), pltpu.VMEM(sums, WIDE),
            pltpu.VMEM((total, inner), WIDE), pltpu.VMEM((total, inner), WIDE), pltpu.VMEM((total, 2 * inner), LOW),
            pltpu.VMEM((seqs // 2, depth, 2 * inner), LOW), pltpu.VMEM((1, inner), WIDE), pltpu.VMEM((EDGE, LANES), WIDE),
            pltpu.VMEM((GROUP, wide), WIDE), pltpu.VMEM((GROUP, LANES), LOW), pltpu.VMEM((EDGE, wide), WIDE),
            pltpu.VMEM((EDGE, wide), WIDE), pltpu.VMEM((EDGE, wide), WIDE), pltpu.VMEM((BLOCK + EDGE, wide), WIDE),
            pltpu.VMEM((HALO + EDGE, wide), WIDE), pltpu.VMEM((HALO, LANES), LOW), pltpu.VMEM((HALO, total), LOW),
            pltpu.VMEM((HALO, total), LOW),
            pltpu.VMEM((EDGE, wide), WIDE), pltpu.VMEM((1, wide), WIDE), pltpu.VMEM((total, wide + LANES), WIDE),
            pltpu.VMEM((total, inner + LANES), LOW), pltpu.VMEM((seqs // 2, depth, inner + LANES), LOW),
            pltpu.VMEM((total, wide - inner), LOW), pltpu.VMEM((seqs // 2, depth, wide - inner), LOW),
            pltpu.VMEM((seqs // 2, depth, wide - inner), LOW), pltpu.VMEM((line, depth, LANES), WIDE),
            pltpu.VMEM((1, total), WIDE), pltpu.VMEM((line, 2 * EDGE, width), WIDE),
            pltpu.VMEM((line, 2 * EDGE, width), WIDE), pltpu.VMEM(small, WIDE),
            pltpu.VMEM((tiles, BLOCK, width), LOW), pltpu.VMEM((seqs, BLOCK, width), LOW),
            DMA((seqs,)), DMA((seqs,)), DMA((seqs,)), DMA((line,)), DMA((line,)), DMA((chunks, 2, line)), DMA((chunks, line)),
            DMA((6,)),
            DMA((ways, blocks)), DMA((line, blocks)), DMA((2, blocks)), DMA((4, seqs // 2)), DMA((4, seqs // 2)), DMA((4, seqs // 2)),
            DMA((ways, pieces)), DMA((line, pieces)), DMA((2, pieces)), DMA, DMA,
            DMA((line,)), DMA((line,)), DMA((line,)), DMA((line,)), DMA((seqs,)), DMA((seqs,)), DMA((2, seqs)),
            DMA((2, seqs)), DMA((4,)), DMA((2,)), DMA((tiles,)),
        ],
        compiler_params=pltpu.CompilerParams(
            collective_id=1, has_side_effects=True, vmem_limit_bytes=VMEM_LIMIT, dimension_semantics=("arbitrary",)
        ),
        name="core",
    )(flags, give, *streamed, *whole)


def finish_kernel(
    take, out_recv, grad_recv, early_got, dw_got, addr_got, small_got,
    out_o, dx_o, prenorm_o, gate_o, pay_o, addr_o, step_o, kernels_o, offsets_o, filters_o, shifts_o,
    stepbias_o, decays_o, through_o, post_o, read_o,
):
    inner, size, heads, width = gate_o.shape[1], addr_o.shape[0], step_o.shape[0], prenorm_o.shape[1]
    offset = lax.rem(lax.axis_index("head") * size, LANES)
    back_turn = lax.rem(LANES - offset, LANES)
    for k in range(out_o.shape[0]):
        out_o[k] = out_recv[take[k]]
        dx_o[k] = grad_recv[take[k]]

    def summed(ref):
        total = ref[0].astype(WIDE)
        for n in range(1, ref.shape[0]):
            total = total + ref[n].astype(WIDE)
        return total

    early = summed(early_got)
    read_o[...] = early[:, :inner].T
    gate_o[...] = early[:, inner:]
    grads = summed(dw_got)
    pay_o[...] = grads[:, :inner]
    step_o[...] = grads[:, inner:].T[:heads]
    addr_o[...] = pltpu.roll(summed(addr_got), back_turn, 1).T[:size]
    totals = jnp.sum(small_got[...], axis=0)
    kernels_o[...] = totals[0:TAPS, :inner]
    offsets_o[...] = totals[4:5, :inner]
    turned = pltpu.roll(totals[:, inner:], back_turn, 1)
    filters_o[...] = turned[0:TAPS, :size]
    shifts_o[...] = turned[4:5, :size]
    post_o[...] = totals[5:6, :inner]
    prenorm_o[...] = totals[6:7, :width]
    for n, ref in enumerate((stepbias_o, decays_o, through_o)):
        ref[...] = totals[7:8, n * LANES : n * LANES + heads]


def finish(take, out_recv, grad_recv, early_got, dw_got, addr_got, small_got):
    seqs, _, width = out_recv.shape
    tiles = take.shape[0]
    _, depth, inner = early_got.shape
    inner = inner // 2
    heads = inner // HDIM
    size = 2 * STATE // addr_got.shape[0]
    operands = (out_recv, grad_recv, early_got, dw_got, addr_got, small_got)
    outs = (
        shape((tiles, BLOCK, width), LOW), shape((tiles, BLOCK, width), LOW), shape((1, width), WIDE),
        shape((depth, inner), WIDE), shape((depth, inner), WIDE), shape((size, depth), WIDE),
        shape((heads, depth), WIDE), shape((TAPS, inner), WIDE), shape((1, inner), WIDE),
        shape((TAPS, size), WIDE), shape((1, size), WIDE), shape((1, heads), WIDE), shape((1, heads), WIDE),
        shape((1, heads), WIDE), shape((1, inner), WIDE), shape((inner, depth), WIDE),
    )
    return pl.pallas_call(
        finish_kernel,
        grid=(1,),
        out_shape=outs,
        in_specs=[SMEM_SPEC] + [fixed(a.shape) for a in operands],
        out_specs=tuple(fixed(a.shape) for a in outs),
        compiler_params=pltpu.CompilerParams(vmem_limit_bytes=VMEM_LIMIT, dimension_semantics=("arbitrary",)),
        name="finish",
    )(take, *operands)


def on_device(
    inputs,
    cotangent,
    lengths,
    placement,
    prenorm,
    gating,
    payload,
    address,
    stepping,
    kernels,
    offsets,
    filters,
    shifts,
    stepbias,
    decays,
    through,
    postnorm,
    readout,
):
    rows, width = inputs.shape
    heads = stepbias.shape[0]
    tiles = rows // BLOCK
    give_in, take_in, give_out, take_out, flags, vec = index(placement, lengths, stepbias, decays, through, tiles)
    gain, post = prenorm[None, :], postnorm[None, :]
    (
        u, normed, gate, pre, conv, act, raw, cum, part, local, state_in, rim, g_part, w_all, r_t
    ) = front(
        give_in, take_in, flags, inputs, cotangent, gating, payload, address, stepping, readout, vec, gain, kernels,
        filters, offsets[None, :], shifts[None, :]
    )
    out_recv, grad_recv, _, _, early_got, dw_got, addr_got, small_got = core(
        flags, give_out, gate, part, act, cum, raw, local, conv, pre, normed, u, g_part, state_in, r_t, w_all, post, vec,
        gain, kernels, filters, rim
    )
    (
        out, dx, prenorm_g, gate_g, pay_g, addr_g, step_g, kernels_g, offsets_g, filters_g, shifts_g, stepbias_g,
        decays_g, through_g, post_g, read_g,
    ) = finish(take_out, out_recv, grad_recv, early_got, dw_got, addr_got, small_got)
    return (
        out.reshape(rows, width),
        dx.reshape(rows, width),
        prenorm_g.reshape(-1),
        gate_g,
        pay_g,
        addr_g.T,
        step_g.T,
        kernels_g,
        offsets_g.reshape(-1),
        filters_g,
        shifts_g.reshape(-1),
        stepbias_g.reshape(-1),
        decays_g.reshape(-1),
        through_g.reshape(-1),
        post_g.reshape(-1),
        read_g,
    )


def solution(mesh):
    in_specs = (
        P("seq", "head"),
        P("seq", "head"),
        P(),
        P(),
        P(),
        P("seq", "head"),
        P("seq", "head"),
        P("seq", None),
        P("seq", "head"),
        P(None, "head"),
        P("head"),
        P(),
        P(),
        P("head"),
        P("head"),
        P("head"),
        P("head"),
        P("head", "seq"),
    )
    out_specs = (
        P("seq", "head"),
        P("seq", "head"),
        P("head"),
        P("seq", "head"),
        P("seq", "head"),
        P("seq", "head"),
        P("seq", "head"),
        P(None, "head"),
        P("head"),
        P(None, "head"),
        P("head"),
        P("head"),
        P("head"),
        P("head"),
        P("head"),
        P("head", "seq"),
    )
    return jax.shard_map(
        on_device, mesh=mesh, in_specs=in_specs, out_specs=out_specs, check_vma=False
    )
```
